32 devices in a mesh: grid: 8 (over z, core), occ: 4 (over y, x).
Axes of the slice: x: 2, y: 2, z: 4, core: 2. Of those that a mesh axis runs over, the one named last changes fastest.
Arguments:
- orbital_values: bfloat16 [2048, 16000], P('grid', 'occ'), may hold values from -6 to 6
- occupied: bfloat16 [16000, 512], P('occ', 'grid'), may hold values from -0.046875 to 0.046875
- trial: bfloat16 [16000, 512], P('occ', 'grid'), may hold values from -0.046875 to 0.046875
- point_weights: float32 [2048], P('grid'), may hold values from 0.1 to 1
- batch_sizes: int32 [64], P('grid'), may hold values from 1 to 32, 1024 in all
- significant: int32 [64, 128], P('grid', 'occ'), may hold values 0 or 1
Outputs:
- exchange: float32 [16000, 512], P('occ', 'grid')
The draws below stay inside these ranges and needn't reach their ends.
Inputs may be any that keep to these rules, and one draw needn't show every extreme that they name: `batch_sizes`: batch sizes sum to 1024 and the largest is exactly 32.
All inputs are finite; a program needn't handle non-finite values. No bound on the sum of `batch_sizes` or of `significant` on one device may be relied on, other than what follows from the above.
Results may differ from the reference program's by a relative error of at most 0.0027.
Values may be sent and summed in bfloat16 or wider, within the bound.
No kernel may reach another device: no remote copies, remote signals or barrier semaphores. Data moves between devices by JAX's collectives and lax.ppermute only.
A program may use at most 64 MiB of HBM per device.

```python
import math
import jax
import jax.numpy as jnp
import numpy as np
from jax import lax

NB = 16000
NOCC = 512
NBLOCK = 128
BCAP = 32
NBATCH = 64
NG = 2048


def plant(entries, stream_key, low, top_value):
    index_at = [jax.random.randint(jax.random.fold_in(stream_key, axis), (), 0, length) for axis, length in enumerate(entries.shape)]
    widest = entries.shape.index(max(entries.shape))
    beside = index_at[:widest] + [(index_at[widest] + 1) % entries.shape[widest]] + index_at[widest + 1:]
    return entries.at[tuple(index_at)].set(low).at[tuple(beside)].set(top_value)


def block_scale(rng, extent, pieces, smallest, top_value):
    loudness, own = 1.0, jax.random.fold_in(rng, 6)
    for dim, shards_of in pieces:
        steps = jnp.exp(jax.random.uniform(jax.random.fold_in(own, dim), (shards_of,), jnp.float32, smallest / len(pieces), top_value / len(pieces)))
        loudness = loudness * jnp.repeat(steps, extent[dim] // shards_of).reshape([-1 if axis == dim else 1 for axis in range(len(extent))])
    return loudness


def length_profile(number_of, total, reach, skew):
    weights = [(1 << 20) // math.isqrt(standing ** skew) + 1 for standing in range(2, number_of + 1)]
    rest, holding = total - reach - (number_of - 1), [1] * (number_of - 1)
    while rest > 0:
        candidates = [i for i in range(number_of - 1) if holding[i] < reach]
        whole, remaining = sum([weights[i] for i in candidates]), rest
        for i in candidates:
            addition = min(reach - holding[i], max(1, remaining * weights[i] // whole), rest)
            holding[i] = holding[i] + addition
            rest = rest - addition
    return np.array([reach] + holding)


def uneven_parts(stream_key, count, total, bound, lean):
    if count == 2:
        one = jax.random.randint(stream_key, (), max(1, total - bound), min(bound, total - 1) + 1)
        return jnp.stack([one, total - one])
    lengths = jnp.asarray(length_profile(count, total, bound, lean), jnp.int32)
    twos = (count - 1) // 2
    donor, taker = lengths[1:1 + 2 * twos:2], lengths[2:2 + 2 * twos:2]
    margin = jnp.minimum(donor - 1, bound - taker)
    passed = jax.random.randint(jax.random.fold_in(stream_key, 1), (twos,), 0, 1 << 20) % (margin + 1)
    lengths = lengths.at[1:1 + 2 * twos:2].set(donor - passed).at[2:2 + 2 * twos:2].set(taker + passed)
    return lengths[jax.random.permutation(jax.random.fold_in(stream_key, 2), count)]


def noise(rng, dims, spread, reach, split=(), kind=jnp.bfloat16):
    level = block_scale(rng, dims, split, -0.22, 0.18) if split else 1.0
    drawn = jax.random.normal(rng, dims, jnp.float32) * spread * level
    return jnp.minimum(jnp.maximum(drawn, -reach), reach).astype(kind)


def setup_inputs(seed: int = 0) -> dict:
    key_of = jax.random.split(jax.random.key(seed), 7)
    return {
        "orbital_values": noise(key_of[0], (NG, NB), 1.0, 6.0, ((0, 8), (1, 4))),
        "occupied": noise(key_of[1], (NB, NOCC), NB ** -0.5, 0.046875, ((0, 4), (1, 8))),
        "trial": noise(key_of[2], (NB, NOCC), NB ** -0.5, 0.046875, ((0, 4), (1, 8))),
        "point_weights": jnp.clip(jnp.exp(math.log(1.0) - 2.3025851 * jax.random.uniform(key_of[3], (NG,), jnp.float32) ** block_scale(key_of[3], (NG,), ((0, 8),), -0.2, 0.2)), 0.1, 1.0),
        "batch_sizes": uneven_parts(key_of[4], NBATCH, NBATCH * BCAP // 2, BCAP, 2).astype(jnp.int32),
        "significant": plant((jax.random.randint(key_of[5], (NBATCH, NBLOCK), 0, 4) < 3).astype(jnp.int32), jax.random.fold_in(key_of[5], 1), 0, 1),
    }


def screen(values, sizes, significant):
    rows, cols = values.shape
    batches = sizes.shape[0]
    blocks = significant.shape[1]
    blocked = values.reshape(batches, rows // batches, blocks, cols // blocks) * significant.astype(values.dtype)[:, None, :, None]
    position = lax.broadcasted_iota(jnp.int32, (batches, rows // batches), 1)
    live = (position < sizes[:, None]).astype(jnp.float32).reshape(rows)
    return (blocked.reshape(rows, cols), live)

def reference(orbital_values, occupied, trial, point_weights, batch_sizes, significant):
    screened, live = screen(orbital_values, batch_sizes, significant)
    orbitals = jnp.dot(screened, occupied, preferred_element_type=jnp.float32)
    response = jnp.dot(screened, trial, preferred_element_type=jnp.float32)
    density = lax.optimization_barrier(jnp.sum(orbitals * response, axis=1)) / math.sqrt(NOCC)
    kernel = ((point_weights * live)[:, None] * (density[:, None] * orbitals + response)).astype(jnp.bfloat16)
    summed = lax.dot_general(screened, kernel, (((0,), (0,)), ((), ())), preferred_element_type=jnp.float32)
    return summed / math.sqrt(NG)
```

```python
import math

import jax
import jax.numpy as jnp
from jax import lax
from jax.experimental import pallas as pl
from jax.experimental.pallas import tpu as pltpu
from jax.sharding import PartitionSpec as P

BF16, F32 = jnp.bfloat16, jnp.float32
VMEM_LIMIT = 48 * 1024 * 1024
WHOLE = pl.BlockSpec(memory_space=pltpu.VMEM)
SCALARS = pl.BlockSpec(memory_space=pltpu.SMEM)


def screen(values, sizes, significant):
    rows, cols = values.shape
    batches = sizes.shape[0]
    blocks = significant.shape[1]
    blocked = (
        values.reshape(batches, rows // batches, blocks, cols // blocks)
        * significant.astype(values.dtype)[:, None, :, None]
    )
    position = lax.broadcasted_iota(jnp.int32, (batches, rows // batches), 1)
    live = (position < sizes[:, None]).astype(jnp.float32).reshape(rows)
    return (blocked.reshape(rows, cols), live)


def any_sizes(orbital_values, occupied, trial, point_weights, batch_sizes, significant):
    screened, live = screen(orbital_values, batch_sizes, significant)
    rows = screened.shape[0]
    grid_count = lax.axis_size("grid")
    columns = occupied.shape[1]
    total = columns * grid_count
    joined = jnp.concatenate((occupied, trial), axis=1)
    panels_all = lax.all_gather(joined, "grid", axis=1, tiled=True)
    terms = jnp.dot(screened, panels_all, preferred_element_type=jnp.float32)
    stacked = (
        terms.reshape(rows, grid_count, 2, columns).transpose(0, 2, 1, 3).reshape(rows, 2, total)
    )
    weight = point_weights * live
    occ_scale = 1.0 / math.sqrt(total)
    shares = lax.psum_scatter(stacked, "occ", scatter_dimension=2, tiled=True)
    orbitals = shares[:, 0]
    response = shares[:, 1]
    density = lax.psum(jnp.sum(orbitals * response, axis=1), "occ") * occ_scale
    kernel = (weight[:, None] * (density[:, None] * orbitals + response)).astype(jnp.bfloat16)
    partial_value = lax.dot_general(
        screened,
        lax.all_gather(kernel, "occ", axis=1, tiled=True),
        (((0,), (0,)), ((), ())),
        preferred_element_type=jnp.float32,
    )
    npoints = rows * grid_count
    return lax.psum_scatter(partial_value, "grid", scatter_dimension=1, tiled=True) / math.sqrt(
        npoints
    )


def compact(mine, got, mine_sig, got_sig, mine_to, got_to, width):
    half, rows = mine.shape
    blocks = mine_sig.shape[0]

    def body(mine_ref, got_ref, msig_ref, gsig_ref, mto_ref, gto_ref, low_ref, high_ref):
        block_of = lax.broadcasted_iota(jnp.int32, (half, blocks), 0)
        first = lax.broadcasted_iota(jnp.int32, (half, blocks), 1) * width
        spread = ((block_of >= first) & (block_of < first + width)).astype(F32).astype(BF16)
        slot = lax.broadcasted_iota(jnp.int32, (rows, 2 * rows), 1)

        def part(value_ref, sig_ref, to_ref):
            kept = jnp.dot(spread, sig_ref[...], preferred_element_type=F32)
            screened = (value_ref[...].astype(F32) * kept).astype(BF16)
            place = (to_ref[...] == slot).astype(F32).astype(BF16)
            return jnp.dot(screened, place, preferred_element_type=F32)

        window = part(mine_ref, msig_ref, mto_ref) + part(got_ref, gsig_ref, gto_ref)
        low_ref[...] = window[:, :rows].astype(BF16)
        high_ref[...] = window[:, rows:].astype(BF16)

    shape = jax.ShapeDtypeStruct((half, rows), BF16)
    return pl.pallas_call(
        body,
        out_shape=(shape, shape),
        in_specs=[WHOLE] * 6,
        out_specs=(WHOLE, WHOLE),
        compiler_params=pltpu.CompilerParams(vmem_limit_bytes=VMEM_LIMIT),
        name="compact",
        cost_estimate=pl.CostEstimate(
            flops=8 * half * rows * rows, bytes_accessed=8 * half * rows, transcendentals=0
        ),
    )(mine, got, mine_sig, got_sig, mine_to, got_to)


def project(panels, windows, tile, shares, me):
    both, half = panels.shape
    piece = tile // shares
    counts = [w.shape[1] // tile for w in windows]
    tiles, number = sum(counts), len(windows)

    def body(me_ref, panels_ref, *refs):
        window_refs, out_refs, terms_ref = refs[:number], refs[number:-1], refs[-1]
        q = 0
        for s in range(number):
            terms = jnp.dot(panels_ref[...], window_refs[s][...], preferred_element_type=F32).T
            for j in range(counts[s]):
                terms_ref[...] = terms[j * tile : (j + 1) * tile].reshape(shares, piece, both)
                for d in range(shares):
                    out_refs[d][q] = terms_ref[me_ref[0] ^ d]
                q += 1

    shape = jax.ShapeDtypeStruct((tiles, piece, both), F32)
    return pl.pallas_call(
        body,
        out_shape=(shape,) * shares,
        in_specs=[SCALARS] + [WHOLE] * (1 + number),
        out_specs=(WHOLE,) * shares,
        scratch_shapes=[pltpu.VMEM((shares, piece, both), F32)],
        compiler_params=pltpu.CompilerParams(vmem_limit_bytes=VMEM_LIMIT),
        name="project",
        cost_estimate=pl.CostEstimate(
            flops=2 * both * half * tiles * tile,
            bytes_accessed=2 * half * (both + tiles * tile) + 4 * tiles * tile * both,
            transcendentals=0,
        ),
    )(me, panels, *windows)


def contract(pieces, windows, tile, me, which):
    shares = len(pieces)
    columns = pieces[0].shape[1]
    half = windows[0].shape[0]
    piece = tile // shares
    own = columns // 2
    number = len(windows)

    def body(me_ref, *refs):
        piece_refs, window_refs = refs[:shares], refs[shares : shares + number]
        out_ref, kernel_ref = refs[shares + number :]
        for d in range(shares):
            whole = piece_refs[d][...].astype(F32)
            for q in range(whole.shape[0] // piece):
                kernel_ref[q, me_ref[0] ^ d] = whole[q * piece : (q + 1) * piece]
        total, q = None, 0
        for s in range(number):
            points = windows[s].shape[1]
            mine = kernel_ref[q : q + points // tile].reshape(points, columns).T
            mine = jnp.where(me_ref[1] == 0, mine[:own], mine[own:]).astype(BF16)
            term = lax.dot_general(
                mine, window_refs[s][...], (((1,), (1,)), ((), ())), preferred_element_type=F32
            )
            total = term if total is None else total + term
            q += points // tile
        out_ref[...] = total

    points = sum(w.shape[1] for w in windows)
    return pl.pallas_call(
        body,
        out_shape=jax.ShapeDtypeStruct((own, half), F32),
        in_specs=[SCALARS] + [WHOLE] * (shares + number),
        out_specs=WHOLE,
        scratch_shapes=[pltpu.VMEM((points // tile, shares, piece, columns), F32)],
        compiler_params=pltpu.CompilerParams(vmem_limit_bytes=VMEM_LIMIT),
        name="contract",
        cost_estimate=pl.CostEstimate(
            flops=2 * own * half * points,
            bytes_accessed=2 * points * half + 4 * own * half,
            transcendentals=0,
        ),
    )(jnp.stack((me, which)), *pieces, *windows)


def per_device(orbital_values, occupied, trial, point_weights, batch_sizes, significant):
    rows, cols = orbital_values.shape
    batches = batch_sizes.shape[0]
    slots = rows // batches
    blocks = significant.shape[1]
    columns = occupied.shape[1]
    grid_count = lax.axis_size("grid")
    occ_count = lax.axis_size("occ")
    chips = grid_count // 2
    shares = 2 * occ_count
    half = cols // 2
    total = columns * grid_count
    place = lax.axis_index("grid")
    chip, core = place // 2, place % 2
    member = core * occ_count + lax.axis_index("occ")

    swap = [(i, i ^ 1) for i in range(grid_count)]

    def along(step):
        return [
            (i, i + 2 * step) for i in range(grid_count) if 0 <= i + 2 * step < grid_count
        ]

    def group(d):
        return [
            (g * occ_count + o, (g ^ (d // occ_count)) * occ_count + (o ^ (d % occ_count)))
            for g in range(grid_count)
            for o in range(occ_count)
        ]

    def halves(whole, axis):
        size = whole.shape[axis] // 2
        mine = lax.dynamic_slice_in_dim(whole, core * size, size, axis)
        return mine, lax.dynamic_slice_in_dim(whole, (1 - core) * size, size, axis)

    mine, other = halves(orbital_values.T, 0)
    got = lax.ppermute(other, "grid", swap)
    mine_sig, other_sig = halves(significant.T, 0)
    got_sig = lax.ppermute(other_sig, "grid", swap)

    told = lax.all_gather(
        jnp.concatenate((batch_sizes.astype(F32), point_weights)), "grid", axis=0, tiled=False
    )
    sizes = told[:, :batches].astype(jnp.int32).reshape(-1)
    weights = told[:, batches:].reshape(-1)

    mine_panel, other_panel = halves(jnp.concatenate((occupied, trial), axis=1).T, 1)
    got_panel = lax.ppermute(other_panel, "grid", swap)
    panels = jnp.where(
        core == 0,
        jnp.concatenate(
            (mine_panel[:columns], got_panel[:columns], mine_panel[columns:], got_panel[columns:])
        ),
        jnp.concatenate(
            (got_panel[:columns], mine_panel[:columns], got_panel[columns:], mine_panel[columns:])
        ),
    )

    batch = lax.broadcasted_iota(jnp.int32, (sizes.shape[0], sizes.shape[0]), 0)
    before = lax.broadcasted_iota(jnp.int32, (sizes.shape[0], sizes.shape[0]), 1) < batch
    start = jnp.sum(jnp.where(before, sizes[None, :], 0), axis=1)
    position = lax.broadcasted_iota(jnp.int32, (sizes.shape[0], slots), 1)
    to = jnp.where(position < sizes[:, None], start[:, None] + position, -4 * rows * grid_count)
    to = to.reshape(grid_count, rows)
    first = start.reshape(chips, -1)[:, 0]
    margin = rows // 2
    nominal = rows * lax.iota(jnp.int32, chips)
    fits = jnp.all(jnp.abs(first - nominal) <= margin) & (jnp.sum(sizes) <= rows * chips)

    base = rows * chip - margin
    mine_to = lax.dynamic_index_in_dim(to, place, 0, keepdims=False) - base
    got_to = lax.dynamic_index_in_dim(to, place ^ 1, 0, keepdims=False) - base
    low, high = compact(
        mine,
        got,
        jnp.repeat(mine_sig.astype(BF16), slots, axis=1),
        jnp.repeat(got_sig.astype(BF16), slots, axis=1),
        mine_to[:, None],
        got_to[:, None],
        cols // blocks,
    )

    tile = margin if margin % (8 * shares) == 0 else rows
    piece = tile // shares
    per_window = rows // tile
    stages = []
    leftward, rightward = low, high
    for t in range(1, chips + 1):
        if t == chips:
            leftward, rightward = leftward[:, :tile], rightward[:, rows - tile :]
        from_right = lax.ppermute(leftward, "grid", along(-1))
        from_left = lax.ppermute(rightward, "grid", along(1))
        if t == 1:
            from_right, from_left = from_right + high, from_left + low
        right = jnp.where(chip + t <= chips, (chip + t) * per_window, -per_window)
        left = jnp.where(chip + 1 - t >= 0, (chip + 1 - t) * per_window, -per_window)
        if t == chips:
            left = left + jnp.where(left >= 0, per_window - 1, 0)
        if 2 * t > chips + 1:
            stages.append([(from_right + from_left, jnp.maximum(left, right))])
        else:
            stages.append([(from_right, right), (from_left, left)])
        leftward, rightward = from_right, from_left

    per_group = -(-chips // 4)
    groups = [sum(stages[t : t + per_group], []) for t in range(0, chips, per_group)]
    tile_count = (chips + 1) * per_window
    tile_iota = lax.iota(jnp.int32, tile_count)[:, None]
    density = jnp.zeros((tile_count, piece), F32)
    values, places = [], []
    for windows in groups:
        parts = project(panels, [w for w, _ in windows], tile, shares, member[None])
        value = parts[0]
        for d in range(1, shares):
            value = value + lax.ppermute(parts[d], ("grid", "occ"), group(d))
        values.append(value)
        product = jnp.sum(value[:, :, : 2 * columns] * value[:, :, 2 * columns :], axis=2)
        q = 0
        for window, index in windows:
            for j in range(window.shape[1] // tile):
                density = density + jnp.where(tile_iota == index + j, product[q][None, :], 0.0)
                places.append(index + j)
                q += 1
    whole_density = density
    for step in range(1, chips):
        around = [(i, (i + 2 * step) % grid_count) for i in range(grid_count)]
        whole_density = whole_density + lax.ppermute(density, "grid", around)
    whole_density = whole_density * (1.0 / math.sqrt(total))

    at = tile_iota * tile - margin + member * piece + lax.iota(jnp.int32, piece)[None, :]
    weight = jnp.sum(
        jnp.where(to.reshape(1, -1) == at.reshape(-1, 1), weights[None, :], 0.0), axis=1
    ).reshape(tile_count, piece)

    values = jnp.concatenate(values, axis=0)
    here = jnp.stack(places)[:, None, None] == lax.iota(jnp.int32, tile_count)[None, :, None]
    density_here = jnp.sum(jnp.where(here, whole_density[None], 0.0), axis=1)[:, :, None]
    weight_here = jnp.sum(jnp.where(here, weight[None], 0.0), axis=1)[:, :, None]
    orbitals, response = values[:, :, : 2 * columns], values[:, :, 2 * columns :]
    kernel = (weight_here * (density_here * orbitals + response)).astype(BF16)
    kernel = kernel.reshape(-1, 2 * columns)
    pieces = [kernel] + [
        lax.ppermute(kernel, ("grid", "occ"), group(d)) for d in range(1, shares)
    ]
    windows = [w for g in groups for w, _ in g]
    theirs = contract(pieces, windows, tile, member, 1 - core)
    back = lax.ppermute(theirs, "grid", swap)
    ours = contract(pieces, windows, tile, member, core)
    exchange = jnp.where(
        core == 0,
        jnp.concatenate((ours, back), axis=1),
        jnp.concatenate((back, ours), axis=1),
    ) * (1.0 / math.sqrt(rows * grid_count))
    exchange = exchange.T

    return lax.cond(
        fits,
        lambda *given: given[0],
        lambda *given: any_sizes(*given[1:]),
        exchange,
        orbital_values,
        occupied,
        trial,
        point_weights,
        batch_sizes,
        significant,
    )


def solution(mesh):
    placed = (
        P("grid", "occ"),
        P("occ", "grid"),
        P("occ", "grid"),
        P("grid"),
        P("grid"),
        P("grid", "occ"),
    )
    return jax.shard_map(
        per_device, mesh=mesh, in_specs=placed, out_specs=P("occ", "grid"), check_vma=False
    )
```

```python
import math

import jax
import jax.numpy as jnp
from jax import lax
from jax.experimental import pallas as pl
from jax.experimental.pallas import tpu as pltpu
from jax.sharding import PartitionSpec as P

BF16, F32 = jnp.bfloat16, jnp.float32
VMEM_LIMIT = 48 * 1024 * 1024
WHOLE = pl.BlockSpec(memory_space=pltpu.VMEM)
SCALARS = pl.BlockSpec(memory_space=pltpu.SMEM)


def screen(values, sizes, significant):
    rows, cols = values.shape
    batches = sizes.shape[0]
    blocks = significant.shape[1]
    blocked = (
        values.reshape(batches, rows // batches, blocks, cols // blocks)
        * significant.astype(values.dtype)[:, None, :, None]
    )
    position = lax.broadcasted_iota(jnp.int32, (batches, rows // batches), 1)
    live = (position < sizes[:, None]).astype(jnp.float32).reshape(rows)
    return (blocked.reshape(rows, cols), live)


def any_sizes(orbital_values, occupied, trial, point_weights, batch_sizes, significant):
    screened, live = screen(orbital_values, batch_sizes, significant)
    rows, cols = screened.shape
    grid_count, occ_count = lax.axis_size("grid"), lax.axis_size("occ")
    columns = occupied.shape[1]
    me = lax.axis_index("grid")
    ring = [(i, (i + 1) % grid_count) for i in range(grid_count)]
    occ_ring = [(i, (i + 1) % occ_count) for i in range(occ_count)]

    def project_one(step, carry):
        panel, terms = carry
        term = jnp.dot(screened, panel, preferred_element_type=F32)
        terms = lax.dynamic_update_index_in_dim(terms, term, (me - step) % grid_count, 0)
        return lax.ppermute(panel, "grid", ring), terms

    joined = jnp.concatenate((occupied, trial), axis=1)
    terms = jnp.zeros((grid_count, rows, 2 * columns), F32)
    terms = lax.fori_loop(0, grid_count, project_one, (joined, terms))[1]

    def add_one(step, carry):
        moving, held = carry
        moving = lax.ppermute(moving, "occ", occ_ring)
        return moving, held + moving

    terms = lax.fori_loop(0, occ_count - 1, add_one, (terms, terms))[1]
    orbitals, response = terms[:, :, :columns], terms[:, :, columns:]
    density = jnp.sum(orbitals * response, axis=(0, 2)) * (1.0 / math.sqrt(columns * grid_count))
    weight = (point_weights * live)[None, :, None]
    kernel = (weight * (density[None, :, None] * orbitals + response)).astype(BF16)

    def contract_one(step, held):
        owner = (me + grid_count - 1 - step) % grid_count
        part = lax.dynamic_index_in_dim(kernel, owner, 0, keepdims=False)
        term = lax.dot_general(
            part, screened, (((0,), (0,)), ((), ())), preferred_element_type=F32
        )
        return lax.ppermute(held, "grid", ring) + term

    return lax.fori_loop(0, grid_count, contract_one, jnp.zeros((columns, cols), F32))


def compact(mine, got, mine_sig, got_sig, mine_to, got_to, width):
    half, rows = mine.shape
    blocks = mine_sig.shape[0]

    def body(mine_ref, got_ref, msig_ref, gsig_ref, mto_ref, gto_ref, low_ref, high_ref):
        block_of = lax.broadcasted_iota(jnp.int32, (half, blocks), 0)
        first = lax.broadcasted_iota(jnp.int32, (half, blocks), 1) * width
        spread = ((block_of >= first) & (block_of < first + width)).astype(F32).astype(BF16)
        slot = lax.broadcasted_iota(jnp.int32, (rows, 2 * rows), 1)

        def part(value_ref, sig_ref, to_ref):
            kept = jnp.dot(spread, sig_ref[...], preferred_element_type=F32)
            screened = (value_ref[...].astype(F32) * kept).astype(BF16)
            place = (to_ref[...] == slot).astype(F32).astype(BF16)
            return jnp.dot(screened, place, preferred_element_type=F32)

        window = part(mine_ref, msig_ref, mto_ref) + part(got_ref, gsig_ref, gto_ref)
        low_ref[...] = window[:, :rows].astype(BF16)
        high_ref[...] = window[:, rows:].astype(BF16)

    shape = jax.ShapeDtypeStruct((half, rows), BF16)
    return pl.pallas_call(
        body,
        out_shape=(shape, shape),
        in_specs=[WHOLE] * 6,
        out_specs=(WHOLE, WHOLE),
        compiler_params=pltpu.CompilerParams(vmem_limit_bytes=VMEM_LIMIT),
        name="compact",
        cost_estimate=pl.CostEstimate(
            flops=8 * half * rows * rows, bytes_accessed=8 * half * rows, transcendentals=0
        ),
    )(mine, got, mine_sig, got_sig, mine_to, got_to)


def project(panels, windows, tile, shares, core):
    both, half = panels[0].shape
    piece = tile // shares
    counts = [w.shape[1] // tile for w in windows]
    tiles, number = sum(counts), len(windows)

    def body(core_ref, *refs):
        panel_refs, window_refs = refs[:number], refs[number : 2 * number]
        keep_ref, give_ref, terms_ref = refs[2 * number :]
        q = 0
        for s in range(number):
            terms = jnp.dot(panel_refs[s][...], window_refs[s][...], preferred_element_type=F32).T
            for j in range(counts[s]):
                terms_ref[...] = terms[j * tile : (j + 1) * tile].reshape(
                    2, shares // 2, piece, both
                )
                keep_ref[q] = terms_ref[core_ref[0]]
                give_ref[q] = terms_ref[1 - core_ref[0]]
                q += 1

    shape = jax.ShapeDtypeStruct((tiles, shares // 2, piece, both), F32)
    return pl.pallas_call(
        body,
        out_shape=(shape, shape),
        in_specs=[SCALARS] + [WHOLE] * (2 * number),
        out_specs=(WHOLE, WHOLE),
        scratch_shapes=[pltpu.VMEM((2, shares // 2, piece, both), F32)],
        compiler_params=pltpu.CompilerParams(vmem_limit_bytes=VMEM_LIMIT),
        name="project",
        cost_estimate=pl.CostEstimate(
            flops=2 * both * half * tiles * tile,
            bytes_accessed=2 * half * (both + tiles * tile) + 4 * tiles * tile * both,
            transcendentals=0,
        ),
    )(core[None], *panels, *windows)


def contract(kernel, windows, core, kind):
    points, columns = kernel.shape
    half = windows[0].shape[0]
    own = columns // 2
    number = len(windows)

    def body(core_ref, kernel_ref, *refs):
        window_refs, mine_ref, other_ref = refs[:number], refs[number], refs[number + 1]
        total, q = None, 0
        for s in range(number):
            size = windows[s].shape[1]
            turned = kernel_ref[q : q + size].astype(F32).T
            low, high = turned[:own], turned[own:]
            first = core_ref[0] == 0
            turned = jnp.concatenate(
                (jnp.where(first, low, high), jnp.where(first, high, low))
            ).astype(BF16)
            term = lax.dot_general(
                turned, window_refs[s][...], (((1,), (1,)), ((), ())), preferred_element_type=F32
            )
            total = term if total is None else total + term
            q += size
        mine_ref[...] = total[:own].astype(kind)
        other_ref[...] = total[own:].astype(kind)

    shape = jax.ShapeDtypeStruct((own, half), kind)
    return pl.pallas_call(
        body,
        out_shape=(shape, shape),
        in_specs=[SCALARS] + [WHOLE] * (1 + number),
        out_specs=(WHOLE, WHOLE),
        compiler_params=pltpu.CompilerParams(vmem_limit_bytes=VMEM_LIMIT),
        name="contract",
        cost_estimate=pl.CostEstimate(
            flops=2 * columns * half * points,
            bytes_accessed=2 * points * half + 4 * columns * half,
            transcendentals=0,
        ),
    )(core[None], kernel, *windows)


def per_device(orbital_values, occupied, trial, point_weights, batch_sizes, significant):
    rows, cols = orbital_values.shape
    batches = batch_sizes.shape[0]
    slots = rows // batches
    blocks = significant.shape[1]
    columns = occupied.shape[1]
    grid_count = lax.axis_size("grid")
    occ_count = lax.axis_size("occ")
    chips = grid_count // 2
    shares = 2 * occ_count
    half = cols // 2
    total = columns * grid_count
    place = lax.axis_index("grid")
    chip, core = place // 2, place % 2
    occ = lax.axis_index("occ")
    member = core * occ_count + occ

    def flip(x, axis, bit):
        count = lax.axis_size(axis)
        return lax.ppermute(x, axis, [(i, i ^ bit) for i in range(count)])

    def along(pairs):
        return [(2 * a + c, 2 * b + (c ^ x)) for a, b, x in pairs for c in range(2)]

    def doubled(x, axis, bit, dim):
        got = flip(x, axis, bit)
        mine = (lax.axis_index(axis) & bit) == 0
        return jnp.where(
            mine, jnp.concatenate((x, got), axis=dim), jnp.concatenate((got, x), axis=dim)
        )

    def halves(whole, axis):
        size = whole.shape[axis] // 2
        mine = lax.dynamic_slice_in_dim(whole, core * size, size, axis)
        return mine, lax.dynamic_slice_in_dim(whole, (1 - core) * size, size, axis)

    grid_bits = [1 << b for b in range(grid_count.bit_length() - 1)]
    occ_bits = [1 << b for b in range(occ_count.bit_length() - 1)]

    mine, other = halves(orbital_values.T, 0)
    got = flip(other, "grid", 1)
    mine_sig, other_sig = halves(significant.T, 0)
    got_sig = flip(other_sig, "grid", 1)

    told = jnp.concatenate((batch_sizes.astype(F32), point_weights))[None]
    for bit in grid_bits:
        told = doubled(told, "grid", bit, 0)
    sizes = told[:, :batches].astype(jnp.int32).reshape(-1)
    weights = told[:, batches:].reshape(-1)

    batch = lax.broadcasted_iota(jnp.int32, (sizes.shape[0], sizes.shape[0]), 0)
    before = lax.broadcasted_iota(jnp.int32, (sizes.shape[0], sizes.shape[0]), 1) < batch
    start = jnp.sum(jnp.where(before, sizes[None, :], 0), axis=1)
    position = lax.broadcasted_iota(jnp.int32, (sizes.shape[0], slots), 1)
    to = jnp.where(position < sizes[:, None], start[:, None] + position, -4 * rows * grid_count)
    to = to.reshape(grid_count, rows)
    first = start.reshape(chips, -1)[:, 0]
    margin = rows // 2
    nominal = rows * lax.iota(jnp.int32, chips)
    fits = jnp.all(jnp.abs(first - nominal) <= margin) & (jnp.sum(sizes) <= rows * chips)

    base = rows * chip - margin
    mine_to = lax.dynamic_index_in_dim(to, place, 0, keepdims=False) - base
    got_to = lax.dynamic_index_in_dim(to, place ^ 1, 0, keepdims=False) - base
    low, high = compact(
        mine,
        got,
        jnp.repeat(mine_sig.astype(BF16), slots, axis=1),
        jnp.repeat(got_sig.astype(BF16), slots, axis=1),
        mine_to[:, None],
        got_to[:, None],
        cols // blocks,
    )

    mine_panel, other_panel = halves(jnp.concatenate((occupied, trial), axis=1).T, 1)
    got_panel = flip(other_panel, "grid", 1)
    panels = jnp.where(
        core == 0,
        jnp.concatenate(
            (mine_panel[:columns], got_panel[:columns], mine_panel[columns:], got_panel[columns:])
        ),
        jnp.concatenate(
            (got_panel[:columns], mine_panel[:columns], got_panel[columns:], mine_panel[columns:])
        ),
    )

    tile = margin if margin % (8 * shares) == 0 else rows
    piece = tile // shares
    per_window = rows // tile
    last = chips - 1
    leftward, rightward = low, high
    stages = []
    for t in range(1, last + 1):
        if t == last:
            to_left, to_right = [(2, 1, 0)], [(last - 2, last - 1, 0)]
            leftward, rightward = leftward[:, :tile], rightward[:, rows - tile :]
        else:
            to_left = [(a, a - 1, 0) for a in range(1, chips) if a + t - 1 <= chips]
            to_right = [(a, a + 1, 0) for a in range(last) if a + 2 - t >= 0]
        from_right = lax.ppermute(leftward, "grid", along(to_left))
        from_left = lax.ppermute(rightward, "grid", along(to_right))
        if t == 1:
            from_right, from_left = from_right + high, from_left + low
            neighbours = [(0, 1, 0), (last, last - 1, 0)]
            far_panels = lax.ppermute(panels, "grid", along(neighbours))
        none = -2 * per_window
        if t == last:
            right = jnp.where(chip == 1, chips * per_window, none)
            left = jnp.where(chip == last - 1, per_window - 1, none)
            window = from_right + from_left
            index = jnp.maximum(left, right)
            stages.append([(panels, window, index), (far_panels, window, index)])
        else:
            right = jnp.where(chip + t <= chips, (chip + t) * per_window, none)
            left = jnp.where(chip + 1 - t >= 0, (chip + 1 - t) * per_window, none)
            stages.append([(panels, from_right, right), (panels, from_left, left)])
            if t == last - 1:
                nearer = chip < chips // 2
                stages[-1].append(
                    (
                        far_panels,
                        jnp.where(nearer, from_right, from_left),
                        jnp.where(nearer, right, left),
                    )
                )
        leftward, rightward = from_right, from_left

    per_group = -(-last // 3)
    groups = [sum(stages[t : t + per_group], []) for t in range(0, last, per_group)]
    tile_count = (chips + 1) * per_window
    tile_iota = lax.iota(jnp.int32, tile_count)
    density = jnp.zeros((tile_count, piece), F32)
    values, places = [], []
    for jobs in groups:
        keep, give = project([p for p, _, _ in jobs], [w for _, w, _ in jobs], tile, shares, core)
        value = keep + flip(give, "grid", 1)
        for bit in reversed(occ_bits):
            upper = (occ & bit) != 0
            low_part, high_part = value[:, :bit], value[:, bit:]
            sent = flip(jnp.where(upper, low_part, high_part), "occ", bit)
            value = jnp.where(upper, high_part, low_part) + sent
        value = value[:, 0]
        values.append(value)
        product = jnp.sum(value[:, :, : 2 * columns] * value[:, :, 2 * columns :], axis=2)
        here = jnp.stack(
            [index + j for _, w, index in jobs for j in range(w.shape[1] // tile)]
        )
        places.append(here)
        density = density + jnp.sum(
            jnp.where((here[:, None] == tile_iota[None, :])[:, :, None], product[:, None], 0.0),
            axis=0,
        )
    for bit in grid_bits[1:]:
        density = density + flip(density, "grid", bit)
    density = density * (1.0 / math.sqrt(total))

    at = tile_iota[:, None] * tile - margin + member * piece + lax.iota(jnp.int32, piece)[None, :]
    weight = jnp.sum(
        jnp.where(to.reshape(1, -1) == at.reshape(-1, 1), weights[None, :], 0.0), axis=1
    ).reshape(tile_count, piece)

    values, places = jnp.concatenate(values, axis=0), jnp.concatenate(places)
    here = (places[:, None] == tile_iota[None, :])[:, :, None]
    density_here = jnp.sum(jnp.where(here, density[None], 0.0), axis=1)[:, :, None]
    weight_here = jnp.sum(jnp.where(here, weight[None], 0.0), axis=1)[:, :, None]
    orbitals, response = values[:, :, : 2 * columns], values[:, :, 2 * columns :]
    kernel = (weight_here * (density_here * orbitals + response)).astype(BF16)[:, None]
    for bit in occ_bits:
        kernel = doubled(kernel, "occ", bit, 1)
    kernel = doubled(kernel, "grid", 1, 1)

    own_kernel, own_windows, far_kernel, far_windows, q = [], [], [], [], 0
    for panel, window, _ in sum(groups, []):
        count = window.shape[1] // tile
        part = kernel[q : q + count].reshape(count * tile, 2 * columns)
        q += count
        (own_kernel if panel is panels else far_kernel).append(part)
        (own_windows if panel is panels else far_windows).append(window)
    far_same, far_cross = contract(jnp.concatenate(far_kernel), far_windows, core, BF16)
    ends = [(1, 0), (last - 1, last)]
    far_same = lax.ppermute(far_same, "grid", along([(a, b, 0) for a, b in ends]))
    far_cross = lax.ppermute(far_cross, "grid", along([(a, b, 1) for a, b in ends]))
    ours, theirs = contract(jnp.concatenate(own_kernel), own_windows, core, F32)
    back = flip(theirs, "grid", 1)

    def slow(*given):
        whole = any_sizes(*given)
        mine, other = halves(whole, 1)
        zero = jnp.zeros_like(far_same)
        return mine, other, zero, zero

    ours, back, far_same, far_cross = lax.cond(
        fits,
        lambda *given: given[:4],
        lambda *given: slow(*given[4:]),
        ours,
        back,
        far_same,
        far_cross,
        orbital_values,
        occupied,
        trial,
        point_weights,
        batch_sizes,
        significant,
    )
    ours, back = ours + far_same.astype(F32), back + far_cross.astype(F32)
    exchange = jnp.where(
        core == 0,
        jnp.concatenate((ours, back), axis=1),
        jnp.concatenate((back, ours), axis=1),
    ) * (1.0 / math.sqrt(rows * grid_count))
    return exchange.T


def solution(mesh):
    placed = (
        P("grid", "occ"),
        P("occ", "grid"),
        P("occ", "grid"),
        P("grid"),
        P("grid"),
        P("grid", "occ"),
    )
    return jax.shard_map(
        per_device, mesh=mesh, in_specs=placed, out_specs=P("occ", "grid"), check_vma=False
    )
```

```python
import math

import jax
import jax.numpy as jnp
from jax import lax
from jax.experimental import pallas as pl
from jax.experimental.pallas import tpu as pltpu
from jax.sharding import PartitionSpec as P

BF16, F32 = jnp.bfloat16, jnp.float32
VMEM_LIMIT = 48 * 1024 * 1024
WHOLE = pl.BlockSpec(memory_space=pltpu.VMEM)
SCALARS = pl.BlockSpec(memory_space=pltpu.SMEM)


def screen(values, sizes, significant):
    rows, cols = values.shape
    batches = sizes.shape[0]
    blocks = significant.shape[1]
    blocked = (
        values.reshape(batches, rows // batches, blocks, cols // blocks)
        * significant.astype(values.dtype)[:, None, :, None]
    )
    position = lax.broadcasted_iota(jnp.int32, (batches, rows // batches), 1)
    live = (position < sizes[:, None]).astype(jnp.float32).reshape(rows)
    return (blocked.reshape(rows, cols), live)


def any_sizes(orbital_values, occupied, trial, point_weights, batch_sizes, significant):
    screened, live = screen(orbital_values, batch_sizes, significant)
    rows, cols = screened.shape
    grid_count, occ_count = lax.axis_size("grid"), lax.axis_size("occ")
    columns = occupied.shape[1]
    me = lax.axis_index("grid")
    ring = [(i, (i + 1) % grid_count) for i in range(grid_count)]
    occ_ring = [(i, (i + 1) % occ_count) for i in range(occ_count)]

    def project_one(step, carry):
        panel, terms = carry
        term = jnp.dot(screened, panel, preferred_element_type=F32)
        terms = lax.dynamic_update_index_in_dim(terms, term, (me - step) % grid_count, 0)
        return lax.ppermute(panel, "grid", ring), terms

    joined = jnp.concatenate((occupied, trial), axis=1)
    terms = jnp.zeros((grid_count, rows, 2 * columns), F32)
    terms = lax.fori_loop(0, grid_count, project_one, (joined, terms))[1]

    def add_one(step, carry):
        moving, held = carry
        moving = lax.ppermute(moving, "occ", occ_ring)
        return moving, held + moving

    terms = lax.fori_loop(0, occ_count - 1, add_one, (terms, terms))[1]
    orbitals, response = terms[:, :, :columns], terms[:, :, columns:]
    density = jnp.sum(orbitals * response, axis=(0, 2)) * (1.0 / math.sqrt(columns * grid_count))
    weight = (point_weights * live)[None, :, None]
    kernel = (weight * (density[None, :, None] * orbitals + response)).astype(BF16)

    def contract_one(step, held):
        owner = (me + grid_count - 1 - step) % grid_count
        part = lax.dynamic_index_in_dim(kernel, owner, 0, keepdims=False)
        term = lax.dot_general(
            part, screened, (((0,), (0,)), ((), ())), preferred_element_type=F32
        )
        return lax.ppermute(held, "grid", ring) + term

    return lax.fori_loop(0, grid_count, contract_one, jnp.zeros((columns, cols), F32))


def compact(mine, got, mine_sig, got_sig, mine_to, got_to, width, tile, first):
    half, rows = mine.shape
    blocks = mine_sig.shape[0]

    def body(first_ref, mine_ref, got_ref, msig_ref, gsig_ref, mto_ref, gto_ref, *outs):
        low_ref, high_ref, edge_ref = outs
        block_of = lax.broadcasted_iota(jnp.int32, (half, blocks), 0)
        begin = lax.broadcasted_iota(jnp.int32, (half, blocks), 1) * width
        spread = ((block_of >= begin) & (block_of < begin + width)).astype(F32).astype(BF16)
        slot = lax.broadcasted_iota(jnp.int32, (rows, 2 * rows), 1)

        def part(value_ref, sig_ref, to_ref):
            kept = jnp.dot(spread, sig_ref[...], preferred_element_type=F32)
            screened = (value_ref[...].astype(F32) * kept).astype(BF16)
            place = (to_ref[...] == slot).astype(F32).astype(BF16)
            return jnp.dot(screened, place, preferred_element_type=F32)

        window = part(mine_ref, msig_ref, mto_ref) + part(got_ref, gsig_ref, gto_ref)
        low_ref[...] = window[:, :rows].astype(BF16)
        high_ref[...] = window[:, rows:].astype(BF16)
        edge_ref[...] = jnp.where(
            first_ref[0] == 0, window[:, rows - tile : rows], window[:, rows : rows + tile]
        ).astype(BF16)

    shape = jax.ShapeDtypeStruct((half, rows), BF16)
    return pl.pallas_call(
        body,
        out_shape=(shape, shape, jax.ShapeDtypeStruct((half, tile), BF16)),
        in_specs=[SCALARS] + [WHOLE] * 6,
        out_specs=(WHOLE, WHOLE, WHOLE),
        compiler_params=pltpu.CompilerParams(vmem_limit_bytes=VMEM_LIMIT),
        name="compact",
        cost_estimate=pl.CostEstimate(
            flops=8 * half * rows * rows, bytes_accessed=8 * half * rows, transcendentals=0
        ),
    )(first[None], mine, got, mine_sig, got_sig, mine_to, got_to)


def read_windows(windows, refs):
    q = 0
    for parts in windows:
        value = refs[q][...]
        for ref in refs[q + 1 : q + len(parts)]:
            value = value + ref[...]
        q += len(parts)
        yield value


def project(panels, windows, tile, shares, core):
    both, half = panels[0].shape
    piece = tile // shares
    counts = [w[0].shape[1] // tile for w in windows]
    tiles, number = sum(counts), len(windows)

    def body(core_ref, *refs):
        panel_refs, window_refs = refs[:number], refs[number:-3]
        keep_ref, give_ref, terms_ref = refs[-3:]
        q = 0
        for s, window in enumerate(read_windows(windows, window_refs)):
            terms = jnp.dot(panel_refs[s][...], window, preferred_element_type=F32).T
            for j in range(counts[s]):
                terms_ref[...] = terms[j * tile : (j + 1) * tile].reshape(
                    2, shares // 2, piece, both
                )
                keep_ref[q] = terms_ref[core_ref[0]]
                give_ref[q] = terms_ref[1 - core_ref[0]]
                q += 1

    shape = jax.ShapeDtypeStruct((tiles, shares // 2, piece, both), F32)
    return pl.pallas_call(
        body,
        out_shape=(shape, shape),
        in_specs=[SCALARS] + [WHOLE] * (number + sum(map(len, windows))),
        out_specs=(WHOLE, WHOLE),
        scratch_shapes=[pltpu.VMEM((2, shares // 2, piece, both), F32)],
        compiler_params=pltpu.CompilerParams(vmem_limit_bytes=VMEM_LIMIT),
        name="project",
        cost_estimate=pl.CostEstimate(
            flops=2 * both * half * tiles * tile,
            bytes_accessed=2 * half * (both + tiles * tile) + 4 * tiles * tile * both,
            transcendentals=0,
        ),
    )(core[None], *panels, *sum(windows, ()))


def contract(kernel, windows, core):
    points, columns = kernel.shape
    half = windows[0][0].shape[0]
    own = columns // 2

    def body(core_ref, kernel_ref, *refs):
        window_refs, mine_ref, other_ref = refs[:-2], refs[-2], refs[-1]
        total, q = None, 0
        for window in read_windows(windows, window_refs):
            size = window.shape[1]
            turned = kernel_ref[q : q + size].astype(F32).T
            low, high = turned[:own], turned[own:]
            first = core_ref[0] == 0
            turned = jnp.concatenate(
                (jnp.where(first, low, high), jnp.where(first, high, low))
            ).astype(BF16)
            term = lax.dot_general(
                turned, window, (((1,), (1,)), ((), ())), preferred_element_type=F32
            )
            total = term if total is None else total + term
            q += size
        mine_ref[...] = total[:own]
        other_ref[...] = total[own:]

    shape = jax.ShapeDtypeStruct((own, half), F32)
    return pl.pallas_call(
        body,
        out_shape=(shape, shape),
        in_specs=[SCALARS] + [WHOLE] * (1 + sum(map(len, windows))),
        out_specs=(WHOLE, WHOLE),
        compiler_params=pltpu.CompilerParams(vmem_limit_bytes=VMEM_LIMIT),
        name="contract",
        cost_estimate=pl.CostEstimate(
            flops=2 * columns * half * points,
            bytes_accessed=2 * points * half + 4 * columns * half,
            transcendentals=0,
        ),
    )(core[None], kernel, *sum(windows, ()))


def finish(core, ours, back, scale):
    own, half = ours.shape

    def body(core_ref, ours_ref, back_ref, out_ref):
        first = core_ref[0] == 0
        out_ref[:, :half] = jnp.where(first, ours_ref[...], back_ref[...]) * scale
        out_ref[:, half:] = jnp.where(first, back_ref[...], ours_ref[...]) * scale

    return pl.pallas_call(
        body,
        out_shape=jax.ShapeDtypeStruct((own, 2 * half), F32),
        in_specs=[SCALARS, WHOLE, WHOLE],
        out_specs=WHOLE,
        compiler_params=pltpu.CompilerParams(vmem_limit_bytes=VMEM_LIMIT),
        name="finish",
    )(core[None], ours, back)


def per_device(orbital_values, occupied, trial, point_weights, batch_sizes, significant):
    rows, cols = orbital_values.shape
    batches = batch_sizes.shape[0]
    slots = rows // batches
    blocks = significant.shape[1]
    columns = occupied.shape[1]
    grid_count = lax.axis_size("grid")
    occ_count = lax.axis_size("occ")
    chips = grid_count // 2
    shares = 2 * occ_count
    half = cols // 2
    total = columns * grid_count
    place = lax.axis_index("grid")
    chip, core = place // 2, place % 2
    occ = lax.axis_index("occ")
    member = core * occ_count + occ

    def flip(x, axis, bit):
        count = lax.axis_size(axis)
        return lax.ppermute(x, axis, [(i, i ^ bit) for i in range(count)])

    def along(pairs):
        return [(2 * a + c, 2 * b + c) for a, b in pairs for c in range(2)]

    def doubled(x, axis, bit, dim):
        got = flip(x, axis, bit)
        mine = (lax.axis_index(axis) & bit) == 0
        return jnp.where(
            mine, jnp.concatenate((x, got), axis=dim), jnp.concatenate((got, x), axis=dim)
        )

    def halves(whole, axis):
        size = whole.shape[axis] // 2
        mine = lax.dynamic_slice_in_dim(whole, core * size, size, axis)
        return mine, lax.dynamic_slice_in_dim(whole, (1 - core) * size, size, axis)

    grid_bits = [1 << b for b in range(grid_count.bit_length() - 1)]
    occ_bits = [1 << b for b in range(occ_count.bit_length() - 1)]

    mine, other = halves(orbital_values.T, 0)
    got = flip(other, "grid", 1)
    mine_sig, other_sig = halves(significant.T, 0)
    got_sig = flip(other_sig, "grid", 1)

    told = jnp.concatenate((batch_sizes.astype(F32), point_weights))[None]
    for bit in grid_bits:
        told = doubled(told, "grid", bit, 0)
    sizes = told[:, :batches].astype(jnp.int32).reshape(-1)
    weights = told[:, batches:].reshape(-1)

    batch = lax.broadcasted_iota(jnp.int32, (sizes.shape[0], sizes.shape[0]), 0)
    before = lax.broadcasted_iota(jnp.int32, (sizes.shape[0], sizes.shape[0]), 1) < batch
    start = jnp.sum(jnp.where(before, sizes[None, :], 0), axis=1)
    position = lax.broadcasted_iota(jnp.int32, (sizes.shape[0], slots), 1)
    to = jnp.where(position < sizes[:, None], start[:, None] + position, -4 * rows * grid_count)
    to = to.reshape(grid_count, rows)
    first = start.reshape(chips, -1)[:, 0]
    margin = rows // 2
    nominal = rows * lax.iota(jnp.int32, chips)
    fits = jnp.all(jnp.abs(first - nominal) <= margin) & (jnp.sum(sizes) <= rows * chips)

    tile = margin if margin % (8 * shares) == 0 else rows
    base = rows * chip - margin
    mine_to = lax.dynamic_index_in_dim(to, place, 0, keepdims=False) - base
    got_to = lax.dynamic_index_in_dim(to, place ^ 1, 0, keepdims=False) - base
    low, high, edge = compact(
        mine,
        got,
        jnp.repeat(mine_sig.astype(BF16), slots, axis=1),
        jnp.repeat(got_sig.astype(BF16), slots, axis=1),
        mine_to[:, None],
        got_to[:, None],
        cols // blocks,
        tile,
        chip,
    )

    mine_panel, other_panel = halves(jnp.concatenate((occupied, trial), axis=1).T, 1)
    got_panel = flip(other_panel, "grid", 1)
    panels = jnp.where(
        core == 0,
        jnp.concatenate(
            (mine_panel[:columns], got_panel[:columns], mine_panel[columns:], got_panel[columns:])
        ),
        jnp.concatenate(
            (got_panel[:columns], mine_panel[:columns], got_panel[columns:], mine_panel[columns:])
        ),
    )

    piece = tile // shares
    per_window = rows // tile
    last = chips - 1
    ends = [(0, 1), (last, last - 1)]
    homes = [(b, a) for a, b in ends]
    none = -2 * per_window
    stages = []
    leftward, rightward = low, high
    far_panels = None
    for t in range(1, last):
        to_left = [(a, a - 1) for a in range(1, chips) if t == 1 or a + t - 1 < chips]
        to_right = [(a, a + 1) for a in range(last) if t == 1 or a + 2 - t > 0]
        from_right = lax.ppermute(leftward, "grid", along(to_left))
        from_left = lax.ppermute(rightward, "grid", along(to_right))
        edge = lax.ppermute(edge, "grid", along([(t - 1, t), (chips - t, last - t)]))
        if t == 1:
            from_right, from_left = from_right + high, from_left + low
            far_panels = lax.ppermute(panels, "grid", along(ends))
        right = jnp.where((chip + t <= last) | (t == 1), (chip + t) * per_window, none)
        left = jnp.where((chip + 1 - t > 0) | (t == 1), (chip + 1 - t) * per_window, none)
        edge_at = jnp.where(
            chip == t, per_window - 1, jnp.where(chip == last - t, chips * per_window, none)
        )
        if 2 * t > last:
            jobs = [((from_right, from_left), jnp.maximum(right, left))]
        else:
            jobs = [((from_right,), right), ((from_left,), left)]
        stages.append(jobs + [((edge,), edge_at)])
        leftward, rightward = from_right, from_left
    late_windows = [
        (
            lax.ppermute(leftward, "grid", along(homes[:1])),
            lax.ppermute(rightward, "grid", along(homes[1:])),
        ),
        (lax.ppermute(edge, "grid", along(homes)),),
    ]

    tile_count = (chips + 1) * per_window
    tile_iota = lax.iota(jnp.int32, tile_count)

    def tiles_of(jobs):
        return jnp.stack([at + j for w, at in jobs for j in range(w[0].shape[1] // tile)])

    def summed(jobs):
        keep, give = project([p for p, _ in jobs], [w for _, w in jobs], tile, shares, core)
        value = keep + flip(give, "grid", 1)
        for bit in reversed(occ_bits):
            upper = (occ & bit) != 0
            low_part, high_part = value[:, :bit], value[:, bit:]
            sent = flip(jnp.where(upper, low_part, high_part), "occ", bit)
            value = jnp.where(upper, high_part, low_part) + sent
        return value[:, 0]

    def shared_density(value, at):
        product = jnp.sum(value[:, :, : 2 * columns] * value[:, :, 2 * columns :], axis=2)
        here = (at[:, None] == tile_iota[None, :])[:, :, None]
        return jnp.sum(jnp.where(here, product[:, None], 0.0), axis=0)

    per_group = -(-len(stages) // 2)
    groups = [
        sum(stages[t : t + per_group], []) for t in range(0, len(stages), per_group)
    ]
    far_jobs = [stages[-1][0], stages[-1][-1]]
    far_tiles = per_window + 1
    windows, values, places = [], [], []
    density = jnp.zeros((tile_count, piece), F32)
    for jobs in groups:
        final = jobs is groups[-1]
        here = [(panels, w) for w, _ in jobs]
        at = tiles_of(jobs)
        if final:
            value = summed(here + [(far_panels, w) for w, _ in far_jobs])
            far_value = value[-far_tiles:]
            density = density + shared_density(value, jnp.concatenate((at, tiles_of(far_jobs))))
            value = value[:-far_tiles]
        else:
            value = summed(here)
            density = density + shared_density(value, at)
        windows += [w for w, _ in jobs]
        values.append(value)
        places.append(at)
    for bit in grid_bits[1:]:
        density = density + flip(density, "grid", bit)
    density = density * (1.0 / math.sqrt(total))

    windows += late_windows
    values.append(lax.ppermute(far_value, "grid", along(homes)))
    outer = lax.iota(jnp.int32, per_window)
    places.append(
        jnp.where(
            chip == 0,
            jnp.concatenate((outer + last * per_window, outer[:1] + chips * per_window)),
            jnp.concatenate((outer + per_window, outer[:1] + per_window - 1)),
        )
    )

    at = tile_iota[:, None] * tile - margin + member * piece + lax.iota(jnp.int32, piece)[None, :]
    weight = jnp.sum(
        jnp.where(to.reshape(1, -1) == at.reshape(-1, 1), weights[None, :], 0.0), axis=1
    ).reshape(tile_count, piece)

    values, places = jnp.concatenate(values, axis=0), jnp.concatenate(places)
    here = (places[:, None] == tile_iota[None, :])[:, :, None]
    density_here = jnp.sum(jnp.where(here, density[None], 0.0), axis=1)[:, :, None]
    weight_here = jnp.sum(jnp.where(here, weight[None], 0.0), axis=1)[:, :, None]
    orbitals, response = values[:, :, : 2 * columns], values[:, :, 2 * columns :]
    kernel = (weight_here * (density_here * orbitals + response)).astype(BF16)[:, None]
    for bit in occ_bits:
        kernel = doubled(kernel, "occ", bit, 1)
    kernel = doubled(kernel, "grid", 1, 1).reshape(-1, 2 * columns)

    ours, theirs = contract(kernel, windows, core)
    back = flip(theirs, "grid", 1)
    scale = 1.0 / math.sqrt(rows * grid_count)
    exchange = lax.cond(
        fits,
        lambda core, ours, back, *given: finish(core, ours, back, scale),
        lambda core, ours, back, *given: any_sizes(*given) * scale,
        core,
        ours,
        back,
        orbital_values,
        occupied,
        trial,
        point_weights,
        batch_sizes,
        significant,
    )
    return exchange.T


def solution(mesh):
    placed = (
        P("grid", "occ"),
        P("occ", "grid"),
        P("occ", "grid"),
        P("grid"),
        P("grid"),
        P("grid", "occ"),
    )
    return jax.shard_map(
        per_device, mesh=mesh, in_specs=placed, out_specs=P("occ", "grid"), check_vma=False
    )
```

```python
import math

import jax
import jax.numpy as jnp
from jax import lax
from jax.experimental import pallas as pl
from jax.experimental.pallas import tpu as pltpu
from jax.sharding import PartitionSpec as P

BF16, F32 = jnp.bfloat16, jnp.float32
VMEM_LIMIT = 48 * 1024 * 1024
WHOLE = pl.BlockSpec(memory_space=pltpu.VMEM)
SCALARS = pl.BlockSpec(memory_space=pltpu.SMEM)


def screen(values, sizes, significant):
    rows, cols = values.shape
    batches = sizes.shape[0]
    blocks = significant.shape[1]
    blocked = (
        values.reshape(batches, rows // batches, blocks, cols // blocks)
        * significant.astype(values.dtype)[:, None, :, None]
    )
    position = lax.broadcasted_iota(jnp.int32, (batches, rows // batches), 1)
    live = (position < sizes[:, None]).astype(jnp.float32).reshape(rows)
    return (blocked.reshape(rows, cols), live)


def any_sizes(orbital_values, occupied, trial, point_weights, batch_sizes, significant):
    screened, live = screen(orbital_values, batch_sizes, significant)
    rows, cols = screened.shape
    grid_count, occ_count = lax.axis_size("grid"), lax.axis_size("occ")
    columns = occupied.shape[1]
    me = lax.axis_index("grid")
    ring = [(i, (i + 1) % grid_count) for i in range(grid_count)]
    occ_ring = [(i, (i + 1) % occ_count) for i in range(occ_count)]

    def project_one(step, carry):
        panel, terms = carry
        term = jnp.dot(screened, panel, preferred_element_type=F32)
        terms = lax.dynamic_update_index_in_dim(terms, term, (me - step) % grid_count, 0)
        return lax.ppermute(panel, "grid", ring), terms

    joined = jnp.concatenate((occupied, trial), axis=1)
    terms = jnp.zeros((grid_count, rows, 2 * columns), F32)
    terms = lax.fori_loop(0, grid_count, project_one, (joined, terms))[1]

    def add_one(step, carry):
        moving, held = carry
        moving = lax.ppermute(moving, "occ", occ_ring)
        return moving, held + moving

    terms = lax.fori_loop(0, occ_count - 1, add_one, (terms, terms))[1]
    orbitals, response = terms[:, :, :columns], terms[:, :, columns:]
    density = jnp.sum(orbitals * response, axis=(0, 2)) * (1.0 / math.sqrt(columns * grid_count))
    weight = (point_weights * live)[None, :, None]
    kernel = (weight * (density[None, :, None] * orbitals + response)).astype(BF16)

    def contract_one(step, held):
        owner = (me + grid_count - 1 - step) % grid_count
        part = lax.dynamic_index_in_dim(kernel, owner, 0, keepdims=False)
        term = lax.dot_general(
            part, screened, (((0,), (0,)), ((), ())), preferred_element_type=F32
        )
        return lax.ppermute(held, "grid", ring) + term

    return lax.fori_loop(0, grid_count, contract_one, jnp.zeros((columns, cols), F32))


def compact(mine, got, mine_sig, got_sig, mine_to, got_to, width, tile, first):
    half, rows = mine.shape
    blocks = mine_sig.shape[0]
    per_window = rows // tile

    def body(first_ref, mine_ref, got_ref, msig_ref, gsig_ref, mto_ref, gto_ref, *outs):
        block_of = lax.broadcasted_iota(jnp.int32, (half, blocks), 0)
        begin = lax.broadcasted_iota(jnp.int32, (half, blocks), 1) * width
        spread = ((block_of >= begin) & (block_of < begin + width)).astype(F32).astype(BF16)
        slot = lax.broadcasted_iota(jnp.int32, (rows, 2 * rows), 1)

        def part(value_ref, sig_ref, to_ref):
            kept = jnp.dot(spread, sig_ref[...], preferred_element_type=F32)
            screened = (value_ref[...].astype(F32) * kept).astype(BF16)
            place = (to_ref[...] == slot).astype(F32).astype(BF16)
            return jnp.dot(screened, place, preferred_element_type=F32)

        window = part(mine_ref, msig_ref, mto_ref) + part(got_ref, gsig_ref, gto_ref)
        for j in range(2 * per_window):
            outs[j][...] = window[:, j * tile : (j + 1) * tile].astype(BF16)
        outs[-1][...] = jnp.where(
            first_ref[0] == 0, window[:, rows - tile : rows], window[:, rows : rows + tile]
        ).astype(BF16)

    shape = jax.ShapeDtypeStruct((half, tile), BF16)
    return pl.pallas_call(
        body,
        out_shape=(shape,) * (2 * per_window + 1),
        in_specs=[SCALARS] + [WHOLE] * 6,
        out_specs=(WHOLE,) * (2 * per_window + 1),
        compiler_params=pltpu.CompilerParams(vmem_limit_bytes=VMEM_LIMIT),
        name="compact",
        cost_estimate=pl.CostEstimate(
            flops=8 * half * rows * rows, bytes_accessed=8 * half * rows, transcendentals=0
        ),
    )(first[None], mine, got, mine_sig, got_sig, mine_to, got_to)


def read_tiles(tiles, refs):
    q, values = 0, []
    for parts in tiles:
        value = refs[q][...]
        for ref in refs[q + 1 : q + len(parts)]:
            value = value + ref[...]
        q += len(parts)
        values.append(value)
    return values


def project(panels, tiles, tile, shares, core):
    both, half = panels[0].shape
    piece = tile // shares
    count, number = len(tiles), len(panels)

    def body(core_ref, *refs):
        panel_refs, tile_refs = refs[:number], refs[number:-3]
        keep_ref, give_ref, terms_ref = refs[-3:]
        values = read_tiles(tiles, tile_refs)
        stacked = jnp.concatenate([ref[...] for ref in panel_refs])
        for s in range(0, count, 2):
            pair = jnp.concatenate(values[s : s + 2], axis=1)
            terms = jnp.dot(stacked, pair, preferred_element_type=F32)
            for p in range(number):
                turned = terms[p * both : (p + 1) * both].T
                for j in range(len(values[s : s + 2])):
                    q = p * count + s + j
                    terms_ref[q] = turned[j * tile : (j + 1) * tile].reshape(
                        2, shares // 2, piece, both
                    )
                    keep_ref[q] = terms_ref[q, core_ref[0]]
                    give_ref[q] = terms_ref[q, 1 - core_ref[0]]

    shape = jax.ShapeDtypeStruct((number * count, shares // 2, piece, both), F32)
    return pl.pallas_call(
        body,
        out_shape=(shape, shape),
        in_specs=[SCALARS] + [WHOLE] * (number + sum(map(len, tiles))),
        out_specs=(WHOLE, WHOLE),
        scratch_shapes=[pltpu.VMEM((number * count, 2, shares // 2, piece, both), F32)],
        compiler_params=pltpu.CompilerParams(vmem_limit_bytes=VMEM_LIMIT),
        name="project",
        cost_estimate=pl.CostEstimate(
            flops=2 * number * both * half * count * tile,
            bytes_accessed=2 * half * (number * both + count * tile)
            + 4 * number * count * tile * both,
            transcendentals=0,
        ),
    )(core[None], *panels, *sum(tiles, ()))


def contract(kernel, tiles, core):
    points, columns = kernel.shape
    half, tile = tiles[0][0].shape
    own = columns // 2
    count = len(tiles)

    def body(core_ref, kernel_ref, *refs):
        tile_refs, mine_ref, other_ref = refs[:-2], refs[-2], refs[-1]
        values = read_tiles(tiles, tile_refs)
        first = core_ref[0] == 0
        total = None
        for s in range(0, count, 2):
            pair = jnp.concatenate(values[s : s + 2], axis=1)
            turned = kernel_ref[s * tile : s * tile + pair.shape[1]].astype(F32).T
            low, high = turned[:own], turned[own:]
            turned = jnp.concatenate(
                (jnp.where(first, low, high), jnp.where(first, high, low))
            ).astype(BF16)
            term = lax.dot_general(
                turned, pair, (((1,), (1,)), ((), ())), preferred_element_type=F32
            )
            total = term if total is None else total + term
        mine_ref[...] = total[:own]
        other_ref[...] = total[own:]

    shape = jax.ShapeDtypeStruct((own, half), F32)
    return pl.pallas_call(
        body,
        out_shape=(shape, shape),
        in_specs=[SCALARS] + [WHOLE] * (1 + sum(map(len, tiles))),
        out_specs=(WHOLE, WHOLE),
        compiler_params=pltpu.CompilerParams(vmem_limit_bytes=VMEM_LIMIT),
        name="contract",
        cost_estimate=pl.CostEstimate(
            flops=2 * columns * half * points,
            bytes_accessed=2 * points * half + 4 * columns * half,
            transcendentals=0,
        ),
    )(core[None], kernel, *sum(tiles, ()))


def finish(core, ours, back, scale):
    own, half = ours.shape

    def body(core_ref, ours_ref, back_ref, out_ref):
        first = core_ref[0] == 0
        out_ref[:, :half] = jnp.where(first, ours_ref[...], back_ref[...]) * scale
        out_ref[:, half:] = jnp.where(first, back_ref[...], ours_ref[...]) * scale

    return pl.pallas_call(
        body,
        out_shape=jax.ShapeDtypeStruct((own, 2 * half), F32),
        in_specs=[SCALARS, WHOLE, WHOLE],
        out_specs=WHOLE,
        compiler_params=pltpu.CompilerParams(vmem_limit_bytes=VMEM_LIMIT),
        name="finish",
    )(core[None], ours, back)


def per_device(orbital_values, occupied, trial, point_weights, batch_sizes, significant):
    rows, cols = orbital_values.shape
    batches = batch_sizes.shape[0]
    slots = rows // batches
    blocks = significant.shape[1]
    columns = occupied.shape[1]
    grid_count = lax.axis_size("grid")
    occ_count = lax.axis_size("occ")
    chips = grid_count // 2
    shares = 2 * occ_count
    half = cols // 2
    total = columns * grid_count
    place = lax.axis_index("grid")
    chip, core = place // 2, place % 2
    occ = lax.axis_index("occ")
    member = core * occ_count + occ

    def flip(x, axis, bit):
        count = lax.axis_size(axis)
        return lax.ppermute(x, axis, [(i, i ^ bit) for i in range(count)])

    def along(pairs):
        return [(2 * a + c, 2 * b + c) for a, b in pairs for c in range(2)]

    def doubled(x, axis, bit, dim):
        got = flip(x, axis, bit)
        mine = (lax.axis_index(axis) & bit) == 0
        return jnp.where(
            mine, jnp.concatenate((x, got), axis=dim), jnp.concatenate((got, x), axis=dim)
        )

    def halves(whole, axis):
        size = whole.shape[axis] // 2
        mine = lax.dynamic_slice_in_dim(whole, core * size, size, axis)
        return mine, lax.dynamic_slice_in_dim(whole, (1 - core) * size, size, axis)

    grid_bits = [1 << b for b in range(grid_count.bit_length() - 1)]
    occ_bits = [1 << b for b in range(occ_count.bit_length() - 1)]

    mine, other = halves(orbital_values.T, 0)
    got = flip(other, "grid", 1)
    mine_sig, other_sig = halves(significant.T, 0)
    got_sig = flip(other_sig, "grid", 1)

    told = jnp.concatenate((batch_sizes.astype(F32), point_weights))[None]
    for bit in grid_bits:
        told = doubled(told, "grid", bit, 0)
    sizes = told[:, :batches].astype(jnp.int32).reshape(-1)
    weights = told[:, batches:].reshape(-1)

    batch = lax.broadcasted_iota(jnp.int32, (sizes.shape[0], sizes.shape[0]), 0)
    before = lax.broadcasted_iota(jnp.int32, (sizes.shape[0], sizes.shape[0]), 1) < batch
    start = jnp.sum(jnp.where(before, sizes[None, :], 0), axis=1)
    position = lax.broadcasted_iota(jnp.int32, (sizes.shape[0], slots), 1)
    to = jnp.where(position < sizes[:, None], start[:, None] + position, -4 * rows * grid_count)
    to = to.reshape(grid_count, rows)
    first = start.reshape(chips, -1)[:, 0]
    margin = rows // 2
    nominal = rows * lax.iota(jnp.int32, chips)
    fits = jnp.all(jnp.abs(first - nominal) <= margin) & (jnp.sum(sizes) <= rows * chips)

    tile = margin if margin % (8 * shares) == 0 else rows
    base = rows * chip - margin
    mine_to = lax.dynamic_index_in_dim(to, place, 0, keepdims=False) - base
    got_to = lax.dynamic_index_in_dim(to, place ^ 1, 0, keepdims=False) - base
    *own_tiles, edge = compact(
        mine,
        got,
        jnp.repeat(mine_sig.astype(BF16), slots, axis=1),
        jnp.repeat(got_sig.astype(BF16), slots, axis=1),
        mine_to[:, None],
        got_to[:, None],
        cols // blocks,
        tile,
        chip,
    )

    mine_panel, other_panel = halves(jnp.concatenate((occupied, trial), axis=1).T, 1)
    got_panel = flip(other_panel, "grid", 1)
    panels = jnp.where(
        core == 0,
        jnp.concatenate(
            (mine_panel[:columns], got_panel[:columns], mine_panel[columns:], got_panel[columns:])
        ),
        jnp.concatenate(
            (got_panel[:columns], mine_panel[:columns], got_panel[columns:], mine_panel[columns:])
        ),
    )

    piece = tile // shares
    per_window = rows // tile
    tile_count = (chips + 1) * per_window
    tile_iota = lax.iota(jnp.int32, tile_count)
    last = chips - 1
    ends = [(0, 1), (last, last - 1)]
    homes = [(b, a) for a, b in ends]
    none = -2 * per_window
    low, high = own_tiles[:per_window], own_tiles[per_window:]

    def sent(tiles, pairs):
        return [lax.ppermute(x, "grid", along(pairs)) for x in tiles]

    stages = []
    leftward, rightward = low, high
    far_panels = None
    for t in range(1, last):
        to_left = [(a, a - 1) for a in range(1, chips) if t == 1 or a + t - 1 < chips]
        to_right = [(a, a + 1) for a in range(last) if t == 1 or a + 2 - t > 0]
        from_right, from_left = [], []
        for x, y in zip(leftward, rightward):
            from_right += sent([x], to_left)
            from_left += sent([y], to_right)
        (edge,) = sent([edge], [(t - 1, t), (chips - t, last - t)])
        if t == 1:
            from_right = [x + y for x, y in zip(from_right, high)]
            from_left = [x + y for x, y in zip(from_left, low)]
            (far_panels,) = sent([panels], ends)
        right = jnp.where((chip + t <= last) | (t == 1), (chip + t) * per_window, none)
        left = jnp.where((chip + 1 - t > 0) | (t == 1), (chip + 1 - t) * per_window, none)
        edge_at = jnp.where(
            chip == t, per_window - 1, jnp.where(chip == last - t, chips * per_window, none)
        )
        if 2 * t > last:
            at = jnp.maximum(right, left)
            jobs = [((x, y), at + j) for j, (x, y) in enumerate(zip(from_right, from_left))]
        else:
            jobs = [((x,), right + j) for j, x in enumerate(from_right)]
            jobs += [((x,), left + j) for j, x in enumerate(from_left)]
        stages.append(jobs + [((edge,), edge_at)])
        leftward, rightward = from_right, from_left
    late = [
        (x, y) for x, y in zip(sent(leftward, homes[:1]), sent(rightward, homes[1:]))
    ]

    def summed(panels, tiles):
        keep, give = project(panels, tiles, tile, shares, core)
        value = keep + flip(give, "grid", 1)
        for bit in reversed(occ_bits):
            upper = (occ & bit) != 0
            low_part, high_part = value[:, :bit], value[:, bit:]
            got = flip(jnp.where(upper, low_part, high_part), "occ", bit)
            value = jnp.where(upper, high_part, low_part) + got
        return value[:, 0]

    def shared_density(value, at):
        product = jnp.sum(value[:, :, : 2 * columns] * value[:, :, 2 * columns :], axis=2)
        here = (at[:, None] == tile_iota[None, :])[:, :, None]
        return jnp.sum(jnp.where(here, product[:, None], 0.0), axis=0)

    per_group = -(-len(stages) // 2)
    first_jobs = sum(stages[:per_group], [])
    second_jobs = sum(stages[per_group:], [])
    first_at = jnp.stack([at for _, at in first_jobs])
    second_at = jnp.stack([at for _, at in second_jobs])
    first_value = summed([panels], [w for w, _ in first_jobs])
    far_count = per_window + 1
    second_tiles, first_value = lax.optimization_barrier(
        ([w for w, _ in second_jobs], first_value)
    )
    value = summed([panels, far_panels], second_tiles)
    far_value = value[-far_count:]
    second_value = value[: len(second_jobs)]
    density = shared_density(first_value, first_at) + shared_density(
        jnp.concatenate((second_value, far_value)),
        jnp.concatenate((second_at, second_at[-far_count:])),
    )
    density, late = lax.optimization_barrier((density, late))
    for bit in grid_bits[1:]:
        density = density + flip(density, "grid", bit)
    density = density * (1.0 / math.sqrt(total))
    density, edge = lax.optimization_barrier((density, edge))
    late = late + [tuple(sent([edge], homes))]

    tiles = [w for w, _ in first_jobs] + second_tiles + late
    values = [first_value, second_value, *sent([far_value], homes)]
    outer = lax.iota(jnp.int32, per_window)
    places = [
        first_at,
        second_at,
        jnp.where(
            chip == 0,
            jnp.concatenate((outer + last * per_window, outer[:1] + chips * per_window)),
            jnp.concatenate((outer + per_window, outer[:1] + per_window - 1)),
        ),
    ]

    at = tile_iota[:, None] * tile - margin + member * piece + lax.iota(jnp.int32, piece)[None, :]
    weight = jnp.sum(
        jnp.where(to.reshape(1, -1) == at.reshape(-1, 1), weights[None, :], 0.0), axis=1
    ).reshape(tile_count, piece)

    values, places = jnp.concatenate(values, axis=0), jnp.concatenate(places)
    here = (places[:, None] == tile_iota[None, :])[:, :, None]
    density_here = jnp.sum(jnp.where(here, density[None], 0.0), axis=1)[:, :, None]
    weight_here = jnp.sum(jnp.where(here, weight[None], 0.0), axis=1)[:, :, None]
    orbitals, response = values[:, :, : 2 * columns], values[:, :, 2 * columns :]
    kernel = (weight_here * (density_here * orbitals + response)).astype(BF16)[:, None]
    for bit in occ_bits:
        kernel = doubled(kernel, "occ", bit, 1)
    kernel = doubled(kernel, "grid", 1, 1).reshape(-1, 2 * columns)

    ours, theirs = contract(kernel, tiles, core)
    back = flip(theirs, "grid", 1)
    scale = 1.0 / math.sqrt(rows * grid_count)
    exchange = lax.cond(
        fits,
        lambda core, ours, back, *given: finish(core, ours, back, scale),
        lambda core, ours, back, *given: any_sizes(*given) * scale,
        core,
        ours,
        back,
        orbital_values,
        occupied,
        trial,
        point_weights,
        batch_sizes,
        significant,
    )
    return exchange.T


def solution(mesh):
    placed = (
        P("grid", "occ"),
        P("occ", "grid"),
        P("occ", "grid"),
        P("grid"),
        P("grid"),
        P("grid", "occ"),
    )
    return jax.shard_map(
        per_device, mesh=mesh, in_specs=placed, out_specs=P("occ", "grid"), check_vma=False
    )
```

```python
import math

import jax
import jax.numpy as jnp
from jax import lax
from jax.experimental import pallas as pl
from jax.experimental.pallas import tpu as pltpu
from jax.sharding import PartitionSpec as P

BF16, F32 = jnp.bfloat16, jnp.float32
VMEM_LIMIT = 48 * 1024 * 1024
WHOLE = pl.BlockSpec(memory_space=pltpu.VMEM)
SCALARS = pl.BlockSpec(memory_space=pltpu.SMEM)


def screen(values, sizes, significant):
    rows, cols = values.shape
    batches = sizes.shape[0]
    blocks = significant.shape[1]
    blocked = (
        values.reshape(batches, rows // batches, blocks, cols // blocks)
        * significant.astype(values.dtype)[:, None, :, None]
    )
    position = lax.broadcasted_iota(jnp.int32, (batches, rows // batches), 1)
    live = (position < sizes[:, None]).astype(jnp.float32).reshape(rows)
    return (blocked.reshape(rows, cols), live)


def any_sizes(orbital_values, occupied, trial, point_weights, batch_sizes, significant):
    screened, live = screen(orbital_values, batch_sizes, significant)
    rows, cols = screened.shape
    grid_count, occ_count = lax.axis_size("grid"), lax.axis_size("occ")
    columns = occupied.shape[1]
    me = lax.axis_index("grid")
    ring = [(i, (i + 1) % grid_count) for i in range(grid_count)]
    occ_ring = [(i, (i + 1) % occ_count) for i in range(occ_count)]

    def project_one(step, carry):
        panel, terms = carry
        term = jnp.dot(screened, panel, preferred_element_type=F32)
        terms = lax.dynamic_update_index_in_dim(terms, term, (me - step) % grid_count, 0)
        return lax.ppermute(panel, "grid", ring), terms

    joined = jnp.concatenate((occupied, trial), axis=1)
    terms = jnp.zeros((grid_count, rows, 2 * columns), F32)
    terms = lax.fori_loop(0, grid_count, project_one, (joined, terms))[1]

    def add_one(step, carry):
        moving, held = carry
        moving = lax.ppermute(moving, "occ", occ_ring)
        return moving, held + moving

    terms = lax.fori_loop(0, occ_count - 1, add_one, (terms, terms))[1]
    orbitals, response = terms[:, :, :columns], terms[:, :, columns:]
    density = jnp.sum(orbitals * response, axis=(0, 2)) * (1.0 / math.sqrt(columns * grid_count))
    weight = (point_weights * live)[None, :, None]
    kernel = (weight * (density[None, :, None] * orbitals + response)).astype(BF16)

    def contract_one(step, held):
        owner = (me + grid_count - 1 - step) % grid_count
        part = lax.dynamic_index_in_dim(kernel, owner, 0, keepdims=False)
        term = lax.dot_general(
            part, screened, (((0,), (0,)), ((), ())), preferred_element_type=F32
        )
        return lax.ppermute(held, "grid", ring) + term

    return lax.fori_loop(0, grid_count, contract_one, jnp.zeros((columns, cols), F32))


def compact(mine, got, mine_sig, got_sig, mine_to, got_to, width, tile, first):
    half, rows = mine.shape
    blocks = mine_sig.shape[0]
    per_window = rows // tile

    def body(first_ref, mine_ref, got_ref, msig_ref, gsig_ref, mto_ref, gto_ref, *outs):
        block_of = lax.broadcasted_iota(jnp.int32, (half, blocks), 0)
        begin = lax.broadcasted_iota(jnp.int32, (half, blocks), 1) * width
        spread = ((block_of >= begin) & (block_of < begin + width)).astype(F32).astype(BF16)
        slot = lax.broadcasted_iota(jnp.int32, (rows, 2 * rows), 1)

        def part(value_ref, sig_ref, to_ref):
            kept = jnp.dot(spread, sig_ref[...], preferred_element_type=F32)
            screened = (value_ref[...].astype(F32) * kept).astype(BF16)
            place = (to_ref[...] == slot).astype(F32).astype(BF16)
            return jnp.dot(screened, place, preferred_element_type=F32)

        window = part(mine_ref, msig_ref, mto_ref) + part(got_ref, gsig_ref, gto_ref)
        for j in range(2 * per_window):
            outs[j][...] = window[:, j * tile : (j + 1) * tile].astype(BF16)
        outs[-1][...] = jnp.where(
            first_ref[0] == 0, window[:, rows - tile : rows], window[:, rows : rows + tile]
        ).astype(BF16)

    shape = jax.ShapeDtypeStruct((half, tile), BF16)
    return pl.pallas_call(
        body,
        out_shape=(shape,) * (2 * per_window + 1),
        in_specs=[SCALARS] + [WHOLE] * 6,
        out_specs=(WHOLE,) * (2 * per_window + 1),
        compiler_params=pltpu.CompilerParams(vmem_limit_bytes=VMEM_LIMIT),
        name="compact",
        cost_estimate=pl.CostEstimate(
            flops=8 * half * rows * rows, bytes_accessed=8 * half * rows, transcendentals=0
        ),
    )(first[None], mine, got, mine_sig, got_sig, mine_to, got_to)


def read_tiles(tiles, refs):
    q, values = 0, []
    for parts in tiles:
        value = refs[q][...]
        for ref in refs[q + 1 : q + len(parts)]:
            value = value + ref[...]
        q += len(parts)
        values.append(value)
    return values


def project(panels, tiles, tile, shares, core):
    both, half = panels[0].shape
    piece = tile // shares
    count, number = len(tiles), len(panels)

    def body(core_ref, *refs):
        panel_refs, tile_refs = refs[:number], refs[number:-3]
        keep_ref, give_ref, terms_ref = refs[-3:]
        values = read_tiles(tiles, tile_refs)
        stacked = jnp.concatenate([ref[...] for ref in panel_refs])
        for s in range(0, count, 2):
            pair = jnp.concatenate(values[s : s + 2], axis=1)
            terms = jnp.dot(stacked, pair, preferred_element_type=F32)
            for p in range(number):
                turned = terms[p * both : (p + 1) * both].T
                for j in range(len(values[s : s + 2])):
                    q = p * count + s + j
                    terms_ref[q] = turned[j * tile : (j + 1) * tile].reshape(
                        2, shares // 2, piece, both
                    )
                    keep_ref[q] = terms_ref[q, core_ref[0]]
                    give_ref[q] = terms_ref[q, 1 - core_ref[0]]

    shape = jax.ShapeDtypeStruct((number * count, shares // 2, piece, both), F32)
    return pl.pallas_call(
        body,
        out_shape=(shape, shape),
        in_specs=[SCALARS] + [WHOLE] * (number + sum(map(len, tiles))),
        out_specs=(WHOLE, WHOLE),
        scratch_shapes=[pltpu.VMEM((number * count, 2, shares // 2, piece, both), F32)],
        compiler_params=pltpu.CompilerParams(vmem_limit_bytes=VMEM_LIMIT),
        name="project",
        cost_estimate=pl.CostEstimate(
            flops=2 * number * both * half * count * tile,
            bytes_accessed=2 * half * (number * both + count * tile)
            + 4 * number * count * tile * both,
            transcendentals=0,
        ),
    )(core[None], *panels, *sum(tiles, ()))


def contract(kernel, tiles, core):
    points, columns = kernel.shape
    half, tile = tiles[0][0].shape
    own = columns // 2
    count = len(tiles)

    def body(core_ref, kernel_ref, *refs):
        tile_refs, mine_ref, other_ref = refs[:-2], refs[-2], refs[-1]
        values = read_tiles(tiles, tile_refs)
        first = core_ref[0] == 0
        total = None
        for s in range(0, count, 2):
            pair = jnp.concatenate(values[s : s + 2], axis=1)
            turned = kernel_ref[s * tile : s * tile + pair.shape[1]].astype(F32).T
            low, high = turned[:own], turned[own:]
            turned = jnp.concatenate(
                (jnp.where(first, low, high), jnp.where(first, high, low))
            ).astype(BF16)
            term = lax.dot_general(
                turned, pair, (((1,), (1,)), ((), ())), preferred_element_type=F32
            )
            total = term if total is None else total + term
        mine_ref[...] = total[:own]
        other_ref[...] = total[own:]

    shape = jax.ShapeDtypeStruct((own, half), F32)
    return pl.pallas_call(
        body,
        out_shape=(shape, shape),
        in_specs=[SCALARS] + [WHOLE] * (1 + sum(map(len, tiles))),
        out_specs=(WHOLE, WHOLE),
        compiler_params=pltpu.CompilerParams(vmem_limit_bytes=VMEM_LIMIT),
        name="contract",
        cost_estimate=pl.CostEstimate(
            flops=2 * columns * half * points,
            bytes_accessed=2 * points * half + 4 * columns * half,
            transcendentals=0,
        ),
    )(core[None], kernel, *sum(tiles, ()))


def finish(core, ours, back, scale):
    own, half = ours.shape

    def body(core_ref, ours_ref, back_ref, out_ref):
        first = core_ref[0] == 0
        out_ref[:, :half] = jnp.where(first, ours_ref[...], back_ref[...]) * scale
        out_ref[:, half:] = jnp.where(first, back_ref[...], ours_ref[...]) * scale

    return pl.pallas_call(
        body,
        out_shape=jax.ShapeDtypeStruct((own, 2 * half), F32),
        in_specs=[SCALARS, WHOLE, WHOLE],
        out_specs=WHOLE,
        compiler_params=pltpu.CompilerParams(vmem_limit_bytes=VMEM_LIMIT),
        name="finish",
    )(core[None], ours, back)


def per_device(orbital_values, occupied, trial, point_weights, batch_sizes, significant):
    rows, cols = orbital_values.shape
    batches = batch_sizes.shape[0]
    slots = rows // batches
    blocks = significant.shape[1]
    columns = occupied.shape[1]
    grid_count = lax.axis_size("grid")
    occ_count = lax.axis_size("occ")
    chips = grid_count // 2
    shares = 2 * occ_count
    half = cols // 2
    total = columns * grid_count
    place = lax.axis_index("grid")
    chip, core = place // 2, place % 2
    occ = lax.axis_index("occ")
    member = core * occ_count + occ

    def flip(x, axis, bit):
        count = lax.axis_size(axis)
        return lax.ppermute(x, axis, [(i, i ^ bit) for i in range(count)])

    def along(pairs):
        return [(2 * a + c, 2 * b + c) for a, b in pairs for c in range(2)]

    def doubled(x, axis, bit, dim):
        got = flip(x, axis, bit)
        mine = (lax.axis_index(axis) & bit) == 0
        return jnp.where(
            mine, jnp.concatenate((x, got), axis=dim), jnp.concatenate((got, x), axis=dim)
        )

    def halves(whole, axis):
        size = whole.shape[axis] // 2
        mine = lax.dynamic_slice_in_dim(whole, core * size, size, axis)
        return mine, lax.dynamic_slice_in_dim(whole, (1 - core) * size, size, axis)

    grid_bits = [1 << b for b in range(grid_count.bit_length() - 1)]
    occ_bits = [1 << b for b in range(occ_count.bit_length() - 1)]

    mine, other = halves(orbital_values.T, 0)
    got = flip(other, "grid", 1)
    mine_sig, other_sig = halves(significant.T, 0)
    got_sig = flip(other_sig, "grid", 1)

    told = jnp.concatenate((batch_sizes.astype(F32), point_weights))[None]
    for bit in grid_bits:
        told = doubled(told, "grid", bit, 0)
    sizes = told[:, :batches].astype(jnp.int32).reshape(-1)
    weights = told[:, batches:].reshape(-1)

    batch = lax.broadcasted_iota(jnp.int32, (sizes.shape[0], sizes.shape[0]), 0)
    before = lax.broadcasted_iota(jnp.int32, (sizes.shape[0], sizes.shape[0]), 1) < batch
    start = jnp.sum(jnp.where(before, sizes[None, :], 0), axis=1)
    position = lax.broadcasted_iota(jnp.int32, (sizes.shape[0], slots), 1)
    to = jnp.where(position < sizes[:, None], start[:, None] + position, -4 * rows * grid_count)
    to = to.reshape(grid_count, rows)
    first = start.reshape(chips, -1)[:, 0]
    margin = rows // 2
    nominal = rows * lax.iota(jnp.int32, chips)
    fits = jnp.all(jnp.abs(first - nominal) <= margin) & (jnp.sum(sizes) <= rows * chips)

    tile = margin if margin % (8 * shares) == 0 else rows
    base = rows * chip - margin
    mine_to = lax.dynamic_index_in_dim(to, place, 0, keepdims=False) - base
    got_to = lax.dynamic_index_in_dim(to, place ^ 1, 0, keepdims=False) - base
    *own_tiles, edge = compact(
        mine,
        got,
        jnp.repeat(mine_sig.astype(BF16), slots, axis=1),
        jnp.repeat(got_sig.astype(BF16), slots, axis=1),
        mine_to[:, None],
        got_to[:, None],
        cols // blocks,
        tile,
        chip,
    )

    mine_panel, other_panel = halves(jnp.concatenate((occupied, trial), axis=1).T, 1)
    got_panel = flip(other_panel, "grid", 1)
    panels = jnp.where(
        core == 0,
        jnp.concatenate(
            (mine_panel[:columns], got_panel[:columns], mine_panel[columns:], got_panel[columns:])
        ),
        jnp.concatenate(
            (got_panel[:columns], mine_panel[:columns], got_panel[columns:], mine_panel[columns:])
        ),
    )

    piece = tile // shares
    per_window = rows // tile
    tile_count = (chips + 1) * per_window
    tile_iota = lax.iota(jnp.int32, tile_count)
    last = chips - 1
    ends = [(0, 1), (last, last - 1)]
    homes = [(b, a) for a, b in ends]
    none = -2 * per_window
    low, high = own_tiles[:per_window], own_tiles[per_window:]

    def sent(tiles, pairs):
        return [lax.ppermute(x, "grid", along(pairs)) for x in tiles]

    stages = []
    leftward, rightward = low, high
    far_panels = None
    for t in range(1, last):
        to_left = [(a, a - 1) for a in range(1, chips) if t == 1 or a + t - 1 < chips]
        to_right = [(a, a + 1) for a in range(last) if t == 1 or a + 2 - t > 0]
        from_right, from_left = [], []
        for x, y in zip(leftward, rightward):
            from_right += sent([x], to_left)
            from_left += sent([y], to_right)
        (edge,) = sent([edge], [(t - 1, t), (chips - t, last - t)])
        if t == 1:
            from_right = [x + y for x, y in zip(from_right, high)]
            from_left = [x + y for x, y in zip(from_left, low)]
            far_panels, edge = lax.optimization_barrier((panels, edge))
            (far_panels,) = sent([far_panels], ends)
        right = jnp.where((chip + t <= last) | (t == 1), (chip + t) * per_window, none)
        left = jnp.where((chip + 1 - t > 0) | (t == 1), (chip + 1 - t) * per_window, none)
        edge_at = jnp.where(
            chip == t, per_window - 1, jnp.where(chip == last - t, chips * per_window, none)
        )
        if 2 * t > last:
            at = jnp.maximum(right, left)
            jobs = [((x, y), at + j) for j, (x, y) in enumerate(zip(from_right, from_left))]
        else:
            jobs = [((x,), right + j) for j, x in enumerate(from_right)]
            jobs += [((x,), left + j) for j, x in enumerate(from_left)]
        stages.append(jobs + [((edge,), edge_at)])
        leftward, rightward = from_right, from_left
    late = [
        (x, y) for x, y in zip(sent(leftward, homes[:1]), sent(rightward, homes[1:]))
    ]

    def summed(panels, tiles, beside=()):
        keep, give = project(panels, tiles, tile, shares, core)
        value = keep + flip(give, "grid", 1)
        for bit in reversed(occ_bits):
            if bit == 1:
                value, beside = lax.optimization_barrier((value, beside))
            upper = (occ & bit) != 0
            low_part, high_part = value[:, :bit], value[:, bit:]
            got = flip(jnp.where(upper, low_part, high_part), "occ", bit)
            value = jnp.where(upper, high_part, low_part) + got
        return value[:, 0], beside

    def shared_density(value, at):
        product = jnp.sum(value[:, :, : 2 * columns] * value[:, :, 2 * columns :], axis=2)
        here = (at[:, None] == tile_iota[None, :])[:, :, None]
        return jnp.sum(jnp.where(here, product[:, None], 0.0), axis=0)

    per_group = -(-len(stages) // 2)
    first_jobs = sum(stages[:per_group], [])
    second_jobs = sum(stages[per_group:], [])
    first_at = jnp.stack([at for _, at in first_jobs])
    second_at = jnp.stack([at for _, at in second_jobs])
    first_value, _ = summed([panels], [w for w, _ in first_jobs])
    far_count = per_window + 1
    second_tiles, late[:1] = lax.optimization_barrier(([w for w, _ in second_jobs], late[:1]))
    value, late[1:] = summed([panels, far_panels], second_tiles, late[1:])
    far_value = value[-far_count:]
    second_value = value[: len(second_jobs)]
    density = shared_density(first_value, first_at) + shared_density(
        jnp.concatenate((second_value, far_value)),
        jnp.concatenate((second_at, second_at[-far_count:])),
    )
    for bit in grid_bits[1:]:
        density = density + flip(density, "grid", bit)
    density = density * (1.0 / math.sqrt(total))
    density, edge = lax.optimization_barrier((density, edge))
    late = late + [tuple(sent([edge], homes))]

    tiles = [w for w, _ in first_jobs] + second_tiles + late
    values = [first_value, second_value, *sent([far_value], homes)]
    outer = lax.iota(jnp.int32, per_window)
    places = [
        first_at,
        second_at,
        jnp.where(
            chip == 0,
            jnp.concatenate((outer + last * per_window, outer[:1] + chips * per_window)),
            jnp.concatenate((outer + per_window, outer[:1] + per_window - 1)),
        ),
    ]

    at = tile_iota[:, None] * tile - margin + member * piece + lax.iota(jnp.int32, piece)[None, :]
    weight = jnp.sum(
        jnp.where(to.reshape(1, -1) == at.reshape(-1, 1), weights[None, :], 0.0), axis=1
    ).reshape(tile_count, piece)

    values, places = jnp.concatenate(values, axis=0), jnp.concatenate(places)
    here = (places[:, None] == tile_iota[None, :])[:, :, None]
    density_here = jnp.sum(jnp.where(here, density[None], 0.0), axis=1)[:, :, None]
    weight_here = jnp.sum(jnp.where(here, weight[None], 0.0), axis=1)[:, :, None]
    orbitals, response = values[:, :, : 2 * columns], values[:, :, 2 * columns :]
    kernel = (weight_here * (density_here * orbitals + response)).astype(BF16)[:, None]
    for bit in occ_bits:
        kernel = doubled(kernel, "occ", bit, 1)
    kernel = doubled(kernel, "grid", 1, 1).reshape(-1, 2 * columns)

    ours, theirs = contract(kernel, tiles, core)
    back = flip(theirs, "grid", 1)
    scale = 1.0 / math.sqrt(rows * grid_count)
    exchange = lax.cond(
        fits,
        lambda core, ours, back, *given: finish(core, ours, back, scale),
        lambda core, ours, back, *given: any_sizes(*given) * scale,
        core,
        ours,
        back,
        orbital_values,
        occupied,
        trial,
        point_weights,
        batch_sizes,
        significant,
    )
    return exchange.T


def solution(mesh):
    placed = (
        P("grid", "occ"),
        P("occ", "grid"),
        P("occ", "grid"),
        P("grid"),
        P("grid"),
        P("grid", "occ"),
    )
    return jax.shard_map(
        per_device, mesh=mesh, in_specs=placed, out_specs=P("occ", "grid"), check_vma=False
    )
```

```python
import math

import jax
import jax.numpy as jnp
from jax import lax
from jax.experimental import pallas as pl
from jax.experimental.pallas import tpu as pltpu
from jax.sharding import PartitionSpec as P

BF16, F32 = jnp.bfloat16, jnp.float32
VMEM_LIMIT = 48 * 1024 * 1024
WHOLE = pl.BlockSpec(memory_space=pltpu.VMEM)
SCALARS = pl.BlockSpec(memory_space=pltpu.SMEM)


def screen(values, sizes, significant):
    rows, cols = values.shape
    batches = sizes.shape[0]
    blocks = significant.shape[1]
    blocked = (
        values.reshape(batches, rows // batches, blocks, cols // blocks)
        * significant.astype(values.dtype)[:, None, :, None]
    )
    position = lax.broadcasted_iota(jnp.int32, (batches, rows // batches), 1)
    live = (position < sizes[:, None]).astype(jnp.float32).reshape(rows)
    return (blocked.reshape(rows, cols), live)


def any_sizes(orbital_values, occupied, trial, point_weights, batch_sizes, significant):
    screened, live = screen(orbital_values, batch_sizes, significant)
    rows, cols = screened.shape
    grid_count, occ_count = lax.axis_size("grid"), lax.axis_size("occ")
    columns = occupied.shape[1]
    me = lax.axis_index("grid")
    ring = [(i, (i + 1) % grid_count) for i in range(grid_count)]
    occ_ring = [(i, (i + 1) % occ_count) for i in range(occ_count)]

    def project_one(step, carry):
        panel, terms = carry
        term = jnp.dot(screened, panel, preferred_element_type=F32)
        terms = lax.dynamic_update_index_in_dim(terms, term, (me - step) % grid_count, 0)
        return lax.ppermute(panel, "grid", ring), terms

    joined = jnp.concatenate((occupied, trial), axis=1)
    terms = jnp.zeros((grid_count, rows, 2 * columns), F32)
    terms = lax.fori_loop(0, grid_count, project_one, (joined, terms))[1]

    def add_one(step, carry):
        moving, held = carry
        moving = lax.ppermute(moving, "occ", occ_ring)
        return moving, held + moving

    terms = lax.fori_loop(0, occ_count - 1, add_one, (terms, terms))[1]
    orbitals, response = terms[:, :, :columns], terms[:, :, columns:]
    density = jnp.sum(orbitals * response, axis=(0, 2)) * (1.0 / math.sqrt(columns * grid_count))
    weight = (point_weights * live)[None, :, None]
    kernel = (weight * (density[None, :, None] * orbitals + response)).astype(BF16)

    def contract_one(step, held):
        owner = (me + grid_count - 1 - step) % grid_count
        part = lax.dynamic_index_in_dim(kernel, owner, 0, keepdims=False)
        term = lax.dot_general(
            part, screened, (((0,), (0,)), ((), ())), preferred_element_type=F32
        )
        return lax.ppermute(held, "grid", ring) + term

    return lax.fori_loop(0, grid_count, contract_one, jnp.zeros((columns, cols), F32))


def compact(mine, got, mine_sig, got_sig, mine_to, got_to, width, tile):
    half, rows = mine.shape
    blocks = mine_sig.shape[0]
    count = rows // tile + 2

    def body(mine_ref, got_ref, msig_ref, gsig_ref, mto_ref, gto_ref, *outs):
        block_of = lax.broadcasted_iota(jnp.int32, (half, blocks), 0)
        begin = lax.broadcasted_iota(jnp.int32, (half, blocks), 1) * width
        spread = ((block_of >= begin) & (block_of < begin + width)).astype(F32).astype(BF16)
        slot = lax.broadcasted_iota(jnp.int32, (rows, count * tile), 1)

        def part(value_ref, sig_ref, to_ref):
            kept = jnp.dot(spread, sig_ref[...], preferred_element_type=F32)
            screened = (value_ref[...].astype(F32) * kept).astype(BF16)
            place = (to_ref[...] == slot).astype(F32).astype(BF16)
            return jnp.dot(screened, place, preferred_element_type=F32)

        window = part(mine_ref, msig_ref, mto_ref) + part(got_ref, gsig_ref, gto_ref)
        for j in range(count):
            outs[j][...] = window[:, j * tile : (j + 1) * tile].astype(BF16)

    shape = jax.ShapeDtypeStruct((half, tile), BF16)
    return pl.pallas_call(
        body,
        out_shape=(shape,) * count,
        in_specs=[WHOLE] * 6,
        out_specs=(WHOLE,) * count,
        compiler_params=pltpu.CompilerParams(vmem_limit_bytes=VMEM_LIMIT),
        name="compact",
        cost_estimate=pl.CostEstimate(
            flops=8 * half * rows * rows, bytes_accessed=8 * half * rows, transcendentals=0
        ),
    )(mine, got, mine_sig, got_sig, mine_to, got_to)


def straighten(tiles, first, last):
    half, tile = first.shape
    count = len(tiles)

    def body(*refs):
        tile_refs, first_ref, last_ref, out_ref = refs[:count], *refs[count:]
        for j in range(count):
            value = tile_refs[j][...]
            if j == 0:
                value = value + first_ref[...]
            if j == count - 1:
                value = value + last_ref[...]
            out_ref[:, j * tile : (j + 1) * tile] = value

    return pl.pallas_call(
        body,
        out_shape=jax.ShapeDtypeStruct((half, count * tile), BF16),
        in_specs=[WHOLE] * (count + 2),
        out_specs=WHOLE,
        compiler_params=pltpu.CompilerParams(vmem_limit_bytes=VMEM_LIMIT),
        name="straighten",
    )(*tiles, first, last)


def stack_panels(mine, got, core):
    both, half = mine.shape
    columns = both // 2

    def body(core_ref, mine_ref, got_ref, out_ref):
        first = core_ref[0] == 0
        for j in range(2):
            low, high = mine_ref[j * columns : (j + 1) * columns], got_ref[j * columns : (j + 1) * columns]
            out_ref[2 * j * columns : (2 * j + 1) * columns] = jnp.where(first, low, high)
            out_ref[(2 * j + 1) * columns : (2 * j + 2) * columns] = jnp.where(first, high, low)

    return pl.pallas_call(
        body,
        out_shape=jax.ShapeDtypeStruct((2 * both, half), BF16),
        in_specs=[SCALARS, WHOLE, WHOLE],
        out_specs=WHOLE,
        compiler_params=pltpu.CompilerParams(vmem_limit_bytes=VMEM_LIMIT),
        name="stack_panels",
    )(core[None], mine, got)


def read_windows(windows, refs):
    q, values = 0, []
    for parts in windows:
        value = [ref[...] for ref in refs[q : q + len(parts)]]
        values.append(jnp.concatenate(value, axis=1) if len(value) > 1 else value[0])
        q += len(parts)
    return values


def project(panels, windows, tile, shares, core):
    both, half = panels[0][0].shape
    piece = tile // shares
    per_window = sum(x.shape[1] for x in windows[0]) // tile
    number = len(windows)
    wanted = list({id(p): p for ps in panels for p in ps}.values())
    index = [[[id(w) for w in wanted].index(id(p)) for p in ps] for ps in panels]
    tiles = per_window * sum(map(len, panels))

    def body(core_ref, *refs):
        panel_refs, values = refs[: len(wanted)], read_windows(windows, refs[len(wanted) : -3])
        keep_ref, give_ref, terms_ref = refs[-3:]
        q = 0
        for s in range(number):
            stacked = [panel_refs[i][...] for i in index[s]]
            stacked = jnp.concatenate(stacked) if len(stacked) > 1 else stacked[0]
            terms = jnp.dot(stacked, values[s], preferred_element_type=F32)
            for p in range(len(index[s])):
                turned = terms[p * both : (p + 1) * both].T
                for j in range(per_window):
                    terms_ref[q] = turned[j * tile : (j + 1) * tile].reshape(
                        2, shares // 2, piece, both
                    )
                    keep_ref[q] = terms_ref[q, core_ref[0]]
                    give_ref[q] = terms_ref[q, 1 - core_ref[0]]
                    q += 1

    shape = jax.ShapeDtypeStruct((tiles, shares // 2, piece, both), F32)
    return pl.pallas_call(
        body,
        out_shape=(shape, shape),
        in_specs=[SCALARS] + [WHOLE] * (len(wanted) + sum(map(len, windows))),
        out_specs=(WHOLE, WHOLE),
        scratch_shapes=[pltpu.VMEM((tiles, 2, shares // 2, piece, both), F32)],
        compiler_params=pltpu.CompilerParams(vmem_limit_bytes=VMEM_LIMIT),
        name="project",
        cost_estimate=pl.CostEstimate(
            flops=2 * both * half * tiles * tile,
            bytes_accessed=2 * half * (both + tiles * tile) + 4 * tiles * tile * both,
            transcendentals=0,
        ),
    )(core[None], *wanted, *sum(windows, ()))


def contract(kernel, windows, core):
    points, columns = kernel.shape
    half = windows[0][0].shape[0]
    own = columns // 2
    count = len(windows)
    rows = points // count

    def body(core_ref, kernel_ref, *refs):
        values, mine_ref, other_ref = read_windows(windows, refs[:-2]), refs[-2], refs[-1]
        first = core_ref[0] == 0
        total = None
        for s in range(count):
            turned = kernel_ref[s * rows : (s + 1) * rows].astype(F32).T
            low, high = turned[:own], turned[own:]
            turned = jnp.concatenate(
                (jnp.where(first, low, high), jnp.where(first, high, low))
            ).astype(BF16)
            term = lax.dot_general(
                turned, values[s], (((1,), (1,)), ((), ())), preferred_element_type=F32
            )
            total = term if total is None else total + term
        mine_ref[...] = total[:own]
        other_ref[...] = total[own:]

    shape = jax.ShapeDtypeStruct((own, half), F32)
    return pl.pallas_call(
        body,
        out_shape=(shape, shape),
        in_specs=[SCALARS] + [WHOLE] * (1 + sum(map(len, windows))),
        out_specs=(WHOLE, WHOLE),
        compiler_params=pltpu.CompilerParams(vmem_limit_bytes=VMEM_LIMIT),
        name="contract",
        cost_estimate=pl.CostEstimate(
            flops=2 * columns * half * points,
            bytes_accessed=2 * points * half + 4 * columns * half,
            transcendentals=0,
        ),
    )(core[None], kernel, *sum(windows, ()))


def finish(core, ours, back, scale):
    own, half = ours.shape

    def body(core_ref, ours_ref, back_ref, out_ref):
        first = core_ref[0] == 0
        out_ref[:, :half] = jnp.where(first, ours_ref[...], back_ref[...]) * scale
        out_ref[:, half:] = jnp.where(first, back_ref[...], ours_ref[...]) * scale

    return pl.pallas_call(
        body,
        out_shape=jax.ShapeDtypeStruct((own, 2 * half), F32),
        in_specs=[SCALARS, WHOLE, WHOLE],
        out_specs=WHOLE,
        compiler_params=pltpu.CompilerParams(vmem_limit_bytes=VMEM_LIMIT),
        name="finish",
    )(core[None], ours, back)


def per_device(orbital_values, occupied, trial, point_weights, batch_sizes, significant):
    rows, cols = orbital_values.shape
    batches = batch_sizes.shape[0]
    slots = rows // batches
    blocks = significant.shape[1]
    columns = occupied.shape[1]
    grid_count = lax.axis_size("grid")
    occ_count = lax.axis_size("occ")
    chips = grid_count // 2
    shares = 2 * occ_count
    half = cols // 2
    total = columns * grid_count
    place = lax.axis_index("grid")
    chip, core = place // 2, place % 2
    occ = lax.axis_index("occ")
    member = core * occ_count + occ

    def flip(x, axis, bit):
        count = lax.axis_size(axis)
        return lax.ppermute(x, axis, [(i, i ^ bit) for i in range(count)])

    def along(pairs):
        return [(2 * a + c, 2 * b + c) for a, b in pairs for c in range(2)]

    def doubled(x, axis, bit, dim):
        got = flip(x, axis, bit)
        mine = (lax.axis_index(axis) & bit) == 0
        return jnp.where(
            mine, jnp.concatenate((x, got), axis=dim), jnp.concatenate((got, x), axis=dim)
        )

    def halves(whole, axis):
        size = whole.shape[axis] // 2
        mine = lax.dynamic_slice_in_dim(whole, core * size, size, axis)
        return mine, lax.dynamic_slice_in_dim(whole, (1 - core) * size, size, axis)

    grid_bits = [1 << b for b in range(grid_count.bit_length() - 1)]
    occ_bits = [1 << b for b in range(occ_count.bit_length() - 1)]

    mine, other = halves(orbital_values.T, 0)
    got = flip(other, "grid", 1)
    mine_sig, other_sig = halves(significant.T, 0)
    got_sig = flip(other_sig, "grid", 1)

    told = jnp.concatenate((batch_sizes.astype(F32), point_weights))[None]
    for bit in grid_bits:
        told = doubled(told, "grid", bit, 0)
    sizes = told[:, :batches].astype(jnp.int32).reshape(-1)
    weights = told[:, batches:].reshape(-1)

    batch = lax.broadcasted_iota(jnp.int32, (sizes.shape[0], sizes.shape[0]), 0)
    before = lax.broadcasted_iota(jnp.int32, (sizes.shape[0], sizes.shape[0]), 1) < batch
    start = jnp.sum(jnp.where(before, sizes[None, :], 0), axis=1)
    position = lax.broadcasted_iota(jnp.int32, (sizes.shape[0], slots), 1)
    to = jnp.where(position < sizes[:, None], start[:, None] + position, -4 * rows * grid_count)
    to = to.reshape(grid_count, rows)
    first = start.reshape(chips, -1)[:, 0]
    margin = rows // 2 if (rows // 2) % (8 * shares) == 0 else rows
    nominal = rows * lax.iota(jnp.int32, chips)
    fits = jnp.all(jnp.abs(first - nominal) <= margin) & (jnp.sum(sizes) <= rows * chips)

    tile = margin
    piece = tile // shares
    base = rows * chip - margin
    mine_to = lax.dynamic_index_in_dim(to, place, 0, keepdims=False) - base
    got_to = lax.dynamic_index_in_dim(to, place ^ 1, 0, keepdims=False) - base
    to_left, *own_tiles, to_right = compact(
        mine,
        got,
        jnp.repeat(mine_sig.astype(BF16), slots, axis=1),
        jnp.repeat(got_sig.astype(BF16), slots, axis=1),
        mine_to[:, None],
        got_to[:, None],
        cols // blocks,
        tile,
    )

    def sent(x, pairs):
        return lax.ppermute(x, "grid", along(pairs))

    last = chips - 1
    leftward_pairs = [(a, a - 1) for a in range(1, chips)]
    rightward_pairs = [(a, a + 1) for a in range(last)]
    own = straighten(own_tiles, sent(to_right, rightward_pairs), sent(to_left, leftward_pairs))

    mine_panel, other_panel = halves(jnp.concatenate((occupied, trial), axis=1).T, 1)
    panels = stack_panels(mine_panel, flip(other_panel, "grid", 1), core)

    per_window = rows // tile
    window_iota = lax.iota(jnp.int32, chips)
    ends = [(0, 1), (last, last - 1)]
    homes = [(b, a) for a, b in ends]
    stages = [[((own,), chip)]]
    leftward = rightward = own
    far_panels = None
    for t in range(1, last):
        from_right = sent(leftward, [(a, b) for a, b in leftward_pairs if a + t <= chips])
        from_left = sent(rightward, [(a, b) for a, b in rightward_pairs if a + 1 - t >= 0])
        if t == 1:
            far_panels = sent(panels, ends)
        right = jnp.where(chip + t < chips, chip + t, -1)
        left = jnp.where(chip - t >= 0, chip - t, -1)
        if 2 * t > last:
            joined = tuple(
                from_right[:, j : j + tile] + from_left[:, j : j + tile]
                for j in range(0, rows, tile)
            )
            stages.append([(joined, jnp.maximum(right, left))])
        else:
            stages.append([((from_right,), right), ((from_left,), left)])
        leftward, rightward = from_right, from_left
    joined = stages[-1][0][0]
    late = [sent(x, homes) for x in joined]

    def summed(panels, windows, beside=()):
        keep, give = project(panels, windows, tile, shares, core)
        value = keep + flip(give, "grid", 1)
        value, beside = lax.optimization_barrier((value, beside))
        for bit in reversed(occ_bits):
            upper = (occ & bit) != 0
            low_part, high_part = value[:, :bit], value[:, bit:]
            got = flip(jnp.where(upper, low_part, high_part), "occ", bit)
            value = jnp.where(upper, high_part, low_part) + got
        return value.reshape(-1, per_window * piece, 4 * columns), beside

    def shared_density(value, at):
        product = jnp.sum(value[:, :, : 2 * columns] * value[:, :, 2 * columns :], axis=2)
        here = (at[:, None] == window_iota[None, :])[:, :, None]
        return jnp.sum(jnp.where(here, product[:, None], 0.0), axis=0)

    early_jobs, late_jobs = sum(stages[:-1], []), stages[-1]
    early_at = jnp.stack([at for _, at in early_jobs])
    late_at = jnp.stack([late_jobs[0][1]])
    early_value, _ = summed([[panels]] * len(early_jobs), [w for w, _ in early_jobs])
    late_value, late[:1] = summed([[panels, far_panels]], [joined], late[:1])
    far_value = late_value[1:]
    density = shared_density(early_value, early_at) + shared_density(
        late_value, jnp.concatenate((late_at, late_at))
    )
    density, late = lax.optimization_barrier((density, late))
    for bit in grid_bits[1:]:
        density = density + flip(density, "grid", bit)
    density = density * (1.0 / math.sqrt(total))

    windows = [w for w, _ in early_jobs] + [joined, tuple(late)]
    values = [early_value, late_value[:1], sent(far_value, homes)]
    places = [early_at, late_at, jnp.where(chip == 0, last, 0)[None]]

    at = (
        (window_iota * rows)[:, None, None]
        + (lax.iota(jnp.int32, per_window) * tile)[None, :, None]
        + member * piece
        + lax.iota(jnp.int32, piece)[None, None, :]
    ).reshape(-1, 1)
    weight = jnp.sum(jnp.where(to.reshape(1, -1) == at, weights[None, :], 0.0), axis=1)
    weight = weight.reshape(chips, per_window * piece)

    values, places = jnp.concatenate(values, axis=0), jnp.concatenate(places)
    here = (places[:, None] == window_iota[None, :])[:, :, None]
    density_here = jnp.sum(jnp.where(here, density[None], 0.0), axis=1)[:, :, None]
    weight_here = jnp.sum(jnp.where(here, weight[None], 0.0), axis=1)[:, :, None]
    orbitals, response = values[:, :, : 2 * columns], values[:, :, 2 * columns :]
    kernel = (weight_here * (density_here * orbitals + response)).astype(BF16)
    kernel = kernel.reshape(-1, 1, piece, 2 * columns)
    for bit in occ_bits:
        kernel = doubled(kernel, "occ", bit, 1)
    kernel = doubled(kernel, "grid", 1, 1).reshape(-1, 2 * columns)

    ours, theirs = contract(kernel, windows, core)
    back = flip(theirs, "grid", 1)
    scale = 1.0 / math.sqrt(rows * grid_count)
    exchange = lax.cond(
        fits,
        lambda core, ours, back, *given: finish(core, ours, back, scale),
        lambda core, ours, back, *given: any_sizes(*given) * scale,
        core,
        ours,
        back,
        orbital_values,
        occupied,
        trial,
        point_weights,
        batch_sizes,
        significant,
    )
    return exchange.T


def solution(mesh):
    placed = (
        P("grid", "occ"),
        P("occ", "grid"),
        P("occ", "grid"),
        P("grid"),
        P("grid"),
        P("grid", "occ"),
    )
    return jax.shard_map(
        per_device, mesh=mesh, in_specs=placed, out_specs=P("occ", "grid"), check_vma=False
    )
```

```python
import math

import jax
import jax.numpy as jnp
from jax import lax
from jax.experimental import pallas as pl
from jax.experimental.pallas import tpu as pltpu
from jax.sharding import PartitionSpec as P

BF16, F32 = jnp.bfloat16, jnp.float32
VMEM_LIMIT = 48 * 1024 * 1024
WHOLE = pl.BlockSpec(memory_space=pltpu.VMEM)
SCALARS = pl.BlockSpec(memory_space=pltpu.SMEM)


def screen(values, sizes, significant):
    rows, cols = values.shape
    batches = sizes.shape[0]
    blocks = significant.shape[1]
    blocked = (
        values.reshape(batches, rows // batches, blocks, cols // blocks)
        * significant.astype(values.dtype)[:, None, :, None]
    )
    position = lax.broadcasted_iota(jnp.int32, (batches, rows // batches), 1)
    live = (position < sizes[:, None]).astype(jnp.float32).reshape(rows)
    return (blocked.reshape(rows, cols), live)


def any_sizes(orbital_values, occupied, trial, point_weights, batch_sizes, significant):
    screened, live = screen(orbital_values, batch_sizes, significant)
    rows, cols = screened.shape
    grid_count, occ_count = lax.axis_size("grid"), lax.axis_size("occ")
    columns = occupied.shape[1]
    me = lax.axis_index("grid")
    ring = [(i, (i + 1) % grid_count) for i in range(grid_count)]
    occ_ring = [(i, (i + 1) % occ_count) for i in range(occ_count)]

    def project_one(step, carry):
        panel, terms = carry
        term = jnp.dot(screened, panel, preferred_element_type=F32)
        terms = lax.dynamic_update_index_in_dim(terms, term, (me - step) % grid_count, 0)
        return lax.ppermute(panel, "grid", ring), terms

    joined = jnp.concatenate((occupied, trial), axis=1)
    terms = jnp.zeros((grid_count, rows, 2 * columns), F32)
    terms = lax.fori_loop(0, grid_count, project_one, (joined, terms))[1]

    def add_one(step, carry):
        moving, held = carry
        moving = lax.ppermute(moving, "occ", occ_ring)
        return moving, held + moving

    terms = lax.fori_loop(0, occ_count - 1, add_one, (terms, terms))[1]
    orbitals, response = terms[:, :, :columns], terms[:, :, columns:]
    density = jnp.sum(orbitals * response, axis=(0, 2)) * (1.0 / math.sqrt(columns * grid_count))
    weight = (point_weights * live)[None, :, None]
    kernel = (weight * (density[None, :, None] * orbitals + response)).astype(BF16)

    def contract_one(step, held):
        owner = (me + grid_count - 1 - step) % grid_count
        part = lax.dynamic_index_in_dim(kernel, owner, 0, keepdims=False)
        term = lax.dot_general(
            part, screened, (((0,), (0,)), ((), ())), preferred_element_type=F32
        )
        return lax.ppermute(held, "grid", ring) + term

    return lax.fori_loop(0, grid_count, contract_one, jnp.zeros((columns, cols), F32))


def compact(mine, got, mine_sig, got_sig, mine_to, got_to, width, tile, odd):
    half, rows = mine.shape
    blocks = mine_sig.shape[0]
    count = rows // tile + 2

    def body(odd_ref, mine_ref, got_ref, msig_ref, gsig_ref, mto_ref, gto_ref, *outs):
        block_of = lax.broadcasted_iota(jnp.int32, (half, blocks), 0)
        begin = lax.broadcasted_iota(jnp.int32, (half, blocks), 1) * width
        spread = ((block_of >= begin) & (block_of < begin + width)).astype(F32).astype(BF16)
        slot = lax.broadcasted_iota(jnp.int32, (rows, count * tile), 1)

        def part(value_ref, sig_ref, to_ref):
            kept = jnp.dot(spread, sig_ref[...], preferred_element_type=F32)
            screened = (value_ref[...].astype(F32) * kept).astype(BF16)
            place = (to_ref[...] == slot).astype(F32).astype(BF16)
            return jnp.dot(screened, place, preferred_element_type=F32)

        window = part(mine_ref, msig_ref, mto_ref) + part(got_ref, gsig_ref, gto_ref)
        for j in range(1, count - 1):
            outs[j][...] = window[:, j * tile : (j + 1) * tile].astype(BF16)
        first, last = window[:, :tile], window[:, (count - 1) * tile :]
        outs[0][...] = jnp.where(odd_ref[0] == 0, first, last).astype(BF16)
        outs[-1][...] = jnp.where(odd_ref[0] == 0, last, first).astype(BF16)

    shape = jax.ShapeDtypeStruct((half, tile), BF16)
    return pl.pallas_call(
        body,
        out_shape=(shape,) * count,
        in_specs=[SCALARS] + [WHOLE] * 6,
        out_specs=(WHOLE,) * count,
        compiler_params=pltpu.CompilerParams(vmem_limit_bytes=VMEM_LIMIT),
        name="compact",
        cost_estimate=pl.CostEstimate(
            flops=8 * half * rows * rows, bytes_accessed=8 * half * rows, transcendentals=0
        ),
    )(odd[None], mine, got, mine_sig, got_sig, mine_to, got_to)


def straighten(tiles, by_a, by_b, odd):
    half, tile = by_a.shape
    count = len(tiles)

    def body(odd_ref, *refs):
        tile_refs, a_ref, b_ref, out_ref = refs[:count], *refs[count:]
        even = odd_ref[0] == 0
        for j in range(count):
            value = tile_refs[j][...]
            if j == 0:
                value = value + jnp.where(even, b_ref[...], a_ref[...])
            if j == count - 1:
                value = value + jnp.where(even, a_ref[...], b_ref[...])
            out_ref[:, j * tile : (j + 1) * tile] = value

    return pl.pallas_call(
        body,
        out_shape=jax.ShapeDtypeStruct((half, count * tile), BF16),
        in_specs=[SCALARS] + [WHOLE] * (count + 2),
        out_specs=WHOLE,
        compiler_params=pltpu.CompilerParams(vmem_limit_bytes=VMEM_LIMIT),
        name="straighten",
    )(odd[None], *tiles, by_a, by_b)


def stack_panels(mine, got, core):
    both, half = mine.shape
    columns = both // 2
    width = -(-half // 128) * 128

    def body(core_ref, mine_ref, got_ref, out_ref):
        first = core_ref[0] == 0
        out_ref[...] = jnp.zeros_like(out_ref)
        for j in range(2):
            low = mine_ref[j * columns : (j + 1) * columns]
            high = got_ref[j * columns : (j + 1) * columns]
            q = 2 * j * columns
            out_ref[q : q + columns, :half] = jnp.where(first, low, high)
            out_ref[q + columns : q + 2 * columns, :half] = jnp.where(first, high, low)

    return pl.pallas_call(
        body,
        out_shape=jax.ShapeDtypeStruct((2 * both, width), BF16),
        in_specs=[SCALARS, WHOLE, WHOLE],
        out_specs=WHOLE,
        compiler_params=pltpu.CompilerParams(vmem_limit_bytes=VMEM_LIMIT),
        name="stack_panels",
    )(core[None], mine, got)


def distinct(arrays):
    return list({id(x): x for x in arrays}.values())


def read_window(addends, arrays, refs):
    ref_of = {id(x): ref for x, ref in zip(arrays, refs)}
    total = None
    for parts in addends:
        value = [ref_of[id(x)][...] for x in parts]
        value = jnp.concatenate(value, axis=1) if len(value) > 1 else value[0]
        total = value if total is None else total + value
    return total


def project(jobs, rows, tile, shares, core):
    both = jobs[0][0].shape[0]
    half = jobs[0][1][0][0].shape[0]
    piece = tile // shares
    tiles = len(jobs) * rows // tile
    panels = distinct([p for p, _ in jobs])
    arrays = distinct([x for _, window in jobs for parts in window for x in parts])
    count = len(panels)

    def body(core_ref, *refs):
        panel_refs, array_refs = refs[:count], refs[count:-3]
        keep_ref, give_ref, terms_ref = refs[-3:]
        q = 0
        for panel, window in jobs:
            panel_ref = panel_refs[[id(p) for p in panels].index(id(panel))]
            value = read_window(window, arrays, array_refs)
            turned = jnp.dot(panel_ref[:, :half], value, preferred_element_type=F32).T
            for j in range(0, rows, tile):
                terms_ref[q] = turned[j : j + tile].reshape(2, shares // 2, piece, both)
                keep_ref[q] = terms_ref[q, core_ref[0]]
                give_ref[q] = terms_ref[q, 1 - core_ref[0]]
                q += 1

    shape = jax.ShapeDtypeStruct((tiles, shares // 2, piece, both), F32)
    return pl.pallas_call(
        body,
        out_shape=(shape, shape),
        in_specs=[SCALARS] + [WHOLE] * (count + len(arrays)),
        out_specs=(WHOLE, WHOLE),
        scratch_shapes=[pltpu.VMEM((tiles, 2, shares // 2, piece, both), F32)],
        compiler_params=pltpu.CompilerParams(vmem_limit_bytes=VMEM_LIMIT),
        name="project",
        cost_estimate=pl.CostEstimate(
            flops=2 * both * half * tiles * tile,
            bytes_accessed=2 * half * (both + tiles * tile) + 4 * tiles * tile * both,
            transcendentals=0,
        ),
    )(core[None], *panels, *arrays)


def contract(kernel, windows, core):
    points, columns = kernel.shape
    half = windows[0][0][0].shape[0]
    own = columns // 2
    rows = points // len(windows)
    arrays = distinct([x for window in windows for parts in window for x in parts])

    def body(core_ref, kernel_ref, *refs):
        array_refs, mine_ref, other_ref = refs[:-2], refs[-2], refs[-1]
        first = core_ref[0] == 0
        total = None
        for s, window in enumerate(windows):
            turned = kernel_ref[s * rows : (s + 1) * rows].astype(F32).T
            low, high = turned[:own], turned[own:]
            turned = jnp.concatenate(
                (jnp.where(first, low, high), jnp.where(first, high, low))
            ).astype(BF16)
            term = lax.dot_general(
                turned,
                read_window(window, arrays, array_refs),
                (((1,), (1,)), ((), ())),
                preferred_element_type=F32,
            )
            total = term if total is None else total + term
        mine_ref[...] = total[:own]
        other_ref[...] = total[own:]

    shape = jax.ShapeDtypeStruct((own, half), F32)
    return pl.pallas_call(
        body,
        out_shape=(shape, shape),
        in_specs=[SCALARS] + [WHOLE] * (1 + len(arrays)),
        out_specs=(WHOLE, WHOLE),
        compiler_params=pltpu.CompilerParams(vmem_limit_bytes=VMEM_LIMIT),
        name="contract",
        cost_estimate=pl.CostEstimate(
            flops=2 * columns * half * points,
            bytes_accessed=2 * points * half + 4 * columns * half,
            transcendentals=0,
        ),
    )(core[None], kernel, *arrays)


def unwritten(shape):
    def body(out_ref):
        pass

    return pl.pallas_call(
        body,
        out_shape=jax.ShapeDtypeStruct(shape, F32),
        out_specs=pl.BlockSpec(memory_space=pl.ANY),
        name="unwritten",
    )()


def finish(core, fits, ours, back, other, scale):
    own, half = ours.shape

    def body(flags_ref, ours_ref, back_ref, other_ref, out_ref, whole_ref, sem):
        @pl.when(flags_ref[1] != 0)
        def _():
            first = flags_ref[0] == 0
            whole_ref[:, :half] = jnp.where(first, ours_ref[...], back_ref[...]) * scale
            whole_ref[:, half:] = jnp.where(first, back_ref[...], ours_ref[...]) * scale
            copy = pltpu.make_async_copy(whole_ref, out_ref, sem)
            copy.start()
            copy.wait()

    return pl.pallas_call(
        body,
        out_shape=jax.ShapeDtypeStruct((own, 2 * half), F32),
        in_specs=[SCALARS, WHOLE, WHOLE, pl.BlockSpec(memory_space=pl.ANY)],
        out_specs=pl.BlockSpec(memory_space=pl.ANY),
        scratch_shapes=[pltpu.VMEM((own, 2 * half), F32), pltpu.SemaphoreType.DMA],
        input_output_aliases={3: 0},
        compiler_params=pltpu.CompilerParams(vmem_limit_bytes=VMEM_LIMIT),
        name="finish",
    )(jnp.stack((core, fits.astype(jnp.int32))), ours, back, other)


def per_device(orbital_values, occupied, trial, point_weights, batch_sizes, significant):
    rows, cols = orbital_values.shape
    batches = batch_sizes.shape[0]
    slots = rows // batches
    blocks = significant.shape[1]
    columns = occupied.shape[1]
    grid_count = lax.axis_size("grid")
    occ_count = lax.axis_size("occ")
    chips = grid_count // 2
    shares = 2 * occ_count
    half = cols // 2
    total = columns * grid_count
    place = lax.axis_index("grid")
    chip, core = place // 2, place % 2
    occ = lax.axis_index("occ")
    member = core * occ_count + occ

    def flip(x, axis, bit):
        count = lax.axis_size(axis)
        return lax.ppermute(x, axis, [(i, i ^ bit) for i in range(count)])

    def along(pairs):
        return [(2 * a + c, 2 * b + c) for a, b in pairs for c in range(2)]

    def doubled(x, axis, bit, dim):
        got = flip(x, axis, bit)
        mine = (lax.axis_index(axis) & bit) == 0
        return jnp.where(
            mine, jnp.concatenate((x, got), axis=dim), jnp.concatenate((got, x), axis=dim)
        )

    def halves(whole, axis):
        size = whole.shape[axis] // 2
        mine = lax.dynamic_slice_in_dim(whole, core * size, size, axis)
        return mine, lax.dynamic_slice_in_dim(whole, (1 - core) * size, size, axis)

    grid_bits = [1 << b for b in range(grid_count.bit_length() - 1)]
    occ_bits = [1 << b for b in range(occ_count.bit_length() - 1)]

    mine, other = halves(orbital_values.T, 0)
    got = flip(other, "grid", 1)
    mine_sig, other_sig = halves(significant.T, 0)
    got_sig = flip(other_sig, "grid", 1)

    told = jnp.concatenate(
        (
            doubled(batch_sizes[None], "grid", 1, 0).astype(F32).reshape(1, -1),
            doubled(point_weights[None], "grid", 1, 0).reshape(1, -1),
        ),
        axis=1,
    )
    if chips <= 4:
        heard = [told]
        for step in range(1, chips):
            around = [(i, (i + 2 * step) % grid_count) for i in range(grid_count)]
            heard.append(lax.ppermute(told, "grid", around))
        heard = jnp.concatenate(heard)
        behind = (chip - lax.iota(jnp.int32, chips)) % chips
        pick = behind[:, None, None] == lax.iota(jnp.int32, chips)[None, :, None]
        told = jnp.sum(jnp.where(pick, heard[None], 0.0), axis=1)
    else:
        for bit in grid_bits[1:]:
            told = doubled(told, "grid", bit, 0)
    sizes = told[:, : 2 * batches].astype(jnp.int32).reshape(-1)
    weights = told[:, 2 * batches :].reshape(-1)

    batch = lax.broadcasted_iota(jnp.int32, (sizes.shape[0], sizes.shape[0]), 0)
    before = lax.broadcasted_iota(jnp.int32, (sizes.shape[0], sizes.shape[0]), 1) < batch
    start = jnp.sum(jnp.where(before, sizes[None, :], 0), axis=1)
    position = lax.broadcasted_iota(jnp.int32, (sizes.shape[0], slots), 1)
    to = jnp.where(position < sizes[:, None], start[:, None] + position, -4 * rows * grid_count)
    to = to.reshape(grid_count, rows)
    first = start.reshape(chips, -1)[:, 0]
    margin = rows // 2 if (rows // 2) % (8 * shares) == 0 else rows
    nominal = rows * lax.iota(jnp.int32, chips)
    fits = jnp.all(jnp.abs(first - nominal) <= margin) & (jnp.sum(sizes) <= rows * chips)

    tile = margin
    piece = tile // shares
    base = rows * chip - margin
    mine_to = lax.dynamic_index_in_dim(to, place, 0, keepdims=False) - base
    got_to = lax.dynamic_index_in_dim(to, place ^ 1, 0, keepdims=False) - base
    odd = chip % 2
    for_b, *own_tiles, for_a = compact(
        mine,
        got,
        jnp.repeat(mine_sig.astype(BF16), slots, axis=1),
        jnp.repeat(got_sig.astype(BF16), slots, axis=1),
        mine_to[:, None],
        got_to[:, None],
        cols // blocks,
        tile,
        odd,
    )

    def sent(x, pairs):
        return lax.ppermute(x, "grid", along(pairs))

    last = chips - 1

    def over(links, t):
        pairs = []
        for a in range(links, last, 2):
            pairs += [(a, a + 1)] if a - t + 1 >= 0 else []
            pairs += [(a + 1, a)] if a + t <= last else []
        return pairs

    own = straighten(own_tiles, sent(for_a, over(0, 1)), sent(for_b, over(1, 1)), odd)

    mine_panel, other_panel = halves(jnp.concatenate((occupied, trial), axis=1).T, 1)
    panels = stack_panels(mine_panel, flip(other_panel, "grid", 1), core)

    per_window = rows // tile
    window_iota = lax.iota(jnp.int32, chips)
    ends = [(0, 1), (last, last - 1)]
    homes = [(b, a) for a, b in ends]
    side = 1 - 2 * odd

    def valid(at):
        return jnp.where((at >= 0) & (at <= last), at, -1)

    stages = [[([(own,)], chip)]]
    by_a = by_b = own
    far_panels = None
    for t in range(1, last):
        by_a, by_b = sent(by_b, over(0, t)), sent(by_a, over(1, t))
        if t == 1:
            far_panels = sent(panels, ends)
        a_at, b_at = valid(chip + side * t), valid(chip - side * t)
        if 2 * t > last:
            stages.append([([(by_a,), (by_b,)], jnp.maximum(a_at, b_at))])
        else:
            stages.append([([(by_a,)], a_at), ([(by_b,)], b_at)])
    late = [sent(by_b[:, j : j + tile], homes) for j in range(0, rows, tile)]

    def summed(jobs, after=None):
        keep, give = project(jobs, rows, tile, shares, core)
        value = keep + flip(give, "grid", 1)
        if after is not None:
            value, after = lax.optimization_barrier((value, after))
        for bit in reversed(occ_bits):
            upper = (occ & bit) != 0
            low_part, high_part = value[:, :bit], value[:, bit:]
            got = flip(jnp.where(upper, low_part, high_part), "occ", bit)
            value = jnp.where(upper, high_part, low_part) + got
        return value.reshape(-1, per_window * piece, 4 * columns)

    def shared_density(value, at):
        product = jnp.sum(value[:, :, : 2 * columns] * value[:, :, 2 * columns :], axis=2)
        here = (at[:, None] == window_iota[None, :])[:, :, None]
        return jnp.sum(jnp.where(here, product[:, None], 0.0), axis=0)

    early_jobs, late_jobs = sum(stages[:-1], []), stages[-1]
    early_at = jnp.stack([at for _, at in early_jobs])
    late_at = late_jobs[0][1][None]
    early_value = summed([(panels, w) for w, _ in early_jobs], by_b)
    far_window = [(by_b,)]
    late_window = [(by_a,), (by_b,)]
    late_value = summed([(panels, late_window), (far_panels, far_window)])
    late_value, far_value = late_value[:1], late_value[1:]
    density = shared_density(early_value, early_at) + shared_density(
        jnp.concatenate((late_value, far_value)), jnp.concatenate((late_at, late_at))
    )
    density, late[:1] = lax.optimization_barrier((density, late[:1]))
    for bit in grid_bits[1:]:
        density = density + flip(density, "grid", bit)
    density = density * (1.0 / math.sqrt(total))

    early_windows = [w for w, _ in early_jobs]
    early_windows[2] = early_windows[2] + [tuple(late)]
    windows = early_windows + [late_window]
    home_value = sent(far_value, homes)
    values = [early_value[:2], early_value[2:3] + home_value, early_value[3:], late_value]
    outer = jnp.where(chip == 0, last, jnp.where(chip == last, 0, early_at[2]))
    places = [early_at[:2], outer[None], early_at[3:], late_at]

    at = (
        (window_iota * rows)[:, None, None]
        + (lax.iota(jnp.int32, per_window) * tile)[None, :, None]
        + member * piece
        + lax.iota(jnp.int32, piece)[None, None, :]
    ).reshape(-1, 1)
    weight = jnp.sum(jnp.where(to.reshape(1, -1) == at, weights[None, :], 0.0), axis=1)
    weight = weight.reshape(chips, per_window * piece)

    values, places = jnp.concatenate(values, axis=0), jnp.concatenate(places)
    here = (places[:, None] == window_iota[None, :])[:, :, None]
    density_here = jnp.sum(jnp.where(here, density[None], 0.0), axis=1)[:, :, None]
    weight_here = jnp.sum(jnp.where(here, weight[None], 0.0), axis=1)[:, :, None]
    orbitals, response = values[:, :, : 2 * columns], values[:, :, 2 * columns :]
    kernel = (weight_here * (density_here * orbitals + response)).astype(BF16)
    kernel = kernel.reshape(-1, 1, piece, 2 * columns)
    for bit in occ_bits:
        kernel = doubled(kernel, "occ", bit, 1)
    kernel = doubled(kernel, "grid", 1, 1).reshape(-1, 2 * columns)

    ours, theirs = contract(kernel, windows, core)
    back = flip(theirs, "grid", 1)
    scale = 1.0 / math.sqrt(rows * grid_count)
    other = lax.cond(
        fits,
        lambda *given: unwritten((columns, cols)),
        lambda *given: any_sizes(*given) * scale,
        orbital_values,
        occupied,
        trial,
        point_weights,
        batch_sizes,
        significant,
    )
    return finish(core, fits, ours, back, other, scale).T


def solution(mesh):
    placed = (
        P("grid", "occ"),
        P("occ", "grid"),
        P("occ", "grid"),
        P("grid"),
        P("grid"),
        P("grid", "occ"),
    )
    return jax.shard_map(
        per_device, mesh=mesh, in_specs=placed, out_specs=P("occ", "grid"), check_vma=False
    )
```

```python
import math

import jax
import jax.numpy as jnp
from jax import lax
from jax.experimental import pallas as pl
from jax.experimental.pallas import tpu as pltpu
from jax.sharding import PartitionSpec as P

BF16, F32 = jnp.bfloat16, jnp.float32
VMEM_LIMIT = 48 * 1024 * 1024
WHOLE = pl.BlockSpec(memory_space=pltpu.VMEM)
SCALARS = pl.BlockSpec(memory_space=pltpu.SMEM)


def screen(values, sizes, significant):
    rows, cols = values.shape
    batches = sizes.shape[0]
    blocks = significant.shape[1]
    blocked = (
        values.reshape(batches, rows // batches, blocks, cols // blocks)
        * significant.astype(values.dtype)[:, None, :, None]
    )
    position = lax.broadcasted_iota(jnp.int32, (batches, rows // batches), 1)
    live = (position < sizes[:, None]).astype(jnp.float32).reshape(rows)
    return (blocked.reshape(rows, cols), live)


def any_sizes(orbital_values, occupied, trial, point_weights, batch_sizes, significant):
    screened, live = screen(orbital_values, batch_sizes, significant)
    rows, cols = screened.shape
    grid_count, occ_count = lax.axis_size("grid"), lax.axis_size("occ")
    columns = occupied.shape[1]
    me = lax.axis_index("grid")
    ring = [(i, (i + 1) % grid_count) for i in range(grid_count)]
    occ_ring = [(i, (i + 1) % occ_count) for i in range(occ_count)]

    def project_one(step, carry):
        panel, terms = carry
        term = jnp.dot(screened, panel, preferred_element_type=F32)
        terms = lax.dynamic_update_index_in_dim(terms, term, (me - step) % grid_count, 0)
        return lax.ppermute(panel, "grid", ring), terms

    joined = jnp.concatenate((occupied, trial), axis=1)
    terms = jnp.zeros((grid_count, rows, 2 * columns), F32)
    terms = lax.fori_loop(0, grid_count, project_one, (joined, terms))[1]

    def add_one(step, carry):
        moving, held = carry
        moving = lax.ppermute(moving, "occ", occ_ring)
        return moving, held + moving

    terms = lax.fori_loop(0, occ_count - 1, add_one, (terms, terms))[1]
    orbitals, response = terms[:, :, :columns], terms[:, :, columns:]
    density = jnp.sum(orbitals * response, axis=(0, 2)) * (1.0 / math.sqrt(columns * grid_count))
    weight = (point_weights * live)[None, :, None]
    kernel = (weight * (density[None, :, None] * orbitals + response)).astype(BF16)

    def contract_one(step, held):
        owner = (me + grid_count - 1 - step) % grid_count
        part = lax.dynamic_index_in_dim(kernel, owner, 0, keepdims=False)
        term = lax.dot_general(
            part, screened, (((0,), (0,)), ((), ())), preferred_element_type=F32
        )
        return lax.ppermute(held, "grid", ring) + term

    return lax.fori_loop(0, grid_count, contract_one, jnp.zeros((columns, cols), F32))


def half_of(whole, which):
    rows, columns = whole.shape
    half = rows // 2
    if half % 16:
        return lax.dynamic_slice_in_dim(whole, which * half, half, 0)

    def body(which_ref, whole_ref, out_ref, sem):
        first = pl.multiple_of(which_ref[0] * half, 16)
        copy = pltpu.make_async_copy(whole_ref.at[pl.ds(first, half)], out_ref, sem)
        copy.start()
        copy.wait()

    return pl.pallas_call(
        body,
        out_shape=jax.ShapeDtypeStruct((half, columns), whole.dtype),
        in_specs=[SCALARS, pl.BlockSpec(memory_space=pl.ANY)],
        out_specs=pl.BlockSpec(memory_space=pl.ANY),
        scratch_shapes=[pltpu.SemaphoreType.DMA],
        name="half_of",
    )(which[None], whole)


def compact(mine, got, mine_sig, got_sig, mine_to, got_to, width, tile, odd):
    half, rows = mine.shape
    blocks = mine_sig.shape[0]
    count = rows // tile + 2

    def body(odd_ref, mine_ref, got_ref, msig_ref, gsig_ref, mto_ref, gto_ref, *outs):
        block_of = lax.broadcasted_iota(jnp.int32, (half, blocks), 0)
        begin = lax.broadcasted_iota(jnp.int32, (half, blocks), 1) * width
        spread = ((block_of >= begin) & (block_of < begin + width)).astype(F32).astype(BF16)
        slot = lax.broadcasted_iota(jnp.int32, (rows, count * tile), 1)

        def part(value_ref, sig_ref, to_ref):
            kept = jnp.dot(spread, sig_ref[...], preferred_element_type=F32)
            screened = (value_ref[...].astype(F32) * kept).astype(BF16)
            place = (to_ref[...] == slot).astype(F32).astype(BF16)
            return jnp.dot(screened, place, preferred_element_type=F32)

        window = part(mine_ref, msig_ref, mto_ref) + part(got_ref, gsig_ref, gto_ref)
        for j in range(1, count - 1):
            outs[j][...] = window[:, j * tile : (j + 1) * tile].astype(BF16)
        first, last = window[:, :tile], window[:, (count - 1) * tile :]
        outs[0][...] = jnp.where(odd_ref[0] == 0, first, last).astype(BF16)
        outs[-1][...] = jnp.where(odd_ref[0] == 0, last, first).astype(BF16)

    shape = jax.ShapeDtypeStruct((half, tile), BF16)
    return pl.pallas_call(
        body,
        out_shape=(shape,) * count,
        in_specs=[SCALARS] + [WHOLE] * 6,
        out_specs=(WHOLE,) * count,
        compiler_params=pltpu.CompilerParams(vmem_limit_bytes=VMEM_LIMIT),
        name="compact",
        cost_estimate=pl.CostEstimate(
            flops=8 * half * rows * rows, bytes_accessed=8 * half * rows, transcendentals=0
        ),
    )(odd[None], mine, got, mine_sig, got_sig, mine_to, got_to)


def straighten(tiles, by_a, by_b, odd):
    half, tile = by_a.shape
    count = len(tiles)

    def body(odd_ref, *refs):
        tile_refs, a_ref, b_ref, out_ref = refs[:count], *refs[count:]
        even = odd_ref[0] == 0
        for j in range(count):
            value = tile_refs[j][...]
            if j == 0:
                value = value + jnp.where(even, b_ref[...], a_ref[...])
            if j == count - 1:
                value = value + jnp.where(even, a_ref[...], b_ref[...])
            out_ref[:, j * tile : (j + 1) * tile] = value

    return pl.pallas_call(
        body,
        out_shape=jax.ShapeDtypeStruct((half, count * tile), BF16),
        in_specs=[SCALARS] + [WHOLE] * (count + 2),
        out_specs=WHOLE,
        compiler_params=pltpu.CompilerParams(vmem_limit_bytes=VMEM_LIMIT),
        name="straighten",
    )(odd[None], *tiles, by_a, by_b)


def stack_panels(mine, got, core):
    both, half = mine.shape
    columns = both // 2
    width = -(-half // 128) * 128

    def body(core_ref, mine_ref, got_ref, out_ref):
        first = core_ref[0] == 0
        out_ref[...] = jnp.zeros_like(out_ref)
        for j in range(2):
            low = mine_ref[j * columns : (j + 1) * columns]
            high = got_ref[j * columns : (j + 1) * columns]
            q = 2 * j * columns
            out_ref[q : q + columns, :half] = jnp.where(first, low, high)
            out_ref[q + columns : q + 2 * columns, :half] = jnp.where(first, high, low)

    return pl.pallas_call(
        body,
        out_shape=jax.ShapeDtypeStruct((2 * both, width), BF16),
        in_specs=[SCALARS, WHOLE, WHOLE],
        out_specs=WHOLE,
        compiler_params=pltpu.CompilerParams(vmem_limit_bytes=VMEM_LIMIT),
        name="stack_panels",
    )(core[None], mine, got)


def distinct(arrays):
    return list({id(x): x for x in arrays}.values())


def read_window(addends, arrays, refs):
    ref_of = {id(x): ref for x, ref in zip(arrays, refs)}
    total = None
    for parts in addends:
        value = [ref_of[id(x)][...] for x in parts]
        value = jnp.concatenate(value, axis=1) if len(value) > 1 else value[0]
        total = value if total is None else total + value
    return total


def split_sum(pairs, occ):
    _, shares, piece, both = pairs[0][0].shape
    tiles = sum(keep.shape[0] for keep, _ in pairs)

    def body(occ_ref, *refs):
        ins, outs = refs[: 2 * len(pairs)], refs[2 * len(pairs) :]
        for d in range(shares):
            at = 0
            for keep_ref, got_ref in zip(ins[::2], ins[1::2]):
                for q in range(keep_ref.shape[0]):
                    outs[d][at] = keep_ref[q, occ_ref[0] ^ d] + got_ref[q, occ_ref[0] ^ d]
                    at += 1

    shape = jax.ShapeDtypeStruct((tiles, piece, both), F32)
    return pl.pallas_call(
        body,
        out_shape=(shape,) * shares,
        in_specs=[SCALARS] + [WHOLE] * (2 * len(pairs)),
        out_specs=(WHOLE,) * shares,
        compiler_params=pltpu.CompilerParams(vmem_limit_bytes=VMEM_LIMIT),
        name="split_sum",
    )(occ[None], *sum(pairs, ()))


def project(jobs, rows, tile, shares, core):
    both = jobs[0][0].shape[0]
    half = jobs[0][1][0][0].shape[0]
    piece = tile // shares
    tiles = len(jobs) * rows // tile
    panels = distinct([p for p, _ in jobs])
    arrays = distinct([x for _, window in jobs for parts in window for x in parts])
    count = len(panels)

    def body(core_ref, *refs):
        panel_refs, array_refs = refs[:count], refs[count:-3]
        keep_ref, give_ref, terms_ref = refs[-3:]
        q = 0
        for panel, window in jobs:
            panel_ref = panel_refs[[id(p) for p in panels].index(id(panel))]
            value = read_window(window, arrays, array_refs)
            turned = jnp.dot(panel_ref[:, :half], value, preferred_element_type=F32).T
            for j in range(0, rows, tile):
                terms_ref[q] = turned[j : j + tile].reshape(2, shares // 2, piece, both)
                keep_ref[q] = terms_ref[q, core_ref[0]]
                give_ref[q] = terms_ref[q, 1 - core_ref[0]]
                q += 1

    shape = jax.ShapeDtypeStruct((tiles, shares // 2, piece, both), F32)
    return pl.pallas_call(
        body,
        out_shape=(shape, shape),
        in_specs=[SCALARS] + [WHOLE] * (count + len(arrays)),
        out_specs=(WHOLE, WHOLE),
        scratch_shapes=[pltpu.VMEM((tiles, 2, shares // 2, piece, both), F32)],
        compiler_params=pltpu.CompilerParams(vmem_limit_bytes=VMEM_LIMIT),
        name="project",
        cost_estimate=pl.CostEstimate(
            flops=2 * both * half * tiles * tile,
            bytes_accessed=2 * half * (both + tiles * tile) + 4 * tiles * tile * both,
            transcendentals=0,
        ),
    )(core[None], *panels, *arrays)


def contract(kernel, windows, core):
    points, columns = kernel.shape
    half = windows[0][0][0].shape[0]
    own = columns // 2
    rows = points // len(windows)
    arrays = distinct([x for window in windows for parts in window for x in parts])

    def body(core_ref, kernel_ref, *refs):
        array_refs, mine_ref, other_ref = refs[:-2], refs[-2], refs[-1]
        first = core_ref[0] == 0
        total = None
        for s, window in enumerate(windows):
            turned = kernel_ref[s * rows : (s + 1) * rows].astype(F32).T
            low, high = turned[:own], turned[own:]
            turned = jnp.concatenate(
                (jnp.where(first, low, high), jnp.where(first, high, low))
            ).astype(BF16)
            term = lax.dot_general(
                turned,
                read_window(window, arrays, array_refs),
                (((1,), (1,)), ((), ())),
                preferred_element_type=F32,
            )
            total = term if total is None else total + term
        mine_ref[...] = total[:own]
        other_ref[...] = total[own:]

    shape = jax.ShapeDtypeStruct((own, half), F32)
    return pl.pallas_call(
        body,
        out_shape=(shape, shape),
        in_specs=[SCALARS] + [WHOLE] * (1 + len(arrays)),
        out_specs=(WHOLE, WHOLE),
        compiler_params=pltpu.CompilerParams(vmem_limit_bytes=VMEM_LIMIT),
        name="contract",
        cost_estimate=pl.CostEstimate(
            flops=2 * columns * half * points,
            bytes_accessed=2 * points * half + 4 * columns * half,
            transcendentals=0,
        ),
    )(core[None], kernel, *arrays)


def unwritten(shape):
    def body(out_ref):
        pass

    return pl.pallas_call(
        body,
        out_shape=jax.ShapeDtypeStruct(shape, F32),
        out_specs=pl.BlockSpec(memory_space=pl.ANY),
        name="unwritten",
    )()


def finish(core, fits, ours, back, other, scale):
    own, half = ours.shape

    def body(flags_ref, ours_ref, back_ref, other_ref, out_ref, whole_ref, sem):
        @pl.when(flags_ref[1] != 0)
        def _():
            first = flags_ref[0] == 0
            whole_ref[:, :half] = jnp.where(first, ours_ref[...], back_ref[...]) * scale
            whole_ref[:, half:] = jnp.where(first, back_ref[...], ours_ref[...]) * scale
            copy = pltpu.make_async_copy(whole_ref, out_ref, sem)
            copy.start()
            copy.wait()

    return pl.pallas_call(
        body,
        out_shape=jax.ShapeDtypeStruct((own, 2 * half), F32),
        in_specs=[SCALARS, WHOLE, WHOLE, pl.BlockSpec(memory_space=pl.ANY)],
        out_specs=pl.BlockSpec(memory_space=pl.ANY),
        scratch_shapes=[pltpu.VMEM((own, 2 * half), F32), pltpu.SemaphoreType.DMA],
        input_output_aliases={3: 0},
        compiler_params=pltpu.CompilerParams(vmem_limit_bytes=VMEM_LIMIT),
        name="finish",
    )(jnp.stack((core, fits.astype(jnp.int32))), ours, back, other)


def per_device(orbital_values, occupied, trial, point_weights, batch_sizes, significant):
    rows, cols = orbital_values.shape
    batches = batch_sizes.shape[0]
    slots = rows // batches
    blocks = significant.shape[1]
    columns = occupied.shape[1]
    grid_count = lax.axis_size("grid")
    occ_count = lax.axis_size("occ")
    chips = grid_count // 2
    shares = 2 * occ_count
    half = cols // 2
    total = columns * grid_count
    place = lax.axis_index("grid")
    chip, core = place // 2, place % 2
    occ = lax.axis_index("occ")
    member = core * occ_count + occ

    def flip(x, axis, bit):
        count = lax.axis_size(axis)
        return lax.ppermute(x, axis, [(i, i ^ bit) for i in range(count)])

    def along(pairs):
        return [(2 * a + c, 2 * b + c) for a, b in pairs for c in range(2)]

    def doubled(x, axis, bit, dim):
        got = flip(x, axis, bit)
        mine = (lax.axis_index(axis) & bit) == 0
        return jnp.where(
            mine, jnp.concatenate((x, got), axis=dim), jnp.concatenate((got, x), axis=dim)
        )

    def halves(whole, axis):
        size = whole.shape[axis] // 2
        mine = lax.dynamic_slice_in_dim(whole, core * size, size, axis)
        return mine, lax.dynamic_slice_in_dim(whole, (1 - core) * size, size, axis)

    grid_bits = [1 << b for b in range(grid_count.bit_length() - 1)]
    occ_bits = [1 << b for b in range(occ_count.bit_length() - 1)]

    mine = half_of(orbital_values.T, core)
    got = flip(half_of(orbital_values.T, 1 - core), "grid", 1)
    mine_sig, other_sig = halves(significant.T, 0)
    got_sig = flip(other_sig, "grid", 1)

    told = jnp.concatenate(
        (
            doubled(batch_sizes[None], "grid", 1, 0).astype(F32).reshape(1, -1),
            doubled(point_weights[None], "grid", 1, 0).reshape(1, -1),
        ),
        axis=1,
    )
    if chips <= 4:
        heard = [told]
        for step in range(1, chips):
            around = [(i, (i + 2 * step) % grid_count) for i in range(grid_count)]
            heard.append(lax.ppermute(told, "grid", around))
        heard = jnp.concatenate(heard)
        behind = (chip - lax.iota(jnp.int32, chips)) % chips
        pick = behind[:, None, None] == lax.iota(jnp.int32, chips)[None, :, None]
        told = jnp.sum(jnp.where(pick, heard[None], 0.0), axis=1)
    else:
        for bit in grid_bits[1:]:
            told = doubled(told, "grid", bit, 0)
    sizes = told[:, : 2 * batches].astype(jnp.int32).reshape(-1)
    weights = told[:, 2 * batches :].reshape(-1)

    batch = lax.broadcasted_iota(jnp.int32, (sizes.shape[0], sizes.shape[0]), 0)
    before = lax.broadcasted_iota(jnp.int32, (sizes.shape[0], sizes.shape[0]), 1) < batch
    start = jnp.sum(jnp.where(before, sizes[None, :], 0), axis=1)
    position = lax.broadcasted_iota(jnp.int32, (sizes.shape[0], slots), 1)
    to = jnp.where(position < sizes[:, None], start[:, None] + position, -4 * rows * grid_count)
    to = to.reshape(grid_count, rows)
    first = start.reshape(chips, -1)[:, 0]
    margin = rows // 2 if (rows // 2) % (8 * shares) == 0 else rows
    nominal = rows * lax.iota(jnp.int32, chips)
    fits = jnp.all(jnp.abs(first - nominal) <= margin) & (jnp.sum(sizes) <= rows * chips)

    tile = margin
    piece = tile // shares
    base = rows * chip - margin
    mine_to = lax.dynamic_index_in_dim(to, place, 0, keepdims=False) - base
    got_to = lax.dynamic_index_in_dim(to, place ^ 1, 0, keepdims=False) - base
    odd = chip % 2
    for_b, *own_tiles, for_a = compact(
        mine,
        got,
        jnp.repeat(mine_sig.astype(BF16), slots, axis=1),
        jnp.repeat(got_sig.astype(BF16), slots, axis=1),
        mine_to[:, None],
        got_to[:, None],
        cols // blocks,
        tile,
        odd,
    )

    def sent(x, pairs):
        return lax.ppermute(x, "grid", along(pairs))

    last = chips - 1

    def over(links, t):
        pairs = []
        for a in range(links, last, 2):
            pairs += [(a, a + 1)] if a - t + 1 >= 0 else []
            pairs += [(a + 1, a)] if a + t <= last else []
        return pairs

    own = straighten(own_tiles, sent(for_a, over(0, 1)), sent(for_b, over(1, 1)), odd)

    mine_panel, other_panel = halves(jnp.concatenate((occupied, trial), axis=1).T, 1)
    panels = stack_panels(mine_panel, flip(other_panel, "grid", 1), core)

    per_window = rows // tile
    window_iota = lax.iota(jnp.int32, chips)
    ends = [(0, 1), (last, last - 1)]
    homes = [(b, a) for a, b in ends]
    side = 1 - 2 * odd

    def valid(at):
        return jnp.where((at >= 0) & (at <= last), at, -1)

    stages = [[([(own,)], chip)]]
    by_a = by_b = own
    far_panels = None
    for t in range(1, last):
        by_a, by_b = sent(by_b, over(0, t)), sent(by_a, over(1, t))
        if t == 1:
            far_panels = sent(panels, ends)
        a_at, b_at = valid(chip + side * t), valid(chip - side * t)
        if 2 * t > last:
            stages.append([([(by_a,), (by_b,)], jnp.maximum(a_at, b_at))])
        else:
            stages.append([([(by_a,)], a_at), ([(by_b,)], b_at)])

    direct = occ_count <= 4
    points = per_window * piece

    def halved(jobs):
        keep, give = project(jobs, rows, tile, shares, core)
        return keep, flip(give, "grid", 1)

    def summed(pairs):
        if direct:
            parts = split_sum(pairs, occ)
            value = parts[0]
            for d in range(1, occ_count):
                value = value + flip(parts[d], "occ", d)
        else:
            value = jnp.concatenate([keep + got for keep, got in pairs])
            for bit in reversed(occ_bits):
                upper = (occ & bit) != 0
                low_part, high_part = value[:, :bit], value[:, bit:]
                got = flip(jnp.where(upper, low_part, high_part), "occ", bit)
                value = jnp.where(upper, high_part, low_part) + got
        return value.reshape(-1, points, 4 * columns)

    def shared_density(value, at):
        product = jnp.sum(value[:, :, : 2 * columns] * value[:, :, 2 * columns :], axis=2)
        here = (at[:, None] == window_iota[None, :])[:, :, None]
        return jnp.sum(jnp.where(here, product[:, None], 0.0), axis=0)

    early_jobs, late_jobs = sum(stages[1:-1], []), stages[-1]
    early_at = jnp.stack([at for _, at in early_jobs])
    late_at = late_jobs[0][1][None]
    early_jobs = stages[0] + early_jobs
    early_at = jnp.concatenate((chip[None], early_at))

    early_pair = halved([(panels, w) for w, _ in early_jobs])

    at = (
        (window_iota * rows)[:, None, None]
        + (lax.iota(jnp.int32, per_window) * tile)[None, :, None]
        + member * piece
        + lax.iota(jnp.int32, piece)[None, None, :]
    ).reshape(-1, 1)
    weight = jnp.sum(jnp.where(to.reshape(1, -1) == at, weights[None, :], 0.0), axis=1)
    weight = weight.reshape(chips, per_window * piece)
    outer = jnp.where(chip == 0, last, jnp.where(chip == last, 0, early_at[2]))
    places = jnp.concatenate((early_at[:2], outer[None], early_at[3:], late_at))
    here = (places[:, None] == window_iota[None, :])[:, :, None]
    weight_here = jnp.sum(jnp.where(here, weight[None], 0.0), axis=1)[:, :, None]

    late, by_a, early_pair, far_panels = lax.optimization_barrier(
        (by_b, by_a, early_pair, far_panels)
    )
    late = sent(late, homes)
    late_window = [(by_a,), (by_b,)]
    late_jobs = [(panels, late_window), (far_panels, [(by_b,)])]

    def kernel_of_all():
        value = summed([early_pair, halved(late_jobs)])
        density = shared_density(value, jnp.concatenate((early_at, late_at, late_at)))
        value, far_value = value[:-1], value[-1:]
        packed = jnp.concatenate(
            (far_value[0], jnp.pad(density, ((0, 0), (0, 4 * columns - points)))), axis=0
        )
        packed = flip(packed, "grid", 2)
        home_value, neighbour = packed[None, :points], packed[points:, :points]
        if chips <= 4:
            others = [flip(density, "grid", 2 * d) for d in range(2, chips)]
            density = density + neighbour + sum(others[1:], others[0])
        else:
            density = density + neighbour
            for bit in grid_bits[2:]:
                density = density + flip(density, "grid", bit)
        density = density * (1.0 / math.sqrt(total))

        values = jnp.concatenate((value[:2], value[2:3] + home_value, value[3:]))
        density_here = jnp.sum(jnp.where(here, density[None], 0.0), axis=1)[:, :, None]
        orbitals, response = values[:, :, : 2 * columns], values[:, :, 2 * columns :]
        kernel = (weight_here * (density_here * orbitals + response)).astype(BF16)
        kernel = kernel.reshape(-1, 1, piece, 2 * columns)
        if direct:
            parts = [kernel] + [flip(kernel, "occ", d) for d in range(1, occ_count)]
            for bit in occ_bits:
                swapped = (occ & bit) != 0
                parts = [
                    jnp.where(swapped, parts[j ^ bit], parts[j]) for j in range(occ_count)
                ]
            kernel = jnp.concatenate(parts, axis=1)
        else:
            for bit in occ_bits:
                kernel = doubled(kernel, "occ", bit, 1)
        return doubled(kernel, "grid", 1, 1).reshape(-1, 2 * columns)

    kernel = lax.cond(
        fits,
        kernel_of_all,
        lambda: jnp.zeros((places.shape[0] * rows, 2 * columns), BF16),
    )
    early_windows = [w for w, _ in early_jobs]
    early_windows[2] = early_windows[2] + [(late,)]
    windows = early_windows + [late_window]
    ours, theirs = contract(kernel, windows, core)
    back = flip(theirs, "grid", 1)
    scale = 1.0 / math.sqrt(rows * grid_count)
    other = lax.cond(
        fits,
        lambda *given: unwritten((columns, cols)),
        lambda *given: any_sizes(*given) * scale,
        orbital_values,
        occupied,
        trial,
        point_weights,
        batch_sizes,
        significant,
    )
    return finish(core, fits, ours, back, other, scale).T


def solution(mesh):
    placed = (
        P("grid", "occ"),
        P("occ", "grid"),
        P("occ", "grid"),
        P("grid"),
        P("grid"),
        P("grid", "occ"),
    )
    return jax.shard_map(
        per_device, mesh=mesh, in_specs=placed, out_specs=P("occ", "grid"), check_vma=False
    )
```

```python
import math

import jax
import jax.numpy as jnp
from jax import lax
from jax.experimental import pallas as pl
from jax.experimental.pallas import tpu as pltpu
from jax.sharding import PartitionSpec as P

BF16, F32 = jnp.bfloat16, jnp.float32
VMEM_LIMIT = 48 * 1024 * 1024
WHOLE = pl.BlockSpec(memory_space=pltpu.VMEM)
SCALARS = pl.BlockSpec(memory_space=pltpu.SMEM)


def screen(values, sizes, significant):
    rows, cols = values.shape
    batches = sizes.shape[0]
    blocks = significant.shape[1]
    blocked = (
        values.reshape(batches, rows // batches, blocks, cols // blocks)
        * significant.astype(values.dtype)[:, None, :, None]
    )
    position = lax.broadcasted_iota(jnp.int32, (batches, rows // batches), 1)
    live = (position < sizes[:, None]).astype(jnp.float32).reshape(rows)
    return (blocked.reshape(rows, cols), live)


def any_sizes(orbital_values, occupied, trial, point_weights, batch_sizes, significant):
    screened, live = screen(orbital_values, batch_sizes, significant)
    rows, cols = screened.shape
    grid_count, occ_count = lax.axis_size("grid"), lax.axis_size("occ")
    columns = occupied.shape[1]
    me = lax.axis_index("grid")
    ring = [(i, (i + 1) % grid_count) for i in range(grid_count)]
    occ_ring = [(i, (i + 1) % occ_count) for i in range(occ_count)]

    def project_one(step, carry):
        panel, terms = carry
        term = jnp.dot(screened, panel, preferred_element_type=F32)
        terms = lax.dynamic_update_index_in_dim(terms, term, (me - step) % grid_count, 0)
        return lax.ppermute(panel, "grid", ring), terms

    joined = jnp.concatenate((occupied, trial), axis=1)
    terms = jnp.zeros((grid_count, rows, 2 * columns), F32)
    terms = lax.fori_loop(0, grid_count, project_one, (joined, terms))[1]

    def add_one(step, carry):
        moving, held = carry
        moving = lax.ppermute(moving, "occ", occ_ring)
        return moving, held + moving

    terms = lax.fori_loop(0, occ_count - 1, add_one, (terms, terms))[1]
    orbitals, response = terms[:, :, :columns], terms[:, :, columns:]
    density = jnp.sum(orbitals * response, axis=(0, 2)) * (1.0 / math.sqrt(columns * grid_count))
    weight = (point_weights * live)[None, :, None]
    kernel = (weight * (density[None, :, None] * orbitals + response)).astype(BF16)

    def contract_one(step, held):
        owner = (me + grid_count - 1 - step) % grid_count
        part = lax.dynamic_index_in_dim(kernel, owner, 0, keepdims=False)
        term = lax.dot_general(
            part, screened, (((0,), (0,)), ((), ())), preferred_element_type=F32
        )
        return lax.ppermute(held, "grid", ring) + term

    return lax.fori_loop(0, grid_count, contract_one, jnp.zeros((columns, cols), F32))


def half_of(whole, which):
    rows, columns = whole.shape
    half = rows // 2
    if half % 16:
        return lax.dynamic_slice_in_dim(whole, which * half, half, 0)

    def body(which_ref, whole_ref, out_ref, sem):
        first = pl.multiple_of(which_ref[0] * half, 16)
        copy = pltpu.make_async_copy(whole_ref.at[pl.ds(first, half)], out_ref, sem)
        copy.start()
        copy.wait()

    return pl.pallas_call(
        body,
        out_shape=jax.ShapeDtypeStruct((half, columns), whole.dtype),
        in_specs=[SCALARS, pl.BlockSpec(memory_space=pl.ANY)],
        out_specs=WHOLE,
        scratch_shapes=[pltpu.SemaphoreType.DMA],
        compiler_params=pltpu.CompilerParams(vmem_limit_bytes=VMEM_LIMIT),
        name="half_of",
    )(which[None], whole)


def compact(mine, got, mine_sig, got_sig, mine_to, got_to, width, tile, odd):
    half, rows = mine.shape
    blocks = mine_sig.shape[0]
    count = rows // tile + 2

    def body(odd_ref, mine_ref, got_ref, msig_ref, gsig_ref, mto_ref, gto_ref, *outs):
        block_of = lax.broadcasted_iota(jnp.int32, (half, blocks), 0)
        begin = lax.broadcasted_iota(jnp.int32, (half, blocks), 1) * width
        spread = ((block_of >= begin) & (block_of < begin + width)).astype(F32).astype(BF16)
        slot = lax.broadcasted_iota(jnp.int32, (rows, count * tile), 1)

        def part(value_ref, sig_ref, to_ref):
            kept = jnp.dot(spread, sig_ref[...], preferred_element_type=F32)
            screened = (value_ref[...].astype(F32) * kept).astype(BF16)
            place = (to_ref[...] == slot).astype(F32).astype(BF16)
            return jnp.dot(screened, place, preferred_element_type=F32)

        window = part(mine_ref, msig_ref, mto_ref) + part(got_ref, gsig_ref, gto_ref)
        for j in range(1, count - 1):
            outs[j][...] = window[:, j * tile : (j + 1) * tile].astype(BF16)
        first, last = window[:, :tile], window[:, (count - 1) * tile :]
        outs[0][...] = jnp.where(odd_ref[0] == 0, first, last).astype(BF16)
        outs[-1][...] = jnp.where(odd_ref[0] == 0, last, first).astype(BF16)

    shape = jax.ShapeDtypeStruct((half, tile), BF16)
    return pl.pallas_call(
        body,
        out_shape=(shape,) * count,
        in_specs=[SCALARS] + [WHOLE] * 6,
        out_specs=(WHOLE,) * count,
        compiler_params=pltpu.CompilerParams(vmem_limit_bytes=VMEM_LIMIT),
        name="compact",
        cost_estimate=pl.CostEstimate(
            flops=8 * half * rows * rows, bytes_accessed=8 * half * rows, transcendentals=0
        ),
    )(odd[None], mine, got, mine_sig, got_sig, mine_to, got_to)


def straighten(tiles, by_a, by_b, odd):
    half, tile = by_a.shape
    count = len(tiles)

    def body(odd_ref, *refs):
        tile_refs, a_ref, b_ref, out_ref = refs[:count], *refs[count:]
        even = odd_ref[0] == 0
        for j in range(count):
            value = tile_refs[j][...]
            if j == 0:
                value = value + jnp.where(even, b_ref[...], a_ref[...])
            if j == count - 1:
                value = value + jnp.where(even, a_ref[...], b_ref[...])
            out_ref[:, j * tile : (j + 1) * tile] = value

    return pl.pallas_call(
        body,
        out_shape=jax.ShapeDtypeStruct((half, count * tile), BF16),
        in_specs=[SCALARS] + [WHOLE] * (count + 2),
        out_specs=WHOLE,
        compiler_params=pltpu.CompilerParams(vmem_limit_bytes=VMEM_LIMIT),
        name="straighten",
    )(odd[None], *tiles, by_a, by_b)


def stack_panels(mine, got, core):
    both, half = mine.shape
    columns = both // 2
    width = -(-half // 128) * 128

    def body(core_ref, mine_ref, got_ref, out_ref):
        first = core_ref[0] == 0
        out_ref[...] = jnp.zeros_like(out_ref)
        for j in range(2):
            low = mine_ref[j * columns : (j + 1) * columns]
            high = got_ref[j * columns : (j + 1) * columns]
            q = 2 * j * columns
            out_ref[q : q + columns, :half] = jnp.where(first, low, high)
            out_ref[q + columns : q + 2 * columns, :half] = jnp.where(first, high, low)

    return pl.pallas_call(
        body,
        out_shape=jax.ShapeDtypeStruct((2 * both, width), BF16),
        in_specs=[SCALARS, WHOLE, WHOLE],
        out_specs=WHOLE,
        compiler_params=pltpu.CompilerParams(vmem_limit_bytes=VMEM_LIMIT),
        name="stack_panels",
    )(core[None], mine, got)


def distinct(arrays):
    return list({id(x): x for x in arrays}.values())


def read_window(addends, arrays, refs):
    ref_of = {id(x): ref for x, ref in zip(arrays, refs)}
    total = None
    for x in addends:
        value = ref_of[id(x)][...]
        total = value if total is None else total + value
    return total


def steps_over(half):
    step = half if half <= 512 else 512
    return step, -(-half // step)


def split_sum(pairs, occ):
    _, shares, piece, both = pairs[0][0].shape
    tiles = sum(keep.shape[0] for keep, _ in pairs)

    def body(occ_ref, *refs):
        ins, outs = refs[: 2 * len(pairs)], refs[2 * len(pairs) :]
        for d in range(shares):
            at = 0
            for keep_ref, got_ref in zip(ins[::2], ins[1::2]):
                for q in range(keep_ref.shape[0]):
                    outs[d][at] = keep_ref[q, occ_ref[0] ^ d] + got_ref[q, occ_ref[0] ^ d]
                    at += 1

    shape = jax.ShapeDtypeStruct((tiles, piece, both), F32)
    return pl.pallas_call(
        body,
        out_shape=(shape,) * shares,
        in_specs=[SCALARS] + [WHOLE] * (2 * len(pairs)),
        out_specs=(WHOLE,) * shares,
        compiler_params=pltpu.CompilerParams(vmem_limit_bytes=VMEM_LIMIT),
        name="split_sum",
    )(occ[None], *sum(pairs, ()))


def project(jobs, tile, shares, core):
    both = jobs[0][0].shape[0]
    half, rows = jobs[0][1][0].shape
    piece = tile // shares
    tiles = len(jobs) * rows // tile
    panels = distinct([p for p, _ in jobs])
    arrays = distinct([x for _, window in jobs for x in window])
    count = len(panels)
    step, steps = steps_over(half)
    padded = panels[0].shape[1]

    def body(core_ref, *refs):
        panel_refs, array_refs = refs[:count], refs[count:-4]
        keep_ref, give_ref, total_ref, terms_ref = refs[-4:]
        i = pl.program_id(0)

        @pl.when(i == 0)
        def _():
            total_ref[...] = jnp.zeros_like(total_ref)

        inside = lax.broadcasted_iota(jnp.int32, (step, rows), 0) + i * step < half
        for s, (panel, window) in enumerate(jobs):
            panel_ref = panel_refs[[id(p) for p in panels].index(id(panel))]
            value = read_window(window, arrays, array_refs)
            if steps * step != half:
                value = jnp.where(inside, value, jnp.zeros_like(value))
            part = panel_ref[:, :step]
            total_ref[s] += jnp.dot(part, value, preferred_element_type=F32)

        @pl.when(i == steps - 1)
        def _():
            q = 0
            for s in range(len(jobs)):
                turned = total_ref[s].T
                for j in range(0, rows, tile):
                    terms_ref[q] = turned[j : j + tile].reshape(2, shares // 2, piece, both)
                    keep_ref[q] = terms_ref[q, core_ref[0]]
                    give_ref[q] = terms_ref[q, 1 - core_ref[0]]
                    q += 1

    shape = jax.ShapeDtypeStruct((tiles, shares // 2, piece, both), F32)
    panel_step = step if steps > 1 else padded
    return pl.pallas_call(
        body,
        grid=(steps,),
        out_shape=(shape, shape),
        in_specs=[SCALARS]
        + [pl.BlockSpec((both, panel_step), lambda i: (0, i))] * count
        + [pl.BlockSpec((step, rows), lambda i: (i, 0))] * len(arrays),
        out_specs=(pl.BlockSpec(shape.shape, lambda i: (0, 0, 0, 0)),) * 2,
        scratch_shapes=[
            pltpu.VMEM((len(jobs), both, rows), F32),
            pltpu.VMEM((tiles, 2, shares // 2, piece, both), F32),
        ],
        compiler_params=pltpu.CompilerParams(vmem_limit_bytes=VMEM_LIMIT),
        name="project",
        cost_estimate=pl.CostEstimate(
            flops=2 * both * half * tiles * tile,
            bytes_accessed=2 * half * (both + tiles * tile) + 4 * tiles * tile * both,
            transcendentals=0,
        ),
    )(core[None], *panels, *arrays)


def in_order(parts, occ):
    tiles, _, piece, columns = parts[0].shape

    def body(occ_ref, *refs):
        for d in range(len(parts)):
            refs[-1][:, occ_ref[0] ^ d] = refs[d][:, 0]

    return pl.pallas_call(
        body,
        out_shape=jax.ShapeDtypeStruct((tiles, len(parts), piece, columns), parts[0].dtype),
        in_specs=[SCALARS] + [WHOLE] * len(parts),
        out_specs=WHOLE,
        compiler_params=pltpu.CompilerParams(vmem_limit_bytes=VMEM_LIMIT),
        name="in_order",
    )(occ[None], *parts)


def contract(kernel, got, windows, core):
    tiles, shares, piece, columns = kernel.shape
    half, rows = windows[0][0].shape
    own = columns // 2
    arrays = distinct([x for window in windows for x in window])
    step, steps = steps_over(half)
    per_window = tiles // len(windows)

    def body(core_ref, kernel_ref, got_ref, *refs):
        array_refs = refs[:-4]
        mine_ref, other_ref, order_ref, turned_ref = refs[-4:]
        first = core_ref[0] == 0

        @pl.when(pl.program_id(0) == 0)
        def _():
            order_ref[:, core_ref[0]] = kernel_ref[...].astype(F32)
            order_ref[:, 1 - core_ref[0]] = got_ref[...].astype(F32)
            for s in range(len(windows)):
                part = order_ref[s * per_window : (s + 1) * per_window]
                turned = part.reshape(rows, columns).T
                low, high = turned[:own], turned[own:]
                turned_ref[s, :own] = jnp.where(first, low, high).astype(BF16)
                turned_ref[s, own:] = jnp.where(first, high, low).astype(BF16)

        total = None
        for s, window in enumerate(windows):
            term = lax.dot_general(
                turned_ref[s],
                read_window(window, arrays, array_refs),
                (((1,), (1,)), ((), ())),
                preferred_element_type=F32,
            )
            total = term if total is None else total + term
        mine_ref[...] = total[:own]
        other_ref[...] = total[own:]

    shape = jax.ShapeDtypeStruct((own, half), F32)
    whole = pl.BlockSpec(kernel.shape, lambda i: (0, 0, 0, 0))
    return pl.pallas_call(
        body,
        grid=(steps,),
        out_shape=(shape, shape),
        in_specs=[SCALARS, whole, whole]
        + [pl.BlockSpec((step, rows), lambda i: (i, 0))] * len(arrays),
        out_specs=(pl.BlockSpec((own, step), lambda i: (0, i)),) * 2,
        scratch_shapes=[
            pltpu.VMEM((tiles, 2, shares, piece, columns), F32),
            pltpu.VMEM((len(windows), columns, rows), BF16),
        ],
        compiler_params=pltpu.CompilerParams(vmem_limit_bytes=VMEM_LIMIT),
        name="contract",
        cost_estimate=pl.CostEstimate(
            flops=2 * columns * half * rows * len(windows),
            bytes_accessed=2 * rows * len(windows) * half + 4 * columns * half,
            transcendentals=0,
        ),
    )(core[None], kernel, got, *arrays)


def unwritten(shape):
    def body(out_ref):
        pass

    return pl.pallas_call(
        body,
        out_shape=jax.ShapeDtypeStruct(shape, F32),
        out_specs=pl.BlockSpec(memory_space=pltpu.HBM),
        name="unwritten",
    )()


def finish(core, fits, ours, back, other, scale):
    own, half = ours.shape

    def body(flags_ref, ours_ref, back_ref, other_ref, out_ref, whole_ref, sem):
        @pl.when(flags_ref[1] != 0)
        def _():
            first = flags_ref[0] == 0
            whole_ref[:, :half] = jnp.where(first, ours_ref[...], back_ref[...]) * scale
            whole_ref[:, half:] = jnp.where(first, back_ref[...], ours_ref[...]) * scale
            copy = pltpu.make_async_copy(whole_ref, out_ref, sem)
            copy.start()
            copy.wait()

    return pl.pallas_call(
        body,
        out_shape=jax.ShapeDtypeStruct((own, 2 * half), F32),
        in_specs=[SCALARS, WHOLE, WHOLE, pl.BlockSpec(memory_space=pltpu.HBM)],
        out_specs=pl.BlockSpec(memory_space=pltpu.HBM),
        scratch_shapes=[pltpu.VMEM((own, 2 * half), F32), pltpu.SemaphoreType.DMA],
        input_output_aliases={3: 0},
        compiler_params=pltpu.CompilerParams(vmem_limit_bytes=VMEM_LIMIT),
        name="finish",
    )(jnp.stack((core, fits.astype(jnp.int32))), ours, back, other)


def per_device(orbital_values, occupied, trial, point_weights, batch_sizes, significant):
    rows, cols = orbital_values.shape
    batches = batch_sizes.shape[0]
    slots = rows // batches
    blocks = significant.shape[1]
    columns = occupied.shape[1]
    grid_count = lax.axis_size("grid")
    occ_count = lax.axis_size("occ")
    chips = grid_count // 2
    shares = 2 * occ_count
    half = cols // 2
    total = columns * grid_count
    place = lax.axis_index("grid")
    chip, core = place // 2, place % 2
    occ = lax.axis_index("occ")
    member = core * occ_count + occ

    def flip(x, axis, bit):
        count = lax.axis_size(axis)
        return lax.ppermute(x, axis, [(i, i ^ bit) for i in range(count)])

    def along(pairs):
        return [(2 * a + c, 2 * b + c) for a, b in pairs for c in range(2)]

    def doubled(x, axis, bit, dim):
        got = flip(x, axis, bit)
        mine = (lax.axis_index(axis) & bit) == 0
        return jnp.where(
            mine, jnp.concatenate((x, got), axis=dim), jnp.concatenate((got, x), axis=dim)
        )

    def halves(whole, axis):
        size = whole.shape[axis] // 2
        mine = lax.dynamic_slice_in_dim(whole, core * size, size, axis)
        return mine, lax.dynamic_slice_in_dim(whole, (1 - core) * size, size, axis)

    grid_bits = [1 << b for b in range(grid_count.bit_length() - 1)]
    occ_bits = [1 << b for b in range(occ_count.bit_length() - 1)]

    mine = half_of(orbital_values.T, core)
    got = flip(half_of(orbital_values.T, 1 - core), "grid", 1)
    mine_sig, other_sig = halves(significant.T, 0)
    got_sig = flip(other_sig, "grid", 1)

    told = jnp.concatenate(
        (
            doubled(batch_sizes[None], "grid", 1, 0).astype(F32).reshape(1, -1),
            doubled(point_weights[None], "grid", 1, 0).reshape(1, -1),
        ),
        axis=1,
    )
    if chips <= 4:
        heard = [told]
        for step in range(1, chips):
            around = [(i, (i + 2 * step) % grid_count) for i in range(grid_count)]
            heard.append(lax.ppermute(told, "grid", around))
        heard = jnp.concatenate(heard)
        behind = (chip - lax.iota(jnp.int32, chips)) % chips
        pick = behind[:, None, None] == lax.iota(jnp.int32, chips)[None, :, None]
        told = jnp.sum(jnp.where(pick, heard[None], 0.0), axis=1)
    else:
        for bit in grid_bits[1:]:
            told = doubled(told, "grid", bit, 0)
    sizes = told[:, : 2 * batches].astype(jnp.int32).reshape(-1)
    weights = told[:, 2 * batches :].reshape(-1)

    batch = lax.broadcasted_iota(jnp.int32, (sizes.shape[0], sizes.shape[0]), 0)
    before = lax.broadcasted_iota(jnp.int32, (sizes.shape[0], sizes.shape[0]), 1) < batch
    start = jnp.sum(jnp.where(before, sizes[None, :], 0), axis=1)
    position = lax.broadcasted_iota(jnp.int32, (sizes.shape[0], slots), 1)
    to = jnp.where(position < sizes[:, None], start[:, None] + position, -4 * rows * grid_count)
    to = to.reshape(grid_count, rows)
    first = start.reshape(chips, -1)[:, 0]
    margin = rows // 2 if (rows // 2) % (8 * shares) == 0 else rows
    nominal = rows * lax.iota(jnp.int32, chips)
    fits = jnp.all(jnp.abs(first - nominal) <= margin) & (jnp.sum(sizes) <= rows * chips)

    tile = margin
    piece = tile // shares
    base = rows * chip - margin
    mine_to = lax.dynamic_index_in_dim(to, place, 0, keepdims=False) - base
    got_to = lax.dynamic_index_in_dim(to, place ^ 1, 0, keepdims=False) - base
    odd = chip % 2
    for_b, *own_tiles, for_a = compact(
        mine,
        got,
        jnp.repeat(mine_sig.astype(BF16), slots, axis=1),
        jnp.repeat(got_sig.astype(BF16), slots, axis=1),
        mine_to[:, None],
        got_to[:, None],
        cols // blocks,
        tile,
        odd,
    )

    def sent(x, pairs):
        return lax.ppermute(x, "grid", along(pairs))

    last = chips - 1

    def over(links, t):
        pairs = []
        for a in range(links, last, 2):
            pairs += [(a, a + 1)] if a - t + 1 >= 0 else []
            pairs += [(a + 1, a)] if a + t <= last else []
        return pairs

    own = straighten(own_tiles, sent(for_a, over(0, 1)), sent(for_b, over(1, 1)), odd)

    mine_panel, other_panel = halves(jnp.concatenate((occupied, trial), axis=1).T, 1)
    panels = stack_panels(mine_panel, flip(other_panel, "grid", 1), core)

    per_window = rows // tile
    window_iota = lax.iota(jnp.int32, chips)
    ends = [(0, 1), (last, last - 1)]
    homes = [(b, a) for a, b in ends]
    side = 1 - 2 * odd

    def valid(at):
        return jnp.where((at >= 0) & (at <= last), at, -1)

    stages = [[([own], chip)]]
    by_a = by_b = own
    far_panels = None
    for t in range(1, last):
        by_a, by_b = sent(by_b, over(0, t)), sent(by_a, over(1, t))
        if t == 1:
            far_panels = sent(panels, ends)
        a_at, b_at = valid(chip + side * t), valid(chip - side * t)
        if 2 * t > last:
            stages.append([([by_a, by_b], jnp.maximum(a_at, b_at))])
        else:
            stages.append([([by_a], a_at), ([by_b], b_at)])

    direct = occ_count <= 4
    points = per_window * piece

    def halved(jobs):
        keep, give = project(jobs, tile, shares, core)
        return keep, flip(give, "grid", 1)

    def summed(pairs):
        if direct:
            parts = split_sum(pairs, occ)
            value = parts[0]
            for d in range(1, occ_count):
                value = value + flip(parts[d], "occ", d)
        else:
            value = jnp.concatenate([keep + got for keep, got in pairs])
            for bit in reversed(occ_bits):
                upper = (occ & bit) != 0
                low_part, high_part = value[:, :bit], value[:, bit:]
                got = flip(jnp.where(upper, low_part, high_part), "occ", bit)
                value = jnp.where(upper, high_part, low_part) + got
        return value.reshape(-1, points, 4 * columns)

    def shared_density(value, at):
        product = jnp.sum(value[:, :, : 2 * columns] * value[:, :, 2 * columns :], axis=2)
        here = (at[:, None] == window_iota[None, :])[:, :, None]
        return jnp.sum(jnp.where(here, product[:, None], 0.0), axis=0)

    early_jobs, late_jobs = sum(stages[1:-1], []), stages[-1]
    early_at = jnp.stack([at for _, at in early_jobs])
    late_at = late_jobs[0][1][None]
    early_jobs = stages[0] + early_jobs
    early_at = jnp.concatenate((chip[None], early_at))

    early_pair = halved([(panels, w) for w, _ in early_jobs])

    at = (
        (window_iota * rows)[:, None, None]
        + (lax.iota(jnp.int32, per_window) * tile)[None, :, None]
        + member * piece
        + lax.iota(jnp.int32, piece)[None, None, :]
    ).reshape(-1, 1)
    weight = jnp.sum(jnp.where(to.reshape(1, -1) == at, weights[None, :], 0.0), axis=1)
    weight = weight.reshape(chips, per_window * piece)
    outer = jnp.where(chip == 0, last, jnp.where(chip == last, 0, early_at[2]))
    places = jnp.concatenate((early_at[:2], outer[None], early_at[3:], late_at))
    here = (places[:, None] == window_iota[None, :])[:, :, None]
    weight_here = jnp.sum(jnp.where(here, weight[None], 0.0), axis=1)[:, :, None]

    late, by_a, early_pair, far_panels, weight_here = lax.optimization_barrier(
        (by_b, by_a, early_pair, far_panels, weight_here)
    )
    late = sent(late, homes)
    late_window = [by_a, by_b]
    late_jobs = [(panels, late_window), (far_panels, [by_b])]

    def kernel_of_all():
        value = summed([early_pair, halved(late_jobs)])
        density = shared_density(value, jnp.concatenate((early_at, late_at, late_at)))
        value, far_value = value[:-1], value[-1:]
        packed = jnp.concatenate(
            (far_value[0], jnp.pad(density, ((0, 0), (0, 4 * columns - points)))), axis=0
        )
        packed = flip(packed, "grid", 2)
        home_value, neighbour = packed[None, :points], packed[points:, :points]
        if chips <= 4:
            others = [flip(density, "grid", 2 * d) for d in range(2, chips)]
            density = density + neighbour + sum(others[1:], others[0])
        else:
            density = density + neighbour
            for bit in grid_bits[2:]:
                density = density + flip(density, "grid", bit)
        density = density * (1.0 / math.sqrt(total))

        values = jnp.concatenate((value[:2], value[2:3] + home_value, value[3:]))
        density_here = jnp.sum(jnp.where(here, density[None], 0.0), axis=1)[:, :, None]
        orbitals, response = values[:, :, : 2 * columns], values[:, :, 2 * columns :]
        kernel = (weight_here * (density_here * orbitals + response)).astype(BF16)
        kernel = kernel.reshape(-1, 1, piece, 2 * columns)
        if direct:
            parts = [kernel] + [flip(kernel, "occ", d) for d in range(1, occ_count)]
            kernel = in_order(parts, occ)
        else:
            for bit in occ_bits:
                kernel = doubled(kernel, "occ", bit, 1)
        return kernel, flip(kernel, "grid", 1)

    no_kernel = jnp.zeros((places.shape[0] * per_window, occ_count, piece, 2 * columns), BF16)
    kernel, got_kernel = lax.cond(fits, kernel_of_all, lambda: (no_kernel, no_kernel))
    early_windows = [w for w, _ in early_jobs]
    early_windows[2] = early_windows[2] + [late]
    windows = early_windows + [late_window]
    ours, theirs = contract(kernel, got_kernel, windows, core)
    back = flip(theirs, "grid", 1)
    scale = 1.0 / math.sqrt(rows * grid_count)
    other = lax.cond(
        fits,
        lambda *given: unwritten((columns, cols)),
        lambda *given: any_sizes(*given) * scale,
        orbital_values,
        occupied,
        trial,
        point_weights,
        batch_sizes,
        significant,
    )
    return finish(core, fits, ours, back, other, scale).T


def solution(mesh):
    placed = (
        P("grid", "occ"),
        P("occ", "grid"),
        P("occ", "grid"),
        P("grid"),
        P("grid"),
        P("grid", "occ"),
    )
    return jax.shard_map(
        per_device, mesh=mesh, in_specs=placed, out_specs=P("occ", "grid"), check_vma=False
    )
```

```python
import math

import jax
import jax.numpy as jnp
from jax import lax
from jax.experimental import pallas as pl
from jax.experimental.pallas import tpu as pltpu
from jax.sharding import PartitionSpec as P

BF16, F32 = jnp.bfloat16, jnp.float32
MIB = 1024 * 1024
WHOLE = pl.BlockSpec(memory_space=pltpu.VMEM)
SCALARS = pl.BlockSpec(memory_space=pltpu.SMEM)


def screen(values, sizes, significant):
    rows, cols = values.shape
    batches = sizes.shape[0]
    blocks = significant.shape[1]
    blocked = (
        values.reshape(batches, rows // batches, blocks, cols // blocks)
        * significant.astype(values.dtype)[:, None, :, None]
    )
    position = lax.broadcasted_iota(jnp.int32, (batches, rows // batches), 1)
    live = (position < sizes[:, None]).astype(jnp.float32).reshape(rows)
    return (blocked.reshape(rows, cols), live)


def any_sizes(orbital_values, occupied, trial, point_weights, batch_sizes, significant):
    screened, live = screen(orbital_values, batch_sizes, significant)
    rows, cols = screened.shape
    grid_count, occ_count = lax.axis_size("grid"), lax.axis_size("occ")
    columns = occupied.shape[1]
    me = lax.axis_index("grid")
    ring = [(i, (i + 1) % grid_count) for i in range(grid_count)]
    occ_ring = [(i, (i + 1) % occ_count) for i in range(occ_count)]

    def project_one(step, carry):
        panel, terms = carry
        term = jnp.dot(screened, panel, preferred_element_type=F32)
        terms = lax.dynamic_update_index_in_dim(terms, term, (me - step) % grid_count, 0)
        return lax.ppermute(panel, "grid", ring), terms

    joined = jnp.concatenate((occupied, trial), axis=1)
    terms = jnp.zeros((grid_count, rows, 2 * columns), F32)
    terms = lax.fori_loop(0, grid_count, project_one, (joined, terms))[1]

    def add_one(step, carry):
        moving, held = carry
        moving = lax.ppermute(moving, "occ", occ_ring)
        return moving, held + moving

    terms = lax.fori_loop(0, occ_count - 1, add_one, (terms, terms))[1]
    orbitals, response = terms[:, :, :columns], terms[:, :, columns:]
    density = jnp.sum(orbitals * response, axis=(0, 2)) * (1.0 / math.sqrt(columns * grid_count))
    weight = (point_weights * live)[None, :, None]
    kernel = (weight * (density[None, :, None] * orbitals + response)).astype(BF16)

    def contract_one(step, held):
        owner = (me + grid_count - 1 - step) % grid_count
        part = lax.dynamic_index_in_dim(kernel, owner, 0, keepdims=False)
        term = lax.dot_general(
            part, screened, (((0,), (0,)), ((), ())), preferred_element_type=F32
        )
        return lax.ppermute(held, "grid", ring) + term

    return lax.fori_loop(0, grid_count, contract_one, jnp.zeros((columns, cols), F32))


def half_of(whole, which):
    rows, columns = whole.shape
    half = rows // 2
    if half % 16:
        return lax.dynamic_slice_in_dim(whole, which * half, half, 0)

    def body(which_ref, whole_ref, out_ref, sem):
        first = pl.multiple_of(which_ref[0] * half, 16)
        copy = pltpu.make_async_copy(whole_ref.at[pl.ds(first, half)], out_ref, sem)
        copy.start()
        copy.wait()

    return pl.pallas_call(
        body,
        out_shape=jax.ShapeDtypeStruct((half, columns), whole.dtype),
        in_specs=[SCALARS, pl.BlockSpec(memory_space=pl.ANY)],
        out_specs=WHOLE,
        scratch_shapes=[pltpu.SemaphoreType.DMA],
        compiler_params=pltpu.CompilerParams(vmem_limit_bytes=4 * MIB),
        name="half_of",
    )(which[None], whole)


def compact(mine, got, mine_sig, got_sig, mine_to, got_to, width, tile, odd):
    half, rows = mine.shape
    blocks = mine_sig.shape[0]
    count = rows // tile + 2

    def body(odd_ref, mine_ref, got_ref, msig_ref, gsig_ref, mto_ref, gto_ref, *outs):
        block_of = lax.broadcasted_iota(jnp.int32, (half, blocks), 0)
        begin = lax.broadcasted_iota(jnp.int32, (half, blocks), 1) * width
        spread = ((block_of >= begin) & (block_of < begin + width)).astype(F32).astype(BF16)
        slot = lax.broadcasted_iota(jnp.int32, (rows, count * tile), 1)

        def part(value_ref, sig_ref, to_ref):
            kept = jnp.dot(spread, sig_ref[...], preferred_element_type=F32)
            screened = (value_ref[...].astype(F32) * kept).astype(BF16)
            place = (to_ref[...] == slot).astype(F32).astype(BF16)
            return jnp.dot(screened, place, preferred_element_type=F32)

        window = part(mine_ref, msig_ref, mto_ref) + part(got_ref, gsig_ref, gto_ref)
        for j in range(1, count - 1):
            outs[j][...] = window[:, j * tile : (j + 1) * tile].astype(BF16)
        first, last = window[:, :tile], window[:, (count - 1) * tile :]
        outs[0][...] = jnp.where(odd_ref[0] == 0, first, last).astype(BF16)
        outs[-1][...] = jnp.where(odd_ref[0] == 0, last, first).astype(BF16)

    shape = jax.ShapeDtypeStruct((half, tile), BF16)
    return pl.pallas_call(
        body,
        out_shape=(shape,) * count,
        in_specs=[SCALARS] + [WHOLE] * 6,
        out_specs=(WHOLE,) * count,
        compiler_params=pltpu.CompilerParams(vmem_limit_bytes=24 * MIB),
        name="compact",
        cost_estimate=pl.CostEstimate(
            flops=8 * half * rows * rows, bytes_accessed=8 * half * rows, transcendentals=0
        ),
    )(odd[None], mine, got, mine_sig, got_sig, mine_to, got_to)


def straighten(tiles, by_a, by_b, odd):
    half, tile = by_a.shape
    count = len(tiles)

    def body(odd_ref, *refs):
        tile_refs, a_ref, b_ref, out_ref = refs[:count], *refs[count:]
        even = odd_ref[0] == 0
        for j in range(count):
            value = tile_refs[j][...]
            if j == 0:
                value = value + jnp.where(even, b_ref[...], a_ref[...])
            if j == count - 1:
                value = value + jnp.where(even, a_ref[...], b_ref[...])
            out_ref[:, j * tile : (j + 1) * tile] = value

    return pl.pallas_call(
        body,
        out_shape=jax.ShapeDtypeStruct((half, count * tile), BF16),
        in_specs=[SCALARS] + [WHOLE] * (count + 2),
        out_specs=WHOLE,
        compiler_params=pltpu.CompilerParams(vmem_limit_bytes=8 * MIB),
        name="straighten",
    )(odd[None], *tiles, by_a, by_b)


def panel_halves(occupied, trial, core):
    columns, cols = occupied.shape
    half = cols // 2
    width = -(-half // 128) * 128

    def body(core_ref, occupied_ref, trial_ref, mine_ref, other_ref):
        first = core_ref[0] == 0
        mine_ref[...] = jnp.zeros_like(mine_ref)
        other_ref[...] = jnp.zeros_like(other_ref)
        for j, ref in enumerate((occupied_ref, trial_ref)):
            low, high = ref[:, :half], ref[:, half:]
            mine_ref[j * columns : (j + 1) * columns, :half] = jnp.where(first, low, high)
            other_ref[j * columns : (j + 1) * columns, :half] = jnp.where(first, high, low)

    shape = jax.ShapeDtypeStruct((2 * columns, width), BF16)
    return pl.pallas_call(
        body,
        out_shape=(shape, shape),
        in_specs=[SCALARS, WHOLE, WHOLE],
        out_specs=(WHOLE, WHOLE),
        compiler_params=pltpu.CompilerParams(vmem_limit_bytes=8 * MIB),
        name="panel_halves",
    )(core[None], occupied, trial)


def stack_panels(mine, got, core):
    both, width = mine.shape
    columns = both // 2

    def body(core_ref, mine_ref, got_ref, out_ref):
        first = core_ref[0] == 0
        for j in range(2):
            low = mine_ref[j * columns : (j + 1) * columns]
            high = got_ref[j * columns : (j + 1) * columns]
            q = 2 * j * columns
            out_ref[q : q + columns] = jnp.where(first, low, high)
            out_ref[q + columns : q + 2 * columns] = jnp.where(first, high, low)

    return pl.pallas_call(
        body,
        out_shape=jax.ShapeDtypeStruct((2 * both, width), BF16),
        in_specs=[SCALARS, WHOLE, WHOLE],
        out_specs=WHOLE,
        compiler_params=pltpu.CompilerParams(vmem_limit_bytes=8 * MIB),
        name="stack_panels",
    )(core[None], mine, got)


def distinct(arrays):
    return list({id(x): x for x in arrays}.values())


def read_window(addends, arrays, refs):
    ref_of = {id(x): ref for x, ref in zip(arrays, refs)}
    total = None
    for x in addends:
        value = ref_of[id(x)][...]
        total = value if total is None else total + value
    return total


def steps_over(half):
    step = half if half <= 512 else 512
    return step, -(-half // step)


def split_sum(pairs, occ):
    _, shares, piece, both = pairs[0][0].shape
    tiles = sum(keep.shape[0] for keep, _ in pairs)

    def body(occ_ref, *refs):
        ins, outs = refs[: 2 * len(pairs)], refs[2 * len(pairs) :]
        for d in range(shares):
            at = 0
            for keep_ref, got_ref in zip(ins[::2], ins[1::2]):
                for q in range(keep_ref.shape[0]):
                    outs[d][at] = keep_ref[q, occ_ref[0] ^ d] + got_ref[q, occ_ref[0] ^ d]
                    at += 1

    shape = jax.ShapeDtypeStruct((tiles, piece, both), F32)
    return pl.pallas_call(
        body,
        out_shape=(shape,) * shares,
        in_specs=[SCALARS] + [WHOLE] * (2 * len(pairs)),
        out_specs=(WHOLE,) * shares,
        compiler_params=pltpu.CompilerParams(vmem_limit_bytes=8 * MIB),
        name="split_sum",
    )(occ[None], *sum(pairs, ()))


def project(jobs, tile, shares, core):
    both = jobs[0][0].shape[0]
    half, rows = jobs[0][1][0].shape
    piece = tile // shares
    tiles = len(jobs) * rows // tile
    panels = distinct([p for p, _ in jobs])
    arrays = distinct([x for _, window in jobs for x in window])
    count = len(panels)
    step, steps = steps_over(half)
    padded = panels[0].shape[1]

    def body(core_ref, *refs):
        panel_refs, array_refs = refs[:count], refs[count:-4]
        keep_ref, give_ref, total_ref, terms_ref = refs[-4:]
        i = pl.program_id(0)

        @pl.when(i == 0)
        def _():
            total_ref[...] = jnp.zeros_like(total_ref)

        inside = lax.broadcasted_iota(jnp.int32, (step, rows), 0) + i * step < half
        for s, (panel, window) in enumerate(jobs):
            panel_ref = panel_refs[[id(p) for p in panels].index(id(panel))]
            value = read_window(window, arrays, array_refs)
            if steps * step != half:
                value = jnp.where(inside, value, jnp.zeros_like(value))
            part = panel_ref[:, :step]
            total_ref[s] += jnp.dot(part, value, preferred_element_type=F32)

        @pl.when(i == steps - 1)
        def _():
            q = 0
            for s in range(len(jobs)):
                turned = total_ref[s].T
                for j in range(0, rows, tile):
                    terms_ref[q] = turned[j : j + tile].reshape(2, shares // 2, piece, both)
                    keep_ref[q] = terms_ref[q, core_ref[0]]
                    give_ref[q] = terms_ref[q, 1 - core_ref[0]]
                    q += 1

    shape = jax.ShapeDtypeStruct((tiles, shares // 2, piece, both), F32)
    panel_step = step if steps > 1 else padded
    return pl.pallas_call(
        body,
        grid=(steps,),
        out_shape=(shape, shape),
        in_specs=[SCALARS]
        + [pl.BlockSpec((both, panel_step), lambda i: (0, i))] * count
        + [pl.BlockSpec((step, rows), lambda i: (i, 0))] * len(arrays),
        out_specs=(pl.BlockSpec(shape.shape, lambda i: (0, 0, 0, 0)),) * 2,
        scratch_shapes=[
            pltpu.VMEM((len(jobs), both, rows), F32),
            pltpu.VMEM((tiles, 2, shares // 2, piece, both), F32),
        ],
        compiler_params=pltpu.CompilerParams(vmem_limit_bytes=12 * MIB),
        name="project",
        cost_estimate=pl.CostEstimate(
            flops=2 * both * half * tiles * tile,
            bytes_accessed=2 * half * (both + tiles * tile) + 4 * tiles * tile * both,
            transcendentals=0,
        ),
    )(core[None], *panels, *arrays)


def in_order(parts, occ):
    tiles, _, piece, columns = parts[0].shape

    def body(occ_ref, *refs):
        for d in range(len(parts)):
            refs[-1][:, occ_ref[0] ^ d] = refs[d][:, 0]

    return pl.pallas_call(
        body,
        out_shape=jax.ShapeDtypeStruct((tiles, len(parts), piece, columns), parts[0].dtype),
        in_specs=[SCALARS] + [WHOLE] * len(parts),
        out_specs=WHOLE,
        compiler_params=pltpu.CompilerParams(vmem_limit_bytes=4 * MIB),
        name="in_order",
    )(occ[None], *parts)


def contract(kernel, got, windows, core):
    tiles, shares, piece, columns = kernel.shape
    half, rows = windows[0][0].shape
    own = columns // 2
    arrays = distinct([x for window in windows for x in window])
    step, steps = steps_over(half)
    per_window = tiles // len(windows)

    def body(core_ref, kernel_ref, got_ref, *refs):
        array_refs = refs[:-4]
        mine_ref, other_ref, order_ref, turned_ref = refs[-4:]
        first = core_ref[0] == 0

        @pl.when(pl.program_id(0) == 0)
        def _():
            order_ref[:, core_ref[0]] = kernel_ref[...].astype(F32)
            order_ref[:, 1 - core_ref[0]] = got_ref[...].astype(F32)
            for s in range(len(windows)):
                part = order_ref[s * per_window : (s + 1) * per_window]
                turned_ref[s] = part.reshape(rows, columns).astype(BF16)

        total = None
        for s, window in enumerate(windows):
            value = read_window(window, arrays, array_refs)
            term = jnp.dot(value, turned_ref[s], preferred_element_type=F32)
            total = term if total is None else total + term
        total = total.T
        mine_ref[...] = jnp.where(first, total[:own], total[own:])
        other_ref[...] = jnp.where(first, total[own:], total[:own])

    shape = jax.ShapeDtypeStruct((own, half), F32)
    whole = pl.BlockSpec(kernel.shape, lambda i: (0, 0, 0, 0))
    return pl.pallas_call(
        body,
        grid=(steps,),
        out_shape=(shape, shape),
        in_specs=[SCALARS, whole, whole]
        + [pl.BlockSpec((step, rows), lambda i: (i, 0))] * len(arrays),
        out_specs=(pl.BlockSpec((own, step), lambda i: (0, i)),) * 2,
        scratch_shapes=[
            pltpu.VMEM((tiles, 2, shares, piece, columns), F32),
            pltpu.VMEM((len(windows), rows, columns), BF16),
        ],
        compiler_params=pltpu.CompilerParams(vmem_limit_bytes=12 * MIB),
        name="contract",
        cost_estimate=pl.CostEstimate(
            flops=2 * columns * half * rows * len(windows),
            bytes_accessed=2 * rows * len(windows) * half + 4 * columns * half,
            transcendentals=0,
        ),
    )(core[None], kernel, got, *arrays)


def unwritten(shape):
    def body(out_ref):
        pass

    return pl.pallas_call(
        body,
        out_shape=jax.ShapeDtypeStruct(shape, F32),
        out_specs=pl.BlockSpec(memory_space=pltpu.HBM),
        name="unwritten",
    )()


def finish(core, fits, ours, back, other, scale):
    own, half = ours.shape

    def body(flags_ref, ours_ref, back_ref, other_ref, out_ref, whole_ref, sem):
        @pl.when(flags_ref[1] != 0)
        def _():
            first = flags_ref[0] == 0
            whole_ref[:, :half] = jnp.where(first, ours_ref[...], back_ref[...]) * scale
            whole_ref[:, half:] = jnp.where(first, back_ref[...], ours_ref[...]) * scale
            copy = pltpu.make_async_copy(whole_ref, out_ref, sem)
            copy.start()
            copy.wait()

    return pl.pallas_call(
        body,
        out_shape=jax.ShapeDtypeStruct((own, 2 * half), F32),
        in_specs=[SCALARS, WHOLE, WHOLE, pl.BlockSpec(memory_space=pltpu.HBM)],
        out_specs=pl.BlockSpec(memory_space=pltpu.HBM),
        scratch_shapes=[pltpu.VMEM((own, 2 * half), F32), pltpu.SemaphoreType.DMA],
        input_output_aliases={3: 0},
        compiler_params=pltpu.CompilerParams(vmem_limit_bytes=8 * MIB),
        name="finish",
    )(jnp.stack((core, fits.astype(jnp.int32))), ours, back, other)


def per_device(orbital_values, occupied, trial, point_weights, batch_sizes, significant):
    rows, cols = orbital_values.shape
    batches = batch_sizes.shape[0]
    slots = rows // batches
    blocks = significant.shape[1]
    columns = occupied.shape[1]
    grid_count = lax.axis_size("grid")
    occ_count = lax.axis_size("occ")
    chips = grid_count // 2
    shares = 2 * occ_count
    half = cols // 2
    total = columns * grid_count
    place = lax.axis_index("grid")
    chip, core = place // 2, place % 2
    occ = lax.axis_index("occ")
    member = core * occ_count + occ

    def flip(x, axis, bit):
        count = lax.axis_size(axis)
        return lax.ppermute(x, axis, [(i, i ^ bit) for i in range(count)])

    def along(pairs):
        return [(2 * a + c, 2 * b + c) for a, b in pairs for c in range(2)]

    def doubled(x, axis, bit, dim):
        got = flip(x, axis, bit)
        mine = (lax.axis_index(axis) & bit) == 0
        return jnp.where(
            mine, jnp.concatenate((x, got), axis=dim), jnp.concatenate((got, x), axis=dim)
        )

    def halves(whole, axis):
        size = whole.shape[axis] // 2
        mine = lax.dynamic_slice_in_dim(whole, core * size, size, axis)
        return mine, lax.dynamic_slice_in_dim(whole, (1 - core) * size, size, axis)

    grid_bits = [1 << b for b in range(grid_count.bit_length() - 1)]
    occ_bits = [1 << b for b in range(occ_count.bit_length() - 1)]

    mine = half_of(orbital_values.T, core)
    got = flip(half_of(orbital_values.T, 1 - core), "grid", 1)
    mine_sig, other_sig = halves(significant.T, 0)
    got_sig = flip(other_sig, "grid", 1)

    told = jnp.concatenate(
        (
            doubled(batch_sizes[None], "grid", 1, 0).astype(F32).reshape(1, -1),
            doubled(point_weights[None], "grid", 1, 0).reshape(1, -1),
        ),
        axis=1,
    )
    if chips <= 4:
        heard = [told]
        for step in range(1, chips):
            around = [(i, (i + 2 * step) % grid_count) for i in range(grid_count)]
            heard.append(lax.ppermute(told, "grid", around))
        heard = jnp.concatenate(heard)
        behind = (chip - lax.iota(jnp.int32, chips)) % chips
        pick = behind[:, None, None] == lax.iota(jnp.int32, chips)[None, :, None]
        told = jnp.sum(jnp.where(pick, heard[None], 0.0), axis=1)
    else:
        for bit in grid_bits[1:]:
            told = doubled(told, "grid", bit, 0)
    sizes = told[:, : 2 * batches].astype(jnp.int32).reshape(-1)
    weights = told[:, 2 * batches :].reshape(-1)

    batch = lax.broadcasted_iota(jnp.int32, (sizes.shape[0], sizes.shape[0]), 0)
    before = lax.broadcasted_iota(jnp.int32, (sizes.shape[0], sizes.shape[0]), 1) < batch
    start = jnp.sum(jnp.where(before, sizes[None, :], 0), axis=1)
    position = lax.broadcasted_iota(jnp.int32, (sizes.shape[0], slots), 1)
    to = jnp.where(position < sizes[:, None], start[:, None] + position, -4 * rows * grid_count)
    to = to.reshape(grid_count, rows)
    first = start.reshape(chips, -1)[:, 0]
    margin = rows // 2 if (rows // 2) % (8 * shares) == 0 else rows
    nominal = rows * lax.iota(jnp.int32, chips)
    fits = jnp.all(jnp.abs(first - nominal) <= margin) & (jnp.sum(sizes) <= rows * chips)

    tile = margin
    piece = tile // shares
    base = rows * chip - margin
    mine_to = lax.dynamic_index_in_dim(to, place, 0, keepdims=False) - base
    got_to = lax.dynamic_index_in_dim(to, place ^ 1, 0, keepdims=False) - base
    odd = chip % 2
    for_b, *own_tiles, for_a = compact(
        mine,
        got,
        jnp.repeat(mine_sig.astype(BF16), slots, axis=1),
        jnp.repeat(got_sig.astype(BF16), slots, axis=1),
        mine_to[:, None],
        got_to[:, None],
        cols // blocks,
        tile,
        odd,
    )

    def sent(x, pairs):
        return lax.ppermute(x, "grid", along(pairs))

    last = chips - 1

    def over(links, t):
        pairs = []
        for a in range(links, last, 2):
            pairs += [(a, a + 1)] if a - t + 1 >= 0 else []
            pairs += [(a + 1, a)] if a + t <= last else []
        return pairs

    by_b = sent(for_b, over(1, 1))
    own = straighten(own_tiles, sent(for_a, over(0, 1)), by_b, odd)

    mine_panel, other_panel = panel_halves(occupied.T, trial.T, core)
    panels = stack_panels(mine_panel, flip(other_panel, "grid", 1), core)

    per_window = rows // tile
    window_iota = lax.iota(jnp.int32, chips)
    ends = [(0, 1), (last, last - 1)]
    homes = [(b, a) for a, b in ends]
    side = 1 - 2 * odd

    def valid(at):
        return jnp.where((at >= 0) & (at <= last), at, -1)

    stages = [[([own], chip)]]
    by_a = by_b = own
    far_panels = None
    for t in range(1, last):
        next_b = sent(by_a, over(1, t))
        by_a, by_b = sent(by_b, over(0, t)), next_b
        if t == 1:
            far_panels = sent(panels, ends)
        a_at, b_at = valid(chip + side * t), valid(chip - side * t)
        if 2 * t > last:
            stages.append([([by_a, by_b], jnp.maximum(a_at, b_at))])
        else:
            stages.append([([by_a], a_at), ([by_b], b_at)])

    direct = occ_count <= 4
    points = per_window * piece

    def halved(jobs):
        keep, give = project(jobs, tile, shares, core)
        return keep, flip(give, "grid", 1)

    def summed(pairs):
        if direct:
            parts = split_sum(pairs, occ)
            value = parts[0]
            for d in range(1, occ_count):
                value = value + flip(parts[d], "occ", d)
        else:
            value = jnp.concatenate([keep + got for keep, got in pairs])
            for bit in reversed(occ_bits):
                upper = (occ & bit) != 0
                low_part, high_part = value[:, :bit], value[:, bit:]
                got = flip(jnp.where(upper, low_part, high_part), "occ", bit)
                value = jnp.where(upper, high_part, low_part) + got
        return value.reshape(-1, points, 4 * columns)

    def shared_density(value, at):
        product = jnp.sum(value[:, :, : 2 * columns] * value[:, :, 2 * columns :], axis=2)
        here = (at[:, None] == window_iota[None, :])[:, :, None]
        return jnp.sum(jnp.where(here, product[:, None], 0.0), axis=0)

    early_jobs, late_jobs = sum(stages[1:-1], []), stages[-1]
    early_at = jnp.stack([at for _, at in early_jobs])
    late_at = late_jobs[0][1][None]
    early_jobs = stages[0] + early_jobs
    early_at = jnp.concatenate((chip[None], early_at))

    early_pair = halved([(panels, w) for w, _ in early_jobs])

    at = (
        (window_iota * rows)[:, None, None]
        + (lax.iota(jnp.int32, per_window) * tile)[None, :, None]
        + member * piece
        + lax.iota(jnp.int32, piece)[None, None, :]
    ).reshape(-1, 1)
    weight = jnp.sum(jnp.where(to.reshape(1, -1) == at, weights[None, :], 0.0), axis=1)
    weight = weight.reshape(chips, per_window * piece)
    outer = jnp.where(chip == 0, last, jnp.where(chip == last, 0, early_at[2]))
    places = jnp.concatenate((early_at[:2], outer[None], early_at[3:], late_at))
    here = (places[:, None] == window_iota[None, :])[:, :, None]
    weight_here = jnp.sum(jnp.where(here, weight[None], 0.0), axis=1)[:, :, None]

    late, by_a, early_pair, far_panels, weight_here, fits = lax.optimization_barrier(
        (by_b, by_a, early_pair, far_panels, weight_here, fits.astype(jnp.int32))
    )
    fits = fits != 0
    late = sent(late, homes)
    late_window = [by_a, by_b]
    late_jobs = [(panels, late_window), (far_panels, [by_b])]

    def kernel_of_all():
        value = summed([early_pair, halved(late_jobs)])
        density = shared_density(value, jnp.concatenate((early_at, late_at, late_at)))
        value, far_value = value[:-1], value[-1:]
        packed = jnp.concatenate(
            (far_value[0], jnp.pad(density, ((0, 0), (0, 4 * columns - points)))), axis=0
        )
        packed = flip(packed, "grid", 2)
        home_value, neighbour = packed[None, :points], packed[points:, :points]
        if chips <= 4:
            others = [flip(density, "grid", 2 * d) for d in range(2, chips)]
            density = density + neighbour + sum(others[1:], others[0])
        else:
            density = density + neighbour
            for bit in grid_bits[2:]:
                density = density + flip(density, "grid", bit)
        density = density * (1.0 / math.sqrt(total))

        values = jnp.concatenate((value[:2], value[2:3] + home_value, value[3:]))
        density_here = jnp.sum(jnp.where(here, density[None], 0.0), axis=1)[:, :, None]
        orbitals, response = values[:, :, : 2 * columns], values[:, :, 2 * columns :]
        kernel = (weight_here * (density_here * orbitals + response)).astype(BF16)
        kernel = kernel.reshape(-1, 1, piece, 2 * columns)
        if direct:
            parts = [kernel] + [flip(kernel, "occ", d) for d in range(1, occ_count)]
            kernel = in_order(parts, occ)
        else:
            for bit in occ_bits:
                kernel = doubled(kernel, "occ", bit, 1)
        return kernel, flip(kernel, "grid", 1)

    no_kernel = jnp.zeros((places.shape[0] * per_window, occ_count, piece, 2 * columns), BF16)
    kernel, got_kernel = lax.cond(fits, kernel_of_all, lambda: (no_kernel, no_kernel))
    early_windows = [w for w, _ in early_jobs]
    early_windows[2] = early_windows[2] + [late]
    windows = early_windows + [late_window]
    ours, theirs = contract(kernel, got_kernel, windows, core)
    back = flip(theirs, "grid", 1)
    scale = 1.0 / math.sqrt(rows * grid_count)
    other = lax.cond(
        fits,
        lambda *given: unwritten((columns, cols)),
        lambda *given: any_sizes(*given) * scale,
        orbital_values,
        occupied,
        trial,
        point_weights,
        batch_sizes,
        significant,
    )
    return finish(core, fits, ours, back, other, scale).T


def solution(mesh):
    placed = (
        P("grid", "occ"),
        P("occ", "grid"),
        P("occ", "grid"),
        P("grid"),
        P("grid"),
        P("grid", "occ"),
    )
    return jax.shard_map(
        per_device, mesh=mesh, in_specs=placed, out_specs=P("occ", "grid"), check_vma=False
    )
```

```python
import math

import jax
import jax.numpy as jnp
from jax import lax
from jax.experimental import pallas as pl
from jax.experimental.pallas import tpu as pltpu
from jax.sharding import PartitionSpec as P

BF16, F32 = jnp.bfloat16, jnp.float32
MIB = 1024 * 1024
WHOLE = pl.BlockSpec(memory_space=pltpu.VMEM)
SCALARS = pl.BlockSpec(memory_space=pltpu.SMEM)


def screen(values, sizes, significant):
    rows, cols = values.shape
    batches = sizes.shape[0]
    blocks = significant.shape[1]
    blocked = (
        values.reshape(batches, rows // batches, blocks, cols // blocks)
        * significant.astype(values.dtype)[:, None, :, None]
    )
    position = lax.broadcasted_iota(jnp.int32, (batches, rows // batches), 1)
    live = (position < sizes[:, None]).astype(jnp.float32).reshape(rows)
    return (blocked.reshape(rows, cols), live)


def any_sizes(orbital_values, occupied, trial, point_weights, batch_sizes, significant):
    screened, live = screen(orbital_values, batch_sizes, significant)
    rows, cols = screened.shape
    grid_count, occ_count = lax.axis_size("grid"), lax.axis_size("occ")
    columns = occupied.shape[1]
    me = lax.axis_index("grid")
    ring = [(i, (i + 1) % grid_count) for i in range(grid_count)]
    occ_ring = [(i, (i + 1) % occ_count) for i in range(occ_count)]

    def project_one(step, carry):
        panel, terms = carry
        term = jnp.dot(screened, panel, preferred_element_type=F32)
        terms = lax.dynamic_update_index_in_dim(terms, term, (me - step) % grid_count, 0)
        return lax.ppermute(panel, "grid", ring), terms

    joined = jnp.concatenate((occupied, trial), axis=1)
    terms = jnp.zeros((grid_count, rows, 2 * columns), F32)
    terms = lax.fori_loop(0, grid_count, project_one, (joined, terms))[1]

    def add_one(step, carry):
        moving, held = carry
        moving = lax.ppermute(moving, "occ", occ_ring)
        return moving, held + moving

    terms = lax.fori_loop(0, occ_count - 1, add_one, (terms, terms))[1]
    orbitals, response = terms[:, :, :columns], terms[:, :, columns:]
    density = jnp.sum(orbitals * response, axis=(0, 2)) * (1.0 / math.sqrt(columns * grid_count))
    weight = (point_weights * live)[None, :, None]
    kernel = (weight * (density[None, :, None] * orbitals + response)).astype(BF16)

    def contract_one(step, held):
        owner = (me + grid_count - 1 - step) % grid_count
        part = lax.dynamic_index_in_dim(kernel, owner, 0, keepdims=False)
        term = lax.dot_general(
            part, screened, (((0,), (0,)), ((), ())), preferred_element_type=F32
        )
        return lax.ppermute(held, "grid", ring) + term

    return lax.fori_loop(0, grid_count, contract_one, jnp.zeros((columns, cols), F32))


def half_of(whole, which):
    rows, columns = whole.shape
    half = rows // 2
    if half % 16:
        return lax.dynamic_slice_in_dim(whole, which * half, half, 0)

    def body(which_ref, whole_ref, out_ref, sem):
        first = pl.multiple_of(which_ref[0] * half, 16)
        copy = pltpu.make_async_copy(whole_ref.at[pl.ds(first, half)], out_ref, sem)
        copy.start()
        copy.wait()

    return pl.pallas_call(
        body,
        out_shape=jax.ShapeDtypeStruct((half, columns), whole.dtype),
        in_specs=[SCALARS, pl.BlockSpec(memory_space=pl.ANY)],
        out_specs=WHOLE,
        scratch_shapes=[pltpu.SemaphoreType.DMA],
        compiler_params=pltpu.CompilerParams(vmem_limit_bytes=4 * MIB),
        name="half_of",
    )(which[None], whole)


def compact(mine, got, mine_sig, got_sig, mine_to, got_to, width, tile, odd):
    half, rows = mine.shape
    blocks = mine_sig.shape[0]
    count = rows // tile + 2

    def body(odd_ref, mine_ref, got_ref, msig_ref, gsig_ref, mto_ref, gto_ref, *outs):
        block_of = lax.broadcasted_iota(jnp.int32, (half, blocks), 0)
        begin = lax.broadcasted_iota(jnp.int32, (half, blocks), 1) * width
        spread = ((block_of >= begin) & (block_of < begin + width)).astype(F32).astype(BF16)
        slot = lax.broadcasted_iota(jnp.int32, (rows, count * tile), 1)

        def part(value_ref, sig_ref, to_ref):
            kept = jnp.dot(spread, sig_ref[...], preferred_element_type=F32)
            screened = (value_ref[...].astype(F32) * kept).astype(BF16)
            place = (to_ref[...] == slot).astype(F32).astype(BF16)
            return jnp.dot(screened, place, preferred_element_type=F32)

        window = part(mine_ref, msig_ref, mto_ref) + part(got_ref, gsig_ref, gto_ref)
        for j in range(1, count - 1):
            outs[j][...] = window[:, j * tile : (j + 1) * tile].astype(BF16)
        first, last = window[:, :tile], window[:, (count - 1) * tile :]
        outs[0][...] = jnp.where(odd_ref[0] == 0, first, last).astype(BF16)
        outs[-1][...] = jnp.where(odd_ref[0] == 0, last, first).astype(BF16)

    shape = jax.ShapeDtypeStruct((half, tile), BF16)
    return pl.pallas_call(
        body,
        out_shape=(shape,) * count,
        in_specs=[SCALARS] + [WHOLE] * 6,
        out_specs=(WHOLE,) * count,
        compiler_params=pltpu.CompilerParams(vmem_limit_bytes=24 * MIB),
        name="compact",
        cost_estimate=pl.CostEstimate(
            flops=8 * half * rows * rows, bytes_accessed=8 * half * rows, transcendentals=0
        ),
    )(odd[None], mine, got, mine_sig, got_sig, mine_to, got_to)


def straighten(tiles, by_a, by_b, odd):
    half, tile = by_a.shape
    count = len(tiles)

    def body(odd_ref, *refs):
        tile_refs, a_ref, b_ref, out_ref = refs[:count], *refs[count:]
        even = odd_ref[0] == 0
        for j in range(count):
            value = tile_refs[j][...]
            if j == 0:
                value = value + jnp.where(even, b_ref[...], a_ref[...])
            if j == count - 1:
                value = value + jnp.where(even, a_ref[...], b_ref[...])
            out_ref[:, j * tile : (j + 1) * tile] = value

    return pl.pallas_call(
        body,
        out_shape=jax.ShapeDtypeStruct((half, count * tile), BF16),
        in_specs=[SCALARS] + [WHOLE] * (count + 2),
        out_specs=WHOLE,
        compiler_params=pltpu.CompilerParams(vmem_limit_bytes=8 * MIB),
        name="straighten",
    )(odd[None], *tiles, by_a, by_b)


def panel_halves(occupied, trial, core):
    columns, cols = occupied.shape
    half = cols // 2
    width = -(-half // 128) * 128

    def body(core_ref, occupied_ref, trial_ref, mine_ref, other_ref):
        first = core_ref[0] == 0
        mine_ref[...] = jnp.zeros_like(mine_ref)
        other_ref[...] = jnp.zeros_like(other_ref)
        for j, ref in enumerate((occupied_ref, trial_ref)):
            low, high = ref[:, :half], ref[:, half:]
            mine_ref[j * columns : (j + 1) * columns, :half] = jnp.where(first, low, high)
            other_ref[j * columns : (j + 1) * columns, :half] = jnp.where(first, high, low)

    shape = jax.ShapeDtypeStruct((2 * columns, width), BF16)
    return pl.pallas_call(
        body,
        out_shape=(shape, shape),
        in_specs=[SCALARS, WHOLE, WHOLE],
        out_specs=(WHOLE, WHOLE),
        compiler_params=pltpu.CompilerParams(vmem_limit_bytes=8 * MIB),
        name="panel_halves",
    )(core[None], occupied, trial)


def stack_panels(mine, got, core):
    both, width = mine.shape
    columns = both // 2

    def body(core_ref, mine_ref, got_ref, out_ref):
        first = core_ref[0] == 0
        for j in range(2):
            low = mine_ref[j * columns : (j + 1) * columns]
            high = got_ref[j * columns : (j + 1) * columns]
            q = 2 * j * columns
            out_ref[q : q + columns] = jnp.where(first, low, high)
            out_ref[q + columns : q + 2 * columns] = jnp.where(first, high, low)

    return pl.pallas_call(
        body,
        out_shape=jax.ShapeDtypeStruct((2 * both, width), BF16),
        in_specs=[SCALARS, WHOLE, WHOLE],
        out_specs=WHOLE,
        compiler_params=pltpu.CompilerParams(vmem_limit_bytes=8 * MIB),
        name="stack_panels",
    )(core[None], mine, got)


def distinct(arrays):
    return list({id(x): x for x in arrays}.values())


def read_window(addends, arrays, refs):
    ref_of = {id(x): ref for x, ref in zip(arrays, refs)}
    total = None
    for x in addends:
        value = ref_of[id(x)][...]
        total = value if total is None else total + value
    return total


def split_sum(pairs, occ):
    _, shares, piece, both = pairs[0][0].shape
    tiles = sum(keep.shape[0] for keep, _ in pairs)

    def body(occ_ref, *refs):
        ins, outs = refs[: 2 * len(pairs)], refs[2 * len(pairs) :]
        for d in range(shares):
            at = 0
            for keep_ref, got_ref in zip(ins[::2], ins[1::2]):
                for q in range(keep_ref.shape[0]):
                    outs[d][at] = keep_ref[q, occ_ref[0] ^ d] + got_ref[q, occ_ref[0] ^ d]
                    at += 1

    shape = jax.ShapeDtypeStruct((tiles, piece, both), F32)
    return pl.pallas_call(
        body,
        out_shape=(shape,) * shares,
        in_specs=[SCALARS] + [WHOLE] * (2 * len(pairs)),
        out_specs=(WHOLE,) * shares,
        compiler_params=pltpu.CompilerParams(vmem_limit_bytes=8 * MIB),
        name="split_sum",
    )(occ[None], *sum(pairs, ()))


def project(jobs, tile, shares, core):
    both = jobs[0][0].shape[0]
    half, rows = jobs[0][1][0].shape
    piece = tile // shares
    tiles = len(jobs) * rows // tile
    panels = distinct([p for p, _ in jobs])
    arrays = distinct([x for _, window in jobs for x in window])
    count = len(panels)

    def body(core_ref, *refs):
        panel_refs, array_refs = refs[:count], refs[count:-3]
        keep_ref, give_ref, terms_ref = refs[-3:]
        q = 0
        for panel, window in jobs:
            panel_ref = panel_refs[[id(p) for p in panels].index(id(panel))]
            value = read_window(window, arrays, array_refs)
            turned = jnp.dot(panel_ref[:, :half], value, preferred_element_type=F32).T
            for j in range(0, rows, tile):
                terms_ref[q] = turned[j : j + tile].reshape(2, shares // 2, piece, both)
                keep_ref[q] = terms_ref[q, core_ref[0]]
                give_ref[q] = terms_ref[q, 1 - core_ref[0]]
                q += 1

    shape = jax.ShapeDtypeStruct((tiles, shares // 2, piece, both), F32)
    return pl.pallas_call(
        body,
        out_shape=(shape, shape),
        in_specs=[SCALARS] + [WHOLE] * (count + len(arrays)),
        out_specs=(WHOLE, WHOLE),
        scratch_shapes=[pltpu.VMEM((tiles, 2, shares // 2, piece, both), F32)],
        compiler_params=pltpu.CompilerParams(vmem_limit_bytes=12 * MIB),
        name="project",
        cost_estimate=pl.CostEstimate(
            flops=2 * both * half * tiles * tile,
            bytes_accessed=2 * half * (both + tiles * tile) + 4 * tiles * tile * both,
            transcendentals=0,
        ),
    )(core[None], *panels, *arrays)


def in_order(parts, occ):
    tiles, _, piece, columns = parts[0].shape

    def body(occ_ref, *refs):
        for d in range(len(parts)):
            refs[-1][:, occ_ref[0] ^ d] = refs[d][:, 0]

    return pl.pallas_call(
        body,
        out_shape=jax.ShapeDtypeStruct((tiles, len(parts), piece, columns), parts[0].dtype),
        in_specs=[SCALARS] + [WHOLE] * len(parts),
        out_specs=WHOLE,
        compiler_params=pltpu.CompilerParams(vmem_limit_bytes=4 * MIB),
        name="in_order",
    )(occ[None], *parts)


def contract(kernel, got, windows, core):
    tiles, shares, piece, columns = kernel.shape
    half, rows = windows[0][0].shape
    own = columns // 2
    arrays = distinct([x for window in windows for x in window])
    per_window = tiles // len(windows)

    def body(core_ref, kernel_ref, got_ref, *refs):
        array_refs = refs[:-3]
        mine_ref, other_ref, order_ref = refs[-3:]
        first = core_ref[0] == 0
        order_ref[:, core_ref[0]] = kernel_ref[...].astype(F32)
        order_ref[:, 1 - core_ref[0]] = got_ref[...].astype(F32)
        total = None
        for s, window in enumerate(windows):
            part = order_ref[s * per_window : (s + 1) * per_window]
            part = part.reshape(rows, columns).astype(BF16)
            value = read_window(window, arrays, array_refs)
            term = jnp.dot(value, part, preferred_element_type=F32)
            total = term if total is None else total + term
        total = total.T
        mine_ref[...] = jnp.where(first, total[:own], total[own:])
        other_ref[...] = jnp.where(first, total[own:], total[:own])

    shape = jax.ShapeDtypeStruct((own, half), F32)
    return pl.pallas_call(
        body,
        out_shape=(shape, shape),
        in_specs=[SCALARS] + [WHOLE] * (2 + len(arrays)),
        out_specs=(WHOLE, WHOLE),
        scratch_shapes=[pltpu.VMEM((tiles, 2, shares, piece, columns), F32)],
        compiler_params=pltpu.CompilerParams(vmem_limit_bytes=20 * MIB),
        name="contract",
        cost_estimate=pl.CostEstimate(
            flops=2 * columns * half * rows * len(windows),
            bytes_accessed=2 * rows * len(windows) * half + 4 * columns * half,
            transcendentals=0,
        ),
    )(core[None], kernel, got, *arrays)


def unwritten(shape):
    def body(out_ref):
        pass

    return pl.pallas_call(
        body,
        out_shape=jax.ShapeDtypeStruct(shape, F32),
        out_specs=pl.BlockSpec(memory_space=pltpu.HBM),
        name="unwritten",
    )()


def finish(core, fits, ours, back, other, scale):
    own, half = ours.shape

    def body(flags_ref, ours_ref, back_ref, other_ref, out_ref, whole_ref, sem):
        @pl.when(flags_ref[1] != 0)
        def _():
            first = flags_ref[0] == 0
            whole_ref[:, :half] = jnp.where(first, ours_ref[...], back_ref[...]) * scale
            whole_ref[:, half:] = jnp.where(first, back_ref[...], ours_ref[...]) * scale
            copy = pltpu.make_async_copy(whole_ref, out_ref, sem)
            copy.start()
            copy.wait()

    return pl.pallas_call(
        body,
        out_shape=jax.ShapeDtypeStruct((own, 2 * half), F32),
        in_specs=[SCALARS, WHOLE, WHOLE, pl.BlockSpec(memory_space=pltpu.HBM)],
        out_specs=pl.BlockSpec(memory_space=pltpu.HBM),
        scratch_shapes=[pltpu.VMEM((own, 2 * half), F32), pltpu.SemaphoreType.DMA],
        input_output_aliases={3: 0},
        compiler_params=pltpu.CompilerParams(vmem_limit_bytes=8 * MIB),
        name="finish",
    )(jnp.stack((core, fits.astype(jnp.int32))), ours, back, other)


def per_device(orbital_values, occupied, trial, point_weights, batch_sizes, significant):
    rows, cols = orbital_values.shape
    batches = batch_sizes.shape[0]
    slots = rows // batches
    blocks = significant.shape[1]
    columns = occupied.shape[1]
    grid_count = lax.axis_size("grid")
    occ_count = lax.axis_size("occ")
    chips = grid_count // 2
    shares = 2 * occ_count
    half = cols // 2
    total = columns * grid_count
    place = lax.axis_index("grid")
    chip, core = place // 2, place % 2
    occ = lax.axis_index("occ")
    member = core * occ_count + occ

    def flip(x, axis, bit):
        count = lax.axis_size(axis)
        return lax.ppermute(x, axis, [(i, i ^ bit) for i in range(count)])

    def along(pairs):
        return [(2 * a + c, 2 * b + c) for a, b in pairs for c in range(2)]

    def doubled(x, axis, bit, dim):
        got = flip(x, axis, bit)
        mine = (lax.axis_index(axis) & bit) == 0
        return jnp.where(
            mine, jnp.concatenate((x, got), axis=dim), jnp.concatenate((got, x), axis=dim)
        )

    def halves(whole, axis):
        size = whole.shape[axis] // 2
        mine = lax.dynamic_slice_in_dim(whole, core * size, size, axis)
        return mine, lax.dynamic_slice_in_dim(whole, (1 - core) * size, size, axis)

    grid_bits = [1 << b for b in range(grid_count.bit_length() - 1)]
    occ_bits = [1 << b for b in range(occ_count.bit_length() - 1)]

    mine = half_of(orbital_values.T, core)
    got = flip(half_of(orbital_values.T, 1 - core), "grid", 1)
    mine_sig, other_sig = halves(significant.T, 0)
    got_sig = flip(other_sig, "grid", 1)

    told = jnp.concatenate(
        (
            doubled(batch_sizes[None], "grid", 1, 0).astype(F32).reshape(1, -1),
            doubled(point_weights[None], "grid", 1, 0).reshape(1, -1),
        ),
        axis=1,
    )
    if chips <= 4:
        heard = [told]
        for step in range(1, chips):
            around = [(i, (i + 2 * step) % grid_count) for i in range(grid_count)]
            heard.append(lax.ppermute(told, "grid", around))
        heard = jnp.concatenate(heard)
        behind = (chip - lax.iota(jnp.int32, chips)) % chips
        pick = behind[:, None, None] == lax.iota(jnp.int32, chips)[None, :, None]
        told = jnp.sum(jnp.where(pick, heard[None], 0.0), axis=1)
    else:
        for bit in grid_bits[1:]:
            told = doubled(told, "grid", bit, 0)
    sizes = told[:, : 2 * batches].astype(jnp.int32).reshape(-1)
    weights = told[:, 2 * batches :].reshape(-1)

    batch = lax.broadcasted_iota(jnp.int32, (sizes.shape[0], sizes.shape[0]), 0)
    before = lax.broadcasted_iota(jnp.int32, (sizes.shape[0], sizes.shape[0]), 1) < batch
    start = jnp.sum(jnp.where(before, sizes[None, :], 0), axis=1)
    position = lax.broadcasted_iota(jnp.int32, (sizes.shape[0], slots), 1)
    to = jnp.where(position < sizes[:, None], start[:, None] + position, -4 * rows * grid_count)
    to = to.reshape(grid_count, rows)
    first = start.reshape(chips, -1)[:, 0]
    margin = rows // 2 if (rows // 2) % (8 * shares) == 0 else rows
    nominal = rows * lax.iota(jnp.int32, chips)
    fits = jnp.all(jnp.abs(first - nominal) <= margin) & (jnp.sum(sizes) <= rows * chips)

    tile = margin
    piece = tile // shares
    base = rows * chip - margin
    mine_to = lax.dynamic_index_in_dim(to, place, 0, keepdims=False) - base
    got_to = lax.dynamic_index_in_dim(to, place ^ 1, 0, keepdims=False) - base
    odd = chip % 2
    for_b, *own_tiles, for_a = compact(
        mine,
        got,
        jnp.repeat(mine_sig.astype(BF16), slots, axis=1),
        jnp.repeat(got_sig.astype(BF16), slots, axis=1),
        mine_to[:, None],
        got_to[:, None],
        cols // blocks,
        tile,
        odd,
    )

    def sent(x, pairs):
        return lax.ppermute(x, "grid", along(pairs))

    last = chips - 1

    def over(links, t):
        pairs = []
        for a in range(links, last, 2):
            pairs += [(a, a + 1)] if a - t + 1 >= 0 else []
            pairs += [(a + 1, a)] if a + t <= last else []
        return pairs

    by_b = sent(for_b, over(1, 1))
    own = straighten(own_tiles, sent(for_a, over(0, 1)), by_b, odd)

    mine_panel, other_panel = panel_halves(occupied.T, trial.T, core)
    panels = stack_panels(mine_panel, flip(other_panel, "grid", 1), core)

    per_window = rows // tile
    window_iota = lax.iota(jnp.int32, chips)
    ends = [(0, 1), (last, last - 1)]
    homes = [(b, a) for a, b in ends]
    side = 1 - 2 * odd

    def valid(at):
        return jnp.where((at >= 0) & (at <= last), at, -1)

    stages = [[([own], chip)]]
    by_a = by_b = own
    far_panels = None
    for t in range(1, last):
        next_b = sent(by_a, over(1, t))
        by_a, by_b = sent(by_b, over(0, t)), next_b
        if t == 1:
            far_panels = sent(panels, ends)
        a_at, b_at = valid(chip + side * t), valid(chip - side * t)
        if 2 * t > last:
            stages.append([([by_a, by_b], jnp.maximum(a_at, b_at))])
        else:
            stages.append([([by_a], a_at), ([by_b], b_at)])

    direct = occ_count <= 4
    points = per_window * piece

    def halved(jobs):
        keep, give = project(jobs, tile, shares, core)
        return keep, flip(give, "grid", 1)

    def summed(pairs):
        if direct:
            parts = split_sum(pairs, occ)
            value = parts[0]
            for d in range(1, occ_count):
                value = value + flip(parts[d], "occ", d)
        else:
            value = jnp.concatenate([keep + got for keep, got in pairs])
            for bit in reversed(occ_bits):
                upper = (occ & bit) != 0
                low_part, high_part = value[:, :bit], value[:, bit:]
                got = flip(jnp.where(upper, low_part, high_part), "occ", bit)
                value = jnp.where(upper, high_part, low_part) + got
        return value.reshape(-1, points, 4 * columns)

    def shared_density(value, at):
        product = jnp.sum(value[:, :, : 2 * columns] * value[:, :, 2 * columns :], axis=2)
        here = (at[:, None] == window_iota[None, :])[:, :, None]
        return jnp.sum(jnp.where(here, product[:, None], 0.0), axis=0)

    early_jobs, late_jobs = sum(stages[1:-1], []), stages[-1]
    early_at = jnp.stack([at for _, at in early_jobs])
    late_at = late_jobs[0][1][None]
    own_job = stages[0][0]
    early_jobs = stages[0] + early_jobs
    early_at = jnp.concatenate((chip[None], early_at))

    early_value = summed(
        [halved([(panels, own_job[0])]), halved([(panels, w) for w, _ in early_jobs[1:]])]
    )
    early_density = shared_density(early_value, early_at)

    at = (
        (window_iota * rows)[:, None, None]
        + (lax.iota(jnp.int32, per_window) * tile)[None, :, None]
        + member * piece
        + lax.iota(jnp.int32, piece)[None, None, :]
    ).reshape(-1, 1)
    weight = jnp.sum(jnp.where(to.reshape(1, -1) == at, weights[None, :], 0.0), axis=1)
    weight = weight.reshape(chips, per_window * piece)
    outer = jnp.where(chip == 0, last, jnp.where(chip == last, 0, early_at[2]))
    places = jnp.concatenate((early_at[:2], outer[None], early_at[3:], late_at))
    here = (places[:, None] == window_iota[None, :])[:, :, None]
    weight_here = jnp.sum(jnp.where(here, weight[None], 0.0), axis=1)[:, :, None]

    late, by_a, early_value, early_density, far_panels, weight_here, fits = (
        lax.optimization_barrier(
            (
                by_b,
                by_a,
                early_value,
                early_density,
                far_panels,
                weight_here,
                fits.astype(jnp.int32),
            )
        )
    )
    fits = fits != 0
    late = sent(late, homes)
    late_window = [by_a, by_b]
    late_jobs = [(panels, late_window), (far_panels, [by_b])]

    def kernel_of_all():
        value = summed([halved(late_jobs)])
        density = early_density + shared_density(value, jnp.concatenate((late_at, late_at)))
        value, far_value = jnp.concatenate((early_value, value[:1])), value[1:]
        packed = jnp.concatenate(
            (far_value[0], jnp.pad(density, ((0, 0), (0, 4 * columns - points)))), axis=0
        )
        packed = flip(packed, "grid", 2)
        home_value, neighbour = packed[None, :points], packed[points:, :points]
        if chips <= 4:
            others = [flip(density, "grid", 2 * d) for d in range(2, chips)]
            density = density + neighbour + sum(others[1:], others[0])
        else:
            density = density + neighbour
            for bit in grid_bits[2:]:
                density = density + flip(density, "grid", bit)
        density = density * (1.0 / math.sqrt(total))

        values = jnp.concatenate((value[:2], value[2:3] + home_value, value[3:]))
        density_here = jnp.sum(jnp.where(here, density[None], 0.0), axis=1)[:, :, None]
        orbitals, response = values[:, :, : 2 * columns], values[:, :, 2 * columns :]
        kernel = (weight_here * (density_here * orbitals + response)).astype(BF16)
        kernel = kernel.reshape(-1, 1, piece, 2 * columns)
        if direct:
            parts = [kernel] + [flip(kernel, "occ", d) for d in range(1, occ_count)]
            kernel = in_order(parts, occ)
        else:
            for bit in occ_bits:
                kernel = doubled(kernel, "occ", bit, 1)
        return kernel, flip(kernel, "grid", 1), unwritten((columns, cols))

    scale = 1.0 / math.sqrt(rows * grid_count)

    def result_for_any_sizes():
        whole = any_sizes(
            orbital_values, occupied, trial, point_weights, batch_sizes, significant
        )
        none = jnp.zeros((places.shape[0] * per_window, occ_count, piece, 2 * columns), BF16)
        return none, none, whole * scale

    kernel, got_kernel, other = lax.cond(fits, kernel_of_all, result_for_any_sizes)
    early_windows = [w for w, _ in early_jobs]
    early_windows[2] = early_windows[2] + [late]
    windows = early_windows + [late_window]
    ours, theirs = contract(kernel, got_kernel, windows, core)
    back = flip(theirs, "grid", 1)
    return finish(core, fits, ours, back, other, scale).T


def solution(mesh):
    placed = (
        P("grid", "occ"),
        P("occ", "grid"),
        P("occ", "grid"),
        P("grid"),
        P("grid"),
        P("grid", "occ"),
    )
    return jax.shard_map(
        per_device, mesh=mesh, in_specs=placed, out_specs=P("occ", "grid"), check_vma=False
    )
```

```python
import math

import jax
import jax.numpy as jnp
from jax import lax
from jax.experimental import pallas as pl
from jax.experimental.pallas import tpu as pltpu
from jax.sharding import PartitionSpec as P

BF16, F32 = jnp.bfloat16, jnp.float32
MIB = 1024 * 1024
WHOLE = pl.BlockSpec(memory_space=pltpu.VMEM)
SCALARS = pl.BlockSpec(memory_space=pltpu.SMEM)


def screen(values, sizes, significant):
    rows, cols = values.shape
    batches = sizes.shape[0]
    blocks = significant.shape[1]
    blocked = (
        values.reshape(batches, rows // batches, blocks, cols // blocks)
        * significant.astype(values.dtype)[:, None, :, None]
    )
    position = lax.broadcasted_iota(jnp.int32, (batches, rows // batches), 1)
    live = (position < sizes[:, None]).astype(jnp.float32).reshape(rows)
    return (blocked.reshape(rows, cols), live)


def any_sizes(orbital_values, occupied, trial, point_weights, batch_sizes, significant):
    screened, live = screen(orbital_values, batch_sizes, significant)
    rows, cols = screened.shape
    grid_count, occ_count = lax.axis_size("grid"), lax.axis_size("occ")
    columns = occupied.shape[1]
    me = lax.axis_index("grid")
    ring = [(i, (i + 1) % grid_count) for i in range(grid_count)]
    occ_ring = [(i, (i + 1) % occ_count) for i in range(occ_count)]

    def project_one(step, carry):
        panel, terms = carry
        term = jnp.dot(screened, panel, preferred_element_type=F32)
        terms = lax.dynamic_update_index_in_dim(terms, term, (me - step) % grid_count, 0)
        return lax.ppermute(panel, "grid", ring), terms

    joined = jnp.concatenate((occupied, trial), axis=1)
    terms = jnp.zeros((grid_count, rows, 2 * columns), F32)
    terms = lax.fori_loop(0, grid_count, project_one, (joined, terms))[1]

    def add_one(step, carry):
        moving, held = carry
        moving = lax.ppermute(moving, "occ", occ_ring)
        return moving, held + moving

    terms = lax.fori_loop(0, occ_count - 1, add_one, (terms, terms))[1]
    orbitals, response = terms[:, :, :columns], terms[:, :, columns:]
    density = jnp.sum(orbitals * response, axis=(0, 2)) * (1.0 / math.sqrt(columns * grid_count))
    weight = (point_weights * live)[None, :, None]
    kernel = (weight * (density[None, :, None] * orbitals + response)).astype(BF16)

    def contract_one(step, held):
        owner = (me + grid_count - 1 - step) % grid_count
        part = lax.dynamic_index_in_dim(kernel, owner, 0, keepdims=False)
        term = lax.dot_general(
            part, screened, (((0,), (0,)), ((), ())), preferred_element_type=F32
        )
        return lax.ppermute(held, "grid", ring) + term

    return lax.fori_loop(0, grid_count, contract_one, jnp.zeros((columns, cols), F32))


def half_of(whole, which):
    rows, columns = whole.shape
    half = rows // 2
    if half % 16:
        return lax.dynamic_slice_in_dim(whole, which * half, half, 0)

    def body(which_ref, whole_ref, out_ref, sem):
        first = pl.multiple_of(which_ref[0] * half, 16)
        copy = pltpu.make_async_copy(whole_ref.at[pl.ds(first, half)], out_ref, sem)
        copy.start()
        copy.wait()

    return pl.pallas_call(
        body,
        out_shape=jax.ShapeDtypeStruct((half, columns), whole.dtype),
        in_specs=[SCALARS, pl.BlockSpec(memory_space=pl.ANY)],
        out_specs=WHOLE,
        scratch_shapes=[pltpu.SemaphoreType.DMA],
        compiler_params=pltpu.CompilerParams(vmem_limit_bytes=4 * MIB),
        name="half_of",
    )(which[None], whole)


def basis_cuts(half):
    cut = -(-half // 256) * 128
    return [(0, cut), (cut, half)]


def compact(mine, got, mine_sig, got_sig, mine_to, got_to, width, tile, odd):
    half, rows = mine.shape
    blocks = mine_sig.shape[0]
    count = rows // tile + 2
    cuts = basis_cuts(half)

    def body(odd_ref, mine_ref, got_ref, msig_ref, gsig_ref, mto_ref, gto_ref, *outs):
        block_of = lax.broadcasted_iota(jnp.int32, (half, blocks), 0)
        begin = lax.broadcasted_iota(jnp.int32, (half, blocks), 1) * width
        spread = ((block_of >= begin) & (block_of < begin + width)).astype(F32).astype(BF16)
        slot = lax.broadcasted_iota(jnp.int32, (rows, count * tile), 1)

        def part(value_ref, sig_ref, to_ref):
            kept = jnp.dot(spread, sig_ref[...], preferred_element_type=F32)
            screened = (value_ref[...].astype(F32) * kept).astype(BF16)
            place = (to_ref[...] == slot).astype(F32).astype(BF16)
            return jnp.dot(screened, place, preferred_element_type=F32)

        window = part(mine_ref, msig_ref, mto_ref) + part(got_ref, gsig_ref, gto_ref)
        tiles = [window[:, j * tile : (j + 1) * tile] for j in range(count)]
        even = odd_ref[0] == 0
        first, last = tiles[0], tiles[-1]
        tiles[0] = jnp.where(even, first, last)
        tiles[-1] = jnp.where(even, last, first)
        for p, (low, high) in enumerate(cuts):
            for j in range(count):
                outs[p * count + j][...] = tiles[j][low:high].astype(BF16)

    shapes = [
        jax.ShapeDtypeStruct((high - low, tile), BF16) for low, high in cuts for _ in range(count)
    ]
    out = pl.pallas_call(
        body,
        out_shape=shapes,
        in_specs=[SCALARS] + [WHOLE] * 6,
        out_specs=[WHOLE] * len(shapes),
        compiler_params=pltpu.CompilerParams(vmem_limit_bytes=24 * MIB),
        name="compact",
        cost_estimate=pl.CostEstimate(
            flops=8 * half * rows * rows, bytes_accessed=8 * half * rows, transcendentals=0
        ),
    )(odd[None], mine, got, mine_sig, got_sig, mine_to, got_to)
    return [out[p * count : (p + 1) * count] for p in range(len(cuts))]


def straighten(tiles, by_a, by_b, odd):
    half, tile = by_a.shape
    count = len(tiles)

    def body(odd_ref, *refs):
        tile_refs, a_ref, b_ref, out_ref = refs[:count], *refs[count:]
        even = odd_ref[0] == 0
        for j in range(count):
            value = tile_refs[j][...]
            if j == 0:
                value = value + jnp.where(even, b_ref[...], a_ref[...])
            if j == count - 1:
                value = value + jnp.where(even, a_ref[...], b_ref[...])
            out_ref[:, j * tile : (j + 1) * tile] = value

    return pl.pallas_call(
        body,
        out_shape=jax.ShapeDtypeStruct((half, count * tile), BF16),
        in_specs=[SCALARS] + [WHOLE] * (count + 2),
        out_specs=WHOLE,
        compiler_params=pltpu.CompilerParams(vmem_limit_bytes=8 * MIB),
        name="straighten",
    )(odd[None], *tiles, by_a, by_b)


def panel_halves(occupied, trial, core):
    columns, cols = occupied.shape
    half = cols // 2
    width = -(-half // 128) * 128

    def body(core_ref, occupied_ref, trial_ref, mine_ref, other_ref):
        first = core_ref[0] == 0
        mine_ref[...] = jnp.zeros_like(mine_ref)
        other_ref[...] = jnp.zeros_like(other_ref)
        for j, ref in enumerate((occupied_ref, trial_ref)):
            low, high = ref[:, :half], ref[:, half:]
            mine_ref[j * columns : (j + 1) * columns, :half] = jnp.where(first, low, high)
            other_ref[j * columns : (j + 1) * columns, :half] = jnp.where(first, high, low)

    shape = jax.ShapeDtypeStruct((2 * columns, width), BF16)
    return pl.pallas_call(
        body,
        out_shape=(shape, shape),
        in_specs=[SCALARS, WHOLE, WHOLE],
        out_specs=(WHOLE, WHOLE),
        compiler_params=pltpu.CompilerParams(vmem_limit_bytes=8 * MIB),
        name="panel_halves",
    )(core[None], occupied, trial)


def stack_panels(mine, got, core):
    both, width = mine.shape
    columns = both // 2

    def body(core_ref, mine_ref, got_ref, out_ref):
        first = core_ref[0] == 0
        for j in range(2):
            low = mine_ref[j * columns : (j + 1) * columns]
            high = got_ref[j * columns : (j + 1) * columns]
            q = 2 * j * columns
            out_ref[q : q + columns] = jnp.where(first, low, high)
            out_ref[q + columns : q + 2 * columns] = jnp.where(first, high, low)

    return pl.pallas_call(
        body,
        out_shape=jax.ShapeDtypeStruct((2 * both, width), BF16),
        in_specs=[SCALARS, WHOLE, WHOLE],
        out_specs=WHOLE,
        compiler_params=pltpu.CompilerParams(vmem_limit_bytes=8 * MIB),
        name="stack_panels",
    )(core[None], mine, got)


def distinct(arrays):
    return list({id(x): x for x in arrays}.values())


def read_window(addends, p, arrays, refs):
    ref_of = {id(x): ref for x, ref in zip(arrays, refs)}
    total = None
    for x in addends:
        value = ref_of[id(x[p])][...]
        total = value if total is None else total + value
    return total


def split_sum(pairs, occ):
    _, shares, piece, both = pairs[0][0].shape
    tiles = sum(keep.shape[0] for keep, _ in pairs)

    def body(occ_ref, *refs):
        ins, outs = refs[: 2 * len(pairs)], refs[2 * len(pairs) :]
        for d in range(shares):
            at = 0
            for keep_ref, got_ref in zip(ins[::2], ins[1::2]):
                for q in range(keep_ref.shape[0]):
                    outs[d][at] = keep_ref[q, occ_ref[0] ^ d] + got_ref[q, occ_ref[0] ^ d]
                    at += 1

    shape = jax.ShapeDtypeStruct((tiles, piece, both), F32)
    return pl.pallas_call(
        body,
        out_shape=(shape,) * shares,
        in_specs=[SCALARS] + [WHOLE] * (2 * len(pairs)),
        out_specs=(WHOLE,) * shares,
        compiler_params=pltpu.CompilerParams(vmem_limit_bytes=8 * MIB),
        name="split_sum",
    )(occ[None], *sum(pairs, ()))


def project(jobs, tile, shares, core):
    both = jobs[0][0].shape[0]
    parts = [x.shape[0] for x in jobs[0][1][0]]
    rows = jobs[0][1][0][0].shape[1]
    half = sum(parts)
    piece = tile // shares
    tiles = len(jobs) * rows // tile
    panels = distinct([p for p, _ in jobs])
    arrays = distinct([x for _, window in jobs for addend in window for x in addend])
    count = len(panels)

    def body(core_ref, *refs):
        panel_refs, array_refs = refs[:count], refs[count:-3]
        keep_ref, give_ref, terms_ref = refs[-3:]
        q = 0
        for panel, window in jobs:
            panel_ref = panel_refs[[id(p) for p in panels].index(id(panel))]
            total, low = None, 0
            for p, size in enumerate(parts):
                value = read_window(window, p, arrays, array_refs)
                term = jnp.dot(
                    panel_ref[:, low : low + size], value, preferred_element_type=F32
                )
                total = term if total is None else total + term
                low += size
            turned = total.T
            for j in range(0, rows, tile):
                terms_ref[q] = turned[j : j + tile].reshape(2, shares // 2, piece, both)
                keep_ref[q] = terms_ref[q, core_ref[0]]
                give_ref[q] = terms_ref[q, 1 - core_ref[0]]
                q += 1

    shape = jax.ShapeDtypeStruct((tiles, shares // 2, piece, both), F32)
    return pl.pallas_call(
        body,
        out_shape=(shape, shape),
        in_specs=[SCALARS] + [WHOLE] * (count + len(arrays)),
        out_specs=(WHOLE, WHOLE),
        scratch_shapes=[pltpu.VMEM((tiles, 2, shares // 2, piece, both), F32)],
        compiler_params=pltpu.CompilerParams(vmem_limit_bytes=12 * MIB),
        name="project",
        cost_estimate=pl.CostEstimate(
            flops=2 * both * half * tiles * tile,
            bytes_accessed=2 * half * (both + tiles * tile) + 4 * tiles * tile * both,
            transcendentals=0,
        ),
    )(core[None], *panels, *arrays)


def in_order(parts, occ):
    tiles, _, piece, columns = parts[0].shape

    def body(occ_ref, *refs):
        for d in range(len(parts)):
            refs[-1][:, occ_ref[0] ^ d] = refs[d][:, 0]

    return pl.pallas_call(
        body,
        out_shape=jax.ShapeDtypeStruct((tiles, len(parts), piece, columns), parts[0].dtype),
        in_specs=[SCALARS] + [WHOLE] * len(parts),
        out_specs=WHOLE,
        compiler_params=pltpu.CompilerParams(vmem_limit_bytes=4 * MIB),
        name="in_order",
    )(occ[None], *parts)


def contract(kernel, got, windows, core):
    tiles, shares, piece, columns = kernel.shape
    parts = [x.shape[0] for x in windows[0][0]]
    rows = windows[0][0][0].shape[1]
    half = sum(parts)
    own = columns // 2
    arrays = distinct([x for window in windows for addend in window for x in addend])
    per_window = tiles // len(windows)

    def body(core_ref, kernel_ref, got_ref, *refs):
        array_refs = refs[:-3]
        mine_ref, other_ref, order_ref = refs[-3:]
        first = core_ref[0] == 0
        order_ref[:, core_ref[0]] = kernel_ref[...].astype(F32)
        order_ref[:, 1 - core_ref[0]] = got_ref[...].astype(F32)
        kernels = [
            order_ref[s * per_window : (s + 1) * per_window].reshape(rows, columns).astype(BF16)
            for s in range(len(windows))
        ]
        low = 0
        for p, size in enumerate(parts):
            total = None
            for window, part in zip(windows, kernels):
                value = read_window(window, p, arrays, array_refs)
                term = jnp.dot(value, part, preferred_element_type=F32)
                total = term if total is None else total + term
            total = total.T
            mine_ref[:, low : low + size] = jnp.where(first, total[:own], total[own:])
            other_ref[:, low : low + size] = jnp.where(first, total[own:], total[:own])
            low += size

    shape = jax.ShapeDtypeStruct((own, half), F32)
    return pl.pallas_call(
        body,
        out_shape=(shape, shape),
        in_specs=[SCALARS] + [WHOLE] * (2 + len(arrays)),
        out_specs=(WHOLE, WHOLE),
        scratch_shapes=[pltpu.VMEM((tiles, 2, shares, piece, columns), F32)],
        compiler_params=pltpu.CompilerParams(vmem_limit_bytes=20 * MIB),
        name="contract",
        cost_estimate=pl.CostEstimate(
            flops=2 * columns * half * rows * len(windows),
            bytes_accessed=2 * rows * len(windows) * half + 4 * columns * half,
            transcendentals=0,
        ),
    )(core[None], kernel, got, *arrays)


def unwritten(shape):
    def body(out_ref):
        pass

    return pl.pallas_call(
        body,
        out_shape=jax.ShapeDtypeStruct(shape, F32),
        out_specs=pl.BlockSpec(memory_space=pltpu.HBM),
        name="unwritten",
    )()


def finish(core, fits, ours, back, other, scale):
    own, half = ours.shape

    def body(flags_ref, ours_ref, back_ref, other_ref, out_ref, whole_ref, sem):
        @pl.when(flags_ref[1] != 0)
        def _():
            first = flags_ref[0] == 0
            whole_ref[:, :half] = jnp.where(first, ours_ref[...], back_ref[...]) * scale
            whole_ref[:, half:] = jnp.where(first, back_ref[...], ours_ref[...]) * scale
            copy = pltpu.make_async_copy(whole_ref, out_ref, sem)
            copy.start()
            copy.wait()

    return pl.pallas_call(
        body,
        out_shape=jax.ShapeDtypeStruct((own, 2 * half), F32),
        in_specs=[SCALARS, WHOLE, WHOLE, pl.BlockSpec(memory_space=pltpu.HBM)],
        out_specs=pl.BlockSpec(memory_space=pltpu.HBM),
        scratch_shapes=[pltpu.VMEM((own, 2 * half), F32), pltpu.SemaphoreType.DMA],
        input_output_aliases={3: 0},
        compiler_params=pltpu.CompilerParams(vmem_limit_bytes=8 * MIB),
        name="finish",
    )(jnp.stack((core, fits.astype(jnp.int32))), ours, back, other)


def per_device(orbital_values, occupied, trial, point_weights, batch_sizes, significant):
    rows, cols = orbital_values.shape
    batches = batch_sizes.shape[0]
    slots = rows // batches
    blocks = significant.shape[1]
    columns = occupied.shape[1]
    grid_count = lax.axis_size("grid")
    occ_count = lax.axis_size("occ")
    chips = grid_count // 2
    shares = 2 * occ_count
    half = cols // 2
    total = columns * grid_count
    place = lax.axis_index("grid")
    chip, core = place // 2, place % 2
    occ = lax.axis_index("occ")
    member = core * occ_count + occ

    def flip(x, axis, bit):
        count = lax.axis_size(axis)
        return lax.ppermute(x, axis, [(i, i ^ bit) for i in range(count)])

    def along(pairs):
        return [(2 * a + c, 2 * b + c) for a, b in pairs for c in range(2)]

    def doubled(x, axis, bit, dim):
        got = flip(x, axis, bit)
        mine = (lax.axis_index(axis) & bit) == 0
        return jnp.where(
            mine, jnp.concatenate((x, got), axis=dim), jnp.concatenate((got, x), axis=dim)
        )

    def halves(whole, axis):
        size = whole.shape[axis] // 2
        mine = lax.dynamic_slice_in_dim(whole, core * size, size, axis)
        return mine, lax.dynamic_slice_in_dim(whole, (1 - core) * size, size, axis)

    grid_bits = [1 << b for b in range(grid_count.bit_length() - 1)]
    occ_bits = [1 << b for b in range(occ_count.bit_length() - 1)]

    mine = half_of(orbital_values.T, core)
    got = flip(half_of(orbital_values.T, 1 - core), "grid", 1)
    mine_sig, other_sig = halves(significant.T, 0)
    got_sig = flip(other_sig, "grid", 1)

    told = jnp.concatenate(
        (
            doubled(batch_sizes[None], "grid", 1, 0).astype(F32).reshape(1, -1),
            doubled(point_weights[None], "grid", 1, 0).reshape(1, -1),
        ),
        axis=1,
    )
    if chips <= 4:
        heard = [told]
        for step in range(1, chips):
            around = [(i, (i + 2 * step) % grid_count) for i in range(grid_count)]
            heard.append(lax.ppermute(told, "grid", around))
        heard = jnp.concatenate(heard)
        behind = (chip - lax.iota(jnp.int32, chips)) % chips
        pick = behind[:, None, None] == lax.iota(jnp.int32, chips)[None, :, None]
        told = jnp.sum(jnp.where(pick, heard[None], 0.0), axis=1)
    else:
        for bit in grid_bits[1:]:
            told = doubled(told, "grid", bit, 0)
    sizes = told[:, : 2 * batches].astype(jnp.int32).reshape(-1)
    weights = told[:, 2 * batches :].reshape(-1)

    batch = lax.broadcasted_iota(jnp.int32, (sizes.shape[0], sizes.shape[0]), 0)
    before = lax.broadcasted_iota(jnp.int32, (sizes.shape[0], sizes.shape[0]), 1) < batch
    start = jnp.sum(jnp.where(before, sizes[None, :], 0), axis=1)
    position = lax.broadcasted_iota(jnp.int32, (sizes.shape[0], slots), 1)
    to = jnp.where(position < sizes[:, None], start[:, None] + position, -4 * rows * grid_count)
    to = to.reshape(grid_count, rows)
    first = start.reshape(chips, -1)[:, 0]
    margin = rows // 2 if (rows // 2) % (8 * shares) == 0 else rows
    nominal = rows * lax.iota(jnp.int32, chips)
    fits = jnp.all(jnp.abs(first - nominal) <= margin) & (jnp.sum(sizes) <= rows * chips)

    tile = margin
    piece = tile // shares
    base = rows * chip - margin
    mine_to = lax.dynamic_index_in_dim(to, place, 0, keepdims=False) - base
    got_to = lax.dynamic_index_in_dim(to, place ^ 1, 0, keepdims=False) - base
    odd = chip % 2
    compacted = compact(
        mine,
        got,
        jnp.repeat(mine_sig.astype(BF16), slots, axis=1),
        jnp.repeat(got_sig.astype(BF16), slots, axis=1),
        mine_to[:, None],
        got_to[:, None],
        cols // blocks,
        tile,
        odd,
    )

    def sent(x, pairs):
        return lax.ppermute(x, "grid", along(pairs))

    last = chips - 1

    def over(links, t):
        pairs = []
        for a in range(links, last, 2):
            pairs += [(a, a + 1)] if a - t + 1 >= 0 else []
            pairs += [(a + 1, a)] if a + t <= last else []
        return pairs

    arrived = [
        (sent(for_b, over(1, 1)), sent(for_a, over(0, 1))) for for_b, *_, for_a in compacted
    ]
    own = tuple(
        straighten(tiles, by_a, by_b, odd)
        for (_, *tiles, _), (by_b, by_a) in zip(compacted, arrived)
    )

    _, occupied_turned, trial_turned = lax.optimization_barrier(
        (compacted[0][0], occupied.T, trial.T)
    )
    mine_panel, other_panel = panel_halves(occupied_turned, trial_turned, core)
    panels = stack_panels(mine_panel, flip(other_panel, "grid", 1), core)

    per_window = rows // tile
    window_iota = lax.iota(jnp.int32, chips)
    ends = [(0, 1), (last, last - 1)]
    homes = [(b, a) for a, b in ends]
    side = 1 - 2 * odd

    def valid(at):
        return jnp.where((at >= 0) & (at <= last), at, -1)

    stages = [[([own], chip)]]
    by_a = by_b = own
    far_panels = None
    for t in range(1, last):
        moved = [(sent(a, over(1, t)), sent(b, over(0, t))) for a, b in zip(by_a, by_b)]
        by_b, by_a = (tuple(x) for x in zip(*moved))
        if t == 1:
            _, far_panels = lax.optimization_barrier(((by_a[0], by_b[0]), panels))
            far_panels = sent(far_panels, ends)
        a_at, b_at = valid(chip + side * t), valid(chip - side * t)
        if 2 * t > last:
            stages.append([([by_a, by_b], jnp.maximum(a_at, b_at))])
        else:
            stages.append([([by_a], a_at), ([by_b], b_at)])

    direct = occ_count <= 4
    points = per_window * piece

    def summed(pairs):
        if direct:
            parts = split_sum(pairs, occ)
            value = parts[0]
            for d in range(1, occ_count):
                value = value + flip(parts[d], "occ", d)
        else:
            value = jnp.concatenate([keep + got for keep, got in pairs])
            for bit in reversed(occ_bits):
                upper = (occ & bit) != 0
                low_part, high_part = value[:, :bit], value[:, bit:]
                got = flip(jnp.where(upper, low_part, high_part), "occ", bit)
                value = jnp.where(upper, high_part, low_part) + got
        return value.reshape(-1, points, 4 * columns)

    def shared_density(value, at):
        product = jnp.sum(value[:, :, : 2 * columns] * value[:, :, 2 * columns :], axis=2)
        here = (at[:, None] == window_iota[None, :])[:, :, None]
        return jnp.sum(jnp.where(here, product[:, None], 0.0), axis=0)

    early_jobs, late_jobs = sum(stages[1:-1], []), stages[-1]
    early_at = jnp.stack([at for _, at in early_jobs])
    late_at = late_jobs[0][1][None]
    early_jobs = stages[0] + early_jobs
    early_at = jnp.concatenate((chip[None], early_at))

    early_pair = project([(panels, w) for w, _ in early_jobs], tile, shares, core)

    at = (
        (window_iota * rows)[:, None, None]
        + (lax.iota(jnp.int32, per_window) * tile)[None, :, None]
        + member * piece
        + lax.iota(jnp.int32, piece)[None, None, :]
    ).reshape(-1, 1)
    weight = jnp.sum(jnp.where(to.reshape(1, -1) == at, weights[None, :], 0.0), axis=1)
    weight = weight.reshape(chips, per_window * piece)
    outer = jnp.where(chip == 0, last, jnp.where(chip == last, 0, early_at[2]))
    places = jnp.concatenate((early_at[:2], outer[None], early_at[3:], late_at))
    here = (places[:, None] == window_iota[None, :])[:, :, None]
    weight_here = jnp.sum(jnp.where(here, weight[None], 0.0), axis=1)[:, :, None]

    late, by_a, early_pair, far_panels, weight_here, fits = lax.optimization_barrier(
        (by_b, by_a, early_pair, far_panels, weight_here, fits.astype(jnp.int32))
    )
    fits = fits != 0
    late = tuple(sent(x, homes) for x in late)
    late_window = [by_a, by_b]
    late_jobs = [(panels, late_window), (far_panels, [by_b])]

    def kernel_of_all():
        late_pair = project(late_jobs, tile, shares, core)
        value = summed([(keep, flip(give, "grid", 1)) for keep, give in (early_pair, late_pair)])
        density = shared_density(value, jnp.concatenate((early_at, late_at, late_at)))
        value, far_value = value[:-1], value[-1:]
        packed = jnp.concatenate(
            (far_value[0], jnp.pad(density, ((0, 0), (0, 4 * columns - points)))), axis=0
        )
        packed = flip(packed, "grid", 2)
        home_value, neighbour = packed[None, :points], packed[points:, :points]
        if chips <= 4:
            others = [flip(density, "grid", 2 * d) for d in range(2, chips)]
            density = density + neighbour + sum(others[1:], others[0])
        else:
            density = density + neighbour
            for bit in grid_bits[2:]:
                density = density + flip(density, "grid", bit)
        density = density * (1.0 / math.sqrt(total))

        values = jnp.concatenate((value[:2], value[2:3] + home_value, value[3:]))
        density_here = jnp.sum(jnp.where(here, density[None], 0.0), axis=1)[:, :, None]
        orbitals, response = values[:, :, : 2 * columns], values[:, :, 2 * columns :]
        kernel = (weight_here * (density_here * orbitals + response)).astype(BF16)
        kernel = kernel.reshape(-1, 1, piece, 2 * columns)
        if direct:
            parts = [kernel] + [flip(kernel, "occ", d) for d in range(1, occ_count)]
            kernel = in_order(parts, occ)
        else:
            for bit in occ_bits:
                kernel = doubled(kernel, "occ", bit, 1)
        return kernel, flip(kernel, "grid", 1), unwritten((columns, cols))

    scale = 1.0 / math.sqrt(rows * grid_count)

    def result_for_any_sizes():
        whole = any_sizes(
            orbital_values, occupied, trial, point_weights, batch_sizes, significant
        )
        none = jnp.zeros((places.shape[0] * per_window, occ_count, piece, 2 * columns), BF16)
        return none, none, whole * scale

    kernel, got_kernel, other = lax.cond(fits, kernel_of_all, result_for_any_sizes)
    early_windows = [w for w, _ in early_jobs]
    early_windows[2] = early_windows[2] + [late]
    windows = early_windows + [late_window]
    ours, theirs = contract(kernel, got_kernel, windows, core)
    back = flip(theirs, "grid", 1)
    return finish(core, fits, ours, back, other, scale).T


def solution(mesh):
    placed = (
        P("grid", "occ"),
        P("occ", "grid"),
        P("occ", "grid"),
        P("grid"),
        P("grid"),
        P("grid", "occ"),
    )
    return jax.shard_map(
        per_device, mesh=mesh, in_specs=placed, out_specs=P("occ", "grid"), check_vma=False
    )
```

```python
import math

import jax
import jax.numpy as jnp
from jax import lax
from jax.experimental import pallas as pl
from jax.experimental.pallas import tpu as pltpu
from jax.sharding import PartitionSpec as P

BF16, F32 = jnp.bfloat16, jnp.float32
MIB = 1024 * 1024
WHOLE = pl.BlockSpec(memory_space=pltpu.VMEM)
SCALARS = pl.BlockSpec(memory_space=pltpu.SMEM)


def screen(values, sizes, significant):
    rows, cols = values.shape
    batches = sizes.shape[0]
    blocks = significant.shape[1]
    blocked = (
        values.reshape(batches, rows // batches, blocks, cols // blocks)
        * significant.astype(values.dtype)[:, None, :, None]
    )
    position = lax.broadcasted_iota(jnp.int32, (batches, rows // batches), 1)
    live = (position < sizes[:, None]).astype(jnp.float32).reshape(rows)
    return (blocked.reshape(rows, cols), live)


def any_sizes(orbital_values, occupied, trial, point_weights, batch_sizes, significant):
    screened, live = screen(orbital_values, batch_sizes, significant)
    rows, cols = screened.shape
    grid_count, occ_count = lax.axis_size("grid"), lax.axis_size("occ")
    columns = occupied.shape[1]
    me = lax.axis_index("grid")
    ring = [(i, (i + 1) % grid_count) for i in range(grid_count)]
    occ_ring = [(i, (i + 1) % occ_count) for i in range(occ_count)]

    def project_one(step, carry):
        panel, terms = carry
        term = jnp.dot(screened, panel, preferred_element_type=F32)
        terms = lax.dynamic_update_index_in_dim(terms, term, (me - step) % grid_count, 0)
        return lax.ppermute(panel, "grid", ring), terms

    joined = jnp.concatenate((occupied, trial), axis=1)
    terms = jnp.zeros((grid_count, rows, 2 * columns), F32)
    terms = lax.fori_loop(0, grid_count, project_one, (joined, terms))[1]

    def add_one(step, carry):
        moving, held = carry
        moving = lax.ppermute(moving, "occ", occ_ring)
        return moving, held + moving

    terms = lax.fori_loop(0, occ_count - 1, add_one, (terms, terms))[1]
    orbitals, response = terms[:, :, :columns], terms[:, :, columns:]
    density = jnp.sum(orbitals * response, axis=(0, 2)) * (1.0 / math.sqrt(columns * grid_count))
    weight = (point_weights * live)[None, :, None]
    kernel = (weight * (density[None, :, None] * orbitals + response)).astype(BF16)

    def contract_one(step, held):
        owner = (me + grid_count - 1 - step) % grid_count
        part = lax.dynamic_index_in_dim(kernel, owner, 0, keepdims=False)
        term = lax.dot_general(
            part, screened, (((0,), (0,)), ((), ())), preferred_element_type=F32
        )
        return lax.ppermute(held, "grid", ring) + term

    return lax.fori_loop(0, grid_count, contract_one, jnp.zeros((columns, cols), F32))


def half_of(whole, which):
    rows, columns = whole.shape
    half = rows // 2
    if half % 16:
        return lax.dynamic_slice_in_dim(whole, which * half, half, 0)

    def body(which_ref, whole_ref, out_ref, sem):
        first = pl.multiple_of(which_ref[0] * half, 16)
        copy = pltpu.make_async_copy(whole_ref.at[pl.ds(first, half)], out_ref, sem)
        copy.start()
        copy.wait()

    return pl.pallas_call(
        body,
        out_shape=jax.ShapeDtypeStruct((half, columns), whole.dtype),
        in_specs=[SCALARS, pl.BlockSpec(memory_space=pl.ANY)],
        out_specs=WHOLE,
        scratch_shapes=[pltpu.SemaphoreType.DMA],
        compiler_params=pltpu.CompilerParams(vmem_limit_bytes=4 * MIB),
        name="half_of",
    )(which[None], whole)


def compact(mine, got, mine_sig, got_sig, mine_to, got_to, width, tile, odd):
    half, rows = mine.shape
    blocks = mine_sig.shape[0]
    count = rows // tile + 2
    cuts = [(0, half)]

    def body(odd_ref, mine_ref, got_ref, msig_ref, gsig_ref, mto_ref, gto_ref, *outs):
        block_of = lax.broadcasted_iota(jnp.int32, (half, blocks), 0)
        begin = lax.broadcasted_iota(jnp.int32, (half, blocks), 1) * width
        spread = ((block_of >= begin) & (block_of < begin + width)).astype(F32).astype(BF16)
        slot = lax.broadcasted_iota(jnp.int32, (rows, count * tile), 1)

        def part(value_ref, sig_ref, to_ref):
            kept = jnp.dot(spread, sig_ref[...], preferred_element_type=F32)
            screened = (value_ref[...].astype(F32) * kept).astype(BF16)
            place = (to_ref[...] == slot).astype(F32).astype(BF16)
            return jnp.dot(screened, place, preferred_element_type=F32)

        window = part(mine_ref, msig_ref, mto_ref) + part(got_ref, gsig_ref, gto_ref)
        tiles = [window[:, j * tile : (j + 1) * tile] for j in range(count)]
        even = odd_ref[0] == 0
        first, last = tiles[0], tiles[-1]
        tiles[0] = jnp.where(even, first, last)
        tiles[-1] = jnp.where(even, last, first)
        for p, (low, high) in enumerate(cuts):
            for j in range(count):
                outs[p * count + j][...] = tiles[j][low:high].astype(BF16)

    shapes = [
        jax.ShapeDtypeStruct((high - low, tile), BF16) for low, high in cuts for _ in range(count)
    ]
    out = pl.pallas_call(
        body,
        out_shape=shapes,
        in_specs=[SCALARS] + [WHOLE] * 6,
        out_specs=[WHOLE] * len(shapes),
        compiler_params=pltpu.CompilerParams(vmem_limit_bytes=24 * MIB),
        name="compact",
        cost_estimate=pl.CostEstimate(
            flops=8 * half * rows * rows, bytes_accessed=8 * half * rows, transcendentals=0
        ),
    )(odd[None], mine, got, mine_sig, got_sig, mine_to, got_to)
    return [out[p * count : (p + 1) * count] for p in range(len(cuts))]


def straighten(tiles, by_b, by_a, odd):
    half, tile = by_a.shape
    count = len(tiles)

    def body(odd_ref, *refs):
        tile_refs, b_ref, a_ref, out_ref = refs[:count], *refs[count:]
        even = odd_ref[0] == 0
        for j in range(count):
            value = tile_refs[j][...]
            if j == 0:
                value = value + jnp.where(even, b_ref[...], a_ref[...])
            if j == count - 1:
                value = value + jnp.where(even, a_ref[...], b_ref[...])
            out_ref[:, j * tile : (j + 1) * tile] = value

    return pl.pallas_call(
        body,
        out_shape=jax.ShapeDtypeStruct((half, count * tile), BF16),
        in_specs=[SCALARS] + [WHOLE] * (count + 2),
        out_specs=WHOLE,
        compiler_params=pltpu.CompilerParams(vmem_limit_bytes=8 * MIB),
        name="straighten",
    )(odd[None], *tiles, by_b, by_a)


def panel_halves(occupied, trial, core):
    columns, cols = occupied.shape
    half = cols // 2
    width = -(-half // 128) * 128

    def body(core_ref, occupied_ref, trial_ref, mine_ref, other_ref):
        first = core_ref[0] == 0
        mine_ref[...] = jnp.zeros_like(mine_ref)
        other_ref[...] = jnp.zeros_like(other_ref)
        for j, ref in enumerate((occupied_ref, trial_ref)):
            low, high = ref[:, :half], ref[:, half:]
            mine_ref[j * columns : (j + 1) * columns, :half] = jnp.where(first, low, high)
            other_ref[j * columns : (j + 1) * columns, :half] = jnp.where(first, high, low)

    shape = jax.ShapeDtypeStruct((2 * columns, width), BF16)
    return pl.pallas_call(
        body,
        out_shape=(shape, shape),
        in_specs=[SCALARS, WHOLE, WHOLE],
        out_specs=(WHOLE, WHOLE),
        compiler_params=pltpu.CompilerParams(vmem_limit_bytes=8 * MIB),
        name="panel_halves",
    )(core[None], occupied, trial)


def stack_panels(mine, got, core):
    both, width = mine.shape
    columns = both // 2

    def body(core_ref, mine_ref, got_ref, out_ref):
        first = core_ref[0] == 0
        for j in range(2):
            low = mine_ref[j * columns : (j + 1) * columns]
            high = got_ref[j * columns : (j + 1) * columns]
            q = 2 * j * columns
            out_ref[q : q + columns] = jnp.where(first, low, high)
            out_ref[q + columns : q + 2 * columns] = jnp.where(first, high, low)

    return pl.pallas_call(
        body,
        out_shape=jax.ShapeDtypeStruct((2 * both, width), BF16),
        in_specs=[SCALARS, WHOLE, WHOLE],
        out_specs=WHOLE,
        compiler_params=pltpu.CompilerParams(vmem_limit_bytes=8 * MIB),
        name="stack_panels",
    )(core[None], mine, got)


def distinct(arrays):
    return list({id(x): x for x in arrays}.values())


def read_window(addends, p, arrays, refs):
    ref_of = {id(x): ref for x, ref in zip(arrays, refs)}
    total = None
    for x in addends:
        value = ref_of[id(x[p])][...]
        total = value if total is None else total + value
    return total


def split_sum(pairs, occ):
    _, shares, piece, both = pairs[0][0].shape
    tiles = sum(keep.shape[0] for keep, _ in pairs)

    def body(occ_ref, *refs):
        ins, outs = refs[: 2 * len(pairs)], refs[2 * len(pairs) :]
        for d in range(shares):
            at = 0
            for keep_ref, got_ref in zip(ins[::2], ins[1::2]):
                for q in range(keep_ref.shape[0]):
                    outs[d][at] = keep_ref[q, occ_ref[0] ^ d] + got_ref[q, occ_ref[0] ^ d]
                    at += 1

    shape = jax.ShapeDtypeStruct((tiles, piece, both), F32)
    return pl.pallas_call(
        body,
        out_shape=(shape,) * shares,
        in_specs=[SCALARS] + [WHOLE] * (2 * len(pairs)),
        out_specs=(WHOLE,) * shares,
        compiler_params=pltpu.CompilerParams(vmem_limit_bytes=8 * MIB),
        name="split_sum",
    )(occ[None], *sum(pairs, ()))


def project(jobs, tile, shares, core):
    both = jobs[0][0].shape[0]
    parts = [x.shape[0] for x in jobs[0][1][0]]
    rows = jobs[0][1][0][0].shape[1]
    half = sum(parts)
    piece = tile // shares
    tiles = len(jobs) * rows // tile
    panels = distinct([p for p, _ in jobs])
    arrays = distinct([x for _, window in jobs for addend in window for x in addend])
    count = len(panels)

    def body(core_ref, *refs):
        panel_refs, array_refs = refs[:count], refs[count:-3]
        keep_ref, give_ref, terms_ref = refs[-3:]
        q = 0
        for panel, window in jobs:
            panel_ref = panel_refs[[id(p) for p in panels].index(id(panel))]
            total, low = None, 0
            for p, size in enumerate(parts):
                value = read_window(window, p, arrays, array_refs)
                term = jnp.dot(
                    panel_ref[:, low : low + size], value, preferred_element_type=F32
                )
                total = term if total is None else total + term
                low += size
            turned = total.T
            for j in range(0, rows, tile):
                terms_ref[q] = turned[j : j + tile].reshape(2, shares // 2, piece, both)
                keep_ref[q] = terms_ref[q, core_ref[0]]
                give_ref[q] = terms_ref[q, 1 - core_ref[0]]
                q += 1

    shape = jax.ShapeDtypeStruct((tiles, shares // 2, piece, both), F32)
    return pl.pallas_call(
        body,
        out_shape=(shape, shape),
        in_specs=[SCALARS] + [WHOLE] * (count + len(arrays)),
        out_specs=(WHOLE, WHOLE),
        scratch_shapes=[pltpu.VMEM((tiles, 2, shares // 2, piece, both), F32)],
        compiler_params=pltpu.CompilerParams(vmem_limit_bytes=12 * MIB),
        name="project",
        cost_estimate=pl.CostEstimate(
            flops=2 * both * half * tiles * tile,
            bytes_accessed=2 * half * (both + tiles * tile) + 4 * tiles * tile * both,
            transcendentals=0,
        ),
    )(core[None], *panels, *arrays)


def in_order(parts, occ):
    tiles, _, piece, columns = parts[0].shape

    def body(occ_ref, *refs):
        for d in range(len(parts)):
            refs[-1][:, occ_ref[0] ^ d] = refs[d][:, 0]

    return pl.pallas_call(
        body,
        out_shape=jax.ShapeDtypeStruct((tiles, len(parts), piece, columns), parts[0].dtype),
        in_specs=[SCALARS] + [WHOLE] * len(parts),
        out_specs=WHOLE,
        compiler_params=pltpu.CompilerParams(vmem_limit_bytes=4 * MIB),
        name="in_order",
    )(occ[None], *parts)


def contract(kernel, got, windows, core):
    tiles, shares, piece, columns = kernel.shape
    parts = [x.shape[0] for x in windows[0][0]]
    rows = windows[0][0][0].shape[1]
    half = sum(parts)
    own = columns // 2
    arrays = distinct([x for window in windows for addend in window for x in addend])
    per_window = tiles // len(windows)

    def body(core_ref, kernel_ref, got_ref, *refs):
        array_refs = refs[:-3]
        mine_ref, other_ref, order_ref = refs[-3:]
        first = core_ref[0] == 0
        order_ref[:, core_ref[0]] = kernel_ref[...].astype(F32)
        order_ref[:, 1 - core_ref[0]] = got_ref[...].astype(F32)
        kernels = [
            order_ref[s * per_window : (s + 1) * per_window].reshape(rows, columns).astype(BF16)
            for s in range(len(windows))
        ]
        low = 0
        for p, size in enumerate(parts):
            total = None
            for window, part in zip(windows, kernels):
                value = read_window(window, p, arrays, array_refs)
                term = jnp.dot(value, part, preferred_element_type=F32)
                total = term if total is None else total + term
            total = total.T
            mine_ref[:, low : low + size] = jnp.where(first, total[:own], total[own:])
            other_ref[:, low : low + size] = jnp.where(first, total[own:], total[:own])
            low += size

    shape = jax.ShapeDtypeStruct((own, half), F32)
    return pl.pallas_call(
        body,
        out_shape=(shape, shape),
        in_specs=[SCALARS] + [WHOLE] * (2 + len(arrays)),
        out_specs=(WHOLE, WHOLE),
        scratch_shapes=[pltpu.VMEM((tiles, 2, shares, piece, columns), F32)],
        compiler_params=pltpu.CompilerParams(vmem_limit_bytes=20 * MIB),
        name="contract",
        cost_estimate=pl.CostEstimate(
            flops=2 * columns * half * rows * len(windows),
            bytes_accessed=2 * rows * len(windows) * half + 4 * columns * half,
            transcendentals=0,
        ),
    )(core[None], kernel, got, *arrays)


def unwritten(shape):
    def body(out_ref):
        pass

    return pl.pallas_call(
        body,
        out_shape=jax.ShapeDtypeStruct(shape, F32),
        out_specs=pl.BlockSpec(memory_space=pltpu.HBM),
        name="unwritten",
    )()


def finish(core, fits, ours, back, other, scale):
    own, half = ours.shape

    def body(flags_ref, ours_ref, back_ref, other_ref, out_ref, whole_ref, sem):
        @pl.when(flags_ref[1] != 0)
        def _():
            first = flags_ref[0] == 0
            whole_ref[:, :half] = jnp.where(first, ours_ref[...], back_ref[...]) * scale
            whole_ref[:, half:] = jnp.where(first, back_ref[...], ours_ref[...]) * scale
            copy = pltpu.make_async_copy(whole_ref, out_ref, sem)
            copy.start()
            copy.wait()

    return pl.pallas_call(
        body,
        out_shape=jax.ShapeDtypeStruct((own, 2 * half), F32),
        in_specs=[SCALARS, WHOLE, WHOLE, pl.BlockSpec(memory_space=pltpu.HBM)],
        out_specs=pl.BlockSpec(memory_space=pltpu.HBM),
        scratch_shapes=[pltpu.VMEM((own, 2 * half), F32), pltpu.SemaphoreType.DMA],
        input_output_aliases={3: 0},
        compiler_params=pltpu.CompilerParams(vmem_limit_bytes=8 * MIB),
        name="finish",
    )(jnp.stack((core, fits.astype(jnp.int32))), ours, back, other)


def per_device(orbital_values, occupied, trial, point_weights, batch_sizes, significant):
    rows, cols = orbital_values.shape
    batches = batch_sizes.shape[0]
    slots = rows // batches
    blocks = significant.shape[1]
    columns = occupied.shape[1]
    grid_count = lax.axis_size("grid")
    occ_count = lax.axis_size("occ")
    chips = grid_count // 2
    shares = 2 * occ_count
    half = cols // 2
    total = columns * grid_count
    place = lax.axis_index("grid")
    chip, core = place // 2, place % 2
    occ = lax.axis_index("occ")
    member = core * occ_count + occ

    def flip(x, axis, bit):
        count = lax.axis_size(axis)
        return lax.ppermute(x, axis, [(i, i ^ bit) for i in range(count)])

    def along(pairs):
        return [(2 * a + c, 2 * b + c) for a, b in pairs for c in range(2)]

    def doubled(x, axis, bit, dim):
        got = flip(x, axis, bit)
        mine = (lax.axis_index(axis) & bit) == 0
        return jnp.where(
            mine, jnp.concatenate((x, got), axis=dim), jnp.concatenate((got, x), axis=dim)
        )

    def halves(whole, axis):
        size = whole.shape[axis] // 2
        mine = lax.dynamic_slice_in_dim(whole, core * size, size, axis)
        return mine, lax.dynamic_slice_in_dim(whole, (1 - core) * size, size, axis)

    grid_bits = [1 << b for b in range(grid_count.bit_length() - 1)]
    occ_bits = [1 << b for b in range(occ_count.bit_length() - 1)]

    mine = half_of(orbital_values.T, core)
    got = flip(half_of(orbital_values.T, 1 - core), "grid", 1)
    mine_sig, other_sig = halves(significant.T, 0)
    got_sig = flip(other_sig, "grid", 1)

    told = jnp.concatenate(
        (
            doubled(batch_sizes[None], "grid", 1, 0).astype(F32).reshape(1, -1),
            doubled(point_weights[None], "grid", 1, 0).reshape(1, -1),
        ),
        axis=1,
    )
    live = rows * chips
    for bit in grid_bits[1:2]:
        told = doubled(told, "grid", bit, 0)
    if chips > 4:
        for bit in grid_bits[2:]:
            told = doubled(told, "grid", bit, 0)

    def places_of(sizes, first):
        count = sizes.shape[0]
        batch = lax.broadcasted_iota(jnp.int32, (count, count), 0)
        before = lax.broadcasted_iota(jnp.int32, (count, count), 1) < batch
        start = first + jnp.sum(jnp.where(before, sizes[None, :], 0), axis=1)
        position = lax.broadcasted_iota(jnp.int32, (count, slots), 1)
        to = jnp.where(position < sizes[:, None], start[:, None] + position, -4 * live)
        return to.reshape(-1, rows), start

    sizes = told[:, : 2 * batches].astype(jnp.int32).reshape(-1)
    first = jnp.where((chip >= 2) & (chips <= 4), live - jnp.sum(sizes), 0)
    near_to, _ = places_of(sizes, first)
    near_place = place if chips > 4 else place % 4
    for bit in grid_bits[2:] if chips <= 4 else []:
        told = doubled(told, "grid", bit, 0)
    margin = rows // 2 if (rows // 2) % (8 * shares) == 0 else rows
    tile = margin
    piece = tile // shares
    base = rows * chip - margin
    mine_to = lax.dynamic_index_in_dim(near_to, near_place, 0, keepdims=False) - base
    got_to = lax.dynamic_index_in_dim(near_to, near_place ^ 1, 0, keepdims=False) - base
    odd = chip % 2
    compacted = compact(
        mine,
        got,
        jnp.repeat(mine_sig.astype(BF16), slots, axis=1),
        jnp.repeat(got_sig.astype(BF16), slots, axis=1),
        mine_to[:, None],
        got_to[:, None],
        cols // blocks,
        tile,
        odd,
    )

    def sent(x, pairs):
        return lax.ppermute(x, "grid", along(pairs))

    last = chips - 1

    def over(links, t):
        pairs = []
        for a in range(links, last, 2):
            pairs += [(a, a + 1)] if a - t + 1 >= 0 else []
            pairs += [(a + 1, a)] if a + t <= last else []
        return pairs

    arrived = [
        (sent(for_b, over(1, 1)), sent(for_a, over(0, 1))) for for_b, *_, for_a in compacted
    ]
    own = tuple(
        straighten(tiles, by_b, by_a, odd)
        for (_, *tiles, _), (by_b, by_a) in zip(compacted, arrived)
    )

    own, told = lax.optimization_barrier((own, told))
    sizes = told[:, : 2 * batches].astype(jnp.int32).reshape(-1)
    weights = told[:, 2 * batches :].reshape(-1)
    to, start = places_of(sizes, 0)
    first = start.reshape(chips, -1)[:, 0]
    nominal = rows * lax.iota(jnp.int32, chips)
    fits = jnp.all(jnp.abs(first - nominal) <= margin) & (jnp.sum(sizes) == live)

    _, occupied_turned, trial_turned = lax.optimization_barrier(
        (compacted[0][0], occupied.T, trial.T)
    )
    mine_panel, other_panel = panel_halves(occupied_turned, trial_turned, core)
    panels = stack_panels(mine_panel, flip(other_panel, "grid", 1), core)

    per_window = rows // tile
    window_iota = lax.iota(jnp.int32, chips)
    ends = [(0, 1), (last, last - 1)]
    homes = [(b, a) for a, b in ends]
    side = 1 - 2 * odd

    def valid(at):
        return jnp.where((at >= 0) & (at <= last), at, -1)

    stages = [[([own], chip)]]
    by_a = by_b = own
    far_panels = None
    for t in range(1, last):
        moved = [(sent(a, over(1, t)), sent(b, over(0, t))) for a, b in zip(by_a, by_b)]
        by_b, by_a = (tuple(x) for x in zip(*moved))
        if t == 1:
            far_panels = sent(panels, ends)
        a_at, b_at = valid(chip + side * t), valid(chip - side * t)
        if 2 * t > last:
            stages.append([([by_a, by_b], jnp.maximum(a_at, b_at))])
        else:
            stages.append([([by_a], a_at), ([by_b], b_at)])

    direct = occ_count <= 4
    points = per_window * piece

    def summed(pairs):
        if direct:
            parts = split_sum(pairs, occ)
            value = parts[0]
            for d in range(1, occ_count):
                value = value + flip(parts[d], "occ", d)
        else:
            value = jnp.concatenate([keep + got for keep, got in pairs])
            for bit in reversed(occ_bits):
                upper = (occ & bit) != 0
                low_part, high_part = value[:, :bit], value[:, bit:]
                got = flip(jnp.where(upper, low_part, high_part), "occ", bit)
                value = jnp.where(upper, high_part, low_part) + got
        return value.reshape(-1, points, 4 * columns)

    def shared_density(value, at):
        product = jnp.sum(value[:, :, : 2 * columns] * value[:, :, 2 * columns :], axis=2)
        here = (at[:, None] == window_iota[None, :])[:, :, None]
        return jnp.sum(jnp.where(here, product[:, None], 0.0), axis=0)

    early_jobs, late_jobs = sum(stages[1:-1], []), stages[-1]
    early_at = jnp.stack([at for _, at in early_jobs])
    late_at = late_jobs[0][1][None]
    early_jobs = stages[0] + early_jobs
    early_at = jnp.concatenate((chip[None], early_at))

    early_pair = project([(panels, w) for w, _ in early_jobs], tile, shares, core)

    at = (
        (window_iota * rows)[:, None, None]
        + (lax.iota(jnp.int32, per_window) * tile)[None, :, None]
        + member * piece
        + lax.iota(jnp.int32, piece)[None, None, :]
    ).reshape(-1, 1)
    weight = jnp.sum(jnp.where(to.reshape(1, -1) == at, weights[None, :], 0.0), axis=1)
    weight = weight.reshape(chips, per_window * piece)
    outer = jnp.where(chip == 0, last, jnp.where(chip == last, 0, early_at[2]))
    places = jnp.concatenate((early_at[:2], outer[None], early_at[3:], late_at))
    here = (places[:, None] == window_iota[None, :])[:, :, None]
    weight_here = jnp.sum(jnp.where(here, weight[None], 0.0), axis=1)[:, :, None]

    late, by_a, early_pair, far_panels, weight_here, fits = lax.optimization_barrier(
        (by_b, by_a, early_pair, far_panels, weight_here, fits.astype(jnp.int32))
    )
    fits = fits != 0
    late = tuple(sent(x, homes) for x in late)
    late_window = [by_a, by_b]
    late_jobs = [(panels, late_window), (far_panels, [by_b])]

    def kernel_of_all():
        late_pair = project(late_jobs, tile, shares, core)
        value = summed([(keep, flip(give, "grid", 1)) for keep, give in (early_pair, late_pair)])
        density = shared_density(value, jnp.concatenate((early_at, late_at, late_at)))
        value, far_value = value[:-1], value[-1:]
        packed = jnp.concatenate(
            (far_value[0], jnp.pad(density, ((0, 0), (0, 4 * columns - points)))), axis=0
        )
        packed = flip(packed, "grid", 2)
        home_value, neighbour = packed[None, :points], packed[points:, :points]
        if chips <= 4:
            others = [flip(density, "grid", 2 * d) for d in range(2, chips)]
            density = density + neighbour + sum(others[1:], others[0])
        else:
            density = density + neighbour
            for bit in grid_bits[2:]:
                density = density + flip(density, "grid", bit)
        density = density * (1.0 / math.sqrt(total))

        values = jnp.concatenate((value[:2], value[2:3] + home_value, value[3:]))
        density_here = jnp.sum(jnp.where(here, density[None], 0.0), axis=1)[:, :, None]
        orbitals, response = values[:, :, : 2 * columns], values[:, :, 2 * columns :]
        kernel = (weight_here * (density_here * orbitals + response)).astype(BF16)
        kernel = kernel.reshape(-1, 1, piece, 2 * columns)
        if direct:
            parts = [kernel] + [flip(kernel, "occ", d) for d in range(1, occ_count)]
            kernel = in_order(parts, occ)
        else:
            for bit in occ_bits:
                kernel = doubled(kernel, "occ", bit, 1)
        return kernel, flip(kernel, "grid", 1), unwritten((columns, cols))

    scale = 1.0 / math.sqrt(rows * grid_count)

    def result_for_any_sizes():
        whole = any_sizes(
            orbital_values, occupied, trial, point_weights, batch_sizes, significant
        )
        none = jnp.zeros((places.shape[0] * per_window, occ_count, piece, 2 * columns), BF16)
        return none, none, whole * scale

    kernel, got_kernel, other = lax.cond(fits, kernel_of_all, result_for_any_sizes)
    early_windows = [w for w, _ in early_jobs]
    early_windows[2] = early_windows[2] + [late]
    windows = early_windows + [late_window]
    ours, theirs = contract(kernel, got_kernel, windows, core)
    back = flip(theirs, "grid", 1)
    return finish(core, fits, ours, back, other, scale).T


def solution(mesh):
    placed = (
        P("grid", "occ"),
        P("occ", "grid"),
        P("occ", "grid"),
        P("grid"),
        P("grid"),
        P("grid", "occ"),
    )
    return jax.shard_map(
        per_device, mesh=mesh, in_specs=placed, out_specs=P("occ", "grid"), check_vma=False
    )
```

```python
import math

import jax
import jax.numpy as jnp
from jax import lax
from jax.experimental import pallas as pl
from jax.experimental.pallas import tpu as pltpu
from jax.sharding import PartitionSpec as P

BF16, F32 = jnp.bfloat16, jnp.float32
MIB = 1024 * 1024
WHOLE = pl.BlockSpec(memory_space=pltpu.VMEM)
SCALARS = pl.BlockSpec(memory_space=pltpu.SMEM)


def screen(values, sizes, significant):
    rows, cols = values.shape
    batches = sizes.shape[0]
    blocks = significant.shape[1]
    blocked = (
        values.reshape(batches, rows // batches, blocks, cols // blocks)
        * significant.astype(values.dtype)[:, None, :, None]
    )
    position = lax.broadcasted_iota(jnp.int32, (batches, rows // batches), 1)
    live = (position < sizes[:, None]).astype(jnp.float32).reshape(rows)
    return (blocked.reshape(rows, cols), live)


def any_sizes(orbital_values, occupied, trial, point_weights, batch_sizes, significant):
    screened, live = screen(orbital_values, batch_sizes, significant)
    rows, cols = screened.shape
    grid_count, occ_count = lax.axis_size("grid"), lax.axis_size("occ")
    columns = occupied.shape[1]
    me = lax.axis_index("grid")
    ring = [(i, (i + 1) % grid_count) for i in range(grid_count)]
    occ_ring = [(i, (i + 1) % occ_count) for i in range(occ_count)]

    def project_one(step, carry):
        panel, terms = carry
        term = jnp.dot(screened, panel, preferred_element_type=F32)
        terms = lax.dynamic_update_index_in_dim(terms, term, (me - step) % grid_count, 0)
        return lax.ppermute(panel, "grid", ring), terms

    joined = jnp.concatenate((occupied, trial), axis=1)
    terms = jnp.zeros((grid_count, rows, 2 * columns), F32)
    terms = lax.fori_loop(0, grid_count, project_one, (joined, terms))[1]

    def add_one(step, carry):
        moving, held = carry
        moving = lax.ppermute(moving, "occ", occ_ring)
        return moving, held + moving

    terms = lax.fori_loop(0, occ_count - 1, add_one, (terms, terms))[1]
    orbitals, response = terms[:, :, :columns], terms[:, :, columns:]
    density = jnp.sum(orbitals * response, axis=(0, 2)) * (1.0 / math.sqrt(columns * grid_count))
    weight = (point_weights * live)[None, :, None]
    kernel = (weight * (density[None, :, None] * orbitals + response)).astype(BF16)

    def contract_one(step, held):
        owner = (me + grid_count - 1 - step) % grid_count
        part = lax.dynamic_index_in_dim(kernel, owner, 0, keepdims=False)
        term = lax.dot_general(
            part, screened, (((0,), (0,)), ((), ())), preferred_element_type=F32
        )
        return lax.ppermute(held, "grid", ring) + term

    return lax.fori_loop(0, grid_count, contract_one, jnp.zeros((columns, cols), F32))


def half_of(whole, which):
    rows, columns = whole.shape
    half = rows // 2
    if half % 16:
        return lax.dynamic_slice_in_dim(whole, which * half, half, 0)

    def body(which_ref, whole_ref, out_ref, sem):
        first = pl.multiple_of(which_ref[0] * half, 16)
        copy = pltpu.make_async_copy(whole_ref.at[pl.ds(first, half)], out_ref, sem)
        copy.start()
        copy.wait()

    return pl.pallas_call(
        body,
        out_shape=jax.ShapeDtypeStruct((half, columns), whole.dtype),
        in_specs=[SCALARS, pl.BlockSpec(memory_space=pl.ANY)],
        out_specs=WHOLE,
        scratch_shapes=[pltpu.SemaphoreType.DMA],
        compiler_params=pltpu.CompilerParams(vmem_limit_bytes=4 * MIB),
        name="half_of",
    )(which[None], whole)


def compact(mine, got, mine_sig, got_sig, mine_to, got_to, width, tile, odd):
    half, rows = mine.shape
    blocks = mine_sig.shape[0]
    count = rows // tile + 2
    cuts = [(0, half)]

    def body(odd_ref, mine_ref, got_ref, msig_ref, gsig_ref, mto_ref, gto_ref, *outs):
        block_of = lax.broadcasted_iota(jnp.int32, (half, blocks), 0)
        begin = lax.broadcasted_iota(jnp.int32, (half, blocks), 1) * width
        spread = ((block_of >= begin) & (block_of < begin + width)).astype(F32).astype(BF16)
        slot = lax.broadcasted_iota(jnp.int32, (rows, count * tile), 1)

        def part(value_ref, sig_ref, to_ref):
            kept = jnp.dot(spread, sig_ref[...], preferred_element_type=F32)
            screened = (value_ref[...].astype(F32) * kept).astype(BF16)
            place = (to_ref[...] == slot).astype(F32).astype(BF16)
            return jnp.dot(screened, place, preferred_element_type=F32)

        window = part(mine_ref, msig_ref, mto_ref) + part(got_ref, gsig_ref, gto_ref)
        tiles = [window[:, j * tile : (j + 1) * tile] for j in range(count)]
        even = odd_ref[0] == 0
        first, last = tiles[0], tiles[-1]
        tiles[0] = jnp.where(even, first, last)
        tiles[-1] = jnp.where(even, last, first)
        for p, (low, high) in enumerate(cuts):
            for j in range(count):
                outs[p * count + j][...] = tiles[j][low:high].astype(BF16)

    shapes = [
        jax.ShapeDtypeStruct((high - low, tile), BF16) for low, high in cuts for _ in range(count)
    ]
    out = pl.pallas_call(
        body,
        out_shape=shapes,
        in_specs=[SCALARS] + [WHOLE] * 6,
        out_specs=[WHOLE] * len(shapes),
        compiler_params=pltpu.CompilerParams(vmem_limit_bytes=16 * MIB),
        name="compact",
        cost_estimate=pl.CostEstimate(
            flops=8 * half * rows * rows, bytes_accessed=8 * half * rows, transcendentals=0
        ),
    )(odd[None], mine, got, mine_sig, got_sig, mine_to, got_to)
    return [out[p * count : (p + 1) * count] for p in range(len(cuts))]


def straighten(tiles, by_b, by_a, odd):
    half, tile = by_a.shape
    count = len(tiles)

    def body(odd_ref, *refs):
        tile_refs, b_ref, a_ref, out_ref = refs[:count], *refs[count:]
        even = odd_ref[0] == 0
        for j in range(count):
            value = tile_refs[j][...]
            if j == 0:
                value = value + jnp.where(even, b_ref[...], a_ref[...])
            if j == count - 1:
                value = value + jnp.where(even, a_ref[...], b_ref[...])
            out_ref[:, j * tile : (j + 1) * tile] = value

    return pl.pallas_call(
        body,
        out_shape=jax.ShapeDtypeStruct((half, count * tile), BF16),
        in_specs=[SCALARS] + [WHOLE] * (count + 2),
        out_specs=WHOLE,
        compiler_params=pltpu.CompilerParams(vmem_limit_bytes=8 * MIB),
        name="straighten",
    )(odd[None], *tiles, by_b, by_a)


def panel_halves(occupied, trial, core):
    columns, cols = occupied.shape
    half = cols // 2
    width = -(-half // 128) * 128

    def body(core_ref, occupied_ref, trial_ref, mine_ref, other_ref):
        first = core_ref[0] == 0
        mine_ref[...] = jnp.zeros_like(mine_ref)
        other_ref[...] = jnp.zeros_like(other_ref)
        for j, ref in enumerate((occupied_ref, trial_ref)):
            low, high = ref[:, :half], ref[:, half:]
            mine_ref[j * columns : (j + 1) * columns, :half] = jnp.where(first, low, high)
            other_ref[j * columns : (j + 1) * columns, :half] = jnp.where(first, high, low)

    shape = jax.ShapeDtypeStruct((2 * columns, width), BF16)
    return pl.pallas_call(
        body,
        out_shape=(shape, shape),
        in_specs=[SCALARS, WHOLE, WHOLE],
        out_specs=(WHOLE, WHOLE),
        compiler_params=pltpu.CompilerParams(vmem_limit_bytes=8 * MIB),
        name="panel_halves",
    )(core[None], occupied, trial)


def stack_panels(mine, got, core):
    both, width = mine.shape
    columns = both // 2

    def body(core_ref, mine_ref, got_ref, out_ref):
        first = core_ref[0] == 0
        for j in range(2):
            low = mine_ref[j * columns : (j + 1) * columns]
            high = got_ref[j * columns : (j + 1) * columns]
            q = 2 * j * columns
            out_ref[q : q + columns] = jnp.where(first, low, high)
            out_ref[q + columns : q + 2 * columns] = jnp.where(first, high, low)

    return pl.pallas_call(
        body,
        out_shape=jax.ShapeDtypeStruct((2 * both, width), BF16),
        in_specs=[SCALARS, WHOLE, WHOLE],
        out_specs=WHOLE,
        compiler_params=pltpu.CompilerParams(vmem_limit_bytes=8 * MIB),
        name="stack_panels",
    )(core[None], mine, got)


def distinct(arrays):
    return list({id(x): x for x in arrays}.values())


def read_window(addends, p, arrays, refs):
    ref_of = {id(x): ref for x, ref in zip(arrays, refs)}
    total = None
    for x in addends:
        value = ref_of[id(x[p])][...]
        total = value if total is None else total + value
    return total


def split_sum(pairs, occ):
    _, shares, piece, both = pairs[0][0].shape
    tiles = sum(keep.shape[0] for keep, _ in pairs)

    def body(occ_ref, *refs):
        ins, outs = refs[: 2 * len(pairs)], refs[2 * len(pairs) :]
        for d in range(shares):
            at = 0
            for keep_ref, got_ref in zip(ins[::2], ins[1::2]):
                for q in range(keep_ref.shape[0]):
                    outs[d][at] = keep_ref[q, occ_ref[0] ^ d] + got_ref[q, occ_ref[0] ^ d]
                    at += 1

    shape = jax.ShapeDtypeStruct((tiles, piece, both), F32)
    return pl.pallas_call(
        body,
        out_shape=(shape,) * shares,
        in_specs=[SCALARS] + [WHOLE] * (2 * len(pairs)),
        out_specs=(WHOLE,) * shares,
        compiler_params=pltpu.CompilerParams(vmem_limit_bytes=8 * MIB),
        name="split_sum",
    )(occ[None], *sum(pairs, ()))


def project(jobs, tile, shares, core):
    both = jobs[0][0].shape[0]
    parts = [x.shape[0] for x in jobs[0][1][0]]
    rows = jobs[0][1][0][0].shape[1]
    half = sum(parts)
    piece = tile // shares
    tiles = len(jobs) * rows // tile
    panels = distinct([p for p, _ in jobs])
    arrays = distinct([x for _, window in jobs for addend in window for x in addend])
    count = len(panels)

    def body(core_ref, *refs):
        panel_refs, array_refs = refs[:count], refs[count:-3]
        keep_ref, give_ref, terms_ref = refs[-3:]
        q = 0
        for panel, window in jobs:
            panel_ref = panel_refs[[id(p) for p in panels].index(id(panel))]
            total, low = None, 0
            for p, size in enumerate(parts):
                value = read_window(window, p, arrays, array_refs)
                term = jnp.dot(
                    panel_ref[:, low : low + size], value, preferred_element_type=F32
                )
                total = term if total is None else total + term
                low += size
            turned = total.T
            for j in range(0, rows, tile):
                terms_ref[q] = turned[j : j + tile].reshape(2, shares // 2, piece, both)
                keep_ref[q] = terms_ref[q, core_ref[0]]
                give_ref[q] = terms_ref[q, 1 - core_ref[0]]
                q += 1

    shape = jax.ShapeDtypeStruct((tiles, shares // 2, piece, both), F32)
    return pl.pallas_call(
        body,
        out_shape=(shape, shape),
        in_specs=[SCALARS] + [WHOLE] * (count + len(arrays)),
        out_specs=(WHOLE, WHOLE),
        scratch_shapes=[pltpu.VMEM((tiles, 2, shares // 2, piece, both), F32)],
        compiler_params=pltpu.CompilerParams(vmem_limit_bytes=12 * MIB),
        name="project",
        cost_estimate=pl.CostEstimate(
            flops=2 * both * half * tiles * tile,
            bytes_accessed=2 * half * (both + tiles * tile) + 4 * tiles * tile * both,
            transcendentals=0,
        ),
    )(core[None], *panels, *arrays)


def in_order(parts, occ):
    tiles, _, piece, columns = parts[0].shape

    def body(occ_ref, *refs):
        for d in range(len(parts)):
            refs[-1][:, occ_ref[0] ^ d] = refs[d][:, 0]

    return pl.pallas_call(
        body,
        out_shape=jax.ShapeDtypeStruct((tiles, len(parts), piece, columns), parts[0].dtype),
        in_specs=[SCALARS] + [WHOLE] * len(parts),
        out_specs=WHOLE,
        compiler_params=pltpu.CompilerParams(vmem_limit_bytes=4 * MIB),
        name="in_order",
    )(occ[None], *parts)


def contract(kernel, got, windows, core):
    tiles, shares, piece, columns = kernel.shape
    parts = [x.shape[0] for x in windows[0][0]]
    rows = windows[0][0][0].shape[1]
    half = sum(parts)
    own = columns // 2
    arrays = distinct([x for window in windows for addend in window for x in addend])
    per_window = tiles // len(windows)

    def body(core_ref, kernel_ref, got_ref, *refs):
        array_refs = refs[:-3]
        mine_ref, other_ref, order_ref = refs[-3:]
        first = core_ref[0] == 0
        order_ref[:, core_ref[0]] = kernel_ref[...].astype(F32)
        order_ref[:, 1 - core_ref[0]] = got_ref[...].astype(F32)
        kernels = [
            order_ref[s * per_window : (s + 1) * per_window].reshape(rows, columns).astype(BF16)
            for s in range(len(windows))
        ]
        low = 0
        for p, size in enumerate(parts):
            total = None
            for window, part in zip(windows, kernels):
                value = read_window(window, p, arrays, array_refs)
                term = jnp.dot(value, part, preferred_element_type=F32)
                total = term if total is None else total + term
            total = total.T
            mine_ref[:, low : low + size] = jnp.where(first, total[:own], total[own:])
            other_ref[:, low : low + size] = jnp.where(first, total[own:], total[:own])
            low += size

    shape = jax.ShapeDtypeStruct((own, half), F32)
    return pl.pallas_call(
        body,
        out_shape=(shape, shape),
        in_specs=[SCALARS] + [WHOLE] * (2 + len(arrays)),
        out_specs=(WHOLE, WHOLE),
        scratch_shapes=[pltpu.VMEM((tiles, 2, shares, piece, columns), F32)],
        compiler_params=pltpu.CompilerParams(vmem_limit_bytes=20 * MIB),
        name="contract",
        cost_estimate=pl.CostEstimate(
            flops=2 * columns * half * rows * len(windows),
            bytes_accessed=2 * rows * len(windows) * half + 4 * columns * half,
            transcendentals=0,
        ),
    )(core[None], kernel, got, *arrays)


def unwritten(shape):
    def body(out_ref):
        pass

    return pl.pallas_call(
        body,
        out_shape=jax.ShapeDtypeStruct(shape, F32),
        out_specs=pl.BlockSpec(memory_space=pltpu.HBM),
        name="unwritten",
    )()


def finish(core, fits, ours, back, other, scale):
    own, half = ours.shape

    def body(flags_ref, ours_ref, back_ref, other_ref, out_ref, whole_ref, sem):
        @pl.when(flags_ref[1] != 0)
        def _():
            first = flags_ref[0] == 0
            whole_ref[:, :half] = jnp.where(first, ours_ref[...], back_ref[...]) * scale
            whole_ref[:, half:] = jnp.where(first, back_ref[...], ours_ref[...]) * scale
            copy = pltpu.make_async_copy(whole_ref, out_ref, sem)
            copy.start()
            copy.wait()

    return pl.pallas_call(
        body,
        out_shape=jax.ShapeDtypeStruct((own, 2 * half), F32),
        in_specs=[SCALARS, WHOLE, WHOLE, pl.BlockSpec(memory_space=pltpu.HBM)],
        out_specs=pl.BlockSpec(memory_space=pltpu.HBM),
        scratch_shapes=[pltpu.VMEM((own, 2 * half), F32), pltpu.SemaphoreType.DMA],
        input_output_aliases={3: 0},
        compiler_params=pltpu.CompilerParams(vmem_limit_bytes=8 * MIB),
        name="finish",
    )(jnp.stack((core, fits.astype(jnp.int32))), ours, back, other)


def per_device(orbital_values, occupied, trial, point_weights, batch_sizes, significant):
    rows, cols = orbital_values.shape
    batches = batch_sizes.shape[0]
    slots = rows // batches
    blocks = significant.shape[1]
    columns = occupied.shape[1]
    grid_count = lax.axis_size("grid")
    occ_count = lax.axis_size("occ")
    chips = grid_count // 2
    shares = 2 * occ_count
    half = cols // 2
    total = columns * grid_count
    place = lax.axis_index("grid")
    chip, core = place // 2, place % 2
    occ = lax.axis_index("occ")
    member = core * occ_count + occ

    def flip(x, axis, bit):
        count = lax.axis_size(axis)
        return lax.ppermute(x, axis, [(i, i ^ bit) for i in range(count)])

    def along(pairs):
        return [(2 * a + c, 2 * b + c) for a, b in pairs for c in range(2)]

    def doubled(x, axis, bit, dim):
        got = flip(x, axis, bit)
        mine = (lax.axis_index(axis) & bit) == 0
        return jnp.where(
            mine, jnp.concatenate((x, got), axis=dim), jnp.concatenate((got, x), axis=dim)
        )

    def halves(whole, axis):
        size = whole.shape[axis] // 2
        mine = lax.dynamic_slice_in_dim(whole, core * size, size, axis)
        return mine, lax.dynamic_slice_in_dim(whole, (1 - core) * size, size, axis)

    grid_bits = [1 << b for b in range(grid_count.bit_length() - 1)]
    occ_bits = [1 << b for b in range(occ_count.bit_length() - 1)]

    mine = half_of(orbital_values.T, core)
    got = flip(half_of(orbital_values.T, 1 - core), "grid", 1)
    mine_sig, other_sig = halves(significant.T, 0)
    got_sig = flip(other_sig, "grid", 1)

    told = jnp.concatenate(
        (
            doubled(batch_sizes[None], "grid", 1, 0).astype(F32).reshape(1, -1),
            doubled(point_weights[None], "grid", 1, 0).reshape(1, -1),
        ),
        axis=1,
    )
    live = rows * chips
    for bit in grid_bits[1:2]:
        told = doubled(told, "grid", bit, 0)
    if chips > 4:
        for bit in grid_bits[2:]:
            told = doubled(told, "grid", bit, 0)

    def places_of(sizes, first):
        count = sizes.shape[0]
        batch = lax.broadcasted_iota(jnp.int32, (count, count), 0)
        before = lax.broadcasted_iota(jnp.int32, (count, count), 1) < batch
        start = first + jnp.sum(jnp.where(before, sizes[None, :], 0), axis=1)
        position = lax.broadcasted_iota(jnp.int32, (count, slots), 1)
        to = jnp.where(position < sizes[:, None], start[:, None] + position, -4 * live)
        return to.reshape(-1, rows), start

    sizes = told[:, : 2 * batches].astype(jnp.int32).reshape(-1)
    first = jnp.where((chip >= 2) & (chips <= 4), live - jnp.sum(sizes), 0)
    near_to, _ = places_of(sizes, first)
    near_place = place if chips > 4 else place % 4
    for bit in grid_bits[2:] if chips <= 4 else []:
        told = doubled(told, "grid", bit, 0)
    margin = rows // 2 if (rows // 2) % (8 * shares) == 0 else rows
    tile = margin
    piece = tile // shares
    base = rows * chip - margin
    mine_to = lax.dynamic_index_in_dim(near_to, near_place, 0, keepdims=False) - base
    got_to = lax.dynamic_index_in_dim(near_to, near_place ^ 1, 0, keepdims=False) - base
    odd = chip % 2
    compacted = compact(
        mine,
        got,
        jnp.repeat(mine_sig.astype(BF16), slots, axis=1),
        jnp.repeat(got_sig.astype(BF16), slots, axis=1),
        mine_to[:, None],
        got_to[:, None],
        cols // blocks,
        tile,
        odd,
    )

    def sent(x, pairs):
        return lax.ppermute(x, "grid", along(pairs))

    last = chips - 1

    def over(links, t):
        pairs = []
        for a in range(links, last, 2):
            pairs += [(a, a + 1)] if a - t + 1 >= 0 else []
            pairs += [(a + 1, a)] if a + t <= last else []
        return pairs

    arrived = [
        (sent(for_b, over(1, 1)), sent(for_a, over(0, 1))) for for_b, *_, for_a in compacted
    ]
    own = tuple(
        straighten(tiles, by_b, by_a, odd)
        for (_, *tiles, _), (by_b, by_a) in zip(compacted, arrived)
    )

    own, told = lax.optimization_barrier((own, told))
    sizes = told[:, : 2 * batches].astype(jnp.int32).reshape(-1)
    weights = told[:, 2 * batches :].reshape(-1)
    to, start = places_of(sizes, 0)
    first = start.reshape(chips, -1)[:, 0]
    nominal = rows * lax.iota(jnp.int32, chips)
    fits = jnp.all(jnp.abs(first - nominal) <= margin) & (jnp.sum(sizes) == live)

    _, occupied_turned, trial_turned = lax.optimization_barrier(
        (compacted[0][0], occupied.T, trial.T)
    )
    mine_panel, other_panel = panel_halves(occupied_turned, trial_turned, core)
    panels = stack_panels(mine_panel, flip(other_panel, "grid", 1), core)

    per_window = rows // tile
    window_iota = lax.iota(jnp.int32, chips)
    ends = [(0, 1), (last, last - 1)]
    homes = [(b, a) for a, b in ends]
    side = 1 - 2 * odd

    def valid(at):
        return jnp.where((at >= 0) & (at <= last), at, -1)

    stages = [[([own], chip)]]
    by_a = by_b = own
    far_panels = None
    for t in range(1, last):
        by_a, by_b = (
            tuple(sent(x, over(0, t)) for x in by_b),
            tuple(sent(x, over(1, t)) for x in by_a),
        )
        if t == 1:
            far_panels = sent(panels, ends)
        a_at, b_at = valid(chip + side * t), valid(chip - side * t)
        if 2 * t > last:
            stages.append([([by_a, by_b], jnp.maximum(a_at, b_at))])
        else:
            stages.append([([by_a], a_at), ([by_b], b_at)])

    direct = occ_count <= 4
    points = per_window * piece

    def summed(pairs):
        if direct:
            parts = split_sum(pairs, occ)
            value = parts[0]
            for d in range(1, occ_count):
                value = value + flip(parts[d], "occ", d)
        else:
            value = jnp.concatenate([keep + got for keep, got in pairs])
            for bit in reversed(occ_bits):
                upper = (occ & bit) != 0
                low_part, high_part = value[:, :bit], value[:, bit:]
                got = flip(jnp.where(upper, low_part, high_part), "occ", bit)
                value = jnp.where(upper, high_part, low_part) + got
        return value.reshape(-1, points, 4 * columns)

    def shared_density(value, at):
        product = jnp.sum(value[:, :, : 2 * columns] * value[:, :, 2 * columns :], axis=2)
        here = (at[:, None] == window_iota[None, :])[:, :, None]
        return jnp.sum(jnp.where(here, product[:, None], 0.0), axis=0)

    early_jobs, late_jobs = sum(stages[1:-1], []), stages[-1]
    early_at = jnp.stack([at for _, at in early_jobs])
    late_at = late_jobs[0][1][None]
    early_jobs = stages[0] + early_jobs
    early_at = jnp.concatenate((chip[None], early_at))

    early_pair = project([(panels, w) for w, _ in early_jobs], tile, shares, core)

    at = (
        (window_iota * rows)[:, None, None]
        + (lax.iota(jnp.int32, per_window) * tile)[None, :, None]
        + member * piece
        + lax.iota(jnp.int32, piece)[None, None, :]
    ).reshape(-1, 1)
    weight = jnp.sum(jnp.where(to.reshape(1, -1) == at, weights[None, :], 0.0), axis=1)
    weight = weight.reshape(chips, per_window * piece)
    outer = jnp.where(chip == 0, last, jnp.where(chip == last, 0, early_at[2]))
    places = jnp.concatenate((early_at[:2], outer[None], early_at[3:], late_at))
    here = (places[:, None] == window_iota[None, :])[:, :, None]
    weight_here = jnp.sum(jnp.where(here, weight[None], 0.0), axis=1)[:, :, None]

    by_a, early_pair = lax.optimization_barrier((by_a, early_pair))
    late, by_a, early_pair, far_panels, weight_here, fits = lax.optimization_barrier(
        (by_b, by_a, early_pair, far_panels, weight_here, fits.astype(jnp.int32))
    )
    fits = fits != 0
    late = tuple(sent(x, homes) for x in late)
    late_window = [by_a, by_b]
    late_jobs = [(panels, late_window), (far_panels, [by_b])]

    def kernel_of_all():
        late_pair = project(late_jobs, tile, shares, core)
        value = summed([(keep, flip(give, "grid", 1)) for keep, give in (early_pair, late_pair)])
        density = shared_density(value, jnp.concatenate((early_at, late_at, late_at)))
        value, far_value = value[:-1], value[-1:]
        packed = jnp.concatenate(
            (far_value[0], jnp.pad(density, ((0, 0), (0, 4 * columns - points)))), axis=0
        )
        packed = flip(packed, "grid", 2)
        home_value, neighbour = packed[None, :points], packed[points:, :points]
        if chips <= 4:
            others = [flip(density, "grid", 2 * d) for d in range(2, chips)]
            density = density + neighbour + sum(others[1:], others[0])
        else:
            density = density + neighbour
            for bit in grid_bits[2:]:
                density = density + flip(density, "grid", bit)
        density = density * (1.0 / math.sqrt(total))

        values = jnp.concatenate((value[:2], value[2:3] + home_value, value[3:]))
        density_here = jnp.sum(jnp.where(here, density[None], 0.0), axis=1)[:, :, None]
        orbitals, response = values[:, :, : 2 * columns], values[:, :, 2 * columns :]
        kernel = (weight_here * (density_here * orbitals + response)).astype(BF16)
        kernel = kernel.reshape(-1, 1, piece, 2 * columns)
        if direct:
            parts = [kernel] + [flip(kernel, "occ", d) for d in range(1, occ_count)]
            kernel = in_order(parts, occ)
        else:
            for bit in occ_bits:
                kernel = doubled(kernel, "occ", bit, 1)
        return kernel, flip(kernel, "grid", 1), unwritten((columns, cols))

    scale = 1.0 / math.sqrt(rows * grid_count)

    def result_for_any_sizes():
        whole = any_sizes(
            orbital_values, occupied, trial, point_weights, batch_sizes, significant
        )
        none = jnp.zeros((places.shape[0] * per_window, occ_count, piece, 2 * columns), BF16)
        return none, none, whole * scale

    kernel, got_kernel, other = lax.cond(fits, kernel_of_all, result_for_any_sizes)
    early_windows = [w for w, _ in early_jobs]
    early_windows[2] = early_windows[2] + [late]
    windows = early_windows + [late_window]
    ours, theirs = contract(kernel, got_kernel, windows, core)
    back = flip(theirs, "grid", 1)
    return finish(core, fits, ours, back, other, scale).T


def solution(mesh):
    placed = (
        P("grid", "occ"),
        P("occ", "grid"),
        P("occ", "grid"),
        P("grid"),
        P("grid"),
        P("grid", "occ"),
    )
    return jax.shard_map(
        per_device, mesh=mesh, in_specs=placed, out_specs=P("occ", "grid"), check_vma=False
    )
```

```python
import math

import jax
import jax.numpy as jnp
from jax import lax
from jax.experimental import pallas as pl
from jax.experimental.pallas import tpu as pltpu
from jax.sharding import PartitionSpec as P

BF16, F32 = jnp.bfloat16, jnp.float32
MIB = 1024 * 1024
WHOLE = pl.BlockSpec(memory_space=pltpu.VMEM)
SCALARS = pl.BlockSpec(memory_space=pltpu.SMEM)


def screen(values, sizes, significant):
    rows, cols = values.shape
    batches = sizes.shape[0]
    blocks = significant.shape[1]
    blocked = (
        values.reshape(batches, rows // batches, blocks, cols // blocks)
        * significant.astype(values.dtype)[:, None, :, None]
    )
    position = lax.broadcasted_iota(jnp.int32, (batches, rows // batches), 1)
    live = (position < sizes[:, None]).astype(jnp.float32).reshape(rows)
    return (blocked.reshape(rows, cols), live)


def any_sizes(orbital_values, occupied, trial, point_weights, batch_sizes, significant):
    screened, live = screen(orbital_values, batch_sizes, significant)
    rows, cols = screened.shape
    grid_count, occ_count = lax.axis_size("grid"), lax.axis_size("occ")
    columns = occupied.shape[1]
    me = lax.axis_index("grid")
    ring = [(i, (i + 1) % grid_count) for i in range(grid_count)]
    occ_ring = [(i, (i + 1) % occ_count) for i in range(occ_count)]

    def project_one(step, carry):
        panel, terms = carry
        term = jnp.dot(screened, panel, preferred_element_type=F32)
        terms = lax.dynamic_update_index_in_dim(terms, term, (me - step) % grid_count, 0)
        return lax.ppermute(panel, "grid", ring), terms

    joined = jnp.concatenate((occupied, trial), axis=1)
    terms = jnp.zeros((grid_count, rows, 2 * columns), F32)
    terms = lax.fori_loop(0, grid_count, project_one, (joined, terms))[1]

    def add_one(step, carry):
        moving, held = carry
        moving = lax.ppermute(moving, "occ", occ_ring)
        return moving, held + moving

    terms = lax.fori_loop(0, occ_count - 1, add_one, (terms, terms))[1]
    orbitals, response = terms[:, :, :columns], terms[:, :, columns:]
    density = jnp.sum(orbitals * response, axis=(0, 2)) * (1.0 / math.sqrt(columns * grid_count))
    weight = (point_weights * live)[None, :, None]
    kernel = (weight * (density[None, :, None] * orbitals + response)).astype(BF16)

    def contract_one(step, held):
        owner = (me + grid_count - 1 - step) % grid_count
        part = lax.dynamic_index_in_dim(kernel, owner, 0, keepdims=False)
        term = lax.dot_general(
            part, screened, (((0,), (0,)), ((), ())), preferred_element_type=F32
        )
        return lax.ppermute(held, "grid", ring) + term

    return lax.fori_loop(0, grid_count, contract_one, jnp.zeros((columns, cols), F32))


def half_of(whole, which):
    rows, columns = whole.shape
    half = rows // 2
    if half % 16:
        return lax.dynamic_slice_in_dim(whole, which * half, half, 0)

    def body(which_ref, whole_ref, out_ref, sem):
        first = pl.multiple_of(which_ref[0] * half, 16)
        copy = pltpu.make_async_copy(whole_ref.at[pl.ds(first, half)], out_ref, sem)
        copy.start()
        copy.wait()

    return pl.pallas_call(
        body,
        out_shape=jax.ShapeDtypeStruct((half, columns), whole.dtype),
        in_specs=[SCALARS, pl.BlockSpec(memory_space=pl.ANY)],
        out_specs=WHOLE,
        scratch_shapes=[pltpu.SemaphoreType.DMA],
        compiler_params=pltpu.CompilerParams(vmem_limit_bytes=4 * MIB),
        name="half_of",
    )(which[None], whole)


def compact(mine, got, mine_sig, got_sig, mine_to, got_to, width, tile, odd):
    half, rows = mine.shape
    blocks = mine_sig.shape[0]
    count = rows // tile + 2
    cuts = [(0, half)]

    def body(odd_ref, mine_ref, got_ref, msig_ref, gsig_ref, mto_ref, gto_ref, *outs):
        block_of = lax.broadcasted_iota(jnp.int32, (half, blocks), 0)
        begin = lax.broadcasted_iota(jnp.int32, (half, blocks), 1) * width
        spread = ((block_of >= begin) & (block_of < begin + width)).astype(F32).astype(BF16)
        slot = lax.broadcasted_iota(jnp.int32, (rows, count * tile), 1)

        def part(value_ref, sig_ref, to_ref):
            kept = jnp.dot(spread, sig_ref[...], preferred_element_type=F32)
            screened = (value_ref[...].astype(F32) * kept).astype(BF16)
            place = (to_ref[...] == slot).astype(F32).astype(BF16)
            return jnp.dot(screened, place, preferred_element_type=F32)

        window = part(mine_ref, msig_ref, mto_ref) + part(got_ref, gsig_ref, gto_ref)
        tiles = [window[:, j * tile : (j + 1) * tile] for j in range(count)]
        even = odd_ref[0] == 0
        first, last = tiles[0], tiles[-1]
        tiles[0] = jnp.where(even, first, last)
        tiles[-1] = jnp.where(even, last, first)
        for p, (low, high) in enumerate(cuts):
            for j in range(count):
                outs[p * count + j][...] = tiles[j][low:high].astype(BF16)

    shapes = [
        jax.ShapeDtypeStruct((high - low, tile), BF16) for low, high in cuts for _ in range(count)
    ]
    out = pl.pallas_call(
        body,
        out_shape=shapes,
        in_specs=[SCALARS] + [WHOLE] * 6,
        out_specs=[WHOLE] * len(shapes),
        compiler_params=pltpu.CompilerParams(vmem_limit_bytes=16 * MIB),
        name="compact",
        cost_estimate=pl.CostEstimate(
            flops=8 * half * rows * rows, bytes_accessed=8 * half * rows, transcendentals=0
        ),
    )(odd[None], mine, got, mine_sig, got_sig, mine_to, got_to)
    return [out[p * count : (p + 1) * count] for p in range(len(cuts))]


def straighten(tiles, by_b, by_a, odd):
    half, tile = by_a.shape
    count = len(tiles)

    def body(odd_ref, *refs):
        tile_refs, b_ref, a_ref, out_ref = refs[:count], *refs[count:]
        even = odd_ref[0] == 0
        for j in range(count):
            value = tile_refs[j][...]
            if j == 0:
                value = value + jnp.where(even, b_ref[...], a_ref[...])
            if j == count - 1:
                value = value + jnp.where(even, a_ref[...], b_ref[...])
            out_ref[:, j * tile : (j + 1) * tile] = value

    return pl.pallas_call(
        body,
        out_shape=jax.ShapeDtypeStruct((half, count * tile), BF16),
        in_specs=[SCALARS] + [WHOLE] * (count + 2),
        out_specs=WHOLE,
        compiler_params=pltpu.CompilerParams(vmem_limit_bytes=8 * MIB),
        name="straighten",
    )(odd[None], *tiles, by_b, by_a)


def panel_halves(occupied, trial, core):
    columns, cols = occupied.shape
    half = cols // 2
    width = -(-half // 128) * 128

    def body(core_ref, occupied_ref, trial_ref, mine_ref, other_ref):
        first = core_ref[0] == 0
        mine_ref[...] = jnp.zeros_like(mine_ref)
        other_ref[...] = jnp.zeros_like(other_ref)
        for j, ref in enumerate((occupied_ref, trial_ref)):
            low, high = ref[:, :half], ref[:, half:]
            mine_ref[j * columns : (j + 1) * columns, :half] = jnp.where(first, low, high)
            other_ref[j * columns : (j + 1) * columns, :half] = jnp.where(first, high, low)

    shape = jax.ShapeDtypeStruct((2 * columns, width), BF16)
    return pl.pallas_call(
        body,
        out_shape=(shape, shape),
        in_specs=[SCALARS, WHOLE, WHOLE],
        out_specs=(WHOLE, WHOLE),
        compiler_params=pltpu.CompilerParams(vmem_limit_bytes=8 * MIB),
        name="panel_halves",
    )(core[None], occupied, trial)


def stack_panels(mine, got, core):
    both, width = mine.shape
    columns = both // 2

    def body(core_ref, mine_ref, got_ref, out_ref):
        first = core_ref[0] == 0
        for j in range(2):
            low = mine_ref[j * columns : (j + 1) * columns]
            high = got_ref[j * columns : (j + 1) * columns]
            q = 2 * j * columns
            out_ref[q : q + columns] = jnp.where(first, low, high)
            out_ref[q + columns : q + 2 * columns] = jnp.where(first, high, low)

    return pl.pallas_call(
        body,
        out_shape=jax.ShapeDtypeStruct((2 * both, width), BF16),
        in_specs=[SCALARS, WHOLE, WHOLE],
        out_specs=WHOLE,
        compiler_params=pltpu.CompilerParams(vmem_limit_bytes=8 * MIB),
        name="stack_panels",
    )(core[None], mine, got)


def distinct(arrays):
    return list({id(x): x for x in arrays}.values())


def read_window(addends, p, arrays, refs):
    ref_of = {id(x): ref for x, ref in zip(arrays, refs)}
    total = None
    for x in addends:
        value = ref_of[id(x[p])][...]
        total = value if total is None else total + value
    return total


def split_sum(pairs, occ):
    _, shares, piece, both = pairs[0][0].shape
    tiles = sum(keep.shape[0] for keep, _ in pairs)

    def body(occ_ref, *refs):
        ins, outs = refs[: 2 * len(pairs)], refs[2 * len(pairs) :]
        for d in range(shares):
            at = 0
            for keep_ref, got_ref in zip(ins[::2], ins[1::2]):
                for q in range(keep_ref.shape[0]):
                    outs[d][at] = keep_ref[q, occ_ref[0] ^ d] + got_ref[q, occ_ref[0] ^ d]
                    at += 1

    shape = jax.ShapeDtypeStruct((tiles, piece, both), F32)
    return pl.pallas_call(
        body,
        out_shape=(shape,) * shares,
        in_specs=[SCALARS] + [WHOLE] * (2 * len(pairs)),
        out_specs=(WHOLE,) * shares,
        compiler_params=pltpu.CompilerParams(vmem_limit_bytes=8 * MIB),
        name="split_sum",
    )(occ[None], *sum(pairs, ()))


def project(jobs, tile, shares, core):
    both = jobs[0][0].shape[0]
    parts = [x.shape[0] for x in jobs[0][1][0]]
    rows = jobs[0][1][0][0].shape[1]
    half = sum(parts)
    piece = tile // shares
    tiles = len(jobs) * rows // tile
    panels = distinct([p for p, _ in jobs])
    arrays = distinct([x for _, window in jobs for addend in window for x in addend])
    count = len(panels)

    def body(core_ref, *refs):
        panel_refs, array_refs = refs[:count], refs[count:-3]
        keep_ref, give_ref, terms_ref = refs[-3:]
        q = 0
        for panel, window in jobs:
            panel_ref = panel_refs[[id(p) for p in panels].index(id(panel))]
            total, low = None, 0
            for p, size in enumerate(parts):
                value = read_window(window, p, arrays, array_refs)
                term = jnp.dot(
                    panel_ref[:, low : low + size], value, preferred_element_type=F32
                )
                total = term if total is None else total + term
                low += size
            turned = total.T
            for j in range(0, rows, tile):
                terms_ref[q] = turned[j : j + tile].reshape(2, shares // 2, piece, both)
                keep_ref[q] = terms_ref[q, core_ref[0]]
                give_ref[q] = terms_ref[q, 1 - core_ref[0]]
                q += 1

    shape = jax.ShapeDtypeStruct((tiles, shares // 2, piece, both), F32)
    return pl.pallas_call(
        body,
        out_shape=(shape, shape),
        in_specs=[SCALARS] + [WHOLE] * (count + len(arrays)),
        out_specs=(WHOLE, WHOLE),
        scratch_shapes=[pltpu.VMEM((tiles, 2, shares // 2, piece, both), F32)],
        compiler_params=pltpu.CompilerParams(vmem_limit_bytes=12 * MIB),
        name="project",
        cost_estimate=pl.CostEstimate(
            flops=2 * both * half * tiles * tile,
            bytes_accessed=2 * half * (both + tiles * tile) + 4 * tiles * tile * both,
            transcendentals=0,
        ),
    )(core[None], *panels, *arrays)


def in_order(parts, occ):
    tiles, _, piece, columns = parts[0].shape

    def body(occ_ref, *refs):
        for d in range(len(parts)):
            refs[-1][:, occ_ref[0] ^ d] = refs[d][:, 0]

    return pl.pallas_call(
        body,
        out_shape=jax.ShapeDtypeStruct((tiles, len(parts), piece, columns), parts[0].dtype),
        in_specs=[SCALARS] + [WHOLE] * len(parts),
        out_specs=WHOLE,
        compiler_params=pltpu.CompilerParams(vmem_limit_bytes=4 * MIB),
        name="in_order",
    )(occ[None], *parts)


def contract(kernel, got, windows, core):
    tiles, shares, piece, columns = kernel.shape
    parts = [x.shape[0] for x in windows[0][0]]
    rows = windows[0][0][0].shape[1]
    half = sum(parts)
    own = columns // 2
    arrays = distinct([x for window in windows for addend in window for x in addend])
    per_window = tiles // len(windows)

    def body(core_ref, kernel_ref, got_ref, *refs):
        array_refs = refs[:-3]
        mine_ref, other_ref, order_ref = refs[-3:]
        first = core_ref[0] == 0
        order_ref[:, core_ref[0]] = kernel_ref[...].astype(F32)
        order_ref[:, 1 - core_ref[0]] = got_ref[...].astype(F32)
        kernels = [
            order_ref[s * per_window : (s + 1) * per_window].reshape(rows, columns).astype(BF16)
            for s in range(len(windows))
        ]
        low = 0
        for p, size in enumerate(parts):
            total = None
            for window, part in zip(windows, kernels):
                value = read_window(window, p, arrays, array_refs)
                term = jnp.dot(value, part, preferred_element_type=F32)
                total = term if total is None else total + term
            total = total.T
            mine_ref[:, low : low + size] = jnp.where(first, total[:own], total[own:])
            other_ref[:, low : low + size] = jnp.where(first, total[own:], total[:own])
            low += size

    shape = jax.ShapeDtypeStruct((own, half), F32)
    return pl.pallas_call(
        body,
        out_shape=(shape, shape),
        in_specs=[SCALARS] + [WHOLE] * (2 + len(arrays)),
        out_specs=(WHOLE, WHOLE),
        scratch_shapes=[pltpu.VMEM((tiles, 2, shares, piece, columns), F32)],
        compiler_params=pltpu.CompilerParams(vmem_limit_bytes=20 * MIB),
        name="contract",
        cost_estimate=pl.CostEstimate(
            flops=2 * columns * half * rows * len(windows),
            bytes_accessed=2 * rows * len(windows) * half + 4 * columns * half,
            transcendentals=0,
        ),
    )(core[None], kernel, got, *arrays)


def unwritten(shape):
    def body(out_ref):
        pass

    return pl.pallas_call(
        body,
        out_shape=jax.ShapeDtypeStruct(shape, F32),
        out_specs=pl.BlockSpec(memory_space=pltpu.HBM),
        name="unwritten",
    )()


def finish(core, fits, ours, back, other, scale):
    own, half = ours.shape

    def body(flags_ref, ours_ref, back_ref, other_ref, out_ref, whole_ref, sem):
        @pl.when(flags_ref[1] != 0)
        def _():
            first = flags_ref[0] == 0
            whole_ref[:, :half] = jnp.where(first, ours_ref[...], back_ref[...]) * scale
            whole_ref[:, half:] = jnp.where(first, back_ref[...], ours_ref[...]) * scale
            copy = pltpu.make_async_copy(whole_ref, out_ref, sem)
            copy.start()
            copy.wait()

    return pl.pallas_call(
        body,
        out_shape=jax.ShapeDtypeStruct((own, 2 * half), F32),
        in_specs=[SCALARS, WHOLE, WHOLE, pl.BlockSpec(memory_space=pltpu.HBM)],
        out_specs=pl.BlockSpec(memory_space=pltpu.HBM),
        scratch_shapes=[pltpu.VMEM((own, 2 * half), F32), pltpu.SemaphoreType.DMA],
        input_output_aliases={3: 0},
        compiler_params=pltpu.CompilerParams(vmem_limit_bytes=8 * MIB),
        name="finish",
    )(jnp.stack((core, fits.astype(jnp.int32))), ours, back, other)


def per_device(orbital_values, occupied, trial, point_weights, batch_sizes, significant):
    rows, cols = orbital_values.shape
    batches = batch_sizes.shape[0]
    slots = rows // batches
    blocks = significant.shape[1]
    columns = occupied.shape[1]
    grid_count = lax.axis_size("grid")
    occ_count = lax.axis_size("occ")
    chips = grid_count // 2
    shares = 2 * occ_count
    half = cols // 2
    total = columns * grid_count
    place = lax.axis_index("grid")
    chip, core = place // 2, place % 2
    occ = lax.axis_index("occ")
    member = core * occ_count + occ

    def flip(x, axis, bit):
        count = lax.axis_size(axis)
        return lax.ppermute(x, axis, [(i, i ^ bit) for i in range(count)])

    def along(pairs):
        return [(2 * a + c, 2 * b + c) for a, b in pairs for c in range(2)]

    def doubled(x, axis, bit, dim):
        got = flip(x, axis, bit)
        mine = (lax.axis_index(axis) & bit) == 0
        return jnp.where(
            mine, jnp.concatenate((x, got), axis=dim), jnp.concatenate((got, x), axis=dim)
        )

    def halves(whole, axis):
        size = whole.shape[axis] // 2
        mine = lax.dynamic_slice_in_dim(whole, core * size, size, axis)
        return mine, lax.dynamic_slice_in_dim(whole, (1 - core) * size, size, axis)

    grid_bits = [1 << b for b in range(grid_count.bit_length() - 1)]
    occ_bits = [1 << b for b in range(occ_count.bit_length() - 1)]

    mine = half_of(orbital_values.T, core)
    got = flip(half_of(orbital_values.T, 1 - core), "grid", 1)
    mine_sig, other_sig = halves(significant.T, 0)
    got_sig = flip(other_sig, "grid", 1)

    told = jnp.concatenate(
        (
            doubled(batch_sizes[None], "grid", 1, 0).astype(F32).reshape(1, -1),
            doubled(point_weights[None], "grid", 1, 0).reshape(1, -1),
        ),
        axis=1,
    )
    live = rows * chips
    for bit in grid_bits[1:2]:
        told = doubled(told, "grid", bit, 0)
    if chips > 4:
        for bit in grid_bits[2:]:
            told = doubled(told, "grid", bit, 0)

    def places_of(sizes, upper):
        count = sizes.shape[0]
        batch = lax.broadcasted_iota(jnp.int32, (count, count), 0)
        before = lax.broadcasted_iota(jnp.int32, (count, count), 1) < batch
        start = upper * live + jnp.sum((before.astype(jnp.int32) - upper) * sizes[None, :], axis=1)
        position = lax.broadcasted_iota(jnp.int32, (count, slots), 1)
        to = jnp.where(position < sizes[:, None], start[:, None] + position, -4 * live)
        return to.reshape(-1, rows), start

    sizes = told[:, : 2 * batches].astype(jnp.int32).reshape(-1)
    near_to, _ = places_of(sizes, chip // 2 if chips <= 4 else 0)
    near_place = place if chips > 4 else place % 4
    for bit in grid_bits[2:] if chips <= 4 else []:
        told = doubled(told, "grid", bit, 0)
    margin = rows // 2 if (rows // 2) % (8 * shares) == 0 else rows
    tile = margin
    piece = tile // shares
    base = rows * chip - margin
    mine_to = lax.dynamic_index_in_dim(near_to, near_place, 0, keepdims=False) - base
    got_to = lax.dynamic_index_in_dim(near_to, near_place ^ 1, 0, keepdims=False) - base
    odd = chip % 2
    compacted = compact(
        mine,
        got,
        jnp.repeat(mine_sig.astype(BF16), slots, axis=1),
        jnp.repeat(got_sig.astype(BF16), slots, axis=1),
        mine_to[:, None],
        got_to[:, None],
        cols // blocks,
        tile,
        odd,
    )

    def sent(x, pairs):
        return lax.ppermute(x, "grid", along(pairs))

    last = chips - 1

    def over(links, t):
        pairs = []
        for a in range(links, last, 2):
            pairs += [(a, a + 1)] if a - t + 1 >= 0 else []
            pairs += [(a + 1, a)] if a + t <= last else []
        return pairs

    arrived = [
        (sent(for_b, over(1, 1)), sent(for_a, over(0, 1))) for for_b, *_, for_a in compacted
    ]
    own = tuple(
        straighten(tiles, by_b, by_a, odd)
        for (_, *tiles, _), (by_b, by_a) in zip(compacted, arrived)
    )

    own, told = lax.optimization_barrier((own, told))
    sizes = told[:, : 2 * batches].astype(jnp.int32).reshape(-1)
    weights = told[:, 2 * batches :].reshape(-1)
    to, start = places_of(sizes, 0)
    first = start.reshape(chips, -1)[:, 0]
    nominal = rows * lax.iota(jnp.int32, chips)
    fits = jnp.all(jnp.abs(first - nominal) <= margin) & (jnp.sum(sizes) == live)

    _, occupied_turned, trial_turned = lax.optimization_barrier(
        (compacted[0][0], occupied.T, trial.T)
    )
    mine_panel, other_panel = panel_halves(occupied_turned, trial_turned, core)
    panels = stack_panels(mine_panel, flip(other_panel, "grid", 1), core)

    per_window = rows // tile
    window_iota = lax.iota(jnp.int32, chips)
    ends = [(0, 1), (last, last - 1)]
    homes = [(b, a) for a, b in ends]
    side = 1 - 2 * odd

    def valid(at):
        return jnp.where((at >= 0) & (at <= last), at, -1)

    stages = [[([own], chip)]]
    by_a = by_b = own
    far_panels = None
    for t in range(1, last):
        by_a, by_b = (
            tuple(sent(x, over(0, t)) for x in by_b),
            tuple(sent(x, over(1, t)) for x in by_a),
        )
        if t == 1:
            far_panels = sent(panels, ends)
        a_at, b_at = valid(chip + side * t), valid(chip - side * t)
        if 2 * t > last:
            stages.append([([by_a, by_b], jnp.maximum(a_at, b_at))])
        else:
            stages.append([([by_a], a_at), ([by_b], b_at)])

    direct = occ_count <= 4
    points = per_window * piece

    def summed(pairs):
        if direct:
            parts = split_sum(pairs, occ)
            value = parts[0]
            for d in range(1, occ_count):
                value = value + flip(parts[d], "occ", d)
        else:
            value = jnp.concatenate([keep + got for keep, got in pairs])
            for bit in reversed(occ_bits):
                upper = (occ & bit) != 0
                low_part, high_part = value[:, :bit], value[:, bit:]
                got = flip(jnp.where(upper, low_part, high_part), "occ", bit)
                value = jnp.where(upper, high_part, low_part) + got
        return value.reshape(-1, points, 4 * columns)

    def shared_density(value, at):
        product = jnp.sum(value[:, :, : 2 * columns] * value[:, :, 2 * columns :], axis=2)
        here = (at[:, None] == window_iota[None, :])[:, :, None]
        return jnp.sum(jnp.where(here, product[:, None], 0.0), axis=0)

    early_jobs, late_jobs = sum(stages[1:-1], []), stages[-1]
    early_at = jnp.stack([at for _, at in early_jobs])
    late_at = late_jobs[0][1][None]
    early_jobs = stages[0] + early_jobs
    early_at = jnp.concatenate((chip[None], early_at))

    def halved(jobs):
        keep, give = project(jobs, tile, shares, core)
        return keep, flip(give, "grid", 1)

    early_value = summed(
        [halved([(panels, early_jobs[0][0])]), halved([(panels, w) for w, _ in early_jobs[1:]])]
    )

    at = (
        (window_iota * rows)[:, None, None]
        + (lax.iota(jnp.int32, per_window) * tile)[None, :, None]
        + member * piece
        + lax.iota(jnp.int32, piece)[None, None, :]
    ).reshape(-1, 1)
    weight = jnp.sum(jnp.where(to.reshape(1, -1) == at, weights[None, :], 0.0), axis=1)
    weight = weight.reshape(chips, per_window * piece)
    outer = jnp.where(chip == 0, last, jnp.where(chip == last, 0, early_at[2]))
    places = jnp.concatenate((early_at[:2], outer[None], early_at[3:], late_at))
    here = (places[:, None] == window_iota[None, :])[:, :, None]
    weight_here = jnp.sum(jnp.where(here, weight[None], 0.0), axis=1)[:, :, None]

    late, by_a, early_value, far_panels, weight_here, fits = lax.optimization_barrier(
        (by_b, by_a, early_value, far_panels, weight_here, fits.astype(jnp.int32))
    )
    fits = fits != 0
    late = tuple(sent(x, homes) for x in late)
    late_window = [by_a, by_b]
    late_jobs = [(panels, late_window), (far_panels, [by_b])]

    def kernel_of_all():
        late_pair = project(late_jobs, tile, shares, core)
        keep, give = late_pair
        value = jnp.concatenate((early_value, summed([(keep, flip(give, "grid", 1))])))
        density = shared_density(value, jnp.concatenate((early_at, late_at, late_at)))
        value, far_value = value[:-1], value[-1:]
        packed = jnp.concatenate(
            (far_value[0], jnp.pad(density, ((0, 0), (0, 4 * columns - points)))), axis=0
        )
        packed = flip(packed, "grid", 2)
        home_value, neighbour = packed[None, :points], packed[points:, :points]
        if chips <= 4:
            others = [flip(density, "grid", 2 * d) for d in range(2, chips)]
            density = density + neighbour + sum(others[1:], others[0])
        else:
            density = density + neighbour
            for bit in grid_bits[2:]:
                density = density + flip(density, "grid", bit)
        density = density * (1.0 / math.sqrt(total))

        values = jnp.concatenate((value[:2], value[2:3] + home_value, value[3:]))
        density_here = jnp.sum(jnp.where(here, density[None], 0.0), axis=1)[:, :, None]
        orbitals, response = values[:, :, : 2 * columns], values[:, :, 2 * columns :]
        kernel = (weight_here * (density_here * orbitals + response)).astype(BF16)
        kernel = kernel.reshape(-1, 1, piece, 2 * columns)
        if direct:
            parts = [kernel] + [flip(kernel, "occ", d) for d in range(1, occ_count)]
            kernel = in_order(parts, occ)
        else:
            for bit in occ_bits:
                kernel = doubled(kernel, "occ", bit, 1)
        return kernel, flip(kernel, "grid", 1), unwritten((columns, cols))

    scale = 1.0 / math.sqrt(rows * grid_count)

    def result_for_any_sizes():
        whole = any_sizes(
            orbital_values, occupied, trial, point_weights, batch_sizes, significant
        )
        none = jnp.zeros((places.shape[0] * per_window, occ_count, piece, 2 * columns), BF16)
        return none, none, whole * scale

    kernel, got_kernel, other = lax.cond(fits, kernel_of_all, result_for_any_sizes)
    early_windows = [w for w, _ in early_jobs]
    early_windows[2] = early_windows[2] + [late]
    windows = early_windows + [late_window]
    ours, theirs = contract(kernel, got_kernel, windows, core)
    back = flip(theirs, "grid", 1)
    return finish(core, fits, ours, back, other, scale).T


def solution(mesh):
    placed = (
        P("grid", "occ"),
        P("occ", "grid"),
        P("occ", "grid"),
        P("grid"),
        P("grid"),
        P("grid", "occ"),
    )
    return jax.shard_map(
        per_device, mesh=mesh, in_specs=placed, out_specs=P("occ", "grid"), check_vma=False
    )
```

```python
import math

import jax
import jax.numpy as jnp
from jax import lax
from jax.experimental import pallas as pl
from jax.experimental.pallas import tpu as pltpu
from jax.sharding import PartitionSpec as P

BF16, F32 = jnp.bfloat16, jnp.float32
MIB = 1024 * 1024
WHOLE = pl.BlockSpec(memory_space=pltpu.VMEM)
SCALARS = pl.BlockSpec(memory_space=pltpu.SMEM)


def screen(values, sizes, significant):
    rows, cols = values.shape
    batches = sizes.shape[0]
    blocks = significant.shape[1]
    blocked = (
        values.reshape(batches, rows // batches, blocks, cols // blocks)
        * significant.astype(values.dtype)[:, None, :, None]
    )
    position = lax.broadcasted_iota(jnp.int32, (batches, rows // batches), 1)
    live = (position < sizes[:, None]).astype(jnp.float32).reshape(rows)
    return (blocked.reshape(rows, cols), live)


def any_sizes(orbital_values, occupied, trial, point_weights, batch_sizes, significant):
    screened, live = screen(orbital_values, batch_sizes, significant)
    rows, cols = screened.shape
    grid_count, occ_count = lax.axis_size("grid"), lax.axis_size("occ")
    columns = occupied.shape[1]
    me = lax.axis_index("grid")
    ring = [(i, (i + 1) % grid_count) for i in range(grid_count)]
    occ_ring = [(i, (i + 1) % occ_count) for i in range(occ_count)]

    def project_one(step, carry):
        panel, terms = carry
        term = jnp.dot(screened, panel, preferred_element_type=F32)
        terms = lax.dynamic_update_index_in_dim(terms, term, (me - step) % grid_count, 0)
        return lax.ppermute(panel, "grid", ring), terms

    joined = jnp.concatenate((occupied, trial), axis=1)
    terms = jnp.zeros((grid_count, rows, 2 * columns), F32)
    terms = lax.fori_loop(0, grid_count, project_one, (joined, terms))[1]

    def add_one(step, carry):
        moving, held = carry
        moving = lax.ppermute(moving, "occ", occ_ring)
        return moving, held + moving

    terms = lax.fori_loop(0, occ_count - 1, add_one, (terms, terms))[1]
    orbitals, response = terms[:, :, :columns], terms[:, :, columns:]
    density = jnp.sum(orbitals * response, axis=(0, 2)) * (1.0 / math.sqrt(columns * grid_count))
    weight = (point_weights * live)[None, :, None]
    kernel = (weight * (density[None, :, None] * orbitals + response)).astype(BF16)

    def contract_one(step, held):
        owner = (me + grid_count - 1 - step) % grid_count
        part = lax.dynamic_index_in_dim(kernel, owner, 0, keepdims=False)
        term = lax.dot_general(
            part, screened, (((0,), (0,)), ((), ())), preferred_element_type=F32
        )
        return lax.ppermute(held, "grid", ring) + term

    return lax.fori_loop(0, grid_count, contract_one, jnp.zeros((columns, cols), F32))


def half_of(whole, which):
    rows, columns = whole.shape
    half = rows // 2
    if half % 16:
        return lax.dynamic_slice_in_dim(whole, which * half, half, 0)

    def body(which_ref, whole_ref, out_ref, sem):
        first = pl.multiple_of(which_ref[0] * half, 16)
        copy = pltpu.make_async_copy(whole_ref.at[pl.ds(first, half)], out_ref, sem)
        copy.start()
        copy.wait()

    return pl.pallas_call(
        body,
        out_shape=jax.ShapeDtypeStruct((half, columns), whole.dtype),
        in_specs=[SCALARS, pl.BlockSpec(memory_space=pl.ANY)],
        out_specs=WHOLE,
        scratch_shapes=[pltpu.SemaphoreType.DMA],
        compiler_params=pltpu.CompilerParams(vmem_limit_bytes=4 * MIB),
        name="half_of",
    )(which[None], whole)


def compact(mine, got, mine_sig, got_sig, mine_to, got_to, width, tile, odd):
    half, rows = mine.shape
    blocks = mine_sig.shape[0]
    count = rows // tile + 2
    cuts = [(0, half)]

    def body(odd_ref, mine_ref, got_any, msig_ref, gsig_ref, mto_ref, gto_ref, *rest):
        outs, got_ref, sem = rest[:-2], rest[-2], rest[-1]
        copy = pltpu.make_async_copy(got_any, got_ref, sem)
        copy.start()
        block_of = lax.broadcasted_iota(jnp.int32, (half, blocks), 0)
        begin = lax.broadcasted_iota(jnp.int32, (half, blocks), 1) * width
        spread = ((block_of >= begin) & (block_of < begin + width)).astype(F32).astype(BF16)
        slot = lax.broadcasted_iota(jnp.int32, (rows, count * tile), 1)

        def part(value_ref, sig_ref, to_ref):
            kept = jnp.dot(spread, sig_ref[...], preferred_element_type=F32)
            screened = (value_ref[...].astype(F32) * kept).astype(BF16)
            place = (to_ref[...] == slot).astype(F32).astype(BF16)
            return jnp.dot(screened, place, preferred_element_type=F32)

        window = part(mine_ref, msig_ref, mto_ref)
        copy.wait()
        window = window + part(got_ref, gsig_ref, gto_ref)
        tiles = [window[:, j * tile : (j + 1) * tile] for j in range(count)]
        even = odd_ref[0] == 0
        first, last = tiles[0], tiles[-1]
        tiles[0] = jnp.where(even, first, last)
        tiles[-1] = jnp.where(even, last, first)
        for p, (low, high) in enumerate(cuts):
            for j in range(count):
                outs[p * count + j][...] = tiles[j][low:high].astype(BF16)

    shapes = [
        jax.ShapeDtypeStruct((high - low, tile), BF16) for low, high in cuts for _ in range(count)
    ]
    out = pl.pallas_call(
        body,
        out_shape=shapes,
        in_specs=[SCALARS, WHOLE, pl.BlockSpec(memory_space=pl.ANY)] + [WHOLE] * 4,
        out_specs=[WHOLE] * len(shapes),
        scratch_shapes=[pltpu.VMEM((half, rows), BF16), pltpu.SemaphoreType.DMA],
        compiler_params=pltpu.CompilerParams(vmem_limit_bytes=16 * MIB),
        name="compact",
        cost_estimate=pl.CostEstimate(
            flops=8 * half * rows * rows, bytes_accessed=8 * half * rows, transcendentals=0
        ),
    )(odd[None], mine, got, mine_sig, got_sig, mine_to, got_to)
    return [out[p * count : (p + 1) * count] for p in range(len(cuts))]


def straighten(tiles, by_b, by_a, odd):
    half, tile = by_a.shape
    count = len(tiles)

    def body(odd_ref, *refs):
        tile_refs, b_ref, a_ref, out_ref = refs[:count], *refs[count:]
        even = odd_ref[0] == 0
        for j in range(count):
            value = tile_refs[j][...]
            if j == 0:
                value = value + jnp.where(even, b_ref[...], a_ref[...])
            if j == count - 1:
                value = value + jnp.where(even, a_ref[...], b_ref[...])
            out_ref[:, j * tile : (j + 1) * tile] = value

    return pl.pallas_call(
        body,
        out_shape=jax.ShapeDtypeStruct((half, count * tile), BF16),
        in_specs=[SCALARS] + [WHOLE] * (count + 2),
        out_specs=WHOLE,
        compiler_params=pltpu.CompilerParams(vmem_limit_bytes=8 * MIB),
        name="straighten",
    )(odd[None], *tiles, by_b, by_a)


def panel_halves(occupied, trial, core):
    columns, cols = occupied.shape
    half = cols // 2
    width = -(-half // 128) * 128

    def body(core_ref, occupied_ref, trial_ref, mine_ref, other_ref):
        first = core_ref[0] == 0
        mine_ref[...] = jnp.zeros_like(mine_ref)
        other_ref[...] = jnp.zeros_like(other_ref)
        for j, ref in enumerate((occupied_ref, trial_ref)):
            low, high = ref[:, :half], ref[:, half:]
            mine_ref[j * columns : (j + 1) * columns, :half] = jnp.where(first, low, high)
            other_ref[j * columns : (j + 1) * columns, :half] = jnp.where(first, high, low)

    shape = jax.ShapeDtypeStruct((2 * columns, width), BF16)
    return pl.pallas_call(
        body,
        out_shape=(shape, shape),
        in_specs=[SCALARS, WHOLE, WHOLE],
        out_specs=(WHOLE, WHOLE),
        compiler_params=pltpu.CompilerParams(vmem_limit_bytes=8 * MIB),
        name="panel_halves",
    )(core[None], occupied, trial)


def stack_panels(mine, got, core):
    both, width = mine.shape
    columns = both // 2

    def body(core_ref, mine_ref, got_ref, out_ref):
        first = core_ref[0] == 0
        for j in range(2):
            low = mine_ref[j * columns : (j + 1) * columns]
            high = got_ref[j * columns : (j + 1) * columns]
            q = 2 * j * columns
            out_ref[q : q + columns] = jnp.where(first, low, high)
            out_ref[q + columns : q + 2 * columns] = jnp.where(first, high, low)

    return pl.pallas_call(
        body,
        out_shape=jax.ShapeDtypeStruct((2 * both, width), BF16),
        in_specs=[SCALARS, WHOLE, WHOLE],
        out_specs=WHOLE,
        compiler_params=pltpu.CompilerParams(vmem_limit_bytes=8 * MIB),
        name="stack_panels",
    )(core[None], mine, got)


def distinct(arrays):
    return list({id(x): x for x in arrays}.values())


def read_window(addends, p, arrays, refs):
    ref_of = {id(x): ref for x, ref in zip(arrays, refs)}
    total = None
    for x in addends:
        value = ref_of[id(x[p])][...]
        total = value if total is None else total + value
    return total


def split_sum(pairs, occ):
    _, shares, piece, both = pairs[0][0].shape
    tiles = sum(keep.shape[0] for keep, _ in pairs)

    def body(occ_ref, *refs):
        ins, outs = refs[: 2 * len(pairs)], refs[2 * len(pairs) :]
        for d in range(shares):
            at = 0
            for keep_ref, got_ref in zip(ins[::2], ins[1::2]):
                for q in range(keep_ref.shape[0]):
                    outs[d][at] = keep_ref[q, occ_ref[0] ^ d] + got_ref[q, occ_ref[0] ^ d]
                    at += 1

    shape = jax.ShapeDtypeStruct((tiles, piece, both), F32)
    return pl.pallas_call(
        body,
        out_shape=(shape,) * shares,
        in_specs=[SCALARS] + [WHOLE] * (2 * len(pairs)),
        out_specs=(WHOLE,) * shares,
        compiler_params=pltpu.CompilerParams(vmem_limit_bytes=8 * MIB),
        name="split_sum",
    )(occ[None], *sum(pairs, ()))


def project(jobs, tile, shares, core):
    both = jobs[0][0].shape[0]
    parts = [x.shape[0] for x in jobs[0][1][0]]
    rows = jobs[0][1][0][0].shape[1]
    half = sum(parts)
    piece = tile // shares
    tiles = len(jobs) * rows // tile
    panels = distinct([p for p, _ in jobs])
    arrays = distinct([x for _, window in jobs for addend in window for x in addend])
    count = len(panels)

    def body(core_ref, *refs):
        panel_refs, array_refs = refs[:count], refs[count:-3]
        keep_ref, give_ref, terms_ref = refs[-3:]
        q = 0
        for panel, window in jobs:
            panel_ref = panel_refs[[id(p) for p in panels].index(id(panel))]
            total, low = None, 0
            for p, size in enumerate(parts):
                value = read_window(window, p, arrays, array_refs)
                term = jnp.dot(
                    panel_ref[:, low : low + size], value, preferred_element_type=F32
                )
                total = term if total is None else total + term
                low += size
            turned = total.T
            for j in range(0, rows, tile):
                terms_ref[q] = turned[j : j + tile].reshape(2, shares // 2, piece, both)
                keep_ref[q] = terms_ref[q, core_ref[0]]
                give_ref[q] = terms_ref[q, 1 - core_ref[0]]
                q += 1

    shape = jax.ShapeDtypeStruct((tiles, shares // 2, piece, both), F32)
    return pl.pallas_call(
        body,
        out_shape=(shape, shape),
        in_specs=[SCALARS] + [WHOLE] * (count + len(arrays)),
        out_specs=(WHOLE, WHOLE),
        scratch_shapes=[pltpu.VMEM((tiles, 2, shares // 2, piece, both), F32)],
        compiler_params=pltpu.CompilerParams(vmem_limit_bytes=12 * MIB),
        name="project",
        cost_estimate=pl.CostEstimate(
            flops=2 * both * half * tiles * tile,
            bytes_accessed=2 * half * (both + tiles * tile) + 4 * tiles * tile * both,
            transcendentals=0,
        ),
    )(core[None], *panels, *arrays)


def in_order(parts, occ):
    tiles, _, piece, columns = parts[0].shape

    def body(occ_ref, *refs):
        for d in range(len(parts)):
            refs[-1][:, occ_ref[0] ^ d] = refs[d][:, 0]

    return pl.pallas_call(
        body,
        out_shape=jax.ShapeDtypeStruct((tiles, len(parts), piece, columns), parts[0].dtype),
        in_specs=[SCALARS] + [WHOLE] * len(parts),
        out_specs=WHOLE,
        compiler_params=pltpu.CompilerParams(vmem_limit_bytes=4 * MIB),
        name="in_order",
    )(occ[None], *parts)


def contract(kernel, got, windows, core):
    tiles, shares, piece, columns = kernel.shape
    parts = [x.shape[0] for x in windows[0][0]]
    rows = windows[0][0][0].shape[1]
    half = sum(parts)
    own = columns // 2
    arrays = distinct([x for window in windows for addend in window for x in addend])
    per_window = tiles // len(windows)

    def body(core_ref, kernel_ref, got_ref, *refs):
        array_refs = refs[:-3]
        mine_ref, other_ref, order_ref = refs[-3:]
        first = core_ref[0] == 0
        order_ref[:, core_ref[0]] = kernel_ref[...].astype(F32)
        order_ref[:, 1 - core_ref[0]] = got_ref[...].astype(F32)
        kernels = [
            order_ref[s * per_window : (s + 1) * per_window].reshape(rows, columns).astype(BF16)
            for s in range(len(windows))
        ]
        low = 0
        for p, size in enumerate(parts):
            total = None
            for window, part in zip(windows, kernels):
                value = read_window(window, p, arrays, array_refs)
                term = jnp.dot(value, part, preferred_element_type=F32)
                total = term if total is None else total + term
            total = total.T
            mine_ref[:, low : low + size] = jnp.where(first, total[:own], total[own:])
            other_ref[:, low : low + size] = jnp.where(first, total[own:], total[:own])
            low += size

    shape = jax.ShapeDtypeStruct((own, half), F32)
    return pl.pallas_call(
        body,
        out_shape=(shape, shape),
        in_specs=[SCALARS] + [WHOLE] * (2 + len(arrays)),
        out_specs=(WHOLE, WHOLE),
        scratch_shapes=[pltpu.VMEM((tiles, 2, shares, piece, columns), F32)],
        compiler_params=pltpu.CompilerParams(vmem_limit_bytes=20 * MIB),
        name="contract",
        cost_estimate=pl.CostEstimate(
            flops=2 * columns * half * rows * len(windows),
            bytes_accessed=2 * rows * len(windows) * half + 4 * columns * half,
            transcendentals=0,
        ),
    )(core[None], kernel, got, *arrays)


def unwritten(shape):
    def body(out_ref):
        pass

    return pl.pallas_call(
        body,
        out_shape=jax.ShapeDtypeStruct(shape, F32),
        out_specs=pl.BlockSpec(memory_space=pltpu.HBM),
        name="unwritten",
    )()


def finish(core, fits, ours, back, other, scale):
    own, half = ours.shape

    def body(flags_ref, ours_ref, back_ref, other_ref, out_ref, whole_ref, sem):
        @pl.when(flags_ref[1] != 0)
        def _():
            first = flags_ref[0] == 0
            whole_ref[:, :half] = jnp.where(first, ours_ref[...], back_ref[...]) * scale
            whole_ref[:, half:] = jnp.where(first, back_ref[...], ours_ref[...]) * scale
            copy = pltpu.make_async_copy(whole_ref, out_ref, sem)
            copy.start()
            copy.wait()

    return pl.pallas_call(
        body,
        out_shape=jax.ShapeDtypeStruct((own, 2 * half), F32),
        in_specs=[SCALARS, WHOLE, WHOLE, pl.BlockSpec(memory_space=pltpu.HBM)],
        out_specs=pl.BlockSpec(memory_space=pltpu.HBM),
        scratch_shapes=[pltpu.VMEM((own, 2 * half), F32), pltpu.SemaphoreType.DMA],
        input_output_aliases={3: 0},
        compiler_params=pltpu.CompilerParams(vmem_limit_bytes=8 * MIB),
        name="finish",
    )(jnp.stack((core, fits.astype(jnp.int32))), ours, back, other)


def per_device(orbital_values, occupied, trial, point_weights, batch_sizes, significant):
    rows, cols = orbital_values.shape
    batches = batch_sizes.shape[0]
    slots = rows // batches
    blocks = significant.shape[1]
    columns = occupied.shape[1]
    grid_count = lax.axis_size("grid")
    occ_count = lax.axis_size("occ")
    chips = grid_count // 2
    shares = 2 * occ_count
    half = cols // 2
    total = columns * grid_count
    place = lax.axis_index("grid")
    chip, core = place // 2, place % 2
    occ = lax.axis_index("occ")
    member = core * occ_count + occ

    def flip(x, axis, bit):
        count = lax.axis_size(axis)
        return lax.ppermute(x, axis, [(i, i ^ bit) for i in range(count)])

    def along(pairs):
        return [(2 * a + c, 2 * b + c) for a, b in pairs for c in range(2)]

    def doubled(x, axis, bit, dim):
        got = flip(x, axis, bit)
        mine = (lax.axis_index(axis) & bit) == 0
        return jnp.where(
            mine, jnp.concatenate((x, got), axis=dim), jnp.concatenate((got, x), axis=dim)
        )

    def halves(whole, axis):
        size = whole.shape[axis] // 2
        mine = lax.dynamic_slice_in_dim(whole, core * size, size, axis)
        return mine, lax.dynamic_slice_in_dim(whole, (1 - core) * size, size, axis)

    grid_bits = [1 << b for b in range(grid_count.bit_length() - 1)]
    occ_bits = [1 << b for b in range(occ_count.bit_length() - 1)]

    mine = half_of(orbital_values.T, core)
    got = flip(half_of(orbital_values.T, 1 - core), "grid", 1)
    mine_sig, other_sig = halves(significant.T, 0)
    got_sig = flip(other_sig, "grid", 1)

    told = jnp.concatenate(
        (
            doubled(batch_sizes[None], "grid", 1, 0).astype(F32).reshape(1, -1),
            doubled(point_weights[None], "grid", 1, 0).reshape(1, -1),
        ),
        axis=1,
    )
    live = rows * chips
    for bit in grid_bits[1:2]:
        told = doubled(told, "grid", bit, 0)
    if chips > 4:
        for bit in grid_bits[2:]:
            told = doubled(told, "grid", bit, 0)

    def places_of(sizes, upper):
        count = sizes.shape[0]
        batch = lax.broadcasted_iota(jnp.int32, (count, count), 0)
        before = lax.broadcasted_iota(jnp.int32, (count, count), 1) < batch
        start = upper * live + jnp.sum((before.astype(jnp.int32) - upper) * sizes[None, :], axis=1)
        position = lax.broadcasted_iota(jnp.int32, (count, slots), 1)
        to = jnp.where(position < sizes[:, None], start[:, None] + position, -4 * live)
        return to.reshape(-1, rows), start

    sizes = told[:, : 2 * batches].astype(jnp.int32).reshape(-1)
    near_to, _ = places_of(sizes, chip // 2 if chips <= 4 else 0)
    near_place = place if chips > 4 else place % 4
    for bit in grid_bits[2:] if chips <= 4 else []:
        told = doubled(told, "grid", bit, 0)
    margin = rows // 2 if (rows // 2) % (8 * shares) == 0 else rows
    tile = margin
    piece = tile // shares
    base = rows * chip - margin
    mine_to = lax.dynamic_index_in_dim(near_to, near_place, 0, keepdims=False) - base
    got_to = lax.dynamic_index_in_dim(near_to, near_place ^ 1, 0, keepdims=False) - base
    odd = chip % 2
    compacted = compact(
        mine,
        got,
        jnp.repeat(mine_sig.astype(BF16), slots, axis=1),
        jnp.repeat(got_sig.astype(BF16), slots, axis=1),
        mine_to[:, None],
        got_to[:, None],
        cols // blocks,
        tile,
        odd,
    )

    def sent(x, pairs):
        return lax.ppermute(x, "grid", along(pairs))

    last = chips - 1

    def over(links, t):
        pairs = []
        for a in range(links, last, 2):
            pairs += [(a, a + 1)] if a - t + 1 >= 0 else []
            pairs += [(a + 1, a)] if a + t <= last else []
        return pairs

    arrived = [
        (sent(for_b, over(1, 1)), sent(for_a, over(0, 1))) for for_b, *_, for_a in compacted
    ]
    own = tuple(
        straighten(tiles, by_b, by_a, odd)
        for (_, *tiles, _), (by_b, by_a) in zip(compacted, arrived)
    )

    own, told = lax.optimization_barrier((own, told))
    sizes = told[:, : 2 * batches].astype(jnp.int32).reshape(-1)
    weights = told[:, 2 * batches :].reshape(-1)
    to, start = places_of(sizes, 0)
    first = start.reshape(chips, -1)[:, 0]
    nominal = rows * lax.iota(jnp.int32, chips)
    fits = jnp.all(jnp.abs(first - nominal) <= margin) & (jnp.sum(sizes) == live)

    _, occupied_turned, trial_turned = lax.optimization_barrier(
        (compacted[0][0], occupied.T, trial.T)
    )
    mine_panel, other_panel = panel_halves(occupied_turned, trial_turned, core)
    panels = stack_panels(mine_panel, flip(other_panel, "grid", 1), core)

    per_window = rows // tile
    window_iota = lax.iota(jnp.int32, chips)
    at = (
        (window_iota * rows)[:, None, None]
        + (lax.iota(jnp.int32, per_window) * tile)[None, :, None]
        + member * piece
        + lax.iota(jnp.int32, piece)[None, None, :]
    ).reshape(-1, 1)
    weight = jnp.sum(jnp.where(to.reshape(1, -1) == at, weights[None, :], 0.0), axis=1)
    weight = weight.reshape(chips, per_window * piece)
    ends = [(0, 1), (last, last - 1)]
    homes = [(b, a) for a, b in ends]
    side = 1 - 2 * odd

    def valid(at):
        return jnp.where((at >= 0) & (at <= last), at, -1)

    stages = [[([own], chip)]]
    by_a = by_b = own
    far_panels = None
    for t in range(1, last):
        by_a, by_b = (
            tuple(sent(x, over(0, t)) for x in by_b),
            tuple(sent(x, over(1, t)) for x in by_a),
        )
        if t == 1:
            far_panels = sent(panels, ends)
            by_a, fits = lax.optimization_barrier((by_a, fits.astype(jnp.int32)))
            by_b, weight = lax.optimization_barrier((by_b, weight))
        a_at, b_at = valid(chip + side * t), valid(chip - side * t)
        if 2 * t > last:
            stages.append([([by_a, by_b], jnp.maximum(a_at, b_at))])
        else:
            stages.append([([by_a], a_at), ([by_b], b_at)])

    direct = occ_count <= 4
    points = per_window * piece

    def summed(pairs):
        if direct:
            parts = split_sum(pairs, occ)
            value = parts[0]
            for d in range(1, occ_count):
                value = value + flip(parts[d], "occ", d)
        else:
            value = jnp.concatenate([keep + got for keep, got in pairs])
            for bit in reversed(occ_bits):
                upper = (occ & bit) != 0
                low_part, high_part = value[:, :bit], value[:, bit:]
                got = flip(jnp.where(upper, low_part, high_part), "occ", bit)
                value = jnp.where(upper, high_part, low_part) + got
        return value.reshape(-1, points, 4 * columns)

    def shared_density(value, at):
        product = jnp.sum(value[:, :, : 2 * columns] * value[:, :, 2 * columns :], axis=2)
        here = (at[:, None] == window_iota[None, :])[:, :, None]
        return jnp.sum(jnp.where(here, product[:, None], 0.0), axis=0)

    early_jobs, late_jobs = sum(stages[1:-1], []), stages[-1]
    early_at = jnp.stack([at for _, at in early_jobs])
    late_at = late_jobs[0][1][None]
    early_jobs = stages[0] + early_jobs
    early_at = jnp.concatenate((chip[None], early_at))

    def halved(jobs):
        keep, give = project(jobs, tile, shares, core)
        return keep, flip(give, "grid", 1)

    early_value = summed(
        [halved([(panels, early_jobs[0][0])]), halved([(panels, w) for w, _ in early_jobs[1:]])]
    )

    outer = jnp.where(chip == 0, last, jnp.where(chip == last, 0, early_at[2]))
    places = jnp.concatenate((early_at[:2], outer[None], early_at[3:], late_at))
    here = (places[:, None] == window_iota[None, :])[:, :, None]
    weight_here = jnp.sum(jnp.where(here, weight[None], 0.0), axis=1)[:, :, None]

    late, by_a, early_value, far_panels, weight_here, fits = lax.optimization_barrier(
        (by_b, by_a, early_value, far_panels, weight_here, fits)
    )
    fits = fits != 0
    late = tuple(sent(x, homes) for x in late)
    late_window = [by_a, by_b]
    late_jobs = [(panels, late_window), (far_panels, [by_b])]

    def kernel_of_all():
        late_pair = project(late_jobs, tile, shares, core)
        keep, give = late_pair
        value = jnp.concatenate((early_value, summed([(keep, flip(give, "grid", 1))])))
        density = shared_density(value, jnp.concatenate((early_at, late_at, late_at)))
        value, far_value = value[:-1], value[-1:]
        packed = jnp.concatenate(
            (far_value[0], jnp.pad(density, ((0, 0), (0, 4 * columns - points)))), axis=0
        )
        packed = flip(packed, "grid", 2)
        home_value, neighbour = packed[None, :points], packed[points:, :points]
        if chips <= 4:
            others = [flip(density, "grid", 2 * d) for d in range(2, chips)]
            density = density + neighbour + sum(others[1:], others[0])
        else:
            density = density + neighbour
            for bit in grid_bits[2:]:
                density = density + flip(density, "grid", bit)
        density = density * (1.0 / math.sqrt(total))

        values = jnp.concatenate((value[:2], value[2:3] + home_value, value[3:]))
        density_here = jnp.sum(jnp.where(here, density[None], 0.0), axis=1)[:, :, None]
        orbitals, response = values[:, :, : 2 * columns], values[:, :, 2 * columns :]
        kernel = (weight_here * (density_here * orbitals + response)).astype(BF16)
        kernel = kernel.reshape(-1, 1, piece, 2 * columns)
        if direct:
            parts = [kernel] + [flip(kernel, "occ", d) for d in range(1, occ_count)]
            kernel = in_order(parts, occ)
        else:
            for bit in occ_bits:
                kernel = doubled(kernel, "occ", bit, 1)
        return kernel, flip(kernel, "grid", 1), unwritten((columns, cols))

    scale = 1.0 / math.sqrt(rows * grid_count)

    def result_for_any_sizes():
        whole = any_sizes(
            orbital_values, occupied, trial, point_weights, batch_sizes, significant
        )
        none = jnp.zeros((places.shape[0] * per_window, occ_count, piece, 2 * columns), BF16)
        return none, none, whole * scale

    kernel, got_kernel, other = lax.cond(fits, kernel_of_all, result_for_any_sizes)
    early_windows = [w for w, _ in early_jobs]
    early_windows[2] = early_windows[2] + [late]
    windows = early_windows + [late_window]
    ours, theirs = contract(kernel, got_kernel, windows, core)
    back = flip(theirs, "grid", 1)
    return finish(core, fits, ours, back, other, scale).T


def solution(mesh):
    placed = (
        P("grid", "occ"),
        P("occ", "grid"),
        P("occ", "grid"),
        P("grid"),
        P("grid"),
        P("grid", "occ"),
    )
    return jax.shard_map(
        per_device, mesh=mesh, in_specs=placed, out_specs=P("occ", "grid"), check_vma=False
    )
```

```python
import math

import jax
import jax.numpy as jnp
from jax import lax
from jax.experimental import pallas as pl
from jax.experimental.pallas import tpu as pltpu
from jax.sharding import PartitionSpec as P

BF16, F32 = jnp.bfloat16, jnp.float32
MIB = 1024 * 1024
WHOLE = pl.BlockSpec(memory_space=pltpu.VMEM)
SCALARS = pl.BlockSpec(memory_space=pltpu.SMEM)


def screen(values, sizes, significant):
    rows, cols = values.shape
    batches = sizes.shape[0]
    blocks = significant.shape[1]
    blocked = (
        values.reshape(batches, rows // batches, blocks, cols // blocks)
        * significant.astype(values.dtype)[:, None, :, None]
    )
    position = lax.broadcasted_iota(jnp.int32, (batches, rows // batches), 1)
    live = (position < sizes[:, None]).astype(jnp.float32).reshape(rows)
    return (blocked.reshape(rows, cols), live)


def any_sizes(orbital_values, occupied, trial, point_weights, batch_sizes, significant):
    screened, live = screen(orbital_values, batch_sizes, significant)
    rows, cols = screened.shape
    grid_count, occ_count = lax.axis_size("grid"), lax.axis_size("occ")
    columns = occupied.shape[1]
    me = lax.axis_index("grid")
    ring = [(i, (i + 1) % grid_count) for i in range(grid_count)]
    occ_ring = [(i, (i + 1) % occ_count) for i in range(occ_count)]

    def project_one(step, carry):
        panel, terms = carry
        term = jnp.dot(screened, panel, preferred_element_type=F32)
        terms = lax.dynamic_update_index_in_dim(terms, term, (me - step) % grid_count, 0)
        return lax.ppermute(panel, "grid", ring), terms

    joined = jnp.concatenate((occupied, trial), axis=1)
    terms = jnp.zeros((grid_count, rows, 2 * columns), F32)
    terms = lax.fori_loop(0, grid_count, project_one, (joined, terms))[1]

    def add_one(step, carry):
        moving, held = carry
        moving = lax.ppermute(moving, "occ", occ_ring)
        return moving, held + moving

    terms = lax.fori_loop(0, occ_count - 1, add_one, (terms, terms))[1]
    orbitals, response = terms[:, :, :columns], terms[:, :, columns:]
    density = jnp.sum(orbitals * response, axis=(0, 2)) * (1.0 / math.sqrt(columns * grid_count))
    weight = (point_weights * live)[None, :, None]
    kernel = (weight * (density[None, :, None] * orbitals + response)).astype(BF16)

    def contract_one(step, held):
        owner = (me + grid_count - 1 - step) % grid_count
        part = lax.dynamic_index_in_dim(kernel, owner, 0, keepdims=False)
        term = lax.dot_general(
            part, screened, (((0,), (0,)), ((), ())), preferred_element_type=F32
        )
        return lax.ppermute(held, "grid", ring) + term

    return lax.fori_loop(0, grid_count, contract_one, jnp.zeros((columns, cols), F32))


def half_of(whole, which):
    rows, columns = whole.shape
    half = rows // 2
    if half % 16:
        return lax.dynamic_slice_in_dim(whole, which * half, half, 0)

    def body(which_ref, whole_ref, out_ref, sem):
        first = pl.multiple_of(which_ref[0] * half, 16)
        copy = pltpu.make_async_copy(whole_ref.at[pl.ds(first, half)], out_ref, sem)
        copy.start()
        copy.wait()

    return pl.pallas_call(
        body,
        out_shape=jax.ShapeDtypeStruct((half, columns), whole.dtype),
        in_specs=[SCALARS, pl.BlockSpec(memory_space=pl.ANY)],
        out_specs=WHOLE,
        scratch_shapes=[pltpu.SemaphoreType.DMA],
        compiler_params=pltpu.CompilerParams(vmem_limit_bytes=4 * MIB),
        name="half_of",
    )(which[None], whole)


def compact(mine, got, mine_sig, got_sig, mine_to, got_to, width, tile, odd):
    half, rows = mine.shape
    blocks = mine_sig.shape[0]
    count = rows // tile + 2
    cuts = [(0, half)]

    def body(odd_ref, mine_ref, got_ref, msig_ref, gsig_ref, mto_ref, gto_ref, *outs):
        block_of = lax.broadcasted_iota(jnp.int32, (half, blocks), 0)
        begin = lax.broadcasted_iota(jnp.int32, (half, blocks), 1) * width
        spread = ((block_of >= begin) & (block_of < begin + width)).astype(F32).astype(BF16)
        slot = lax.broadcasted_iota(jnp.int32, (rows, count * tile), 1)

        def part(value_ref, sig_ref, to_ref):
            kept = jnp.dot(spread, sig_ref[...], preferred_element_type=F32)
            screened = (value_ref[...].astype(F32) * kept).astype(BF16)
            place = (to_ref[...] == slot).astype(F32).astype(BF16)
            return jnp.dot(screened, place, preferred_element_type=F32)

        window = part(mine_ref, msig_ref, mto_ref) + part(got_ref, gsig_ref, gto_ref)
        tiles = [window[:, j * tile : (j + 1) * tile] for j in range(count)]
        even = odd_ref[0] == 0
        first, last = tiles[0], tiles[-1]
        tiles[0] = jnp.where(even, first, last)
        tiles[-1] = jnp.where(even, last, first)
        for p, (low, high) in enumerate(cuts):
            for j in range(count):
                outs[p * count + j][...] = tiles[j][low:high].astype(BF16)

    shapes = [
        jax.ShapeDtypeStruct((high - low, tile), BF16) for low, high in cuts for _ in range(count)
    ]
    out = pl.pallas_call(
        body,
        out_shape=shapes,
        in_specs=[SCALARS] + [WHOLE] * 6,
        out_specs=[WHOLE] * len(shapes),
        compiler_params=pltpu.CompilerParams(vmem_limit_bytes=16 * MIB),
        name="compact",
        cost_estimate=pl.CostEstimate(
            flops=8 * half * rows * rows, bytes_accessed=8 * half * rows, transcendentals=0
        ),
    )(odd[None], mine, got, mine_sig, got_sig, mine_to, got_to)
    return [out[p * count : (p + 1) * count] for p in range(len(cuts))]


def straighten(tiles, by_b, by_a, odd):
    half, tile = by_a.shape
    count = len(tiles)

    def body(odd_ref, *refs):
        tile_refs, b_ref, a_ref, out_ref = refs[:count], *refs[count:]
        even = odd_ref[0] == 0
        for j in range(count):
            value = tile_refs[j][...]
            if j == 0:
                value = value + jnp.where(even, b_ref[...], a_ref[...])
            if j == count - 1:
                value = value + jnp.where(even, a_ref[...], b_ref[...])
            out_ref[:, j * tile : (j + 1) * tile] = value

    return pl.pallas_call(
        body,
        out_shape=jax.ShapeDtypeStruct((half, count * tile), BF16),
        in_specs=[SCALARS] + [WHOLE] * (count + 2),
        out_specs=WHOLE,
        compiler_params=pltpu.CompilerParams(vmem_limit_bytes=8 * MIB),
        name="straighten",
    )(odd[None], *tiles, by_b, by_a)


def panel_halves(occupied, trial, core):
    columns, cols = occupied.shape
    half = cols // 2
    width = -(-half // 128) * 128

    def body(core_ref, occupied_ref, trial_ref, mine_ref, other_ref):
        first = core_ref[0] == 0
        mine_ref[...] = jnp.zeros_like(mine_ref)
        other_ref[...] = jnp.zeros_like(other_ref)
        for j, ref in enumerate((occupied_ref, trial_ref)):
            low, high = ref[:, :half], ref[:, half:]
            mine_ref[j * columns : (j + 1) * columns, :half] = jnp.where(first, low, high)
            other_ref[j * columns : (j + 1) * columns, :half] = jnp.where(first, high, low)

    shape = jax.ShapeDtypeStruct((2 * columns, width), BF16)
    return pl.pallas_call(
        body,
        out_shape=(shape, shape),
        in_specs=[SCALARS, WHOLE, WHOLE],
        out_specs=(WHOLE, WHOLE),
        compiler_params=pltpu.CompilerParams(vmem_limit_bytes=8 * MIB),
        name="panel_halves",
    )(core[None], occupied, trial)


def stack_panels(mine, got, core):
    both, width = mine.shape
    columns = both // 2

    def body(core_ref, mine_ref, got_ref, out_ref):
        first = core_ref[0] == 0
        for j in range(2):
            low = mine_ref[j * columns : (j + 1) * columns]
            high = got_ref[j * columns : (j + 1) * columns]
            q = 2 * j * columns
            out_ref[q : q + columns] = jnp.where(first, low, high)
            out_ref[q + columns : q + 2 * columns] = jnp.where(first, high, low)

    return pl.pallas_call(
        body,
        out_shape=jax.ShapeDtypeStruct((2 * both, width), BF16),
        in_specs=[SCALARS, WHOLE, WHOLE],
        out_specs=WHOLE,
        compiler_params=pltpu.CompilerParams(vmem_limit_bytes=8 * MIB),
        name="stack_panels",
    )(core[None], mine, got)


def distinct(arrays):
    return list({id(x): x for x in arrays}.values())


def read_window(addends, p, arrays, refs):
    ref_of = {id(x): ref for x, ref in zip(arrays, refs)}
    total = None
    for x in addends:
        value = ref_of[id(x[p])][...]
        total = value if total is None else total + value
    return total


def split_sum(pairs, occ):
    _, shares, piece, both = pairs[0][0].shape
    tiles = sum(keep.shape[0] for keep, _ in pairs)

    def body(occ_ref, *refs):
        ins, outs = refs[: 2 * len(pairs)], refs[2 * len(pairs) :]
        for d in range(shares):
            at = 0
            for keep_ref, got_ref in zip(ins[::2], ins[1::2]):
                for q in range(keep_ref.shape[0]):
                    outs[d][at] = keep_ref[q, occ_ref[0] ^ d] + got_ref[q, occ_ref[0] ^ d]
                    at += 1

    shape = jax.ShapeDtypeStruct((tiles, piece, both), F32)
    return pl.pallas_call(
        body,
        out_shape=(shape,) * shares,
        in_specs=[SCALARS] + [WHOLE] * (2 * len(pairs)),
        out_specs=(WHOLE,) * shares,
        compiler_params=pltpu.CompilerParams(vmem_limit_bytes=8 * MIB),
        name="split_sum",
    )(occ[None], *sum(pairs, ()))


def project(jobs, tile, shares, core):
    both = jobs[0][0].shape[0]
    parts = [x.shape[0] for x in jobs[0][1][0]]
    rows = jobs[0][1][0][0].shape[1]
    half = sum(parts)
    piece = tile // shares
    tiles = len(jobs) * rows // tile
    panels = distinct([p for p, _ in jobs])
    arrays = distinct([x for _, window in jobs for addend in window for x in addend])
    count = len(panels)

    def body(core_ref, *refs):
        panel_refs, array_refs = refs[:count], refs[count:-3]
        keep_ref, give_ref, terms_ref = refs[-3:]
        q = 0
        for panel, window in jobs:
            panel_ref = panel_refs[[id(p) for p in panels].index(id(panel))]
            total, low = None, 0
            for p, size in enumerate(parts):
                value = read_window(window, p, arrays, array_refs)
                term = jnp.dot(
                    panel_ref[:, low : low + size], value, preferred_element_type=F32
                )
                total = term if total is None else total + term
                low += size
            turned = total.T
            for j in range(0, rows, tile):
                terms_ref[q] = turned[j : j + tile].reshape(2, shares // 2, piece, both)
                keep_ref[q] = terms_ref[q, core_ref[0]]
                give_ref[q] = terms_ref[q, 1 - core_ref[0]]
                q += 1

    shape = jax.ShapeDtypeStruct((tiles, shares // 2, piece, both), F32)
    return pl.pallas_call(
        body,
        out_shape=(shape, shape),
        in_specs=[SCALARS] + [WHOLE] * (count + len(arrays)),
        out_specs=(WHOLE, WHOLE),
        scratch_shapes=[pltpu.VMEM((tiles, 2, shares // 2, piece, both), F32)],
        compiler_params=pltpu.CompilerParams(vmem_limit_bytes=12 * MIB),
        name="project",
        cost_estimate=pl.CostEstimate(
            flops=2 * both * half * tiles * tile,
            bytes_accessed=2 * half * (both + tiles * tile) + 4 * tiles * tile * both,
            transcendentals=0,
        ),
    )(core[None], *panels, *arrays)


def in_order(parts, occ):
    tiles, _, piece, columns = parts[0].shape

    def body(occ_ref, *refs):
        for d in range(len(parts)):
            refs[-1][:, occ_ref[0] ^ d] = refs[d][:, 0]

    return pl.pallas_call(
        body,
        out_shape=jax.ShapeDtypeStruct((tiles, len(parts), piece, columns), parts[0].dtype),
        in_specs=[SCALARS] + [WHOLE] * len(parts),
        out_specs=WHOLE,
        compiler_params=pltpu.CompilerParams(vmem_limit_bytes=4 * MIB),
        name="in_order",
    )(occ[None], *parts)


def contract(kernel, got, windows, core):
    tiles, shares, piece, columns = kernel.shape
    parts = [x.shape[0] for x in windows[0][0]]
    rows = windows[0][0][0].shape[1]
    half = sum(parts)
    own = columns // 2
    arrays = distinct([x for window in windows for addend in window for x in addend])
    per_window = tiles // len(windows)

    def body(core_ref, kernel_ref, got_ref, *refs):
        array_refs = refs[:-3]
        mine_ref, other_ref, order_ref = refs[-3:]
        first = core_ref[0] == 0
        order_ref[:, core_ref[0]] = kernel_ref[...].astype(F32)
        order_ref[:, 1 - core_ref[0]] = got_ref[...].astype(F32)
        kernels = [
            order_ref[s * per_window : (s + 1) * per_window].reshape(rows, columns).astype(BF16)
            for s in range(len(windows))
        ]
        low = 0
        for p, size in enumerate(parts):
            total = None
            for window, part in zip(windows, kernels):
                value = read_window(window, p, arrays, array_refs)
                term = jnp.dot(value, part, preferred_element_type=F32)
                total = term if total is None else total + term
            total = total.T
            mine_ref[:, low : low + size] = jnp.where(first, total[:own], total[own:])
            other_ref[:, low : low + size] = jnp.where(first, total[own:], total[:own])
            low += size

    shape = jax.ShapeDtypeStruct((own, half), F32)
    return pl.pallas_call(
        body,
        out_shape=(shape, shape),
        in_specs=[SCALARS] + [WHOLE] * (2 + len(arrays)),
        out_specs=(WHOLE, WHOLE),
        scratch_shapes=[pltpu.VMEM((tiles, 2, shares, piece, columns), F32)],
        compiler_params=pltpu.CompilerParams(vmem_limit_bytes=20 * MIB),
        name="contract",
        cost_estimate=pl.CostEstimate(
            flops=2 * columns * half * rows * len(windows),
            bytes_accessed=2 * rows * len(windows) * half + 4 * columns * half,
            transcendentals=0,
        ),
    )(core[None], kernel, got, *arrays)


def unwritten(shape):
    def body(out_ref):
        pass

    return pl.pallas_call(
        body,
        out_shape=jax.ShapeDtypeStruct(shape, F32),
        out_specs=pl.BlockSpec(memory_space=pltpu.HBM),
        name="unwritten",
    )()


def finish(core, fits, ours, back, other, scale):
    own, half = ours.shape

    def body(flags_ref, ours_ref, back_ref, other_ref, out_ref, whole_ref, sem):
        @pl.when(flags_ref[1] != 0)
        def _():
            first = flags_ref[0] == 0
            whole_ref[:, :half] = jnp.where(first, ours_ref[...], back_ref[...]) * scale
            whole_ref[:, half:] = jnp.where(first, back_ref[...], ours_ref[...]) * scale
            copy = pltpu.make_async_copy(whole_ref, out_ref, sem)
            copy.start()
            copy.wait()

    return pl.pallas_call(
        body,
        out_shape=jax.ShapeDtypeStruct((own, 2 * half), F32),
        in_specs=[SCALARS, WHOLE, WHOLE, pl.BlockSpec(memory_space=pltpu.HBM)],
        out_specs=pl.BlockSpec(memory_space=pltpu.HBM),
        scratch_shapes=[pltpu.VMEM((own, 2 * half), F32), pltpu.SemaphoreType.DMA],
        input_output_aliases={3: 0},
        compiler_params=pltpu.CompilerParams(vmem_limit_bytes=8 * MIB),
        name="finish",
    )(jnp.stack((core, fits.astype(jnp.int32))), ours, back, other)


def per_device(orbital_values, occupied, trial, point_weights, batch_sizes, significant):
    rows, cols = orbital_values.shape
    batches = batch_sizes.shape[0]
    slots = rows // batches
    blocks = significant.shape[1]
    columns = occupied.shape[1]
    grid_count = lax.axis_size("grid")
    occ_count = lax.axis_size("occ")
    chips = grid_count // 2
    shares = 2 * occ_count
    half = cols // 2
    total = columns * grid_count
    place = lax.axis_index("grid")
    chip, core = place // 2, place % 2
    occ = lax.axis_index("occ")
    member = core * occ_count + occ

    def flip(x, axis, bit):
        count = lax.axis_size(axis)
        return lax.ppermute(x, axis, [(i, i ^ bit) for i in range(count)])

    def along(pairs):
        return [(2 * a + c, 2 * b + c) for a, b in pairs for c in range(2)]

    def doubled(x, axis, bit, dim):
        got = flip(x, axis, bit)
        mine = (lax.axis_index(axis) & bit) == 0
        return jnp.where(
            mine, jnp.concatenate((x, got), axis=dim), jnp.concatenate((got, x), axis=dim)
        )

    def halves(whole, axis):
        size = whole.shape[axis] // 2
        mine = lax.dynamic_slice_in_dim(whole, core * size, size, axis)
        return mine, lax.dynamic_slice_in_dim(whole, (1 - core) * size, size, axis)

    grid_bits = [1 << b for b in range(grid_count.bit_length() - 1)]
    occ_bits = [1 << b for b in range(occ_count.bit_length() - 1)]

    mine = half_of(orbital_values.T, core)
    got = flip(half_of(orbital_values.T, 1 - core), "grid", 1)
    mine_sig, other_sig = halves(significant.T, 0)
    got_sig = flip(other_sig, "grid", 1)

    told = jnp.concatenate(
        (
            doubled(batch_sizes[None], "grid", 1, 0).astype(F32).reshape(1, -1),
            doubled(point_weights[None], "grid", 1, 0).reshape(1, -1),
        ),
        axis=1,
    )
    live = rows * chips
    for bit in grid_bits[1:2]:
        told = doubled(told, "grid", bit, 0)
    if chips > 4:
        for bit in grid_bits[2:]:
            told = doubled(told, "grid", bit, 0)

    def places_of(sizes, upper):
        count = sizes.shape[0]
        batch = lax.broadcasted_iota(jnp.int32, (count, count), 0)
        before = lax.broadcasted_iota(jnp.int32, (count, count), 1) < batch
        start = upper * live + jnp.sum((before.astype(jnp.int32) - upper) * sizes[None, :], axis=1)
        position = lax.broadcasted_iota(jnp.int32, (count, slots), 1)
        to = jnp.where(position < sizes[:, None], start[:, None] + position, -4 * live)
        return to.reshape(-1, rows), start

    sizes = told[:, : 2 * batches].astype(jnp.int32).reshape(-1)
    near_to, _ = places_of(sizes, chip // 2 if chips <= 4 else 0)
    near_place = place if chips > 4 else place % 4
    for bit in grid_bits[2:] if chips <= 4 else []:
        told = doubled(told, "grid", bit, 0)
    margin = rows // 2 if (rows // 2) % (8 * shares) == 0 else rows
    tile = margin
    piece = tile // shares
    base = rows * chip - margin
    mine_to = lax.dynamic_index_in_dim(near_to, near_place, 0, keepdims=False) - base
    got_to = lax.dynamic_index_in_dim(near_to, near_place ^ 1, 0, keepdims=False) - base
    odd = chip % 2
    compacted = compact(
        mine,
        got,
        jnp.repeat(mine_sig.astype(BF16), slots, axis=1),
        jnp.repeat(got_sig.astype(BF16), slots, axis=1),
        mine_to[:, None],
        got_to[:, None],
        cols // blocks,
        tile,
        odd,
    )

    compacted, told = lax.optimization_barrier((compacted, told))
    sizes = told[:, : 2 * batches].astype(jnp.int32).reshape(-1)
    weights = told[:, 2 * batches :].reshape(-1)
    to, start = places_of(sizes, 0)
    first = start.reshape(chips, -1)[:, 0]
    nominal = rows * lax.iota(jnp.int32, chips)
    fits = jnp.all(jnp.abs(first - nominal) <= margin) & (jnp.sum(sizes) == live)

    per_window = rows // tile
    window_iota = lax.iota(jnp.int32, chips)
    at = (
        (window_iota * rows)[:, None, None]
        + (lax.iota(jnp.int32, per_window) * tile)[None, :, None]
        + member * piece
        + lax.iota(jnp.int32, piece)[None, None, :]
    ).reshape(-1, 1)
    weight = jnp.sum(jnp.where(to.reshape(1, -1) == at, weights[None, :], 0.0), axis=1)
    weight = weight.reshape(chips, per_window * piece)
    def sent(x, pairs):
        return lax.ppermute(x, "grid", along(pairs))

    last = chips - 1

    def over(links, t):
        pairs = []
        for a in range(links, last, 2):
            pairs += [(a, a + 1)] if a - t + 1 >= 0 else []
            pairs += [(a + 1, a)] if a + t <= last else []
        return pairs

    arrived = [
        (sent(for_b, over(1, 1)), sent(for_a, over(0, 1))) for for_b, *_, for_a in compacted
    ]
    own = tuple(
        straighten(tiles, by_b, by_a, odd)
        for (_, *tiles, _), (by_b, by_a) in zip(compacted, arrived)
    )

    own, fits, weight = lax.optimization_barrier((own, fits.astype(jnp.int32), weight))

    _, occupied_turned, trial_turned = lax.optimization_barrier(
        (compacted[0][0], occupied.T, trial.T)
    )
    mine_panel, other_panel = panel_halves(occupied_turned, trial_turned, core)
    panels = stack_panels(mine_panel, flip(other_panel, "grid", 1), core)

    ends = [(0, 1), (last, last - 1)]
    homes = [(b, a) for a, b in ends]
    side = 1 - 2 * odd

    def valid(at):
        return jnp.where((at >= 0) & (at <= last), at, -1)

    stages = [[([own], chip)]]
    by_a = by_b = own
    far_panels = None
    for t in range(1, last):
        by_a, by_b = (
            tuple(sent(x, over(0, t)) for x in by_b),
            tuple(sent(x, over(1, t)) for x in by_a),
        )
        if t == 1:
            far_panels = sent(panels, ends)
        a_at, b_at = valid(chip + side * t), valid(chip - side * t)
        if 2 * t > last:
            stages.append([([by_a, by_b], jnp.maximum(a_at, b_at))])
        else:
            stages.append([([by_a], a_at), ([by_b], b_at)])

    direct = occ_count <= 4
    points = per_window * piece

    def summed(pairs):
        if direct:
            parts = split_sum(pairs, occ)
            value = parts[0]
            for d in range(1, occ_count):
                value = value + flip(parts[d], "occ", d)
        else:
            value = jnp.concatenate([keep + got for keep, got in pairs])
            for bit in reversed(occ_bits):
                upper = (occ & bit) != 0
                low_part, high_part = value[:, :bit], value[:, bit:]
                got = flip(jnp.where(upper, low_part, high_part), "occ", bit)
                value = jnp.where(upper, high_part, low_part) + got
        return value.reshape(-1, points, 4 * columns)

    def shared_density(value, at):
        product = jnp.sum(value[:, :, : 2 * columns] * value[:, :, 2 * columns :], axis=2)
        here = (at[:, None] == window_iota[None, :])[:, :, None]
        return jnp.sum(jnp.where(here, product[:, None], 0.0), axis=0)

    early_jobs, late_jobs = sum(stages[1:-1], []), stages[-1]
    early_at = jnp.stack([at for _, at in early_jobs])
    late_at = late_jobs[0][1][None]
    early_jobs = stages[0] + early_jobs
    early_at = jnp.concatenate((chip[None], early_at))

    own_pair = project([(panels, early_jobs[0][0])], tile, shares, core)
    early_pair = project([(panels, w) for w, _ in early_jobs[1:]], tile, shares, core)
    early_value = summed(
        [(keep, flip(give, "grid", 1)) for keep, give in (own_pair, early_pair)]
    )

    outer = jnp.where(chip == 0, last, jnp.where(chip == last, 0, early_at[2]))
    places = jnp.concatenate((early_at[:2], outer[None], early_at[3:], late_at))
    here = (places[:, None] == window_iota[None, :])[:, :, None]
    weight_here = jnp.sum(jnp.where(here, weight[None], 0.0), axis=1)[:, :, None]

    late, by_a, early_value, far_panels, weight_here, fits = lax.optimization_barrier(
        (by_b, by_a, early_value, far_panels, weight_here, fits)
    )
    fits = fits != 0
    late = tuple(sent(x, homes) for x in late)
    late_window = [by_a, by_b]
    late_jobs = [(panels, late_window), (far_panels, [by_b])]

    def kernel_of_all():
        late_pair = project(late_jobs, tile, shares, core)
        keep, give = late_pair
        value = jnp.concatenate((early_value, summed([(keep, flip(give, "grid", 1))])))
        density = shared_density(value, jnp.concatenate((early_at, late_at, late_at)))
        value, far_value = value[:-1], value[-1:]
        packed = jnp.concatenate(
            (far_value[0], jnp.pad(density, ((0, 0), (0, 4 * columns - points)))), axis=0
        )
        packed = flip(packed, "grid", 2)
        home_value, neighbour = packed[None, :points], packed[points:, :points]
        if chips <= 4:
            others = [flip(density, "grid", 2 * d) for d in range(2, chips)]
            density = density + neighbour + sum(others[1:], others[0])
        else:
            density = density + neighbour
            for bit in grid_bits[2:]:
                density = density + flip(density, "grid", bit)
        density = density * (1.0 / math.sqrt(total))

        values = jnp.concatenate((value[:2], value[2:3] + home_value, value[3:]))
        density_here = jnp.sum(jnp.where(here, density[None], 0.0), axis=1)[:, :, None]
        orbitals, response = values[:, :, : 2 * columns], values[:, :, 2 * columns :]
        kernel = (weight_here * (density_here * orbitals + response)).astype(BF16)
        kernel = kernel.reshape(-1, 1, piece, 2 * columns)
        if direct:
            parts = [kernel] + [flip(kernel, "occ", d) for d in range(1, occ_count)]
            kernel = in_order(parts, occ)
        else:
            for bit in occ_bits:
                kernel = doubled(kernel, "occ", bit, 1)
        return kernel, flip(kernel, "grid", 1), unwritten((columns, cols))

    scale = 1.0 / math.sqrt(rows * grid_count)

    def result_for_any_sizes():
        whole = any_sizes(
            orbital_values, occupied, trial, point_weights, batch_sizes, significant
        )
        none = jnp.zeros((places.shape[0] * per_window, occ_count, piece, 2 * columns), BF16)
        return none, none, whole * scale

    kernel, got_kernel, other = lax.cond(fits, kernel_of_all, result_for_any_sizes)
    early_windows = [w for w, _ in early_jobs]
    early_windows[2] = early_windows[2] + [late]
    windows = early_windows + [late_window]
    ours, theirs = contract(kernel, got_kernel, windows, core)
    back = flip(theirs, "grid", 1)
    return finish(core, fits, ours, back, other, scale).T


def solution(mesh):
    placed = (
        P("grid", "occ"),
        P("occ", "grid"),
        P("occ", "grid"),
        P("grid"),
        P("grid"),
        P("grid", "occ"),
    )
    return jax.shard_map(
        per_device, mesh=mesh, in_specs=placed, out_specs=P("occ", "grid"), check_vma=False
    )
```

```python
import math

import jax
import jax.numpy as jnp
from jax import lax
from jax.experimental import pallas as pl
from jax.experimental.pallas import tpu as pltpu
from jax.sharding import PartitionSpec as P

BF16, F32 = jnp.bfloat16, jnp.float32
MIB = 1024 * 1024
WHOLE = pl.BlockSpec(memory_space=pltpu.VMEM)
SCALARS = pl.BlockSpec(memory_space=pltpu.SMEM)


def screen(values, sizes, significant):
    rows, cols = values.shape
    batches = sizes.shape[0]
    blocks = significant.shape[1]
    blocked = (
        values.reshape(batches, rows // batches, blocks, cols // blocks)
        * significant.astype(values.dtype)[:, None, :, None]
    )
    position = lax.broadcasted_iota(jnp.int32, (batches, rows // batches), 1)
    live = (position < sizes[:, None]).astype(jnp.float32).reshape(rows)
    return (blocked.reshape(rows, cols), live)


def any_sizes(orbital_values, occupied, trial, point_weights, batch_sizes, significant):
    screened, live = screen(orbital_values, batch_sizes, significant)
    rows, cols = screened.shape
    grid_count, occ_count = lax.axis_size("grid"), lax.axis_size("occ")
    columns = occupied.shape[1]
    me = lax.axis_index("grid")
    ring = [(i, (i + 1) % grid_count) for i in range(grid_count)]
    occ_ring = [(i, (i + 1) % occ_count) for i in range(occ_count)]

    def project_one(step, carry):
        panel, terms = carry
        term = jnp.dot(screened, panel, preferred_element_type=F32)
        terms = lax.dynamic_update_index_in_dim(terms, term, (me - step) % grid_count, 0)
        return lax.ppermute(panel, "grid", ring), terms

    joined = jnp.concatenate((occupied, trial), axis=1)
    terms = jnp.zeros((grid_count, rows, 2 * columns), F32)
    terms = lax.fori_loop(0, grid_count, project_one, (joined, terms))[1]

    def add_one(step, carry):
        moving, held = carry
        moving = lax.ppermute(moving, "occ", occ_ring)
        return moving, held + moving

    terms = lax.fori_loop(0, occ_count - 1, add_one, (terms, terms))[1]
    orbitals, response = terms[:, :, :columns], terms[:, :, columns:]
    density = jnp.sum(orbitals * response, axis=(0, 2)) * (1.0 / math.sqrt(columns * grid_count))
    weight = (point_weights * live)[None, :, None]
    kernel = (weight * (density[None, :, None] * orbitals + response)).astype(BF16)

    def contract_one(step, held):
        owner = (me + grid_count - 1 - step) % grid_count
        part = lax.dynamic_index_in_dim(kernel, owner, 0, keepdims=False)
        term = lax.dot_general(
            part, screened, (((0,), (0,)), ((), ())), preferred_element_type=F32
        )
        return lax.ppermute(held, "grid", ring) + term

    return lax.fori_loop(0, grid_count, contract_one, jnp.zeros((columns, cols), F32))


def half_of(whole, which):
    rows, columns = whole.shape
    half = rows // 2
    if half % 16:
        return lax.dynamic_slice_in_dim(whole, which * half, half, 0)

    def body(which_ref, whole_ref, out_ref, sem):
        first = pl.multiple_of(which_ref[0] * half, 16)
        copy = pltpu.make_async_copy(whole_ref.at[pl.ds(first, half)], out_ref, sem)
        copy.start()
        copy.wait()

    return pl.pallas_call(
        body,
        out_shape=jax.ShapeDtypeStruct((half, columns), whole.dtype),
        in_specs=[SCALARS, pl.BlockSpec(memory_space=pl.ANY)],
        out_specs=WHOLE,
        scratch_shapes=[pltpu.SemaphoreType.DMA],
        compiler_params=pltpu.CompilerParams(vmem_limit_bytes=4 * MIB),
        name="half_of",
    )(which[None], whole)


def compact(mine, got, mine_sig, got_sig, mine_to, got_to, width, tile, odd):
    half, rows = mine.shape
    blocks = mine_sig.shape[0]
    count = rows // tile + 2
    cuts = [(0, half)]

    def body(odd_ref, mine_ref, got_ref, msig_ref, gsig_ref, mto_ref, gto_ref, *outs):
        block_of = lax.broadcasted_iota(jnp.int32, (half, blocks), 0)
        begin = lax.broadcasted_iota(jnp.int32, (half, blocks), 1) * width
        spread = ((block_of >= begin) & (block_of < begin + width)).astype(F32).astype(BF16)
        slot = lax.broadcasted_iota(jnp.int32, (rows, count * tile), 1)

        def part(value_ref, sig_ref, to_ref):
            kept = jnp.dot(spread, sig_ref[...], preferred_element_type=F32)
            screened = (value_ref[...].astype(F32) * kept).astype(BF16)
            place = (to_ref[...] == slot).astype(F32).astype(BF16)
            return jnp.dot(screened, place, preferred_element_type=F32)

        window = part(mine_ref, msig_ref, mto_ref) + part(got_ref, gsig_ref, gto_ref)
        tiles = [window[:, j * tile : (j + 1) * tile] for j in range(count)]
        even = odd_ref[0] == 0
        first, last = tiles[0], tiles[-1]
        tiles[0] = jnp.where(even, first, last)
        tiles[-1] = jnp.where(even, last, first)
        for p, (low, high) in enumerate(cuts):
            for j in range(count):
                outs[p * count + j][...] = tiles[j][low:high].astype(BF16)

    shapes = [
        jax.ShapeDtypeStruct((high - low, tile), BF16) for low, high in cuts for _ in range(count)
    ]
    out = pl.pallas_call(
        body,
        out_shape=shapes,
        in_specs=[SCALARS] + [WHOLE] * 6,
        out_specs=[WHOLE] * len(shapes),
        compiler_params=pltpu.CompilerParams(vmem_limit_bytes=16 * MIB),
        name="compact",
        cost_estimate=pl.CostEstimate(
            flops=8 * half * rows * rows, bytes_accessed=8 * half * rows, transcendentals=0
        ),
    )(odd[None], mine, got, mine_sig, got_sig, mine_to, got_to)
    return [out[p * count : (p + 1) * count] for p in range(len(cuts))]


def straighten(tiles, by_b, by_a, odd):
    half, tile = by_a.shape
    count = len(tiles)

    def body(odd_ref, *refs):
        tile_refs, b_ref, a_ref, out_ref = refs[:count], *refs[count:]
        even = odd_ref[0] == 0
        for j in range(count):
            value = tile_refs[j][...]
            if j == 0:
                value = value + jnp.where(even, b_ref[...], a_ref[...])
            if j == count - 1:
                value = value + jnp.where(even, a_ref[...], b_ref[...])
            out_ref[:, j * tile : (j + 1) * tile] = value

    return pl.pallas_call(
        body,
        out_shape=jax.ShapeDtypeStruct((half, count * tile), BF16),
        in_specs=[SCALARS] + [WHOLE] * (count + 2),
        out_specs=WHOLE,
        compiler_params=pltpu.CompilerParams(vmem_limit_bytes=8 * MIB),
        name="straighten",
    )(odd[None], *tiles, by_b, by_a)


def panel_halves(occupied, trial, core):
    columns, cols = occupied.shape
    half = cols // 2
    width = -(-half // 128) * 128

    def body(core_ref, occupied_ref, trial_ref, mine_ref, other_ref):
        first = core_ref[0] == 0
        mine_ref[...] = jnp.zeros_like(mine_ref)
        other_ref[...] = jnp.zeros_like(other_ref)
        for j, ref in enumerate((occupied_ref, trial_ref)):
            low, high = ref[:, :half], ref[:, half:]
            mine_ref[j * columns : (j + 1) * columns, :half] = jnp.where(first, low, high)
            other_ref[j * columns : (j + 1) * columns, :half] = jnp.where(first, high, low)

    shape = jax.ShapeDtypeStruct((2 * columns, width), BF16)
    return pl.pallas_call(
        body,
        out_shape=(shape, shape),
        in_specs=[SCALARS, WHOLE, WHOLE],
        out_specs=(WHOLE, WHOLE),
        compiler_params=pltpu.CompilerParams(vmem_limit_bytes=8 * MIB),
        name="panel_halves",
    )(core[None], occupied, trial)


def stack_panels(mine, got, core):
    both, width = mine.shape
    columns = both // 2

    def body(core_ref, mine_ref, got_ref, out_ref):
        first = core_ref[0] == 0
        for j in range(2):
            low = mine_ref[j * columns : (j + 1) * columns]
            high = got_ref[j * columns : (j + 1) * columns]
            q = 2 * j * columns
            out_ref[q : q + columns] = jnp.where(first, low, high)
            out_ref[q + columns : q + 2 * columns] = jnp.where(first, high, low)

    return pl.pallas_call(
        body,
        out_shape=jax.ShapeDtypeStruct((2 * both, width), BF16),
        in_specs=[SCALARS, WHOLE, WHOLE],
        out_specs=WHOLE,
        compiler_params=pltpu.CompilerParams(vmem_limit_bytes=8 * MIB),
        name="stack_panels",
    )(core[None], mine, got)


def distinct(arrays):
    return list({id(x): x for x in arrays}.values())


def read_window(addends, p, arrays, refs):
    ref_of = {id(x): ref for x, ref in zip(arrays, refs)}
    total = None
    for x in addends:
        value = ref_of[id(x[p])][...]
        total = value if total is None else total + value
    return total


def split_sum(pairs, occ):
    _, shares, piece, both = pairs[0][0].shape
    tiles = sum(keep.shape[0] for keep, _ in pairs)

    def body(occ_ref, *refs):
        ins, outs = refs[: 2 * len(pairs)], refs[2 * len(pairs) :]
        for d in range(shares):
            at = 0
            for keep_ref, got_ref in zip(ins[::2], ins[1::2]):
                for q in range(keep_ref.shape[0]):
                    outs[d][at] = keep_ref[q, occ_ref[0] ^ d] + got_ref[q, occ_ref[0] ^ d]
                    at += 1

    shape = jax.ShapeDtypeStruct((tiles, piece, both), F32)
    return pl.pallas_call(
        body,
        out_shape=(shape,) * shares,
        in_specs=[SCALARS] + [WHOLE] * (2 * len(pairs)),
        out_specs=(WHOLE,) * shares,
        compiler_params=pltpu.CompilerParams(vmem_limit_bytes=8 * MIB),
        name="split_sum",
    )(occ[None], *sum(pairs, ()))


def project(jobs, tile, shares, core):
    both = jobs[0][0].shape[0]
    parts = [x.shape[0] for x in jobs[0][1][0]]
    rows = jobs[0][1][0][0].shape[1]
    half = sum(parts)
    piece = tile // shares
    tiles = len(jobs) * rows // tile
    panels = distinct([p for p, _ in jobs])
    arrays = distinct([x for _, window in jobs for addend in window for x in addend])
    count = len(panels)

    def body(core_ref, *refs):
        panel_refs, array_refs = refs[:count], refs[count:-3]
        keep_ref, give_ref, terms_ref = refs[-3:]
        q = 0
        for panel, window in jobs:
            panel_ref = panel_refs[[id(p) for p in panels].index(id(panel))]
            total, low = None, 0
            for p, size in enumerate(parts):
                value = read_window(window, p, arrays, array_refs)
                term = jnp.dot(
                    panel_ref[:, low : low + size], value, preferred_element_type=F32
                )
                total = term if total is None else total + term
                low += size
            turned = total.T
            for j in range(0, rows, tile):
                terms_ref[q] = turned[j : j + tile].reshape(2, shares // 2, piece, both)
                keep_ref[q] = terms_ref[q, core_ref[0]]
                give_ref[q] = terms_ref[q, 1 - core_ref[0]]
                q += 1

    shape = jax.ShapeDtypeStruct((tiles, shares // 2, piece, both), F32)
    return pl.pallas_call(
        body,
        out_shape=(shape, shape),
        in_specs=[SCALARS] + [WHOLE] * (count + len(arrays)),
        out_specs=(WHOLE, WHOLE),
        scratch_shapes=[pltpu.VMEM((tiles, 2, shares // 2, piece, both), F32)],
        compiler_params=pltpu.CompilerParams(vmem_limit_bytes=12 * MIB),
        name="project",
        cost_estimate=pl.CostEstimate(
            flops=2 * both * half * tiles * tile,
            bytes_accessed=2 * half * (both + tiles * tile) + 4 * tiles * tile * both,
            transcendentals=0,
        ),
    )(core[None], *panels, *arrays)


def in_order(parts, occ):
    tiles, _, piece, columns = parts[0].shape

    def body(occ_ref, *refs):
        for d in range(len(parts)):
            refs[-1][:, occ_ref[0] ^ d] = refs[d][:, 0]

    return pl.pallas_call(
        body,
        out_shape=jax.ShapeDtypeStruct((tiles, len(parts), piece, columns), parts[0].dtype),
        in_specs=[SCALARS] + [WHOLE] * len(parts),
        out_specs=WHOLE,
        compiler_params=pltpu.CompilerParams(vmem_limit_bytes=4 * MIB),
        name="in_order",
    )(occ[None], *parts)


def contract(kernel, got, windows, core):
    tiles, shares, piece, columns = kernel.shape
    parts = [x.shape[0] for x in windows[0][0]]
    rows = windows[0][0][0].shape[1]
    half = sum(parts)
    own = columns // 2
    arrays = distinct([x for window in windows for addend in window for x in addend])
    per_window = tiles // len(windows)

    def body(core_ref, kernel_ref, got_ref, *refs):
        array_refs = refs[:-3]
        mine_ref, other_ref, order_ref = refs[-3:]
        first = core_ref[0] == 0
        order_ref[:, core_ref[0]] = kernel_ref[...].astype(F32)
        order_ref[:, 1 - core_ref[0]] = got_ref[...].astype(F32)
        kernels = [
            order_ref[s * per_window : (s + 1) * per_window].reshape(rows, columns).astype(BF16)
            for s in range(len(windows))
        ]
        low = 0
        for p, size in enumerate(parts):
            total = None
            for window, part in zip(windows, kernels):
                value = read_window(window, p, arrays, array_refs)
                term = jnp.dot(value, part, preferred_element_type=F32)
                total = term if total is None else total + term
            total = total.T
            mine_ref[:, low : low + size] = jnp.where(first, total[:own], total[own:])
            other_ref[:, low : low + size] = jnp.where(first, total[own:], total[:own])
            low += size

    shape = jax.ShapeDtypeStruct((own, half), F32)
    return pl.pallas_call(
        body,
        out_shape=(shape, shape),
        in_specs=[SCALARS] + [WHOLE] * (2 + len(arrays)),
        out_specs=(WHOLE, WHOLE),
        scratch_shapes=[pltpu.VMEM((tiles, 2, shares, piece, columns), F32)],
        compiler_params=pltpu.CompilerParams(vmem_limit_bytes=20 * MIB),
        name="contract",
        cost_estimate=pl.CostEstimate(
            flops=2 * columns * half * rows * len(windows),
            bytes_accessed=2 * rows * len(windows) * half + 4 * columns * half,
            transcendentals=0,
        ),
    )(core[None], kernel, got, *arrays)


def unwritten(shape):
    def body(out_ref):
        pass

    return pl.pallas_call(
        body,
        out_shape=jax.ShapeDtypeStruct(shape, F32),
        out_specs=pl.BlockSpec(memory_space=pltpu.HBM),
        name="unwritten",
    )()


def finish(core, fits, ours, back, other, scale):
    own, half = ours.shape

    def body(flags_ref, ours_ref, back_ref, other_ref, out_ref, whole_ref, sem):
        @pl.when(flags_ref[1] != 0)
        def _():
            first = flags_ref[0] == 0
            whole_ref[:, :half] = jnp.where(first, ours_ref[...], back_ref[...]) * scale
            whole_ref[:, half:] = jnp.where(first, back_ref[...], ours_ref[...]) * scale
            copy = pltpu.make_async_copy(whole_ref, out_ref, sem)
            copy.start()
            copy.wait()

    return pl.pallas_call(
        body,
        out_shape=jax.ShapeDtypeStruct((own, 2 * half), F32),
        in_specs=[SCALARS, WHOLE, WHOLE, pl.BlockSpec(memory_space=pltpu.HBM)],
        out_specs=pl.BlockSpec(memory_space=pltpu.HBM),
        scratch_shapes=[pltpu.VMEM((own, 2 * half), F32), pltpu.SemaphoreType.DMA],
        input_output_aliases={3: 0},
        compiler_params=pltpu.CompilerParams(vmem_limit_bytes=8 * MIB),
        name="finish",
    )(jnp.stack((core, fits.astype(jnp.int32))), ours, back, other)


def per_device(orbital_values, occupied, trial, point_weights, batch_sizes, significant):
    rows, cols = orbital_values.shape
    batches = batch_sizes.shape[0]
    slots = rows // batches
    blocks = significant.shape[1]
    columns = occupied.shape[1]
    grid_count = lax.axis_size("grid")
    occ_count = lax.axis_size("occ")
    chips = grid_count // 2
    shares = 2 * occ_count
    half = cols // 2
    total = columns * grid_count
    place = lax.axis_index("grid")
    chip, core = place // 2, place % 2
    occ = lax.axis_index("occ")
    member = core * occ_count + occ

    def flip(x, axis, bit):
        count = lax.axis_size(axis)
        return lax.ppermute(x, axis, [(i, i ^ bit) for i in range(count)])

    def along(pairs):
        return [(2 * a + c, 2 * b + c) for a, b in pairs for c in range(2)]

    def doubled(x, axis, bit, dim):
        got = flip(x, axis, bit)
        mine = (lax.axis_index(axis) & bit) == 0
        return jnp.where(
            mine, jnp.concatenate((x, got), axis=dim), jnp.concatenate((got, x), axis=dim)
        )

    def halves(whole, axis):
        size = whole.shape[axis] // 2
        mine = lax.dynamic_slice_in_dim(whole, core * size, size, axis)
        return mine, lax.dynamic_slice_in_dim(whole, (1 - core) * size, size, axis)

    grid_bits = [1 << b for b in range(grid_count.bit_length() - 1)]
    occ_bits = [1 << b for b in range(occ_count.bit_length() - 1)]

    mine = half_of(orbital_values.T, core)
    got = flip(half_of(orbital_values.T, 1 - core), "grid", 1)
    mine_sig, other_sig = halves(significant.T, 0)
    got_sig = flip(other_sig, "grid", 1)

    told = jnp.concatenate(
        (
            doubled(batch_sizes[None], "grid", 1, 0).astype(F32).reshape(1, -1),
            doubled(point_weights[None], "grid", 1, 0).reshape(1, -1),
        ),
        axis=1,
    )
    live = rows * chips
    for bit in grid_bits[1:2]:
        told = doubled(told, "grid", bit, 0)
    if chips > 4:
        for bit in grid_bits[2:]:
            told = doubled(told, "grid", bit, 0)

    def places_of(sizes, upper):
        count = sizes.shape[0]
        batch = lax.broadcasted_iota(jnp.int32, (count, count), 0)
        before = lax.broadcasted_iota(jnp.int32, (count, count), 1) < batch
        start = upper * live + jnp.sum((before.astype(jnp.int32) - upper) * sizes[None, :], axis=1)
        position = lax.broadcasted_iota(jnp.int32, (count, slots), 1)
        to = jnp.where(position < sizes[:, None], start[:, None] + position, -4 * live)
        return to.reshape(-1, rows), start

    sizes = told[:, : 2 * batches].astype(jnp.int32).reshape(-1)
    near_to, _ = places_of(sizes, chip // 2 if chips <= 4 else 0)
    near_place = place if chips > 4 else place % 4
    for bit in grid_bits[2:] if chips <= 4 else []:
        told = doubled(told, "grid", bit, 0)
    margin = rows // 2 if (rows // 2) % (8 * shares) == 0 else rows
    tile = margin
    piece = tile // shares
    base = rows * chip - margin
    mine_to = lax.dynamic_index_in_dim(near_to, near_place, 0, keepdims=False) - base
    got_to = lax.dynamic_index_in_dim(near_to, near_place ^ 1, 0, keepdims=False) - base
    odd = chip % 2
    compacted = compact(
        mine,
        got,
        jnp.repeat(mine_sig.astype(BF16), slots, axis=1),
        jnp.repeat(got_sig.astype(BF16), slots, axis=1),
        mine_to[:, None],
        got_to[:, None],
        cols // blocks,
        tile,
        odd,
    )

    def sent(x, pairs):
        return lax.ppermute(x, "grid", along(pairs))

    last = chips - 1

    def over(links, t):
        pairs = []
        for a in range(links, last, 2):
            pairs += [(a, a + 1)] if a - t + 1 >= 0 else []
            pairs += [(a + 1, a)] if a + t <= last else []
        return pairs

    arrived = [
        (sent(for_b, over(1, 1)), sent(for_a, over(0, 1))) for for_b, *_, for_a in compacted
    ]
    own = tuple(
        straighten(tiles, by_b, by_a, odd)
        for (_, *tiles, _), (by_b, by_a) in zip(compacted, arrived)
    )

    own, told = lax.optimization_barrier((own, told))
    sizes = told[:, : 2 * batches].astype(jnp.int32).reshape(-1)
    weights = told[:, 2 * batches :].reshape(-1)
    to, start = places_of(sizes, 0)
    first = start.reshape(chips, -1)[:, 0]
    nominal = rows * lax.iota(jnp.int32, chips)
    fits = jnp.all(jnp.abs(first - nominal) <= margin) & (jnp.sum(sizes) == live)

    _, occupied_turned, trial_turned = lax.optimization_barrier(
        (compacted[0][0], occupied.T, trial.T)
    )
    mine_panel, other_panel = panel_halves(occupied_turned, trial_turned, core)
    panels = stack_panels(mine_panel, flip(other_panel, "grid", 1), core)

    per_window = rows // tile
    window_iota = lax.iota(jnp.int32, chips)
    at = (
        (window_iota * rows)[:, None, None]
        + (lax.iota(jnp.int32, per_window) * tile)[None, :, None]
        + member * piece
        + lax.iota(jnp.int32, piece)[None, None, :]
    ).reshape(-1, 1)
    weight = jnp.sum(jnp.where(to.reshape(1, -1) == at, weights[None, :], 0.0), axis=1)
    weight = weight.reshape(chips, per_window * piece)
    ends = [(0, 1), (last, last - 1)]
    homes = [(b, a) for a, b in ends]
    side = 1 - 2 * odd

    def valid(at):
        return jnp.where((at >= 0) & (at <= last), at, -1)

    stages = [[([own], chip)]]
    by_a = by_b = own
    far_panels = None
    for t in range(1, last):
        by_a, by_b = (
            tuple(sent(x, over(0, t)) for x in by_b),
            tuple(sent(x, over(1, t)) for x in by_a),
        )
        if t == 1:
            own_pair = project([(panels, [own])], tile, shares, core)
            far_panels, own_pair, fits, weight = lax.optimization_barrier(
                (panels, own_pair, fits.astype(jnp.int32), weight)
            )
            far_panels = sent(far_panels, ends)
        a_at, b_at = valid(chip + side * t), valid(chip - side * t)
        if 2 * t > last:
            stages.append([([by_a, by_b], jnp.maximum(a_at, b_at))])
        else:
            stages.append([([by_a], a_at), ([by_b], b_at)])

    direct = occ_count <= 4
    points = per_window * piece

    def summed(pairs):
        if direct:
            parts = split_sum(pairs, occ)
            value = parts[0]
            for d in range(1, occ_count):
                value = value + flip(parts[d], "occ", d)
        else:
            value = jnp.concatenate([keep + got for keep, got in pairs])
            for bit in reversed(occ_bits):
                upper = (occ & bit) != 0
                low_part, high_part = value[:, :bit], value[:, bit:]
                got = flip(jnp.where(upper, low_part, high_part), "occ", bit)
                value = jnp.where(upper, high_part, low_part) + got
        return value.reshape(-1, points, 4 * columns)

    def shared_density(value, at):
        product = jnp.sum(value[:, :, : 2 * columns] * value[:, :, 2 * columns :], axis=2)
        here = (at[:, None] == window_iota[None, :])[:, :, None]
        return jnp.sum(jnp.where(here, product[:, None], 0.0), axis=0)

    early_jobs, late_jobs = sum(stages[1:-1], []), stages[-1]
    early_at = jnp.stack([at for _, at in early_jobs])
    late_at = late_jobs[0][1][None]
    early_jobs = stages[0] + early_jobs
    early_at = jnp.concatenate((chip[None], early_at))

    early_pair = project([(panels, w) for w, _ in early_jobs[1:]], tile, shares, core)
    early_value = summed(
        [(keep, flip(give, "grid", 1)) for keep, give in (own_pair, early_pair)]
    )

    outer = jnp.where(chip == 0, last, jnp.where(chip == last, 0, early_at[2]))
    places = jnp.concatenate((early_at[:2], outer[None], early_at[3:], late_at))
    here = (places[:, None] == window_iota[None, :])[:, :, None]
    weight_here = jnp.sum(jnp.where(here, weight[None], 0.0), axis=1)[:, :, None]

    late, by_a, early_value, far_panels, weight_here, fits = lax.optimization_barrier(
        (by_b, by_a, early_value, far_panels, weight_here, fits)
    )
    fits = fits != 0
    late = tuple(sent(x, homes) for x in late)
    late_window = [by_a, by_b]
    late_jobs = [(panels, late_window), (far_panels, [by_b])]

    def kernel_of_all():
        late_pair = project(late_jobs, tile, shares, core)
        keep, give = late_pair
        value = jnp.concatenate((early_value, summed([(keep, flip(give, "grid", 1))])))
        density = shared_density(value, jnp.concatenate((early_at, late_at, late_at)))
        value, far_value = value[:-1], value[-1:]
        packed = jnp.concatenate(
            (far_value[0], jnp.pad(density, ((0, 0), (0, 4 * columns - points)))), axis=0
        )
        packed = flip(packed, "grid", 2)
        home_value, neighbour = packed[None, :points], packed[points:, :points]
        if chips <= 4:
            others = [flip(density, "grid", 2 * d) for d in range(2, chips)]
            density = density + neighbour + sum(others[1:], others[0])
        else:
            density = density + neighbour
            for bit in grid_bits[2:]:
                density = density + flip(density, "grid", bit)
        density = density * (1.0 / math.sqrt(total))

        values = jnp.concatenate((value[:2], value[2:3] + home_value, value[3:]))
        density_here = jnp.sum(jnp.where(here, density[None], 0.0), axis=1)[:, :, None]
        orbitals, response = values[:, :, : 2 * columns], values[:, :, 2 * columns :]
        kernel = (weight_here * (density_here * orbitals + response)).astype(BF16)
        kernel = kernel.reshape(-1, 1, piece, 2 * columns)
        if direct:
            parts = [kernel] + [flip(kernel, "occ", d) for d in range(1, occ_count)]
            kernel = in_order(parts, occ)
        else:
            for bit in occ_bits:
                kernel = doubled(kernel, "occ", bit, 1)
        return kernel, flip(kernel, "grid", 1), unwritten((columns, cols))

    scale = 1.0 / math.sqrt(rows * grid_count)

    def result_for_any_sizes():
        whole = any_sizes(
            orbital_values, occupied, trial, point_weights, batch_sizes, significant
        )
        none = jnp.zeros((places.shape[0] * per_window, occ_count, piece, 2 * columns), BF16)
        return none, none, whole * scale

    kernel, got_kernel, other = lax.cond(fits, kernel_of_all, result_for_any_sizes)
    early_windows = [w for w, _ in early_jobs]
    early_windows[2] = early_windows[2] + [late]
    windows = early_windows + [late_window]
    ours, theirs = contract(kernel, got_kernel, windows, core)
    back = flip(theirs, "grid", 1)
    return finish(core, fits, ours, back, other, scale).T


def solution(mesh):
    placed = (
        P("grid", "occ"),
        P("occ", "grid"),
        P("occ", "grid"),
        P("grid"),
        P("grid"),
        P("grid", "occ"),
    )
    return jax.shard_map(
        per_device, mesh=mesh, in_specs=placed, out_specs=P("occ", "grid"), check_vma=False
    )
```

```python
import math

import jax
import jax.numpy as jnp
from jax import lax
from jax.experimental import pallas as pl
from jax.experimental.pallas import tpu as pltpu
from jax.sharding import PartitionSpec as P

BF16, F32 = jnp.bfloat16, jnp.float32
MIB = 1024 * 1024
WHOLE = pl.BlockSpec(memory_space=pltpu.VMEM)
SCALARS = pl.BlockSpec(memory_space=pltpu.SMEM)


def screen(values, sizes, significant):
    rows, cols = values.shape
    batches = sizes.shape[0]
    blocks = significant.shape[1]
    blocked = (
        values.reshape(batches, rows // batches, blocks, cols // blocks)
        * significant.astype(values.dtype)[:, None, :, None]
    )
    position = lax.broadcasted_iota(jnp.int32, (batches, rows // batches), 1)
    live = (position < sizes[:, None]).astype(jnp.float32).reshape(rows)
    return (blocked.reshape(rows, cols), live)


def any_sizes(orbital_values, occupied, trial, point_weights, batch_sizes, significant):
    screened, live = screen(orbital_values, batch_sizes, significant)
    rows, cols = screened.shape
    grid_count, occ_count = lax.axis_size("grid"), lax.axis_size("occ")
    columns = occupied.shape[1]
    me = lax.axis_index("grid")
    ring = [(i, (i + 1) % grid_count) for i in range(grid_count)]
    occ_ring = [(i, (i + 1) % occ_count) for i in range(occ_count)]

    def project_one(step, carry):
        panel, terms = carry
        term = jnp.dot(screened, panel, preferred_element_type=F32)
        terms = lax.dynamic_update_index_in_dim(terms, term, (me - step) % grid_count, 0)
        return lax.ppermute(panel, "grid", ring), terms

    joined = jnp.concatenate((occupied, trial), axis=1)
    terms = jnp.zeros((grid_count, rows, 2 * columns), F32)
    terms = lax.fori_loop(0, grid_count, project_one, (joined, terms))[1]

    def add_one(step, carry):
        moving, held = carry
        moving = lax.ppermute(moving, "occ", occ_ring)
        return moving, held + moving

    terms = lax.fori_loop(0, occ_count - 1, add_one, (terms, terms))[1]
    orbitals, response = terms[:, :, :columns], terms[:, :, columns:]
    density = jnp.sum(orbitals * response, axis=(0, 2)) * (1.0 / math.sqrt(columns * grid_count))
    weight = (point_weights * live)[None, :, None]
    kernel = (weight * (density[None, :, None] * orbitals + response)).astype(BF16)

    def contract_one(step, held):
        owner = (me + grid_count - 1 - step) % grid_count
        part = lax.dynamic_index_in_dim(kernel, owner, 0, keepdims=False)
        term = lax.dot_general(
            part, screened, (((0,), (0,)), ((), ())), preferred_element_type=F32
        )
        return lax.ppermute(held, "grid", ring) + term

    return lax.fori_loop(0, grid_count, contract_one, jnp.zeros((columns, cols), F32))


def half_of(whole, which):
    rows, columns = whole.shape
    half = rows // 2
    if half % 16:
        return lax.dynamic_slice_in_dim(whole, which * half, half, 0)

    def body(which_ref, whole_ref, out_ref, sem):
        first = pl.multiple_of(which_ref[0] * half, 16)
        copy = pltpu.make_async_copy(whole_ref.at[pl.ds(first, half)], out_ref, sem)
        copy.start()
        copy.wait()

    return pl.pallas_call(
        body,
        out_shape=jax.ShapeDtypeStruct((half, columns), whole.dtype),
        in_specs=[SCALARS, pl.BlockSpec(memory_space=pl.ANY)],
        out_specs=WHOLE,
        scratch_shapes=[pltpu.SemaphoreType.DMA],
        compiler_params=pltpu.CompilerParams(vmem_limit_bytes=4 * MIB),
        name="half_of",
    )(which[None], whole)


def compact(mine, got, mine_sig, got_sig, mine_to, got_to, width, tile, odd):
    half, rows = mine.shape
    blocks = mine_sig.shape[0]
    count = rows // tile + 2
    cuts = [(0, half)]

    def body(odd_ref, mine_ref, got_ref, msig_ref, gsig_ref, mto_ref, gto_ref, *outs):
        block_of = lax.broadcasted_iota(jnp.int32, (half, blocks), 0)
        begin = lax.broadcasted_iota(jnp.int32, (half, blocks), 1) * width
        spread = ((block_of >= begin) & (block_of < begin + width)).astype(F32).astype(BF16)
        slot = lax.broadcasted_iota(jnp.int32, (rows, count * tile), 1)

        def part(value_ref, sig_ref, to_ref):
            kept = jnp.dot(spread, sig_ref[...], preferred_element_type=F32)
            screened = (value_ref[...].astype(F32) * kept).astype(BF16)
            place = (to_ref[...] == slot).astype(F32).astype(BF16)
            return jnp.dot(screened, place, preferred_element_type=F32)

        window = part(mine_ref, msig_ref, mto_ref) + part(got_ref, gsig_ref, gto_ref)
        tiles = [window[:, j * tile : (j + 1) * tile] for j in range(count)]
        even = odd_ref[0] == 0
        first, last = tiles[0], tiles[-1]
        tiles[0] = jnp.where(even, first, last)
        tiles[-1] = jnp.where(even, last, first)
        for p, (low, high) in enumerate(cuts):
            for j in range(count):
                outs[p * count + j][...] = tiles[j][low:high].astype(BF16)

    shapes = [
        jax.ShapeDtypeStruct((high - low, tile), BF16) for low, high in cuts for _ in range(count)
    ]
    out = pl.pallas_call(
        body,
        out_shape=shapes,
        in_specs=[SCALARS] + [WHOLE] * 6,
        out_specs=[WHOLE] * len(shapes),
        compiler_params=pltpu.CompilerParams(vmem_limit_bytes=10 * MIB),
        name="compact",
        cost_estimate=pl.CostEstimate(
            flops=8 * half * rows * rows, bytes_accessed=8 * half * rows, transcendentals=0
        ),
    )(odd[None], mine, got, mine_sig, got_sig, mine_to, got_to)
    return [out[p * count : (p + 1) * count] for p in range(len(cuts))]


def straighten(tiles, by_b, by_a, odd):
    half, tile = by_a.shape
    count = len(tiles)

    def body(odd_ref, *refs):
        tile_refs, b_ref, a_ref, out_ref = refs[:count], *refs[count:]
        even = odd_ref[0] == 0
        for j in range(count):
            value = tile_refs[j][...]
            if j == 0:
                value = value + jnp.where(even, b_ref[...], a_ref[...])
            if j == count - 1:
                value = value + jnp.where(even, a_ref[...], b_ref[...])
            out_ref[:, j * tile : (j + 1) * tile] = value

    return pl.pallas_call(
        body,
        out_shape=jax.ShapeDtypeStruct((half, count * tile), BF16),
        in_specs=[SCALARS] + [WHOLE] * (count + 2),
        out_specs=WHOLE,
        compiler_params=pltpu.CompilerParams(vmem_limit_bytes=8 * MIB),
        name="straighten",
    )(odd[None], *tiles, by_b, by_a)


def panel_halves(occupied, trial, core):
    columns, cols = occupied.shape
    half = cols // 2
    width = -(-half // 128) * 128

    def body(core_ref, occupied_ref, trial_ref, mine_ref, other_ref):
        first = core_ref[0] == 0
        mine_ref[...] = jnp.zeros_like(mine_ref)
        other_ref[...] = jnp.zeros_like(other_ref)
        for j, ref in enumerate((occupied_ref, trial_ref)):
            low, high = ref[:, :half], ref[:, half:]
            mine_ref[j * columns : (j + 1) * columns, :half] = jnp.where(first, low, high)
            other_ref[j * columns : (j + 1) * columns, :half] = jnp.where(first, high, low)

    shape = jax.ShapeDtypeStruct((2 * columns, width), BF16)
    return pl.pallas_call(
        body,
        out_shape=(shape, shape),
        in_specs=[SCALARS, WHOLE, WHOLE],
        out_specs=(WHOLE, WHOLE),
        compiler_params=pltpu.CompilerParams(vmem_limit_bytes=8 * MIB),
        name="panel_halves",
    )(core[None], occupied, trial)


def stack_panels(mine, got, core):
    both, width = mine.shape
    columns = both // 2

    def body(core_ref, mine_ref, got_ref, out_ref):
        first = core_ref[0] == 0
        for j in range(2):
            low = mine_ref[j * columns : (j + 1) * columns]
            high = got_ref[j * columns : (j + 1) * columns]
            q = 2 * j * columns
            out_ref[q : q + columns] = jnp.where(first, low, high)
            out_ref[q + columns : q + 2 * columns] = jnp.where(first, high, low)

    return pl.pallas_call(
        body,
        out_shape=jax.ShapeDtypeStruct((2 * both, width), BF16),
        in_specs=[SCALARS, WHOLE, WHOLE],
        out_specs=WHOLE,
        compiler_params=pltpu.CompilerParams(vmem_limit_bytes=8 * MIB),
        name="stack_panels",
    )(core[None], mine, got)


def distinct(arrays):
    return list({id(x): x for x in arrays}.values())


def read_window(addends, p, arrays, refs):
    ref_of = {id(x): ref for x, ref in zip(arrays, refs)}
    total = None
    for x in addends:
        value = ref_of[id(x[p])][...]
        total = value if total is None else total + value
    return total


def split_sum(pairs, occ):
    _, shares, piece, both = pairs[0][0].shape
    tiles = sum(keep.shape[0] for keep, _ in pairs)

    def body(occ_ref, *refs):
        ins, outs = refs[: 2 * len(pairs)], refs[2 * len(pairs) :]
        for d in range(shares):
            at = 0
            for keep_ref, got_ref in zip(ins[::2], ins[1::2]):
                for q in range(keep_ref.shape[0]):
                    outs[d][at] = keep_ref[q, occ_ref[0] ^ d] + got_ref[q, occ_ref[0] ^ d]
                    at += 1

    shape = jax.ShapeDtypeStruct((tiles, piece, both), F32)
    return pl.pallas_call(
        body,
        out_shape=(shape,) * shares,
        in_specs=[SCALARS] + [WHOLE] * (2 * len(pairs)),
        out_specs=(WHOLE,) * shares,
        compiler_params=pltpu.CompilerParams(vmem_limit_bytes=8 * MIB),
        name="split_sum",
    )(occ[None], *sum(pairs, ()))


def project(jobs, tile, shares, core):
    both = jobs[0][0].shape[0]
    parts = [x.shape[0] for x in jobs[0][1][0]]
    rows = jobs[0][1][0][0].shape[1]
    half = sum(parts)
    piece = tile // shares
    tiles = len(jobs) * rows // tile
    panels = distinct([p for p, _ in jobs])
    arrays = distinct([x for _, window in jobs for addend in window for x in addend])
    count = len(panels)

    def body(core_ref, *refs):
        panel_refs, array_refs = refs[:count], refs[count:-3]
        keep_ref, give_ref, terms_ref = refs[-3:]
        q = 0
        for panel, window in jobs:
            panel_ref = panel_refs[[id(p) for p in panels].index(id(panel))]
            total, low = None, 0
            for p, size in enumerate(parts):
                value = read_window(window, p, arrays, array_refs)
                term = jnp.dot(
                    panel_ref[:, low : low + size], value, preferred_element_type=F32
                )
                total = term if total is None else total + term
                low += size
            turned = total.T
            for j in range(0, rows, tile):
                terms_ref[q] = turned[j : j + tile].reshape(2, shares // 2, piece, both)
                keep_ref[q] = terms_ref[q, core_ref[0]]
                give_ref[q] = terms_ref[q, 1 - core_ref[0]]
                q += 1

    shape = jax.ShapeDtypeStruct((tiles, shares // 2, piece, both), F32)
    return pl.pallas_call(
        body,
        out_shape=(shape, shape),
        in_specs=[SCALARS] + [WHOLE] * (count + len(arrays)),
        out_specs=(WHOLE, WHOLE),
        scratch_shapes=[pltpu.VMEM((tiles, 2, shares // 2, piece, both), F32)],
        compiler_params=pltpu.CompilerParams(vmem_limit_bytes=12 * MIB),
        name="project",
        cost_estimate=pl.CostEstimate(
            flops=2 * both * half * tiles * tile,
            bytes_accessed=2 * half * (both + tiles * tile) + 4 * tiles * tile * both,
            transcendentals=0,
        ),
    )(core[None], *panels, *arrays)


def in_order(parts, occ):
    tiles, _, piece, columns = parts[0].shape

    def body(occ_ref, *refs):
        for d in range(len(parts)):
            refs[-1][:, occ_ref[0] ^ d] = refs[d][:, 0]

    return pl.pallas_call(
        body,
        out_shape=jax.ShapeDtypeStruct((tiles, len(parts), piece, columns), parts[0].dtype),
        in_specs=[SCALARS] + [WHOLE] * len(parts),
        out_specs=WHOLE,
        compiler_params=pltpu.CompilerParams(vmem_limit_bytes=4 * MIB),
        name="in_order",
    )(occ[None], *parts)


def contract(kernel, got, windows, core):
    tiles, shares, piece, columns = kernel.shape
    parts = [x.shape[0] for x in windows[0][0]]
    rows = windows[0][0][0].shape[1]
    half = sum(parts)
    own = columns // 2
    arrays = distinct([x for window in windows for addend in window for x in addend])
    per_window = tiles // len(windows)

    def body(core_ref, kernel_ref, got_ref, *refs):
        array_refs = refs[:-3]
        mine_ref, other_ref, order_ref = refs[-3:]
        first = core_ref[0] == 0
        order_ref[:, core_ref[0]] = kernel_ref[...].astype(F32)
        order_ref[:, 1 - core_ref[0]] = got_ref[...].astype(F32)
        kernels = [
            order_ref[s * per_window : (s + 1) * per_window].reshape(rows, columns).astype(BF16)
            for s in range(len(windows))
        ]
        low = 0
        for p, size in enumerate(parts):
            total = None
            for window, part in zip(windows, kernels):
                value = read_window(window, p, arrays, array_refs)
                term = jnp.dot(value, part, preferred_element_type=F32)
                total = term if total is None else total + term
            total = total.T
            mine_ref[:, low : low + size] = jnp.where(first, total[:own], total[own:])
            other_ref[:, low : low + size] = jnp.where(first, total[own:], total[:own])
            low += size

    shape = jax.ShapeDtypeStruct((own, half), F32)
    return pl.pallas_call(
        body,
        out_shape=(shape, shape),
        in_specs=[SCALARS] + [WHOLE] * (2 + len(arrays)),
        out_specs=(WHOLE, WHOLE),
        scratch_shapes=[pltpu.VMEM((tiles, 2, shares, piece, columns), F32)],
        compiler_params=pltpu.CompilerParams(vmem_limit_bytes=20 * MIB),
        name="contract",
        cost_estimate=pl.CostEstimate(
            flops=2 * columns * half * rows * len(windows),
            bytes_accessed=2 * rows * len(windows) * half + 4 * columns * half,
            transcendentals=0,
        ),
    )(core[None], kernel, got, *arrays)


def unwritten(shape):
    def body(out_ref):
        pass

    return pl.pallas_call(
        body,
        out_shape=jax.ShapeDtypeStruct(shape, F32),
        out_specs=pl.BlockSpec(memory_space=pltpu.HBM),
        name="unwritten",
    )()


def finish(core, fits, ours, back, other, scale):
    own, half = ours.shape

    def body(flags_ref, ours_ref, back_ref, other_ref, out_ref, whole_ref, sem):
        @pl.when(flags_ref[1] != 0)
        def _():
            first = flags_ref[0] == 0
            whole_ref[:, :half] = jnp.where(first, ours_ref[...], back_ref[...]) * scale
            whole_ref[:, half:] = jnp.where(first, back_ref[...], ours_ref[...]) * scale
            copy = pltpu.make_async_copy(whole_ref, out_ref, sem)
            copy.start()
            copy.wait()

    return pl.pallas_call(
        body,
        out_shape=jax.ShapeDtypeStruct((own, 2 * half), F32),
        in_specs=[SCALARS, WHOLE, WHOLE, pl.BlockSpec(memory_space=pltpu.HBM)],
        out_specs=pl.BlockSpec(memory_space=pltpu.HBM),
        scratch_shapes=[pltpu.VMEM((own, 2 * half), F32), pltpu.SemaphoreType.DMA],
        input_output_aliases={3: 0},
        compiler_params=pltpu.CompilerParams(vmem_limit_bytes=8 * MIB),
        name="finish",
    )(jnp.stack((core, fits.astype(jnp.int32))), ours, back, other)


def per_device(orbital_values, occupied, trial, point_weights, batch_sizes, significant):
    rows, cols = orbital_values.shape
    batches = batch_sizes.shape[0]
    slots = rows // batches
    blocks = significant.shape[1]
    columns = occupied.shape[1]
    grid_count = lax.axis_size("grid")
    occ_count = lax.axis_size("occ")
    chips = grid_count // 2
    shares = 2 * occ_count
    half = cols // 2
    total = columns * grid_count
    place = lax.axis_index("grid")
    chip, core = place // 2, place % 2
    occ = lax.axis_index("occ")
    member = core * occ_count + occ

    def flip(x, axis, bit):
        count = lax.axis_size(axis)
        return lax.ppermute(x, axis, [(i, i ^ bit) for i in range(count)])

    def along(pairs):
        return [(2 * a + c, 2 * b + c) for a, b in pairs for c in range(2)]

    def doubled(x, axis, bit, dim):
        got = flip(x, axis, bit)
        mine = (lax.axis_index(axis) & bit) == 0
        return jnp.where(
            mine, jnp.concatenate((x, got), axis=dim), jnp.concatenate((got, x), axis=dim)
        )

    def halves(whole, axis):
        size = whole.shape[axis] // 2
        mine = lax.dynamic_slice_in_dim(whole, core * size, size, axis)
        return mine, lax.dynamic_slice_in_dim(whole, (1 - core) * size, size, axis)

    grid_bits = [1 << b for b in range(grid_count.bit_length() - 1)]
    occ_bits = [1 << b for b in range(occ_count.bit_length() - 1)]

    mine = half_of(orbital_values.T, core)
    got = flip(half_of(orbital_values.T, 1 - core), "grid", 1)
    mine_sig, other_sig = halves(significant.T, 0)
    got_sig = flip(other_sig, "grid", 1)

    told = jnp.concatenate(
        (
            doubled(batch_sizes[None], "grid", 1, 0).astype(F32).reshape(1, -1),
            doubled(point_weights[None], "grid", 1, 0).reshape(1, -1),
        ),
        axis=1,
    )
    live = rows * chips
    for bit in grid_bits[1:2]:
        told = doubled(told, "grid", bit, 0)
    if chips > 4:
        for bit in grid_bits[2:]:
            told = doubled(told, "grid", bit, 0)

    def places_of(sizes, upper):
        count = sizes.shape[0]
        batch = lax.broadcasted_iota(jnp.int32, (count, count), 0)
        before = lax.broadcasted_iota(jnp.int32, (count, count), 1) < batch
        start = upper * live + jnp.sum((before.astype(jnp.int32) - upper) * sizes[None, :], axis=1)
        position = lax.broadcasted_iota(jnp.int32, (count, slots), 1)
        to = jnp.where(position < sizes[:, None], start[:, None] + position, -4 * live)
        return to.reshape(-1, rows), start

    sizes = told[:, : 2 * batches].astype(jnp.int32).reshape(-1)
    near_to, _ = places_of(sizes, chip // 2 if chips <= 4 else 0)
    near_place = place if chips > 4 else place % 4
    margin = rows // 2 if (rows // 2) % (8 * shares) == 0 else rows
    tile = margin
    piece = tile // shares
    base = rows * chip - margin
    mine_to = lax.dynamic_index_in_dim(near_to, near_place, 0, keepdims=False) - base
    got_to = lax.dynamic_index_in_dim(near_to, near_place ^ 1, 0, keepdims=False) - base
    odd = chip % 2
    compacted = compact(
        mine,
        got,
        jnp.repeat(mine_sig.astype(BF16), slots, axis=1),
        jnp.repeat(got_sig.astype(BF16), slots, axis=1),
        mine_to[:, None],
        got_to[:, None],
        cols // blocks,
        tile,
        odd,
    )

    told, _ = lax.optimization_barrier((told, compacted))
    for bit in grid_bits[2:] if chips <= 4 else []:
        told = doubled(told, "grid", bit, 0)
    sizes = told[:, : 2 * batches].astype(jnp.int32).reshape(-1)
    weights = told[:, 2 * batches :].reshape(-1)
    to, start = places_of(sizes, 0)
    first = start.reshape(chips, -1)[:, 0]
    nominal = rows * lax.iota(jnp.int32, chips)
    fits = jnp.all(jnp.abs(first - nominal) <= margin) & (jnp.sum(sizes) == live)

    per_window = rows // tile
    window_iota = lax.iota(jnp.int32, chips)
    at = (
        (window_iota * rows)[:, None, None]
        + (lax.iota(jnp.int32, per_window) * tile)[None, :, None]
        + member * piece
        + lax.iota(jnp.int32, piece)[None, None, :]
    ).reshape(-1, 1)
    weight = jnp.sum(jnp.where(to.reshape(1, -1) == at, weights[None, :], 0.0), axis=1)
    weight = weight.reshape(chips, per_window * piece)
    def sent(x, pairs):
        return lax.ppermute(x, "grid", along(pairs))

    last = chips - 1

    def over(links, t):
        pairs = []
        for a in range(links, last, 2):
            pairs += [(a, a + 1)] if a - t + 1 >= 0 else []
            pairs += [(a + 1, a)] if a + t <= last else []
        return pairs

    arrived = [
        (sent(for_b, over(1, 1)), sent(for_a, over(0, 1))) for for_b, *_, for_a in compacted
    ]
    own = tuple(
        straighten(tiles, by_b, by_a, odd)
        for (_, *tiles, _), (by_b, by_a) in zip(compacted, arrived)
    )

    own, fits, weight = lax.optimization_barrier((own, fits.astype(jnp.int32), weight))

    _, occupied_turned, trial_turned = lax.optimization_barrier(
        (compacted[0][0], occupied.T, trial.T)
    )
    mine_panel, other_panel = panel_halves(occupied_turned, trial_turned, core)
    panels = stack_panels(mine_panel, flip(other_panel, "grid", 1), core)

    ends = [(0, 1), (last, last - 1)]
    homes = [(b, a) for a, b in ends]
    side = 1 - 2 * odd

    def valid(at):
        return jnp.where((at >= 0) & (at <= last), at, -1)

    stages = [[([own], chip)]]
    by_a = by_b = own
    far_panels = None
    for t in range(1, last):
        by_a, by_b = (
            tuple(sent(x, over(0, t)) for x in by_b),
            tuple(sent(x, over(1, t)) for x in by_a),
        )
        if t == 1:
            far_panels = sent(panels, ends)
        a_at, b_at = valid(chip + side * t), valid(chip - side * t)
        if 2 * t > last:
            stages.append([([by_a, by_b], jnp.maximum(a_at, b_at))])
        else:
            stages.append([([by_a], a_at), ([by_b], b_at)])

    direct = occ_count <= 4
    points = per_window * piece

    def summed(pairs):
        if direct:
            parts = split_sum(pairs, occ)
            value = parts[0]
            for d in range(1, occ_count):
                value = value + flip(parts[d], "occ", d)
        else:
            value = jnp.concatenate([keep + got for keep, got in pairs])
            for bit in reversed(occ_bits):
                upper = (occ & bit) != 0
                low_part, high_part = value[:, :bit], value[:, bit:]
                got = flip(jnp.where(upper, low_part, high_part), "occ", bit)
                value = jnp.where(upper, high_part, low_part) + got
        return value.reshape(-1, points, 4 * columns)

    def shared_density(value, at):
        product = jnp.sum(value[:, :, : 2 * columns] * value[:, :, 2 * columns :], axis=2)
        here = (at[:, None] == window_iota[None, :])[:, :, None]
        return jnp.sum(jnp.where(here, product[:, None], 0.0), axis=0)

    early_jobs, late_jobs = sum(stages[1:-1], []), stages[-1]
    early_at = jnp.stack([at for _, at in early_jobs])
    late_at = late_jobs[0][1][None]
    early_jobs = stages[0] + early_jobs
    early_at = jnp.concatenate((chip[None], early_at))

    own_pair = project([(panels, early_jobs[0][0])], tile, shares, core)
    early_pair = project([(panels, w) for w, _ in early_jobs[1:]], tile, shares, core)
    early_value = summed(
        [(keep, flip(give, "grid", 1)) for keep, give in (own_pair, early_pair)]
    )

    outer = jnp.where(chip == 0, last, jnp.where(chip == last, 0, early_at[2]))
    places = jnp.concatenate((early_at[:2], outer[None], early_at[3:], late_at))
    here = (places[:, None] == window_iota[None, :])[:, :, None]
    weight_here = jnp.sum(jnp.where(here, weight[None], 0.0), axis=1)[:, :, None]

    late, by_a, early_value, far_panels, weight_here, fits = lax.optimization_barrier(
        (by_b, by_a, early_value, far_panels, weight_here, fits)
    )
    fits = fits != 0
    late = tuple(sent(x, homes) for x in late)
    late_window = [by_a, by_b]
    late_jobs = [(panels, late_window), (far_panels, [by_b])]

    def kernel_of_all():
        late_pair = project(late_jobs, tile, shares, core)
        keep, give = late_pair
        value = jnp.concatenate((early_value, summed([(keep, flip(give, "grid", 1))])))
        density = shared_density(value, jnp.concatenate((early_at, late_at, late_at)))
        value, far_value = value[:-1], value[-1:]
        packed = jnp.concatenate(
            (far_value[0], jnp.pad(density, ((0, 0), (0, 4 * columns - points)))), axis=0
        )
        packed = flip(packed, "grid", 2)
        home_value, neighbour = packed[None, :points], packed[points:, :points]
        if chips <= 4:
            others = [flip(density, "grid", 2 * d) for d in range(2, chips)]
            density = density + neighbour + sum(others[1:], others[0])
        else:
            density = density + neighbour
            for bit in grid_bits[2:]:
                density = density + flip(density, "grid", bit)
        density = density * (1.0 / math.sqrt(total))

        values = jnp.concatenate((value[:2], value[2:3] + home_value, value[3:]))
        density_here = jnp.sum(jnp.where(here, density[None], 0.0), axis=1)[:, :, None]
        orbitals, response = values[:, :, : 2 * columns], values[:, :, 2 * columns :]
        kernel = (weight_here * (density_here * orbitals + response)).astype(BF16)
        kernel = kernel.reshape(-1, 1, piece, 2 * columns)
        if direct:
            parts = [kernel] + [flip(kernel, "occ", d) for d in range(1, occ_count)]
            kernel = in_order(parts, occ)
        else:
            for bit in occ_bits:
                kernel = doubled(kernel, "occ", bit, 1)
        return kernel, flip(kernel, "grid", 1), unwritten((columns, cols))

    scale = 1.0 / math.sqrt(rows * grid_count)

    def result_for_any_sizes():
        whole = any_sizes(
            orbital_values, occupied, trial, point_weights, batch_sizes, significant
        )
        none = jnp.zeros((places.shape[0] * per_window, occ_count, piece, 2 * columns), BF16)
        return none, none, whole * scale

    kernel, got_kernel, other = lax.cond(fits, kernel_of_all, result_for_any_sizes)
    early_windows = [w for w, _ in early_jobs]
    early_windows[2] = early_windows[2] + [late]
    windows = early_windows + [late_window]
    ours, theirs = contract(kernel, got_kernel, windows, core)
    back = flip(theirs, "grid", 1)
    return finish(core, fits, ours, back, other, scale).T


def solution(mesh):
    placed = (
        P("grid", "occ"),
        P("occ", "grid"),
        P("occ", "grid"),
        P("grid"),
        P("grid"),
        P("grid", "occ"),
    )
    return jax.shard_map(
        per_device, mesh=mesh, in_specs=placed, out_specs=P("occ", "grid"), check_vma=False
    )
```

```python
import math

import jax
import jax.numpy as jnp
from jax import lax
from jax.experimental import pallas as pl
from jax.experimental.pallas import tpu as pltpu
from jax.sharding import PartitionSpec as P

BF16, F32 = jnp.bfloat16, jnp.float32
MIB = 1024 * 1024
WHOLE = pl.BlockSpec(memory_space=pltpu.VMEM)
SCALARS = pl.BlockSpec(memory_space=pltpu.SMEM)


def screen(values, sizes, significant):
    rows, cols = values.shape
    batches = sizes.shape[0]
    blocks = significant.shape[1]
    blocked = (
        values.reshape(batches, rows // batches, blocks, cols // blocks)
        * significant.astype(values.dtype)[:, None, :, None]
    )
    position = lax.broadcasted_iota(jnp.int32, (batches, rows // batches), 1)
    live = (position < sizes[:, None]).astype(jnp.float32).reshape(rows)
    return (blocked.reshape(rows, cols), live)


def any_sizes(orbital_values, occupied, trial, point_weights, batch_sizes, significant):
    screened, live = screen(orbital_values, batch_sizes, significant)
    rows, cols = screened.shape
    grid_count, occ_count = lax.axis_size("grid"), lax.axis_size("occ")
    columns = occupied.shape[1]
    me = lax.axis_index("grid")
    ring = [(i, (i + 1) % grid_count) for i in range(grid_count)]
    occ_ring = [(i, (i + 1) % occ_count) for i in range(occ_count)]

    def project_one(step, carry):
        panel, terms = carry
        term = jnp.dot(screened, panel, preferred_element_type=F32)
        terms = lax.dynamic_update_index_in_dim(terms, term, (me - step) % grid_count, 0)
        return lax.ppermute(panel, "grid", ring), terms

    joined = jnp.concatenate((occupied, trial), axis=1)
    terms = jnp.zeros((grid_count, rows, 2 * columns), F32)
    terms = lax.fori_loop(0, grid_count, project_one, (joined, terms))[1]

    def add_one(step, carry):
        moving, held = carry
        moving = lax.ppermute(moving, "occ", occ_ring)
        return moving, held + moving

    terms = lax.fori_loop(0, occ_count - 1, add_one, (terms, terms))[1]
    orbitals, response = terms[:, :, :columns], terms[:, :, columns:]
    density = jnp.sum(orbitals * response, axis=(0, 2)) * (1.0 / math.sqrt(columns * grid_count))
    weight = (point_weights * live)[None, :, None]
    kernel = (weight * (density[None, :, None] * orbitals + response)).astype(BF16)

    def contract_one(step, held):
        owner = (me + grid_count - 1 - step) % grid_count
        part = lax.dynamic_index_in_dim(kernel, owner, 0, keepdims=False)
        term = lax.dot_general(
            part, screened, (((0,), (0,)), ((), ())), preferred_element_type=F32
        )
        return lax.ppermute(held, "grid", ring) + term

    return lax.fori_loop(0, grid_count, contract_one, jnp.zeros((columns, cols), F32))


def half_of(whole, which):
    rows, columns = whole.shape
    half = rows // 2
    if half % 16:
        return lax.dynamic_slice_in_dim(whole, which * half, half, 0)

    def body(which_ref, whole_ref, out_ref, sem):
        first = pl.multiple_of(which_ref[0] * half, 16)
        copy = pltpu.make_async_copy(whole_ref.at[pl.ds(first, half)], out_ref, sem)
        copy.start()
        copy.wait()

    return pl.pallas_call(
        body,
        out_shape=jax.ShapeDtypeStruct((half, columns), whole.dtype),
        in_specs=[SCALARS, pl.BlockSpec(memory_space=pl.ANY)],
        out_specs=WHOLE,
        scratch_shapes=[pltpu.SemaphoreType.DMA],
        compiler_params=pltpu.CompilerParams(vmem_limit_bytes=4 * MIB),
        name="half_of",
    )(which[None], whole)


def compact(mine, got, mine_sig, got_sig, mine_to, got_to, width, tile, odd):
    half, rows = mine.shape
    blocks = mine_sig.shape[0]
    count = rows // tile + 2
    cuts = [(0, half)]

    def body(odd_ref, mine_ref, got_ref, msig_ref, gsig_ref, mto_ref, gto_ref, *outs):
        block_of = lax.broadcasted_iota(jnp.int32, (half, blocks), 0)
        begin = lax.broadcasted_iota(jnp.int32, (half, blocks), 1) * width
        spread = ((block_of >= begin) & (block_of < begin + width)).astype(F32).astype(BF16)
        slot = lax.broadcasted_iota(jnp.int32, (rows, count * tile), 1)

        def part(value_ref, sig_ref, to_ref):
            kept = jnp.dot(spread, sig_ref[...], preferred_element_type=F32)
            screened = (value_ref[...].astype(F32) * kept).astype(BF16)
            place = (to_ref[...] == slot).astype(F32).astype(BF16)
            return jnp.dot(screened, place, preferred_element_type=F32)

        window = part(mine_ref, msig_ref, mto_ref) + part(got_ref, gsig_ref, gto_ref)
        tiles = [window[:, j * tile : (j + 1) * tile] for j in range(count)]
        even = odd_ref[0] == 0
        first, last = tiles[0], tiles[-1]
        tiles[0] = jnp.where(even, first, last)
        tiles[-1] = jnp.where(even, last, first)
        for p, (low, high) in enumerate(cuts):
            for j in range(count):
                outs[p * count + j][...] = tiles[j][low:high].astype(BF16)

    shapes = [
        jax.ShapeDtypeStruct((high - low, tile), BF16) for low, high in cuts for _ in range(count)
    ]
    out = pl.pallas_call(
        body,
        out_shape=shapes,
        in_specs=[SCALARS] + [WHOLE] * 6,
        out_specs=[WHOLE] * len(shapes),
        compiler_params=pltpu.CompilerParams(vmem_limit_bytes=10 * MIB),
        name="compact",
        cost_estimate=pl.CostEstimate(
            flops=8 * half * rows * rows, bytes_accessed=8 * half * rows, transcendentals=0
        ),
    )(odd[None], mine, got, mine_sig, got_sig, mine_to, got_to)
    return [out[p * count : (p + 1) * count] for p in range(len(cuts))]


def straighten(tiles, by_b, by_a, odd):
    half, tile = by_a.shape
    count = len(tiles)

    def body(odd_ref, *refs):
        tile_refs, b_ref, a_ref, out_ref = refs[:count], *refs[count:]
        even = odd_ref[0] == 0
        for j in range(count):
            value = tile_refs[j][...]
            if j == 0:
                value = value + jnp.where(even, b_ref[...], a_ref[...])
            if j == count - 1:
                value = value + jnp.where(even, a_ref[...], b_ref[...])
            out_ref[:, j * tile : (j + 1) * tile] = value

    return pl.pallas_call(
        body,
        out_shape=jax.ShapeDtypeStruct((half, count * tile), BF16),
        in_specs=[SCALARS] + [WHOLE] * (count + 2),
        out_specs=WHOLE,
        compiler_params=pltpu.CompilerParams(vmem_limit_bytes=8 * MIB),
        name="straighten",
    )(odd[None], *tiles, by_b, by_a)


def panel_halves(occupied, trial, core):
    columns, cols = occupied.shape
    half = cols // 2
    width = -(-half // 128) * 128

    def body(core_ref, occupied_ref, trial_ref, mine_ref, other_ref):
        first = core_ref[0] == 0
        mine_ref[...] = jnp.zeros_like(mine_ref)
        other_ref[...] = jnp.zeros_like(other_ref)
        for j, ref in enumerate((occupied_ref, trial_ref)):
            low, high = ref[:, :half], ref[:, half:]
            mine_ref[j * columns : (j + 1) * columns, :half] = jnp.where(first, low, high)
            other_ref[j * columns : (j + 1) * columns, :half] = jnp.where(first, high, low)

    shape = jax.ShapeDtypeStruct((2 * columns, width), BF16)
    return pl.pallas_call(
        body,
        out_shape=(shape, shape),
        in_specs=[SCALARS, WHOLE, WHOLE],
        out_specs=(WHOLE, WHOLE),
        compiler_params=pltpu.CompilerParams(vmem_limit_bytes=8 * MIB),
        name="panel_halves",
    )(core[None], occupied, trial)


def stack_panels(mine, got, core):
    both, width = mine.shape
    columns = both // 2

    def body(core_ref, mine_ref, got_ref, out_ref):
        first = core_ref[0] == 0
        for j in range(2):
            low = mine_ref[j * columns : (j + 1) * columns]
            high = got_ref[j * columns : (j + 1) * columns]
            q = 2 * j * columns
            out_ref[q : q + columns] = jnp.where(first, low, high)
            out_ref[q + columns : q + 2 * columns] = jnp.where(first, high, low)

    return pl.pallas_call(
        body,
        out_shape=jax.ShapeDtypeStruct((2 * both, width), BF16),
        in_specs=[SCALARS, WHOLE, WHOLE],
        out_specs=WHOLE,
        compiler_params=pltpu.CompilerParams(vmem_limit_bytes=8 * MIB),
        name="stack_panels",
    )(core[None], mine, got)


def distinct(arrays):
    return list({id(x): x for x in arrays}.values())


def read_window(addends, p, arrays, refs):
    ref_of = {id(x): ref for x, ref in zip(arrays, refs)}
    total = None
    for x in addends:
        value = ref_of[id(x[p])][...]
        total = value if total is None else total + value
    return total


def split_sum(pairs, occ):
    _, shares, piece, both = pairs[0][0].shape
    tiles = sum(keep.shape[0] for keep, _ in pairs)

    def body(occ_ref, *refs):
        ins, outs = refs[: 2 * len(pairs)], refs[2 * len(pairs) :]
        for d in range(shares):
            at = 0
            for keep_ref, got_ref in zip(ins[::2], ins[1::2]):
                for q in range(keep_ref.shape[0]):
                    outs[d][at] = keep_ref[q, occ_ref[0] ^ d] + got_ref[q, occ_ref[0] ^ d]
                    at += 1

    shape = jax.ShapeDtypeStruct((tiles, piece, both), F32)
    return pl.pallas_call(
        body,
        out_shape=(shape,) * shares,
        in_specs=[SCALARS] + [WHOLE] * (2 * len(pairs)),
        out_specs=(WHOLE,) * shares,
        compiler_params=pltpu.CompilerParams(vmem_limit_bytes=8 * MIB),
        name="split_sum",
    )(occ[None], *sum(pairs, ()))


def project(jobs, tile, shares, core):
    both = jobs[0][0].shape[0]
    parts = [x.shape[0] for x in jobs[0][1][0]]
    rows = jobs[0][1][0][0].shape[1]
    half = sum(parts)
    piece = tile // shares
    tiles = len(jobs) * rows // tile
    panels = distinct([p for p, _ in jobs])
    arrays = distinct([x for _, window in jobs for addend in window for x in addend])
    count = len(panels)

    def body(core_ref, *refs):
        panel_refs, array_refs = refs[:count], refs[count:-3]
        keep_ref, give_ref, terms_ref = refs[-3:]
        q = 0
        for panel, window in jobs:
            panel_ref = panel_refs[[id(p) for p in panels].index(id(panel))]
            total, low = None, 0
            for p, size in enumerate(parts):
                value = read_window(window, p, arrays, array_refs)
                term = jnp.dot(
                    panel_ref[:, low : low + size], value, preferred_element_type=F32
                )
                total = term if total is None else total + term
                low += size
            turned = total.T
            for j in range(0, rows, tile):
                terms_ref[q] = turned[j : j + tile].reshape(2, shares // 2, piece, both)
                keep_ref[q] = terms_ref[q, core_ref[0]]
                give_ref[q] = terms_ref[q, 1 - core_ref[0]]
                q += 1

    shape = jax.ShapeDtypeStruct((tiles, shares // 2, piece, both), F32)
    return pl.pallas_call(
        body,
        out_shape=(shape, shape),
        in_specs=[SCALARS] + [WHOLE] * (count + len(arrays)),
        out_specs=(WHOLE, WHOLE),
        scratch_shapes=[pltpu.VMEM((tiles, 2, shares // 2, piece, both), F32)],
        compiler_params=pltpu.CompilerParams(vmem_limit_bytes=12 * MIB),
        name="project",
        cost_estimate=pl.CostEstimate(
            flops=2 * both * half * tiles * tile,
            bytes_accessed=2 * half * (both + tiles * tile) + 4 * tiles * tile * both,
            transcendentals=0,
        ),
    )(core[None], *panels, *arrays)


def in_order(parts, occ):
    tiles, _, piece, columns = parts[0].shape

    def body(occ_ref, *refs):
        for d in range(len(parts)):
            refs[-1][:, occ_ref[0] ^ d] = refs[d][:, 0]

    return pl.pallas_call(
        body,
        out_shape=jax.ShapeDtypeStruct((tiles, len(parts), piece, columns), parts[0].dtype),
        in_specs=[SCALARS] + [WHOLE] * len(parts),
        out_specs=WHOLE,
        compiler_params=pltpu.CompilerParams(vmem_limit_bytes=4 * MIB),
        name="in_order",
    )(occ[None], *parts)


def contract(kernel, got, windows, core):
    tiles, shares, piece, columns = kernel.shape
    parts = [x.shape[0] for x in windows[0][0]]
    rows = windows[0][0][0].shape[1]
    half = sum(parts)
    own = columns // 2
    arrays = distinct([x for window in windows for addend in window for x in addend])
    per_window = tiles // len(windows)

    def body(core_ref, kernel_ref, got_ref, *refs):
        array_refs = refs[:-3]
        mine_ref, other_ref, order_ref = refs[-3:]
        first = core_ref[0] == 0
        order_ref[:, core_ref[0]] = kernel_ref[...].astype(F32)
        order_ref[:, 1 - core_ref[0]] = got_ref[...].astype(F32)
        kernels = [
            order_ref[s * per_window : (s + 1) * per_window].reshape(rows, columns).astype(BF16)
            for s in range(len(windows))
        ]
        low = 0
        for p, size in enumerate(parts):
            total = None
            for window, part in zip(windows, kernels):
                value = read_window(window, p, arrays, array_refs)
                term = jnp.dot(value, part, preferred_element_type=F32)
                total = term if total is None else total + term
            total = total.T
            mine_ref[:, low : low + size] = jnp.where(first, total[:own], total[own:])
            other_ref[:, low : low + size] = jnp.where(first, total[own:], total[:own])
            low += size

    shape = jax.ShapeDtypeStruct((own, half), F32)
    return pl.pallas_call(
        body,
        out_shape=(shape, shape),
        in_specs=[SCALARS] + [WHOLE] * (2 + len(arrays)),
        out_specs=(WHOLE, WHOLE),
        scratch_shapes=[pltpu.VMEM((tiles, 2, shares, piece, columns), F32)],
        compiler_params=pltpu.CompilerParams(vmem_limit_bytes=20 * MIB),
        name="contract",
        cost_estimate=pl.CostEstimate(
            flops=2 * columns * half * rows * len(windows),
            bytes_accessed=2 * rows * len(windows) * half + 4 * columns * half,
            transcendentals=0,
        ),
    )(core[None], kernel, got, *arrays)


def unwritten(shape):
    def body(out_ref):
        pass

    return pl.pallas_call(
        body,
        out_shape=jax.ShapeDtypeStruct(shape, F32),
        out_specs=pl.BlockSpec(memory_space=pltpu.HBM),
        name="unwritten",
    )()


def finish(core, fits, ours, back, other, scale):
    own, half = ours.shape

    def body(flags_ref, ours_ref, back_ref, other_ref, out_ref, whole_ref, sem):
        @pl.when(flags_ref[1] != 0)
        def _():
            first = flags_ref[0] == 0
            whole_ref[:, :half] = jnp.where(first, ours_ref[...], back_ref[...]) * scale
            whole_ref[:, half:] = jnp.where(first, back_ref[...], ours_ref[...]) * scale
            copy = pltpu.make_async_copy(whole_ref, out_ref, sem)
            copy.start()
            copy.wait()

    return pl.pallas_call(
        body,
        out_shape=jax.ShapeDtypeStruct((own, 2 * half), F32),
        in_specs=[SCALARS, WHOLE, WHOLE, pl.BlockSpec(memory_space=pltpu.HBM)],
        out_specs=pl.BlockSpec(memory_space=pltpu.HBM),
        scratch_shapes=[pltpu.VMEM((own, 2 * half), F32), pltpu.SemaphoreType.DMA],
        input_output_aliases={3: 0},
        compiler_params=pltpu.CompilerParams(vmem_limit_bytes=8 * MIB),
        name="finish",
    )(jnp.stack((core, fits.astype(jnp.int32))), ours, back, other)


def per_device(orbital_values, occupied, trial, point_weights, batch_sizes, significant):
    rows, cols = orbital_values.shape
    batches = batch_sizes.shape[0]
    slots = rows // batches
    blocks = significant.shape[1]
    columns = occupied.shape[1]
    grid_count = lax.axis_size("grid")
    occ_count = lax.axis_size("occ")
    chips = grid_count // 2
    shares = 2 * occ_count
    half = cols // 2
    total = columns * grid_count
    place = lax.axis_index("grid")
    chip, core = place // 2, place % 2
    occ = lax.axis_index("occ")
    member = core * occ_count + occ

    def flip(x, axis, bit):
        count = lax.axis_size(axis)
        return lax.ppermute(x, axis, [(i, i ^ bit) for i in range(count)])

    def along(pairs):
        return [(2 * a + c, 2 * b + c) for a, b in pairs for c in range(2)]

    def doubled(x, axis, bit, dim):
        got = flip(x, axis, bit)
        mine = (lax.axis_index(axis) & bit) == 0
        return jnp.where(
            mine, jnp.concatenate((x, got), axis=dim), jnp.concatenate((got, x), axis=dim)
        )

    def halves(whole, axis):
        size = whole.shape[axis] // 2
        mine = lax.dynamic_slice_in_dim(whole, core * size, size, axis)
        return mine, lax.dynamic_slice_in_dim(whole, (1 - core) * size, size, axis)

    grid_bits = [1 << b for b in range(grid_count.bit_length() - 1)]
    occ_bits = [1 << b for b in range(occ_count.bit_length() - 1)]

    mine = half_of(orbital_values.T, core)
    got = flip(half_of(orbital_values.T, 1 - core), "grid", 1)
    mine_sig, other_sig = halves(significant.T, 0)
    got_sig = flip(other_sig, "grid", 1)

    told = jnp.concatenate(
        (
            doubled(batch_sizes[None], "grid", 1, 0).astype(F32).reshape(1, -1),
            doubled(point_weights[None], "grid", 1, 0).reshape(1, -1),
        ),
        axis=1,
    )
    live = rows * chips
    for bit in grid_bits[1:2]:
        told = doubled(told, "grid", bit, 0)
    if chips > 4:
        for bit in grid_bits[2:]:
            told = doubled(told, "grid", bit, 0)

    def places_of(sizes, upper):
        count = sizes.shape[0]
        batch = lax.broadcasted_iota(jnp.int32, (count, count), 0)
        before = lax.broadcasted_iota(jnp.int32, (count, count), 1) < batch
        start = upper * live + jnp.sum((before.astype(jnp.int32) - upper) * sizes[None, :], axis=1)
        position = lax.broadcasted_iota(jnp.int32, (count, slots), 1)
        to = jnp.where(position < sizes[:, None], start[:, None] + position, -4 * live)
        return to.reshape(-1, rows), start

    sizes = told[:, : 2 * batches].astype(jnp.int32).reshape(-1)
    near_to, _ = places_of(sizes, chip // 2 if chips <= 4 else 0)
    near_place = place if chips > 4 else place % 4
    margin = rows // 2 if (rows // 2) % (8 * shares) == 0 else rows
    tile = margin
    piece = tile // shares
    base = rows * chip - margin
    mine_to = lax.dynamic_index_in_dim(near_to, near_place, 0, keepdims=False) - base
    got_to = lax.dynamic_index_in_dim(near_to, near_place ^ 1, 0, keepdims=False) - base
    odd = chip % 2
    compacted = compact(
        mine,
        got,
        jnp.repeat(mine_sig.astype(BF16), slots, axis=1),
        jnp.repeat(got_sig.astype(BF16), slots, axis=1),
        mine_to[:, None],
        got_to[:, None],
        cols // blocks,
        tile,
        odd,
    )

    told, _ = lax.optimization_barrier((told, compacted))
    for bit in grid_bits[2:] if chips <= 4 else []:
        told = doubled(told, "grid", bit, 0)
    sizes = told[:, : 2 * batches].astype(jnp.int32).reshape(-1)
    weights = told[:, 2 * batches :].reshape(-1)
    to, start = places_of(sizes, 0)
    first = start.reshape(chips, -1)[:, 0]
    nominal = rows * lax.iota(jnp.int32, chips)
    fits = jnp.all(jnp.abs(first - nominal) <= margin) & (jnp.sum(sizes) == live)

    per_window = rows // tile
    window_iota = lax.iota(jnp.int32, chips)
    at = (
        (window_iota * rows)[:, None, None]
        + (lax.iota(jnp.int32, per_window) * tile)[None, :, None]
        + member * piece
        + lax.iota(jnp.int32, piece)[None, None, :]
    ).reshape(-1, 1)
    weight = jnp.sum(jnp.where(to.reshape(1, -1) == at, weights[None, :], 0.0), axis=1)
    weight = weight.reshape(chips, per_window * piece)
    def sent(x, pairs):
        return lax.ppermute(x, "grid", along(pairs))

    last = chips - 1

    def over(links, t):
        pairs = []
        for a in range(links, last, 2):
            pairs += [(a, a + 1)] if a - t + 1 >= 0 else []
            pairs += [(a + 1, a)] if a + t <= last else []
        return pairs

    arrived = [
        (sent(for_b, over(1, 1)), sent(for_a, over(0, 1))) for for_b, *_, for_a in compacted
    ]
    own = tuple(
        straighten(tiles, by_b, by_a, odd)
        for (_, *tiles, _), (by_b, by_a) in zip(compacted, arrived)
    )

    own, fits, weight = lax.optimization_barrier((own, fits.astype(jnp.int32), weight))

    _, occupied_turned, trial_turned = lax.optimization_barrier(
        (compacted[0][0], occupied.T, trial.T)
    )
    mine_panel, other_panel = panel_halves(occupied_turned, trial_turned, core)
    panels = stack_panels(mine_panel, flip(other_panel, "grid", 1), core)

    ends = [(0, 1), (last, last - 1)]
    homes = [(b, a) for a, b in ends]
    side = 1 - 2 * odd

    def valid(at):
        return jnp.where((at >= 0) & (at <= last), at, -1)

    stages = [[([own], chip)]]
    by_a = by_b = own
    far_panels = None
    for t in range(1, last):
        by_a, by_b = (
            tuple(sent(x, over(0, t)) for x in by_b),
            tuple(sent(x, over(1, t)) for x in by_a),
        )
        if t == 1:
            far_panels = sent(panels, ends)
        a_at, b_at = valid(chip + side * t), valid(chip - side * t)
        if 2 * t > last:
            stages.append([([by_a, by_b], jnp.maximum(a_at, b_at))])
        else:
            stages.append([([by_a], a_at), ([by_b], b_at)])

    direct = occ_count <= 4
    points = per_window * piece

    def summed(pairs):
        if direct:
            parts = split_sum(pairs, occ)
            value = parts[0]
            for d in range(1, occ_count):
                value = value + flip(parts[d], "occ", d)
        else:
            value = jnp.concatenate([keep + got for keep, got in pairs])
            for bit in reversed(occ_bits):
                upper = (occ & bit) != 0
                low_part, high_part = value[:, :bit], value[:, bit:]
                got = flip(jnp.where(upper, low_part, high_part), "occ", bit)
                value = jnp.where(upper, high_part, low_part) + got
        return value.reshape(-1, points, 4 * columns)

    def shared_density(value, at):
        product = jnp.sum(value[:, :, : 2 * columns] * value[:, :, 2 * columns :], axis=2)
        here = (at[:, None] == window_iota[None, :])[:, :, None]
        return jnp.sum(jnp.where(here, product[:, None], 0.0), axis=0)

    early_jobs, late_jobs = sum(stages[1:-1], []), stages[-1]
    early_at = jnp.stack([at for _, at in early_jobs])
    late_at = late_jobs[0][1][None]
    early_jobs = stages[0] + early_jobs
    early_at = jnp.concatenate((chip[None], early_at))

    keep, give = project([(panels, w) for w, _ in early_jobs], tile, shares, core)
    early_value = summed([(keep, flip(give, "grid", 1))])

    outer = jnp.where(chip == 0, last, jnp.where(chip == last, 0, early_at[2]))
    places = jnp.concatenate((early_at[:2], outer[None], early_at[3:], late_at))
    here = (places[:, None] == window_iota[None, :])[:, :, None]
    weight_here = jnp.sum(jnp.where(here, weight[None], 0.0), axis=1)[:, :, None]

    late, by_a, early_value, far_panels, weight_here, fits = lax.optimization_barrier(
        (by_b, by_a, early_value, far_panels, weight_here, fits)
    )
    fits = fits != 0
    late = tuple(sent(x, homes) for x in late)
    late_window = [by_a, by_b]
    late_jobs = [(panels, late_window), (far_panels, [by_b])]

    def kernel_of_all():
        late_pair = project(late_jobs, tile, shares, core)
        keep, give = late_pair
        value = jnp.concatenate((early_value, summed([(keep, flip(give, "grid", 1))])))
        density = shared_density(value, jnp.concatenate((early_at, late_at, late_at)))
        value, far_value = value[:-1], value[-1:]
        packed = jnp.concatenate(
            (far_value[0], jnp.pad(density, ((0, 0), (0, 4 * columns - points)))), axis=0
        )
        packed = flip(packed, "grid", 2)
        home_value, neighbour = packed[None, :points], packed[points:, :points]
        if chips <= 4:
            others = [flip(density, "grid", 2 * d) for d in range(2, chips)]
            density = density + neighbour + sum(others[1:], others[0])
        else:
            density = density + neighbour
            for bit in grid_bits[2:]:
                density = density + flip(density, "grid", bit)
        density = density * (1.0 / math.sqrt(total))

        values = jnp.concatenate((value[:2], value[2:3] + home_value, value[3:]))
        density_here = jnp.sum(jnp.where(here, density[None], 0.0), axis=1)[:, :, None]
        orbitals, response = values[:, :, : 2 * columns], values[:, :, 2 * columns :]
        kernel = (weight_here * (density_here * orbitals + response)).astype(BF16)
        kernel = kernel.reshape(-1, 1, piece, 2 * columns)
        if direct:
            parts = [kernel] + [flip(kernel, "occ", d) for d in range(1, occ_count)]
            kernel = in_order(parts, occ)
        else:
            for bit in occ_bits:
                kernel = doubled(kernel, "occ", bit, 1)
        return kernel, flip(kernel, "grid", 1), unwritten((columns, cols))

    scale = 1.0 / math.sqrt(rows * grid_count)

    def result_for_any_sizes():
        whole = any_sizes(
            orbital_values, occupied, trial, point_weights, batch_sizes, significant
        )
        none = jnp.zeros((places.shape[0] * per_window, occ_count, piece, 2 * columns), BF16)
        return none, none, whole * scale

    kernel, got_kernel, other = lax.cond(fits, kernel_of_all, result_for_any_sizes)
    early_windows = [w for w, _ in early_jobs]
    early_windows[2] = early_windows[2] + [late]
    windows = early_windows + [late_window]
    ours, theirs = contract(kernel, got_kernel, windows, core)
    back = flip(theirs, "grid", 1)
    return finish(core, fits, ours, back, other, scale).T


def solution(mesh):
    placed = (
        P("grid", "occ"),
        P("occ", "grid"),
        P("occ", "grid"),
        P("grid"),
        P("grid"),
        P("grid", "occ"),
    )
    return jax.shard_map(
        per_device, mesh=mesh, in_specs=placed, out_specs=P("occ", "grid"), check_vma=False
    )
```

```python
import math

import jax
import jax.numpy as jnp
from jax import lax
from jax.experimental import pallas as pl
from jax.experimental.pallas import tpu as pltpu
from jax.sharding import PartitionSpec as P

BF16, F32 = jnp.bfloat16, jnp.float32
MIB = 1024 * 1024
WHOLE = pl.BlockSpec(memory_space=pltpu.VMEM)
SCALARS = pl.BlockSpec(memory_space=pltpu.SMEM)


def screen(values, sizes, significant):
    rows, cols = values.shape
    batches = sizes.shape[0]
    blocks = significant.shape[1]
    blocked = (
        values.reshape(batches, rows // batches, blocks, cols // blocks)
        * significant.astype(values.dtype)[:, None, :, None]
    )
    position = lax.broadcasted_iota(jnp.int32, (batches, rows // batches), 1)
    live = (position < sizes[:, None]).astype(jnp.float32).reshape(rows)
    return (blocked.reshape(rows, cols), live)


def any_sizes(orbital_values, occupied, trial, point_weights, batch_sizes, significant):
    screened, live = screen(orbital_values, batch_sizes, significant)
    rows, cols = screened.shape
    grid_count, occ_count = lax.axis_size("grid"), lax.axis_size("occ")
    columns = occupied.shape[1]
    me = lax.axis_index("grid")
    ring = [(i, (i + 1) % grid_count) for i in range(grid_count)]
    occ_ring = [(i, (i + 1) % occ_count) for i in range(occ_count)]

    def project_one(step, carry):
        panel, terms = carry
        term = jnp.dot(screened, panel, preferred_element_type=F32)
        terms = lax.dynamic_update_index_in_dim(terms, term, (me - step) % grid_count, 0)
        return lax.ppermute(panel, "grid", ring), terms

    joined = jnp.concatenate((occupied, trial), axis=1)
    terms = jnp.zeros((grid_count, rows, 2 * columns), F32)
    terms = lax.fori_loop(0, grid_count, project_one, (joined, terms))[1]

    def add_one(step, carry):
        moving, held = carry
        moving = lax.ppermute(moving, "occ", occ_ring)
        return moving, held + moving

    terms = lax.fori_loop(0, occ_count - 1, add_one, (terms, terms))[1]
    orbitals, response = terms[:, :, :columns], terms[:, :, columns:]
    density = jnp.sum(orbitals * response, axis=(0, 2)) * (1.0 / math.sqrt(columns * grid_count))
    weight = (point_weights * live)[None, :, None]
    kernel = (weight * (density[None, :, None] * orbitals + response)).astype(BF16)

    def contract_one(step, held):
        owner = (me + grid_count - 1 - step) % grid_count
        part = lax.dynamic_index_in_dim(kernel, owner, 0, keepdims=False)
        term = lax.dot_general(
            part, screened, (((0,), (0,)), ((), ())), preferred_element_type=F32
        )
        return lax.ppermute(held, "grid", ring) + term

    return lax.fori_loop(0, grid_count, contract_one, jnp.zeros((columns, cols), F32))


def half_of(whole, which):
    rows, columns = whole.shape
    half = rows // 2
    if half % 16:
        return lax.dynamic_slice_in_dim(whole, which * half, half, 0)

    def body(which_ref, whole_ref, out_ref, sem):
        first = pl.multiple_of(which_ref[0] * half, 16)
        copy = pltpu.make_async_copy(whole_ref.at[pl.ds(first, half)], out_ref, sem)
        copy.start()
        copy.wait()

    return pl.pallas_call(
        body,
        out_shape=jax.ShapeDtypeStruct((half, columns), whole.dtype),
        in_specs=[SCALARS, pl.BlockSpec(memory_space=pl.ANY)],
        out_specs=WHOLE,
        scratch_shapes=[pltpu.SemaphoreType.DMA],
        compiler_params=pltpu.CompilerParams(vmem_limit_bytes=4 * MIB),
        name="half_of",
    )(which[None], whole)


def compact(values, core, got, mine_sig, got_sig, mine_to, got_to, width, tile, odd):
    half, rows = got.shape
    blocks = mine_sig.shape[0]
    if half % 16:
        values = lax.dynamic_slice_in_dim(values, core * half, half, 0)
    count = rows // tile + 2
    cuts = [(0, half)]

    def body(flags_ref, values_ref, got_ref, msig_ref, gsig_ref, mto_ref, gto_ref, *rest):
        outs, mine_ref, sem = rest[:-2], rest[-2], rest[-1]
        if values_ref.shape[0] != half:
            values_ref = values_ref.at[pl.ds(pl.multiple_of(flags_ref[1] * half, 16), half)]
        copy = pltpu.make_async_copy(values_ref, mine_ref, sem)
        copy.start()
        block_of = lax.broadcasted_iota(jnp.int32, (half, blocks), 0)
        begin = lax.broadcasted_iota(jnp.int32, (half, blocks), 1) * width
        spread = ((block_of >= begin) & (block_of < begin + width)).astype(F32).astype(BF16)
        slot = lax.broadcasted_iota(jnp.int32, (rows, count * tile), 1)

        def part(value_ref, sig_ref, to_ref):
            kept = jnp.dot(spread, sig_ref[...], preferred_element_type=F32)
            screened = (value_ref[...].astype(F32) * kept).astype(BF16)
            place = (to_ref[...] == slot).astype(F32).astype(BF16)
            return jnp.dot(screened, place, preferred_element_type=F32)

        window = part(got_ref, gsig_ref, gto_ref)
        copy.wait()
        window = window + part(mine_ref, msig_ref, mto_ref)
        tiles = [window[:, j * tile : (j + 1) * tile] for j in range(count)]
        even = flags_ref[0] == 0
        first, last = tiles[0], tiles[-1]
        tiles[0] = jnp.where(even, first, last)
        tiles[-1] = jnp.where(even, last, first)
        for p, (low, high) in enumerate(cuts):
            for j in range(count):
                outs[p * count + j][...] = tiles[j][low:high].astype(BF16)

    shapes = [
        jax.ShapeDtypeStruct((high - low, tile), BF16) for low, high in cuts for _ in range(count)
    ]
    out = pl.pallas_call(
        body,
        out_shape=shapes,
        in_specs=[SCALARS, pl.BlockSpec(memory_space=pl.ANY)] + [WHOLE] * 5,
        out_specs=[WHOLE] * len(shapes),
        scratch_shapes=[pltpu.VMEM((half, rows), BF16), pltpu.SemaphoreType.DMA],
        compiler_params=pltpu.CompilerParams(vmem_limit_bytes=10 * MIB),
        name="compact",
        cost_estimate=pl.CostEstimate(
            flops=8 * half * rows * rows, bytes_accessed=8 * half * rows, transcendentals=0
        ),
    )(jnp.stack((odd, core)), values, got, mine_sig, got_sig, mine_to, got_to)
    return [out[p * count : (p + 1) * count] for p in range(len(cuts))]


def straighten(tiles, by_b, by_a, odd):
    half, tile = by_a.shape
    count = len(tiles)

    def body(odd_ref, *refs):
        tile_refs, b_ref, a_ref, out_ref = refs[:count], *refs[count:]
        even = odd_ref[0] == 0
        for j in range(count):
            value = tile_refs[j][...]
            if j == 0:
                value = value + jnp.where(even, b_ref[...], a_ref[...])
            if j == count - 1:
                value = value + jnp.where(even, a_ref[...], b_ref[...])
            out_ref[:, j * tile : (j + 1) * tile] = value

    return pl.pallas_call(
        body,
        out_shape=jax.ShapeDtypeStruct((half, count * tile), BF16),
        in_specs=[SCALARS] + [WHOLE] * (count + 2),
        out_specs=WHOLE,
        compiler_params=pltpu.CompilerParams(vmem_limit_bytes=8 * MIB),
        name="straighten",
    )(odd[None], *tiles, by_b, by_a)


def panel_halves(occupied, trial, core):
    columns, cols = occupied.shape
    half = cols // 2
    width = -(-half // 128) * 128

    def body(core_ref, occupied_ref, trial_ref, mine_ref, other_ref):
        first = core_ref[0] == 0
        mine_ref[...] = jnp.zeros_like(mine_ref)
        other_ref[...] = jnp.zeros_like(other_ref)
        for j, ref in enumerate((occupied_ref, trial_ref)):
            low, high = ref[:, :half], ref[:, half:]
            mine_ref[j * columns : (j + 1) * columns, :half] = jnp.where(first, low, high)
            other_ref[j * columns : (j + 1) * columns, :half] = jnp.where(first, high, low)

    shape = jax.ShapeDtypeStruct((2 * columns, width), BF16)
    return pl.pallas_call(
        body,
        out_shape=(shape, shape),
        in_specs=[SCALARS, WHOLE, WHOLE],
        out_specs=(WHOLE, WHOLE),
        compiler_params=pltpu.CompilerParams(vmem_limit_bytes=8 * MIB),
        name="panel_halves",
    )(core[None], occupied, trial)


def stack_panels(mine, got, core):
    both, width = mine.shape
    columns = both // 2

    def body(core_ref, mine_ref, got_ref, out_ref):
        first = core_ref[0] == 0
        for j in range(2):
            low = mine_ref[j * columns : (j + 1) * columns]
            high = got_ref[j * columns : (j + 1) * columns]
            q = 2 * j * columns
            out_ref[q : q + columns] = jnp.where(first, low, high)
            out_ref[q + columns : q + 2 * columns] = jnp.where(first, high, low)

    return pl.pallas_call(
        body,
        out_shape=jax.ShapeDtypeStruct((2 * both, width), BF16),
        in_specs=[SCALARS, WHOLE, WHOLE],
        out_specs=WHOLE,
        compiler_params=pltpu.CompilerParams(vmem_limit_bytes=8 * MIB),
        name="stack_panels",
    )(core[None], mine, got)


def distinct(arrays):
    return list({id(x): x for x in arrays}.values())


def read_window(addends, p, arrays, refs):
    ref_of = {id(x): ref for x, ref in zip(arrays, refs)}
    total = None
    for x in addends:
        value = ref_of[id(x[p])][...]
        total = value if total is None else total + value
    return total


def split_sum(pairs, occ):
    _, shares, piece, both = pairs[0][0].shape
    tiles = sum(keep.shape[0] for keep, _ in pairs)

    def body(occ_ref, *refs):
        ins, outs = refs[: 2 * len(pairs)], refs[2 * len(pairs) :]
        for d in range(shares):
            at = 0
            for keep_ref, got_ref in zip(ins[::2], ins[1::2]):
                for q in range(keep_ref.shape[0]):
                    outs[d][at] = keep_ref[q, occ_ref[0] ^ d] + got_ref[q, occ_ref[0] ^ d]
                    at += 1

    shape = jax.ShapeDtypeStruct((tiles, piece, both), F32)
    return pl.pallas_call(
        body,
        out_shape=(shape,) * shares,
        in_specs=[SCALARS] + [WHOLE] * (2 * len(pairs)),
        out_specs=(WHOLE,) * shares,
        compiler_params=pltpu.CompilerParams(vmem_limit_bytes=8 * MIB),
        name="split_sum",
    )(occ[None], *sum(pairs, ()))


def project(jobs, tile, shares, core):
    both = jobs[0][0].shape[0]
    parts = [x.shape[0] for x in jobs[0][1][0]]
    rows = jobs[0][1][0][0].shape[1]
    half = sum(parts)
    piece = tile // shares
    tiles = len(jobs) * rows // tile
    panels = distinct([p for p, _ in jobs])
    arrays = distinct([x for _, window in jobs for addend in window for x in addend])
    count = len(panels)

    def body(core_ref, *refs):
        panel_refs, array_refs = refs[:count], refs[count:-3]
        keep_ref, give_ref, terms_ref = refs[-3:]
        q = 0
        for panel, window in jobs:
            panel_ref = panel_refs[[id(p) for p in panels].index(id(panel))]
            total, low = None, 0
            for p, size in enumerate(parts):
                value = read_window(window, p, arrays, array_refs)
                term = jnp.dot(
                    panel_ref[:, low : low + size], value, preferred_element_type=F32
                )
                total = term if total is None else total + term
                low += size
            turned = total.T
            for j in range(0, rows, tile):
                terms_ref[q] = turned[j : j + tile].reshape(2, shares // 2, piece, both)
                keep_ref[q] = terms_ref[q, core_ref[0]]
                give_ref[q] = terms_ref[q, 1 - core_ref[0]]
                q += 1

    shape = jax.ShapeDtypeStruct((tiles, shares // 2, piece, both), F32)
    return pl.pallas_call(
        body,
        out_shape=(shape, shape),
        in_specs=[SCALARS] + [WHOLE] * (count + len(arrays)),
        out_specs=(WHOLE, WHOLE),
        scratch_shapes=[pltpu.VMEM((tiles, 2, shares // 2, piece, both), F32)],
        compiler_params=pltpu.CompilerParams(vmem_limit_bytes=12 * MIB),
        name="project",
        cost_estimate=pl.CostEstimate(
            flops=2 * both * half * tiles * tile,
            bytes_accessed=2 * half * (both + tiles * tile) + 4 * tiles * tile * both,
            transcendentals=0,
        ),
    )(core[None], *panels, *arrays)


def in_order(parts, occ):
    tiles, _, piece, columns = parts[0].shape

    def body(occ_ref, *refs):
        for d in range(len(parts)):
            refs[-1][:, occ_ref[0] ^ d] = refs[d][:, 0]

    return pl.pallas_call(
        body,
        out_shape=jax.ShapeDtypeStruct((tiles, len(parts), piece, columns), parts[0].dtype),
        in_specs=[SCALARS] + [WHOLE] * len(parts),
        out_specs=WHOLE,
        compiler_params=pltpu.CompilerParams(vmem_limit_bytes=4 * MIB),
        name="in_order",
    )(occ[None], *parts)


def contract(kernel, got, windows, core):
    tiles, shares, piece, columns = kernel.shape
    parts = [x.shape[0] for x in windows[0][0]]
    rows = windows[0][0][0].shape[1]
    half = sum(parts)
    own = columns // 2
    arrays = distinct([x for window in windows for addend in window for x in addend])
    per_window = tiles // len(windows)

    def body(core_ref, kernel_ref, got_ref, *refs):
        array_refs = refs[:-3]
        mine_ref, other_ref, order_ref = refs[-3:]
        first = core_ref[0] == 0
        order_ref[:, core_ref[0]] = kernel_ref[...].astype(F32)
        order_ref[:, 1 - core_ref[0]] = got_ref[...].astype(F32)
        kernels = [
            order_ref[s * per_window : (s + 1) * per_window].reshape(rows, columns).astype(BF16)
            for s in range(len(windows))
        ]
        low = 0
        for p, size in enumerate(parts):
            total = None
            for window, part in zip(windows, kernels):
                value = read_window(window, p, arrays, array_refs)
                term = jnp.dot(value, part, preferred_element_type=F32)
                total = term if total is None else total + term
            total = total.T
            mine_ref[:, low : low + size] = jnp.where(first, total[:own], total[own:])
            other_ref[:, low : low + size] = jnp.where(first, total[own:], total[:own])
            low += size

    shape = jax.ShapeDtypeStruct((own, half), F32)
    return pl.pallas_call(
        body,
        out_shape=(shape, shape),
        in_specs=[SCALARS] + [WHOLE] * (2 + len(arrays)),
        out_specs=(WHOLE, WHOLE),
        scratch_shapes=[pltpu.VMEM((tiles, 2, shares, piece, columns), F32)],
        compiler_params=pltpu.CompilerParams(vmem_limit_bytes=20 * MIB),
        name="contract",
        cost_estimate=pl.CostEstimate(
            flops=2 * columns * half * rows * len(windows),
            bytes_accessed=2 * rows * len(windows) * half + 4 * columns * half,
            transcendentals=0,
        ),
    )(core[None], kernel, got, *arrays)


def unwritten(shape):
    def body(out_ref):
        pass

    return pl.pallas_call(
        body,
        out_shape=jax.ShapeDtypeStruct(shape, F32),
        out_specs=pl.BlockSpec(memory_space=pltpu.HBM),
        name="unwritten",
    )()


def finish(core, fits, ours, back, other, scale):
    own, half = ours.shape

    def body(flags_ref, ours_ref, back_ref, other_ref, out_ref, whole_ref, sem):
        @pl.when(flags_ref[1] != 0)
        def _():
            first = flags_ref[0] == 0
            whole_ref[:, :half] = jnp.where(first, ours_ref[...], back_ref[...]) * scale
            whole_ref[:, half:] = jnp.where(first, back_ref[...], ours_ref[...]) * scale
            copy = pltpu.make_async_copy(whole_ref, out_ref, sem)
            copy.start()
            copy.wait()

    return pl.pallas_call(
        body,
        out_shape=jax.ShapeDtypeStruct((own, 2 * half), F32),
        in_specs=[SCALARS, WHOLE, WHOLE, pl.BlockSpec(memory_space=pltpu.HBM)],
        out_specs=pl.BlockSpec(memory_space=pltpu.HBM),
        scratch_shapes=[pltpu.VMEM((own, 2 * half), F32), pltpu.SemaphoreType.DMA],
        input_output_aliases={3: 0},
        compiler_params=pltpu.CompilerParams(vmem_limit_bytes=8 * MIB),
        name="finish",
    )(jnp.stack((core, fits.astype(jnp.int32))), ours, back, other)


def per_device(orbital_values, occupied, trial, point_weights, batch_sizes, significant):
    rows, cols = orbital_values.shape
    batches = batch_sizes.shape[0]
    slots = rows // batches
    blocks = significant.shape[1]
    columns = occupied.shape[1]
    grid_count = lax.axis_size("grid")
    occ_count = lax.axis_size("occ")
    chips = grid_count // 2
    shares = 2 * occ_count
    half = cols // 2
    total = columns * grid_count
    place = lax.axis_index("grid")
    chip, core = place // 2, place % 2
    occ = lax.axis_index("occ")
    member = core * occ_count + occ

    def flip(x, axis, bit):
        count = lax.axis_size(axis)
        return lax.ppermute(x, axis, [(i, i ^ bit) for i in range(count)])

    def along(pairs):
        return [(2 * a + c, 2 * b + c) for a, b in pairs for c in range(2)]

    def doubled(x, axis, bit, dim):
        got = flip(x, axis, bit)
        mine = (lax.axis_index(axis) & bit) == 0
        return jnp.where(
            mine, jnp.concatenate((x, got), axis=dim), jnp.concatenate((got, x), axis=dim)
        )

    def halves(whole, axis):
        size = whole.shape[axis] // 2
        mine = lax.dynamic_slice_in_dim(whole, core * size, size, axis)
        return mine, lax.dynamic_slice_in_dim(whole, (1 - core) * size, size, axis)

    grid_bits = [1 << b for b in range(grid_count.bit_length() - 1)]
    occ_bits = [1 << b for b in range(occ_count.bit_length() - 1)]

    got = flip(half_of(orbital_values.T, 1 - core), "grid", 1)
    mine_sig, other_sig = halves(significant.T, 0)
    got_sig = flip(other_sig, "grid", 1)

    told = jnp.concatenate(
        (
            doubled(batch_sizes[None], "grid", 1, 0).astype(F32).reshape(1, -1),
            doubled(point_weights[None], "grid", 1, 0).reshape(1, -1),
        ),
        axis=1,
    )
    live = rows * chips
    for bit in grid_bits[1:2]:
        told = doubled(told, "grid", bit, 0)
    if chips > 4:
        for bit in grid_bits[2:]:
            told = doubled(told, "grid", bit, 0)

    def places_of(sizes, upper):
        count = sizes.shape[0]
        batch = lax.broadcasted_iota(jnp.int32, (count, count), 0)
        before = lax.broadcasted_iota(jnp.int32, (count, count), 1) < batch
        start = upper * live + jnp.sum((before.astype(jnp.int32) - upper) * sizes[None, :], axis=1)
        position = lax.broadcasted_iota(jnp.int32, (count, slots), 1)
        to = jnp.where(position < sizes[:, None], start[:, None] + position, -4 * live)
        return to.reshape(-1, rows), start

    sizes = told[:, : 2 * batches].astype(jnp.int32).reshape(-1)
    near_to, _ = places_of(sizes, chip // 2 if chips <= 4 else 0)
    near_place = place if chips > 4 else place % 4
    margin = rows // 2 if (rows // 2) % (8 * shares) == 0 else rows
    tile = margin
    piece = tile // shares
    base = rows * chip - margin
    mine_to = lax.dynamic_index_in_dim(near_to, near_place, 0, keepdims=False) - base
    got_to = lax.dynamic_index_in_dim(near_to, near_place ^ 1, 0, keepdims=False) - base
    odd = chip % 2
    compacted = compact(
        orbital_values.T,
        core,
        got,
        jnp.repeat(mine_sig.astype(BF16), slots, axis=1),
        jnp.repeat(got_sig.astype(BF16), slots, axis=1),
        mine_to[:, None],
        got_to[:, None],
        cols // blocks,
        tile,
        odd,
    )

    told, _ = lax.optimization_barrier((told, compacted))
    for bit in grid_bits[2:] if chips <= 4 else []:
        told = doubled(told, "grid", bit, 0)
    sizes = told[:, : 2 * batches].astype(jnp.int32).reshape(-1)
    weights = told[:, 2 * batches :].reshape(-1)
    to, start = places_of(sizes, 0)
    first = start.reshape(chips, -1)[:, 0]
    nominal = rows * lax.iota(jnp.int32, chips)
    fits = jnp.all(jnp.abs(first - nominal) <= margin) & (jnp.sum(sizes) == live)

    per_window = rows // tile
    window_iota = lax.iota(jnp.int32, chips)
    at = (
        (window_iota * rows)[:, None, None]
        + (lax.iota(jnp.int32, per_window) * tile)[None, :, None]
        + member * piece
        + lax.iota(jnp.int32, piece)[None, None, :]
    ).reshape(-1, 1)
    weight = jnp.sum(jnp.where(to.reshape(1, -1) == at, weights[None, :], 0.0), axis=1)
    weight = weight.reshape(chips, per_window * piece)
    def sent(x, pairs):
        return lax.ppermute(x, "grid", along(pairs))

    last = chips - 1

    def over(links, t):
        pairs = []
        for a in range(links, last, 2):
            pairs += [(a, a + 1)] if a - t + 1 >= 0 else []
            pairs += [(a + 1, a)] if a + t <= last else []
        return pairs

    arrived = [
        (sent(for_b, over(1, 1)), sent(for_a, over(0, 1))) for for_b, *_, for_a in compacted
    ]
    own = tuple(
        straighten(tiles, by_b, by_a, odd)
        for (_, *tiles, _), (by_b, by_a) in zip(compacted, arrived)
    )

    own, fits, weight = lax.optimization_barrier((own, fits.astype(jnp.int32), weight))

    _, occupied_turned, trial_turned = lax.optimization_barrier(
        (compacted[0][0], occupied.T, trial.T)
    )
    mine_panel, other_panel = panel_halves(occupied_turned, trial_turned, core)
    panels = stack_panels(mine_panel, flip(other_panel, "grid", 1), core)

    ends = [(0, 1), (last, last - 1)]
    homes = [(b, a) for a, b in ends]
    side = 1 - 2 * odd

    def valid(at):
        return jnp.where((at >= 0) & (at <= last), at, -1)

    stages = [[([own], chip)]]
    by_a = by_b = own
    far_panels = None
    for t in range(1, last):
        by_a, by_b = (
            tuple(sent(x, over(0, t)) for x in by_b),
            tuple(sent(x, over(1, t)) for x in by_a),
        )
        if t == 1:
            far_panels = sent(panels, ends)
        a_at, b_at = valid(chip + side * t), valid(chip - side * t)
        if 2 * t > last:
            stages.append([([by_a, by_b], jnp.maximum(a_at, b_at))])
        else:
            stages.append([([by_a], a_at), ([by_b], b_at)])

    direct = occ_count <= 4
    points = per_window * piece

    def summed(pairs):
        if direct:
            parts = split_sum(pairs, occ)
            value = parts[0]
            for d in range(1, occ_count):
                value = value + flip(parts[d], "occ", d)
        else:
            value = jnp.concatenate([keep + got for keep, got in pairs])
            for bit in reversed(occ_bits):
                upper = (occ & bit) != 0
                low_part, high_part = value[:, :bit], value[:, bit:]
                got = flip(jnp.where(upper, low_part, high_part), "occ", bit)
                value = jnp.where(upper, high_part, low_part) + got
        return value.reshape(-1, points, 4 * columns)

    def shared_density(value, at):
        product = jnp.sum(value[:, :, : 2 * columns] * value[:, :, 2 * columns :], axis=2)
        here = (at[:, None] == window_iota[None, :])[:, :, None]
        return jnp.sum(jnp.where(here, product[:, None], 0.0), axis=0)

    early_jobs, late_jobs = sum(stages[1:-1], []), stages[-1]
    early_at = jnp.stack([at for _, at in early_jobs])
    late_at = late_jobs[0][1][None]
    early_jobs = stages[0] + early_jobs
    early_at = jnp.concatenate((chip[None], early_at))

    keep, give = project([(panels, w) for w, _ in early_jobs], tile, shares, core)
    early_value = summed([(keep, flip(give, "grid", 1))])

    outer = jnp.where(chip == 0, last, jnp.where(chip == last, 0, early_at[2]))
    places = jnp.concatenate((early_at[:2], outer[None], early_at[3:], late_at))
    here = (places[:, None] == window_iota[None, :])[:, :, None]
    weight_here = jnp.sum(jnp.where(here, weight[None], 0.0), axis=1)[:, :, None]

    late, by_a, early_value, far_panels, weight_here, fits = lax.optimization_barrier(
        (by_b, by_a, early_value, far_panels, weight_here, fits)
    )
    fits = fits != 0
    late = tuple(sent(x, homes) for x in late)
    late_window = [by_a, by_b]
    late_jobs = [(panels, late_window), (far_panels, [by_b])]

    def kernel_of_all():
        late_pair = project(late_jobs, tile, shares, core)
        keep, give = late_pair
        value = jnp.concatenate((early_value, summed([(keep, flip(give, "grid", 1))])))
        density = shared_density(value, jnp.concatenate((early_at, late_at, late_at)))
        value, far_value = value[:-1], value[-1:]
        packed = jnp.concatenate(
            (far_value[0], jnp.pad(density, ((0, 0), (0, 4 * columns - points)))), axis=0
        )
        packed = flip(packed, "grid", 2)
        home_value, neighbour = packed[None, :points], packed[points:, :points]
        if chips <= 4:
            others = [flip(density, "grid", 2 * d) for d in range(2, chips)]
            density = density + neighbour + sum(others[1:], others[0])
        else:
            density = density + neighbour
            for bit in grid_bits[2:]:
                density = density + flip(density, "grid", bit)
        density = density * (1.0 / math.sqrt(total))

        values = jnp.concatenate((value[:2], value[2:3] + home_value, value[3:]))
        density_here = jnp.sum(jnp.where(here, density[None], 0.0), axis=1)[:, :, None]
        orbitals, response = values[:, :, : 2 * columns], values[:, :, 2 * columns :]
        kernel = (weight_here * (density_here * orbitals + response)).astype(BF16)
        kernel = kernel.reshape(-1, 1, piece, 2 * columns)
        if direct:
            parts = [kernel] + [flip(kernel, "occ", d) for d in range(1, occ_count)]
            kernel = in_order(parts, occ)
        else:
            for bit in occ_bits:
                kernel = doubled(kernel, "occ", bit, 1)
        return kernel, flip(kernel, "grid", 1), unwritten((columns, cols))

    scale = 1.0 / math.sqrt(rows * grid_count)

    def result_for_any_sizes():
        whole = any_sizes(
            orbital_values, occupied, trial, point_weights, batch_sizes, significant
        )
        none = jnp.zeros((places.shape[0] * per_window, occ_count, piece, 2 * columns), BF16)
        return none, none, whole * scale

    kernel, got_kernel, other = lax.cond(fits, kernel_of_all, result_for_any_sizes)
    early_windows = [w for w, _ in early_jobs]
    early_windows[2] = early_windows[2] + [late]
    windows = early_windows + [late_window]
    ours, theirs = contract(kernel, got_kernel, windows, core)
    back = flip(theirs, "grid", 1)
    return finish(core, fits, ours, back, other, scale).T


def solution(mesh):
    placed = (
        P("grid", "occ"),
        P("occ", "grid"),
        P("occ", "grid"),
        P("grid"),
        P("grid"),
        P("grid", "occ"),
    )
    return jax.shard_map(
        per_device, mesh=mesh, in_specs=placed, out_specs=P("occ", "grid"), check_vma=False
    )
```

```python
import math

import jax
import jax.numpy as jnp
from jax import lax
from jax.experimental import pallas as pl
from jax.experimental.pallas import tpu as pltpu
from jax.sharding import PartitionSpec as P

BF16, F32 = jnp.bfloat16, jnp.float32
MIB = 1024 * 1024
WHOLE = pl.BlockSpec(memory_space=pltpu.VMEM)
SCALARS = pl.BlockSpec(memory_space=pltpu.SMEM)


def screen(values, sizes, significant):
    rows, cols = values.shape
    batches = sizes.shape[0]
    blocks = significant.shape[1]
    blocked = (
        values.reshape(batches, rows // batches, blocks, cols // blocks)
        * significant.astype(values.dtype)[:, None, :, None]
    )
    position = lax.broadcasted_iota(jnp.int32, (batches, rows // batches), 1)
    live = (position < sizes[:, None]).astype(jnp.float32).reshape(rows)
    return (blocked.reshape(rows, cols), live)


def any_sizes(orbital_values, occupied, trial, point_weights, batch_sizes, significant):
    screened, live = screen(orbital_values, batch_sizes, significant)
    rows, cols = screened.shape
    grid_count, occ_count = lax.axis_size("grid"), lax.axis_size("occ")
    columns = occupied.shape[1]
    me = lax.axis_index("grid")
    ring = [(i, (i + 1) % grid_count) for i in range(grid_count)]
    occ_ring = [(i, (i + 1) % occ_count) for i in range(occ_count)]

    def project_one(step, carry):
        panel, terms = carry
        term = jnp.dot(screened, panel, preferred_element_type=F32)
        terms = lax.dynamic_update_index_in_dim(terms, term, (me - step) % grid_count, 0)
        return lax.ppermute(panel, "grid", ring), terms

    joined = jnp.concatenate((occupied, trial), axis=1)
    terms = jnp.zeros((grid_count, rows, 2 * columns), F32)
    terms = lax.fori_loop(0, grid_count, project_one, (joined, terms))[1]

    def add_one(step, carry):
        moving, held = carry
        moving = lax.ppermute(moving, "occ", occ_ring)
        return moving, held + moving

    terms = lax.fori_loop(0, occ_count - 1, add_one, (terms, terms))[1]
    orbitals, response = terms[:, :, :columns], terms[:, :, columns:]
    density = jnp.sum(orbitals * response, axis=(0, 2)) * (1.0 / math.sqrt(columns * grid_count))
    weight = (point_weights * live)[None, :, None]
    kernel = (weight * (density[None, :, None] * orbitals + response)).astype(BF16)

    def contract_one(step, held):
        owner = (me + grid_count - 1 - step) % grid_count
        part = lax.dynamic_index_in_dim(kernel, owner, 0, keepdims=False)
        term = lax.dot_general(
            part, screened, (((0,), (0,)), ((), ())), preferred_element_type=F32
        )
        return lax.ppermute(held, "grid", ring) + term

    return lax.fori_loop(0, grid_count, contract_one, jnp.zeros((columns, cols), F32))


def half_of(whole, which):
    rows, columns = whole.shape
    half = rows // 2
    if half % 16:
        return lax.dynamic_slice_in_dim(whole, which * half, half, 0)

    def body(which_ref, whole_ref, out_ref, sem):
        first = pl.multiple_of(which_ref[0] * half, 16)
        copy = pltpu.make_async_copy(whole_ref.at[pl.ds(first, half)], out_ref, sem)
        copy.start()
        copy.wait()

    return pl.pallas_call(
        body,
        out_shape=jax.ShapeDtypeStruct((half, columns), whole.dtype),
        in_specs=[SCALARS, pl.BlockSpec(memory_space=pl.ANY)],
        out_specs=WHOLE,
        scratch_shapes=[pltpu.SemaphoreType.DMA],
        compiler_params=pltpu.CompilerParams(vmem_limit_bytes=4 * MIB),
        name="half_of",
    )(which[None], whole)


def compact(values, core, got, mine_sig, got_sig, mine_to, got_to, width, tile, odd):
    half, rows = got.shape
    blocks = mine_sig.shape[0]
    if half % 16:
        values = lax.dynamic_slice_in_dim(values, core * half, half, 0)
    count = rows // tile + 2
    cuts = [(0, half)]

    def body(flags_ref, values_ref, got_ref, msig_ref, gsig_ref, mto_ref, gto_ref, *rest):
        outs, mine_ref, sem = rest[:-2], rest[-2], rest[-1]
        if values_ref.shape[0] != half:
            values_ref = values_ref.at[pl.ds(pl.multiple_of(flags_ref[1] * half, 16), half)]
        copy = pltpu.make_async_copy(values_ref, mine_ref, sem)
        copy.start()
        block_of = lax.broadcasted_iota(jnp.int32, (half, blocks), 0)
        begin = lax.broadcasted_iota(jnp.int32, (half, blocks), 1) * width
        spread = ((block_of >= begin) & (block_of < begin + width)).astype(F32).astype(BF16)
        slot = lax.broadcasted_iota(jnp.int32, (rows, count * tile), 1)

        def part(value_ref, sig_ref, to_ref):
            kept = jnp.dot(spread, sig_ref[...], preferred_element_type=F32)
            screened = (value_ref[...].astype(F32) * kept).astype(BF16)
            place = (to_ref[...] == slot).astype(F32).astype(BF16)
            return jnp.dot(screened, place, preferred_element_type=F32)

        window = part(got_ref, gsig_ref, gto_ref)
        copy.wait()
        window = window + part(mine_ref, msig_ref, mto_ref)
        tiles = [window[:, j * tile : (j + 1) * tile] for j in range(count)]
        even = flags_ref[0] == 0
        first, last = tiles[0], tiles[-1]
        tiles[0] = jnp.where(even, first, last)
        tiles[-1] = jnp.where(even, last, first)
        for p, (low, high) in enumerate(cuts):
            for j in range(count):
                outs[p * count + j][...] = tiles[j][low:high].astype(BF16)

    shapes = [
        jax.ShapeDtypeStruct((high - low, tile), BF16) for low, high in cuts for _ in range(count)
    ]
    out = pl.pallas_call(
        body,
        out_shape=shapes,
        in_specs=[SCALARS, pl.BlockSpec(memory_space=pl.ANY)] + [WHOLE] * 5,
        out_specs=[WHOLE] * len(shapes),
        scratch_shapes=[pltpu.VMEM((half, rows), BF16), pltpu.SemaphoreType.DMA],
        compiler_params=pltpu.CompilerParams(vmem_limit_bytes=10 * MIB),
        name="compact",
        cost_estimate=pl.CostEstimate(
            flops=8 * half * rows * rows, bytes_accessed=8 * half * rows, transcendentals=0
        ),
    )(jnp.stack((odd, core)), values, got, mine_sig, got_sig, mine_to, got_to)
    return [out[p * count : (p + 1) * count] for p in range(len(cuts))]


def straighten(tiles, by_b, by_a, odd):
    half, tile = by_a.shape
    count = len(tiles)

    def body(odd_ref, *refs):
        tile_refs, b_ref, a_ref, out_ref = refs[:count], *refs[count:]
        even = odd_ref[0] == 0
        for j in range(count):
            value = tile_refs[j][...]
            if j == 0:
                value = value + jnp.where(even, b_ref[...], a_ref[...])
            if j == count - 1:
                value = value + jnp.where(even, a_ref[...], b_ref[...])
            out_ref[:, j * tile : (j + 1) * tile] = value

    return pl.pallas_call(
        body,
        out_shape=jax.ShapeDtypeStruct((half, count * tile), BF16),
        in_specs=[SCALARS] + [WHOLE] * (count + 2),
        out_specs=WHOLE,
        compiler_params=pltpu.CompilerParams(vmem_limit_bytes=8 * MIB),
        name="straighten",
    )(odd[None], *tiles, by_b, by_a)


def panel_halves(occupied, trial, core):
    columns, cols = occupied.shape
    half = cols // 2
    width = -(-half // 128) * 128

    def body(core_ref, occupied_ref, trial_ref, mine_ref, other_ref):
        first = core_ref[0] == 0
        mine_ref[...] = jnp.zeros_like(mine_ref)
        other_ref[...] = jnp.zeros_like(other_ref)
        for j, ref in enumerate((occupied_ref, trial_ref)):
            low, high = ref[:, :half], ref[:, half:]
            mine_ref[j * columns : (j + 1) * columns, :half] = jnp.where(first, low, high)
            other_ref[j * columns : (j + 1) * columns, :half] = jnp.where(first, high, low)

    shape = jax.ShapeDtypeStruct((2 * columns, width), BF16)
    return pl.pallas_call(
        body,
        out_shape=(shape, shape),
        in_specs=[SCALARS, WHOLE, WHOLE],
        out_specs=(WHOLE, WHOLE),
        compiler_params=pltpu.CompilerParams(vmem_limit_bytes=8 * MIB),
        name="panel_halves",
    )(core[None], occupied, trial)


def stack_panels(mine, got, core):
    both, width = mine.shape
    columns = both // 2

    def body(core_ref, mine_ref, got_ref, out_ref):
        first = core_ref[0] == 0
        for j in range(2):
            low = mine_ref[j * columns : (j + 1) * columns]
            high = got_ref[j * columns : (j + 1) * columns]
            q = 2 * j * columns
            out_ref[q : q + columns] = jnp.where(first, low, high)
            out_ref[q + columns : q + 2 * columns] = jnp.where(first, high, low)

    return pl.pallas_call(
        body,
        out_shape=jax.ShapeDtypeStruct((2 * both, width), BF16),
        in_specs=[SCALARS, WHOLE, WHOLE],
        out_specs=WHOLE,
        compiler_params=pltpu.CompilerParams(vmem_limit_bytes=8 * MIB),
        name="stack_panels",
    )(core[None], mine, got)


def distinct(arrays):
    return list({id(x): x for x in arrays}.values())


def read_window(addends, p, arrays, refs):
    ref_of = {id(x): ref for x, ref in zip(arrays, refs)}
    total = None
    for x in addends:
        value = ref_of[id(x[p])][...]
        total = value if total is None else total + value
    return total


def split_sum(pairs, occ):
    _, shares, piece, both = pairs[0][0].shape
    tiles = sum(keep.shape[0] for keep, _ in pairs)

    def body(occ_ref, *refs):
        ins, outs = refs[: 2 * len(pairs)], refs[2 * len(pairs) :]
        for d in range(shares):
            at = 0
            for keep_ref, got_ref in zip(ins[::2], ins[1::2]):
                for q in range(keep_ref.shape[0]):
                    outs[d][at] = keep_ref[q, occ_ref[0] ^ d] + got_ref[q, occ_ref[0] ^ d]
                    at += 1

    shape = jax.ShapeDtypeStruct((tiles, piece, both), F32)
    return pl.pallas_call(
        body,
        out_shape=(shape,) * shares,
        in_specs=[SCALARS] + [WHOLE] * (2 * len(pairs)),
        out_specs=(WHOLE,) * shares,
        compiler_params=pltpu.CompilerParams(vmem_limit_bytes=8 * MIB),
        name="split_sum",
    )(occ[None], *sum(pairs, ()))


def project(jobs, tile, shares, core):
    both = jobs[0][0].shape[0]
    parts = [x.shape[0] for x in jobs[0][1][0]]
    rows = jobs[0][1][0][0].shape[1]
    half = sum(parts)
    piece = tile // shares
    tiles = len(jobs) * rows // tile
    panels = distinct([p for p, _ in jobs])
    arrays = distinct([x for _, window in jobs for addend in window for x in addend])
    count = len(panels)

    def body(core_ref, *refs):
        panel_refs, array_refs = refs[:count], refs[count:-3]
        keep_ref, give_ref, terms_ref = refs[-3:]
        q = 0
        for panel, window in jobs:
            panel_ref = panel_refs[[id(p) for p in panels].index(id(panel))]
            total, low = None, 0
            for p, size in enumerate(parts):
                value = read_window(window, p, arrays, array_refs)
                term = jnp.dot(
                    panel_ref[:, low : low + size], value, preferred_element_type=F32
                )
                total = term if total is None else total + term
                low += size
            turned = total.T
            for j in range(0, rows, tile):
                terms_ref[q] = turned[j : j + tile].reshape(2, shares // 2, piece, both)
                keep_ref[q] = terms_ref[q, core_ref[0]]
                give_ref[q] = terms_ref[q, 1 - core_ref[0]]
                q += 1

    shape = jax.ShapeDtypeStruct((tiles, shares // 2, piece, both), F32)
    return pl.pallas_call(
        body,
        out_shape=(shape, shape),
        in_specs=[SCALARS] + [WHOLE] * (count + len(arrays)),
        out_specs=(WHOLE, WHOLE),
        scratch_shapes=[pltpu.VMEM((tiles, 2, shares // 2, piece, both), F32)],
        compiler_params=pltpu.CompilerParams(vmem_limit_bytes=12 * MIB),
        name="project",
        cost_estimate=pl.CostEstimate(
            flops=2 * both * half * tiles * tile,
            bytes_accessed=2 * half * (both + tiles * tile) + 4 * tiles * tile * both,
            transcendentals=0,
        ),
    )(core[None], *panels, *arrays)


def in_order(parts, occ):
    tiles, _, piece, columns = parts[0].shape

    def body(occ_ref, *refs):
        for d in range(len(parts)):
            refs[-1][:, occ_ref[0] ^ d] = refs[d][:, 0]

    return pl.pallas_call(
        body,
        out_shape=jax.ShapeDtypeStruct((tiles, len(parts), piece, columns), parts[0].dtype),
        in_specs=[SCALARS] + [WHOLE] * len(parts),
        out_specs=WHOLE,
        compiler_params=pltpu.CompilerParams(vmem_limit_bytes=4 * MIB),
        name="in_order",
    )(occ[None], *parts)


def contract(kernel, got, windows, core, fetched):
    tiles, shares, piece, columns = kernel.shape
    parts = [x.shape[0] for x in windows[0][0]]
    rows = windows[0][0][0].shape[1]
    half = sum(parts)
    own = columns // 2
    arrays = distinct([x for window in windows for addend in window for x in addend])
    per_window = tiles // len(windows)
    coming = [i for i, x in enumerate(arrays) if any(x is y for y in fetched)]

    def body(core_ref, kernel_ref, got_ref, *refs):
        array_refs = list(refs[: len(arrays)])
        mine_ref, other_ref, order_ref, *held, sems = refs[len(arrays) :]
        copies = {}
        for n, i in enumerate(coming):
            copies[i] = pltpu.make_async_copy(array_refs[i], held[n], sems.at[n])
            copies[i].start()
            array_refs[i] = held[n]
        first = core_ref[0] == 0
        order_ref[:, core_ref[0]] = kernel_ref[...].astype(F32)
        order_ref[:, 1 - core_ref[0]] = got_ref[...].astype(F32)
        kernels = [
            order_ref[s * per_window : (s + 1) * per_window].reshape(rows, columns).astype(BF16)
            for s in range(len(windows))
        ]
        low = 0
        for p, size in enumerate(parts):
            total = None
            for window, part in zip(windows, kernels):
                for i in [i for i in copies if any(arrays[i] is x[p] for x in window)]:
                    copies.pop(i).wait()
                value = read_window(window, p, arrays, array_refs)
                term = jnp.dot(value, part, preferred_element_type=F32)
                total = term if total is None else total + term
            total = total.T
            mine_ref[:, low : low + size] = jnp.where(first, total[:own], total[own:])
            other_ref[:, low : low + size] = jnp.where(first, total[own:], total[:own])
            low += size

    shape = jax.ShapeDtypeStruct((own, half), F32)
    return pl.pallas_call(
        body,
        out_shape=(shape, shape),
        in_specs=[SCALARS, WHOLE, WHOLE]
        + [
            pl.BlockSpec(memory_space=pl.ANY) if i in coming else WHOLE for i in range(len(arrays))
        ],
        out_specs=(WHOLE, WHOLE),
        scratch_shapes=[pltpu.VMEM((tiles, 2, shares, piece, columns), F32)]
        + [pltpu.VMEM(arrays[i].shape, BF16) for i in coming]
        + [pltpu.SemaphoreType.DMA((len(coming),))],
        compiler_params=pltpu.CompilerParams(vmem_limit_bytes=20 * MIB),
        name="contract",
        cost_estimate=pl.CostEstimate(
            flops=2 * columns * half * rows * len(windows),
            bytes_accessed=2 * rows * len(windows) * half + 4 * columns * half,
            transcendentals=0,
        ),
    )(core[None], kernel, got, *arrays)


def unwritten(shape):
    def body(out_ref):
        pass

    return pl.pallas_call(
        body,
        out_shape=jax.ShapeDtypeStruct(shape, F32),
        out_specs=pl.BlockSpec(memory_space=pltpu.HBM),
        name="unwritten",
    )()


def finish(core, fits, ours, back, other, scale):
    own, half = ours.shape

    def body(flags_ref, ours_ref, back_ref, other_ref, out_ref, whole_ref, sem):
        @pl.when(flags_ref[1] != 0)
        def _():
            first = flags_ref[0] == 0
            whole_ref[:, :half] = jnp.where(first, ours_ref[...], back_ref[...]) * scale
            whole_ref[:, half:] = jnp.where(first, back_ref[...], ours_ref[...]) * scale
            copy = pltpu.make_async_copy(whole_ref, out_ref, sem)
            copy.start()
            copy.wait()

    return pl.pallas_call(
        body,
        out_shape=jax.ShapeDtypeStruct((own, 2 * half), F32),
        in_specs=[SCALARS, WHOLE, WHOLE, pl.BlockSpec(memory_space=pltpu.HBM)],
        out_specs=pl.BlockSpec(memory_space=pltpu.HBM),
        scratch_shapes=[pltpu.VMEM((own, 2 * half), F32), pltpu.SemaphoreType.DMA],
        input_output_aliases={3: 0},
        compiler_params=pltpu.CompilerParams(vmem_limit_bytes=8 * MIB),
        name="finish",
    )(jnp.stack((core, fits.astype(jnp.int32))), ours, back, other)


def per_device(orbital_values, occupied, trial, point_weights, batch_sizes, significant):
    rows, cols = orbital_values.shape
    batches = batch_sizes.shape[0]
    slots = rows // batches
    blocks = significant.shape[1]
    columns = occupied.shape[1]
    grid_count = lax.axis_size("grid")
    occ_count = lax.axis_size("occ")
    chips = grid_count // 2
    shares = 2 * occ_count
    half = cols // 2
    total = columns * grid_count
    place = lax.axis_index("grid")
    chip, core = place // 2, place % 2
    occ = lax.axis_index("occ")
    member = core * occ_count + occ

    def flip(x, axis, bit):
        count = lax.axis_size(axis)
        return lax.ppermute(x, axis, [(i, i ^ bit) for i in range(count)])

    def along(pairs):
        return [(2 * a + c, 2 * b + c) for a, b in pairs for c in range(2)]

    def doubled(x, axis, bit, dim):
        got = flip(x, axis, bit)
        mine = (lax.axis_index(axis) & bit) == 0
        return jnp.where(
            mine, jnp.concatenate((x, got), axis=dim), jnp.concatenate((got, x), axis=dim)
        )

    def halves(whole, axis):
        size = whole.shape[axis] // 2
        mine = lax.dynamic_slice_in_dim(whole, core * size, size, axis)
        return mine, lax.dynamic_slice_in_dim(whole, (1 - core) * size, size, axis)

    grid_bits = [1 << b for b in range(grid_count.bit_length() - 1)]
    occ_bits = [1 << b for b in range(occ_count.bit_length() - 1)]

    got = flip(half_of(orbital_values.T, 1 - core), "grid", 1)
    mine_sig, other_sig = halves(significant.T, 0)
    got_sig = flip(other_sig, "grid", 1)

    told = jnp.concatenate(
        (
            doubled(batch_sizes[None], "grid", 1, 0).astype(F32).reshape(1, -1),
            doubled(point_weights[None], "grid", 1, 0).reshape(1, -1),
        ),
        axis=1,
    )
    live = rows * chips
    for bit in grid_bits[1:2]:
        told = doubled(told, "grid", bit, 0)
    if chips > 4:
        for bit in grid_bits[2:]:
            told = doubled(told, "grid", bit, 0)

    def places_of(sizes, upper):
        count = sizes.shape[0]
        batch = lax.broadcasted_iota(jnp.int32, (count, count), 0)
        before = lax.broadcasted_iota(jnp.int32, (count, count), 1) < batch
        start = upper * live + jnp.sum((before.astype(jnp.int32) - upper) * sizes[None, :], axis=1)
        position = lax.broadcasted_iota(jnp.int32, (count, slots), 1)
        to = jnp.where(position < sizes[:, None], start[:, None] + position, -4 * live)
        return to.reshape(-1, rows), start

    sizes = told[:, : 2 * batches].astype(jnp.int32).reshape(-1)
    near_to, _ = places_of(sizes, chip // 2 if chips <= 4 else 0)
    near_place = place if chips > 4 else place % 4
    margin = rows // 2 if (rows // 2) % (8 * shares) == 0 else rows
    tile = margin
    piece = tile // shares
    base = rows * chip - margin
    mine_to = lax.dynamic_index_in_dim(near_to, near_place, 0, keepdims=False) - base
    got_to = lax.dynamic_index_in_dim(near_to, near_place ^ 1, 0, keepdims=False) - base
    odd = chip % 2
    compacted = compact(
        orbital_values.T,
        core,
        got,
        jnp.repeat(mine_sig.astype(BF16), slots, axis=1),
        jnp.repeat(got_sig.astype(BF16), slots, axis=1),
        mine_to[:, None],
        got_to[:, None],
        cols // blocks,
        tile,
        odd,
    )

    told, _ = lax.optimization_barrier((told, compacted))
    for bit in grid_bits[2:] if chips <= 4 else []:
        told = doubled(told, "grid", bit, 0)
    sizes = told[:, : 2 * batches].astype(jnp.int32).reshape(-1)
    weights = told[:, 2 * batches :].reshape(-1)
    to, start = places_of(sizes, 0)
    first = start.reshape(chips, -1)[:, 0]
    nominal = rows * lax.iota(jnp.int32, chips)
    fits = jnp.all(jnp.abs(first - nominal) <= margin) & (jnp.sum(sizes) == live)

    per_window = rows // tile
    window_iota = lax.iota(jnp.int32, chips)
    at = (
        (window_iota * rows)[:, None, None]
        + (lax.iota(jnp.int32, per_window) * tile)[None, :, None]
        + member * piece
        + lax.iota(jnp.int32, piece)[None, None, :]
    ).reshape(-1, 1)
    weight = jnp.sum(jnp.where(to.reshape(1, -1) == at, weights[None, :], 0.0), axis=1)
    weight = weight.reshape(chips, per_window * piece)
    def sent(x, pairs):
        return lax.ppermute(x, "grid", along(pairs))

    last = chips - 1

    def over(links, t):
        pairs = []
        for a in range(links, last, 2):
            pairs += [(a, a + 1)] if a - t + 1 >= 0 else []
            pairs += [(a + 1, a)] if a + t <= last else []
        return pairs

    arrived = [
        (sent(for_b, over(1, 1)), sent(for_a, over(0, 1))) for for_b, *_, for_a in compacted
    ]
    own = tuple(
        straighten(tiles, by_b, by_a, odd)
        for (_, *tiles, _), (by_b, by_a) in zip(compacted, arrived)
    )

    own, fits, weight = lax.optimization_barrier((own, fits.astype(jnp.int32), weight))

    _, occupied_turned, trial_turned = lax.optimization_barrier(
        (compacted[0][0], occupied.T, trial.T)
    )
    mine_panel, other_panel = panel_halves(occupied_turned, trial_turned, core)
    panels = stack_panels(mine_panel, flip(other_panel, "grid", 1), core)

    ends = [(0, 1), (last, last - 1)]
    homes = [(b, a) for a, b in ends]
    side = 1 - 2 * odd

    def valid(at):
        return jnp.where((at >= 0) & (at <= last), at, -1)

    stages = [[([own], chip)]]
    by_a = by_b = own
    far_panels = None
    for t in range(1, last):
        by_a, by_b = (
            tuple(sent(x, over(0, t)) for x in by_b),
            tuple(sent(x, over(1, t)) for x in by_a),
        )
        if t == 1:
            far_panels = sent(panels, ends)
        a_at, b_at = valid(chip + side * t), valid(chip - side * t)
        if 2 * t > last:
            stages.append([([by_a, by_b], jnp.maximum(a_at, b_at))])
        else:
            stages.append([([by_a], a_at), ([by_b], b_at)])

    direct = occ_count <= 4
    points = per_window * piece

    def summed(pairs):
        if direct:
            parts = split_sum(pairs, occ)
            value = parts[0]
            for d in range(1, occ_count):
                value = value + flip(parts[d], "occ", d)
        else:
            value = jnp.concatenate([keep + got for keep, got in pairs])
            for bit in reversed(occ_bits):
                upper = (occ & bit) != 0
                low_part, high_part = value[:, :bit], value[:, bit:]
                got = flip(jnp.where(upper, low_part, high_part), "occ", bit)
                value = jnp.where(upper, high_part, low_part) + got
        return value.reshape(-1, points, 4 * columns)

    def shared_density(value, at):
        product = jnp.sum(value[:, :, : 2 * columns] * value[:, :, 2 * columns :], axis=2)
        here = (at[:, None] == window_iota[None, :])[:, :, None]
        return jnp.sum(jnp.where(here, product[:, None], 0.0), axis=0)

    early_jobs, late_jobs = sum(stages[1:-1], []), stages[-1]
    early_at = jnp.stack([at for _, at in early_jobs])
    late_at = late_jobs[0][1][None]
    early_jobs = stages[0] + early_jobs
    early_at = jnp.concatenate((chip[None], early_at))

    keep, give = project([(panels, w) for w, _ in early_jobs], tile, shares, core)
    early_value = summed([(keep, flip(give, "grid", 1))])

    outer = jnp.where(chip == 0, last, jnp.where(chip == last, 0, early_at[2]))
    places = jnp.concatenate((early_at[:2], outer[None], early_at[3:], late_at))
    here = (places[:, None] == window_iota[None, :])[:, :, None]
    weight_here = jnp.sum(jnp.where(here, weight[None], 0.0), axis=1)[:, :, None]

    late, by_a, early_value, far_panels, weight_here, fits = lax.optimization_barrier(
        (by_b, by_a, early_value, far_panels, weight_here, fits)
    )
    fits = fits != 0
    late = tuple(sent(x, homes) for x in late)
    late_window = [by_a, by_b]
    late_jobs = [(panels, late_window), (far_panels, [by_b])]

    def kernel_of_all():
        late_pair = project(late_jobs, tile, shares, core)
        keep, give = late_pair
        value = jnp.concatenate((early_value, summed([(keep, flip(give, "grid", 1))])))
        density = shared_density(value, jnp.concatenate((early_at, late_at, late_at)))
        value, far_value = value[:-1], value[-1:]
        packed = jnp.concatenate(
            (far_value[0], jnp.pad(density, ((0, 0), (0, 4 * columns - points)))), axis=0
        )
        packed = flip(packed, "grid", 2)
        home_value, neighbour = packed[None, :points], packed[points:, :points]
        if chips <= 4:
            others = [flip(density, "grid", 2 * d) for d in range(2, chips)]
            density = density + neighbour + sum(others[1:], others[0])
        else:
            density = density + neighbour
            for bit in grid_bits[2:]:
                density = density + flip(density, "grid", bit)
        density = density * (1.0 / math.sqrt(total))

        values = jnp.concatenate((value[:2], value[2:3] + home_value, value[3:]))
        density_here = jnp.sum(jnp.where(here, density[None], 0.0), axis=1)[:, :, None]
        orbitals, response = values[:, :, : 2 * columns], values[:, :, 2 * columns :]
        kernel = (weight_here * (density_here * orbitals + response)).astype(BF16)
        kernel = kernel.reshape(-1, 1, piece, 2 * columns)
        if direct:
            parts = [kernel] + [flip(kernel, "occ", d) for d in range(1, occ_count)]
            kernel = in_order(parts, occ)
        else:
            for bit in occ_bits:
                kernel = doubled(kernel, "occ", bit, 1)
        return kernel, flip(kernel, "grid", 1), unwritten((columns, cols))

    scale = 1.0 / math.sqrt(rows * grid_count)

    def result_for_any_sizes():
        whole = any_sizes(
            orbital_values, occupied, trial, point_weights, batch_sizes, significant
        )
        none = jnp.zeros((places.shape[0] * per_window, occ_count, piece, 2 * columns), BF16)
        return none, none, whole * scale

    kernel, got_kernel, other = lax.cond(fits, kernel_of_all, result_for_any_sizes)
    early_windows = [w for w, _ in early_jobs]
    early_windows[2] = early_windows[2] + [late]
    windows = early_windows + [late_window]
    ours, theirs = contract(kernel, got_kernel, windows, core, late + by_a + by_b)
    back = flip(theirs, "grid", 1)
    return finish(core, fits, ours, back, other, scale).T


def solution(mesh):
    placed = (
        P("grid", "occ"),
        P("occ", "grid"),
        P("occ", "grid"),
        P("grid"),
        P("grid"),
        P("grid", "occ"),
    )
    return jax.shard_map(
        per_device, mesh=mesh, in_specs=placed, out_specs=P("occ", "grid"), check_vma=False
    )
```
